32 devices in a mesh: groups: 2 (over y), seq: 8 (over z, x), head: 2 (over core).
Axes of the slice: x: 2, y: 2, z: 4, core: 2. Of those that a mesh axis runs over, the one named last changes fastest.
Arguments:
- queries: bfloat16 [2048, 64, 128], P(('groups', 'seq'), 'head'), parts along dimension 0, may hold values from -200 to 200
- keys: bfloat16 [2048, 8, 128], P(('groups', 'seq'), 'head'), parts along dimension 0, may hold values from -6 to 6
- values: bfloat16 [2048, 8, 128], P(('groups', 'seq'), 'head'), parts along dimension 0, may hold values from -6 to 6
- chosen: int32 [16, 4], P('groups'), parts along dimension 0, may hold values from -1 to 7, as said below
Outputs:
- attended: bfloat16 [2048, 64, 128], P(('groups', 'seq'), 'head'), parts along dimension 0
The draws below stay inside these ranges and needn't reach their ends.
There are 2 independent parts, one for each index of `groups`. The reference program is written for one: setup_inputs(seed, part) draws one part's arguments, and reference() takes and returns one part's arrays. A program takes and returns all parts, laid end to end along the dimension named above; each array names one. Nothing has to cross between parts.
Inputs may be any that keep to these rules, and one draw needn't show every extreme that they name: `chosen`: row b lists block b itself and min(3, b) distinct earlier blocks, in any order; its other entries are -1.
All inputs are finite; a program needn't handle non-finite values.
Results may differ from the reference program's by a relative error of at most 0.0033.
Values may be sent and summed in bfloat16 or wider, within the bound.
No kernel may reach another device: no remote copies, remote signals or barrier semaphores. Data moves between devices by JAX's collectives and lax.ppermute only.
A program may use at most 64 MiB of HBM per device.

```python
import jax
import jax.numpy as jnp
from jax import lax

HEADS = 64
KV_HEADS = 8
HEAD_DIM = 128
BLOCK = 128
PICKS = 4
NBLK = 8
TOKENS = 1024


def base_keys(key):
    drawn_keys = jax.random.normal(key, (TOKENS, KV_HEADS, HEAD_DIM), jnp.float32)
    return jnp.clip(drawn_keys, -6.0, 6.0)


def draw_keys(key, part):
    drawn_keys = base_keys(key)
    return drawn_keys.astype(jnp.bfloat16)


def draw_queries(key, part):
    key = jax.random.fold_in(key, 13)
    result = 1.5 * jax.random.normal(key, (TOKENS, HEADS, HEAD_DIM), jnp.float32)
    return jnp.clip(result, -9.0, 9.0).astype(jnp.bfloat16)


def draw_chosen(key, part):
    key = jax.random.fold_in(key, 7)
    key_noise, key_heat, key_order = jax.random.split(key, 3)
    source = jnp.arange(NBLK, dtype=jnp.int32)[None, :]
    target = jnp.arange(NBLK, dtype=jnp.int32)[:, None]
    noise = jax.random.randint(key_noise, (NBLK, NBLK), 0, 2 ** 20, dtype=jnp.int32)
    heat = jax.random.randint(key_heat, (NBLK,), 0, 2 ** 21, dtype=jnp.int32)
    heat = jnp.where(jnp.arange(NBLK) < 8, heat, 0)[None, :]
    ranking_score = (noise + heat) * NBLK + source
    ranking_score = jnp.where(source < target, ranking_score, jnp.where(source == target, 2 ** 30, -1 - source))
    top_values, top_index = lax.top_k(ranking_score, PICKS)
    selected = jnp.where(top_values < 0, -1, top_index).astype(jnp.int32)
    shuffle = jax.random.randint(key_order, (NBLK, PICKS), 0, 2 ** 20, dtype=jnp.int32) * PICKS + jnp.arange(PICKS, dtype=jnp.int32)[None, :]
    ranking = jnp.argsort(shuffle, axis=1, stable=True)
    return jnp.take_along_axis(selected, ranking, axis=1)


def block_levels(key, shape, cuts, smallest, largest):
    def one(axis_at, blocks):
        draws = jax.random.uniform(jax.random.fold_in(jax.random.fold_in(key, 6), axis_at), (blocks,), jnp.float32, smallest / len(cuts), largest / len(cuts))
        return jnp.repeat(jnp.exp(draws), shape[axis_at] // blocks).reshape((-1,) + (1,) * (len(shape) - axis_at - 1))

    factor_of = one(*cuts[0])
    for cut in cuts[1:]:
        factor_of = factor_of * one(*cut)
    return factor_of


def normal_values(own_key, shape, width, limit, pieces=(), kind=jnp.bfloat16):
    level = block_levels(own_key, shape, pieces, -0.22, 0.18) if pieces else 1.0
    drawn = jax.random.normal(own_key, shape, jnp.float32) * width * level
    return jnp.minimum(jnp.maximum(drawn, -limit), limit).astype(kind)


def setup_inputs(seed: int = 0, part: int = 0) -> dict:
    key_of = jax.random.split(jax.random.key(seed), 5)
    part_splits = jax.random.split(jax.random.fold_in(key_of[4], part), 5)
    return {
        "queries": draw_queries(jax.random.fold_in(jax.random.fold_in(key_of[4], part), 71), part),
        "keys": draw_keys(jax.random.fold_in(jax.random.fold_in(key_of[4], part), 71), part),
        "values": normal_values(part_splits[2], (TOKENS, KV_HEADS, HEAD_DIM), 1.0, 6.0, ((0, 8), (1, 2))),
        "chosen": draw_chosen(jax.random.fold_in(jax.random.fold_in(key_of[4], part), 71), part),
    }


def partial_block(grouped, key_block, value_block, slot_code, score_scale):
    scores = jnp.einsum('qkgd,jkd->kgqj', grouped, key_block) * score_scale
    query_rows = jnp.arange(grouped.shape[0])[:, None]
    key_rows = jnp.arange(key_block.shape[0])[None, :]
    allowed = (slot_code == 0) | ((slot_code == 1) & (key_rows <= query_rows))
    maxima = jnp.max(jnp.where(allowed, scores, -1e30), axis=-1)
    probs = jnp.where(allowed, jnp.exp(scores - maxima[..., None]), 0.0).astype(jnp.bfloat16)
    wide_probs = probs.astype(jnp.float32)
    totals = jnp.sum(wide_probs, axis=-1)
    partial_value = jnp.einsum('kgqj,jkd->qkgd', wide_probs, value_block)
    return partial_value, maxima, totals


def combine(partial_value, maxima, totals):
    top = jnp.max(maxima, axis=0)
    weights = jnp.exp(maxima - top)
    denominator = jnp.sum(weights * totals, axis=0)
    numerator = jnp.sum(jnp.transpose(weights, (0, 3, 1, 2))[..., None] * partial_value, axis=0)
    return numerator / jnp.transpose(denominator, (2, 0, 1))[..., None]


def reference(queries, keys, values, chosen):
    group_size = HEADS // KV_HEADS
    score_scale = HEAD_DIM ** -0.5

    def one_block(target):
        start = (target * BLOCK).astype(jnp.int32)
        grouped = lax.dynamic_slice_in_dim(queries, start, BLOCK, 0).astype(jnp.float32)
        grouped = grouped.reshape(BLOCK, KV_HEADS, group_size, HEAD_DIM)

        def one_slot(source):
            slot_code = jnp.where(source < 0, 2, jnp.where(source == target, 1, 0))
            begin = (jnp.maximum(source, 0) * BLOCK).astype(jnp.int32)
            key_block = lax.dynamic_slice_in_dim(keys, begin, BLOCK, 0).astype(jnp.float32)
            value_block = lax.dynamic_slice_in_dim(values, begin, BLOCK, 0).astype(jnp.float32)
            return partial_block(grouped, key_block, value_block, slot_code, score_scale)

        partial_value, maxima, totals = lax.map(one_slot, chosen[target])
        merged = combine(partial_value, maxima, totals)
        return merged.reshape(BLOCK, HEADS, HEAD_DIM).astype(jnp.bfloat16)

    result = lax.map(one_block, jnp.arange(NBLK, dtype=jnp.int32))
    return result.reshape(TOKENS, HEADS, HEAD_DIM)
```

```python
import functools
import math

import jax
import jax.numpy as jnp
from jax import lax
from jax.experimental import pallas as pl
from jax.experimental.pallas import tpu as pltpu
from jax.sharding import PartitionSpec as P

NO_KEY = -1e30
ROW_CHUNK = 256


def attend_kernel(
    listed_ref, q_ref, k_own_ref, v_own_ref, k_all_ref, v_all_ref, out_ref,
    k_buf, v_buf, k_wide, v_wide, sems, *, kv_dev, slots,
):
    tokens, heads, dim = q_ref.shape
    group = heads // kv_dev
    block = tokens * kv_dev
    target = listed_ref[slots]
    own_at = jnp.int32(0)
    for j in range(slots):
        own_at = jnp.where(listed_ref[j] == target, j, own_at)
    copies = []
    bias = []
    for j in range(slots - 1):
        source = listed_ref[jnp.where(j >= own_at, j + 1, j)]
        bias.append(jnp.where(source < 0, NO_KEY, 0.0).astype(jnp.float32))
        begin = pl.multiple_of(jnp.maximum(source, 0) * block, block)
        for n, (whole, buf) in enumerate(((k_all_ref, k_buf), (v_all_ref, v_buf))):
            copy = pltpu.make_async_copy(
                whole.at[pl.ds(begin, block), :],
                buf.at[pl.ds(j * block, block), :],
                sems.at[n, j],
            )
            copy.start()
            copies.append(copy)
    k_wide[pl.ds(0, block), :] = k_own_ref[...].astype(jnp.float32)
    v_wide[pl.ds(0, block), :] = v_own_ref[...].astype(jnp.float32)
    for copy in copies:
        copy.wait()
    rest = (slots - 1) * block
    k_wide[pl.ds(block, rest), :] = k_buf[...].astype(jnp.float32)
    v_wide[pl.ds(block, rest), :] = v_buf[...].astype(jnp.float32)

    factor = dim ** (-0.5) * math.log2(math.e)
    keys = slots * tokens
    ones = jnp.ones((keys, dim), jnp.bfloat16)
    chunk_tokens = ROW_CHUNK // group
    for h in range(kv_dev):
        k_h = k_wide[pl.ds(h, keys, stride=kv_dev), :].astype(jnp.bfloat16)
        v_h = v_wide[pl.ds(h, keys, stride=kv_dev), :].astype(jnp.bfloat16)
        v_ones = jnp.concatenate([v_h, ones], axis=1)
        for first in range(0, tokens, chunk_tokens):
            q = q_ref[pl.ds(first, chunk_tokens), pl.ds(h * group, group), :]
            q = q.astype(jnp.float32).reshape(ROW_CHUNK, dim).astype(jnp.bfloat16)
            s = lax.dot_general(
                q, k_h, (((1,), (1,)), ((), ())), preferred_element_type=jnp.float32
            )
            row = lax.broadcasted_iota(jnp.int32, (ROW_CHUNK, tokens), 0) // group + first
            key = lax.broadcasted_iota(jnp.int32, (ROW_CHUNK, tokens), 1)
            parts = [jnp.where(key <= row, s[:, :tokens], NO_KEY)]
            for j in range(1, slots):
                parts.append(s[:, j * tokens : (j + 1) * tokens] + bias[j - 1])
            top = parts[0]
            for part in parts[1:]:
                top = jnp.maximum(top, part)
            top = jnp.max(top, axis=1, keepdims=True)
            probs = jnp.concatenate(
                [jnp.exp2((part - top) * factor).astype(jnp.bfloat16) for part in parts], axis=1
            )
            both = jnp.dot(probs, v_ones, preferred_element_type=jnp.float32)
            merged = both[:, :dim] / both[:, dim:]
            out_ref[pl.ds(first, chunk_tokens), pl.ds(h * group, group), :] = (
                merged.reshape(chunk_tokens, group, dim).astype(jnp.bfloat16)
            )


def attend(listed, queries, k_own, v_own, k_all, v_all, kv_dev, slots):
    block, dim = k_own.shape
    rest = (slots - 1) * block
    vmem = pl.BlockSpec(memory_space=pltpu.VMEM)
    hbm = pl.BlockSpec(memory_space=pl.ANY)
    return pl.pallas_call(
        functools.partial(attend_kernel, kv_dev=kv_dev, slots=slots),
        out_shape=jax.ShapeDtypeStruct(queries.shape, jnp.bfloat16),
        in_specs=[pl.BlockSpec(memory_space=pltpu.SMEM), vmem, vmem, vmem, hbm, hbm],
        out_specs=vmem,
        scratch_shapes=[
            pltpu.VMEM((rest, dim), jnp.bfloat16),
            pltpu.VMEM((rest, dim), jnp.bfloat16),
            pltpu.VMEM((slots * block, dim), jnp.float32),
            pltpu.VMEM((slots * block, dim), jnp.float32),
            pltpu.SemaphoreType.DMA((2, slots - 1)),
        ],
        compiler_params=pltpu.CompilerParams(vmem_limit_bytes=32 * 2**20),
        name="attend",
    )(listed, queries, k_own, v_own, k_all, v_all)


def per_device(queries, keys, values, chosen):
    tokens, kv_dev, dim = keys.shape
    slots = chosen.shape[1]
    target = lax.axis_index("seq").astype(jnp.int32)
    listed = jnp.concatenate([lax.dynamic_index_in_dim(chosen, target, 0, False), target[None]])
    k_own = keys.reshape(tokens * kv_dev, dim)
    v_own = values.reshape(tokens * kv_dev, dim)
    k_all = lax.all_gather(k_own, "seq", axis=0, tiled=True)
    v_all = lax.all_gather(v_own, "seq", axis=0, tiled=True)
    return attend(listed, queries, k_own, v_own, k_all, v_all, kv_dev, slots)


def solution(mesh):
    rows = P(("groups", "seq"), "head", None)
    return jax.shard_map(
        per_device,
        mesh=mesh,
        in_specs=(rows, rows, rows, P("groups", None)),
        out_specs=rows,
        check_vma=False,
    )
```

```python
import functools
import math

import jax
import jax.numpy as jnp
from jax import lax
from jax.experimental import pallas as pl
from jax.experimental.pallas import tpu as pltpu
from jax.sharding import PartitionSpec as P

NO_KEY = -1e30
ROW_CHUNK = 256
PAIR = 2
MOST_CLIMBED = 16


def attend_kernel(
    listed_ref, q_ref, k_own_ref, v_own_ref, *refs, kv_dev, slots, choices,
):
    k_refs, v_refs = refs[:choices], refs[choices : 2 * choices]
    out_ref, k_buf, v_buf, k_wide, v_wide, sems = refs[2 * choices :]
    tokens, heads, dim = q_ref.shape
    group = heads // kv_dev
    block = tokens * kv_dev
    bias = []
    for j in range(slots - 1):
        source = listed_ref[j]
        bias.append(jnp.where(source < 0, NO_KEY, 0.0).astype(jnp.float32))
        for i in range(choices):

            @pl.when(jnp.maximum(source, 0) == i)
            def _start(i=i, j=j):
                for n, (parts, buf) in enumerate(((k_refs, k_buf), (v_refs, v_buf))):
                    pltpu.make_async_copy(
                        parts[i], buf.at[pl.ds(j * block, block), :], sems.at[n, j]
                    ).start()

    k_wide[pl.ds(0, block), :] = k_own_ref[...].astype(jnp.float32)
    v_wide[pl.ds(0, block), :] = v_own_ref[...].astype(jnp.float32)
    for j in range(slots - 1):
        for n, (parts, buf) in enumerate(((k_refs, k_buf), (v_refs, v_buf))):
            pltpu.make_async_copy(
                parts[0], buf.at[pl.ds(j * block, block), :], sems.at[n, j]
            ).wait()
    rest = (slots - 1) * block
    k_wide[pl.ds(block, rest), :] = k_buf[...].astype(jnp.float32)
    v_wide[pl.ds(block, rest), :] = v_buf[...].astype(jnp.float32)

    factor = dim ** (-0.5) * math.log2(math.e)
    keys = slots * tokens
    ones = jnp.ones((keys, dim), jnp.bfloat16)
    chunk_tokens = ROW_CHUNK // group
    for h in range(kv_dev):
        k_h = k_wide[pl.ds(h, keys, stride=kv_dev), :].astype(jnp.bfloat16)
        v_h = v_wide[pl.ds(h, keys, stride=kv_dev), :].astype(jnp.bfloat16)
        v_ones = jnp.concatenate([v_h, ones], axis=1)
        for first in range(0, tokens, chunk_tokens):
            q = q_ref[pl.ds(first, chunk_tokens), pl.ds(h * group, group), :]
            q = q.astype(jnp.float32).reshape(ROW_CHUNK, dim).astype(jnp.bfloat16)
            s = lax.dot_general(
                q, k_h, (((1,), (1,)), ((), ())), preferred_element_type=jnp.float32
            )
            row = lax.broadcasted_iota(jnp.int32, (ROW_CHUNK, tokens), 0) // group + first
            key = lax.broadcasted_iota(jnp.int32, (ROW_CHUNK, tokens), 1)
            parts = [jnp.where(key <= row, s[:, :tokens], NO_KEY)]
            for j in range(1, slots):
                parts.append(s[:, j * tokens : (j + 1) * tokens] + bias[j - 1])
            top = parts[0]
            for part in parts[1:]:
                top = jnp.maximum(top, part)
            top = jnp.max(top, axis=1, keepdims=True)
            probs = jnp.concatenate(
                [jnp.exp2((part - top) * factor).astype(jnp.bfloat16) for part in parts], axis=1
            )
            both = jnp.dot(probs, v_ones, preferred_element_type=jnp.float32)
            merged = both[:, :dim] / both[:, dim:]
            out_ref[pl.ds(first, chunk_tokens), pl.ds(h * group, group), :] = (
                merged.reshape(chunk_tokens, group, dim).astype(jnp.bfloat16)
            )


def attend(listed, queries, k_own, v_own, k_parts, v_parts, kv_dev, slots):
    block, dim = k_own.shape
    rest = (slots - 1) * block
    choices = len(k_parts)
    vmem = pl.BlockSpec(memory_space=pltpu.VMEM)
    hbm = pl.BlockSpec(memory_space=pltpu.HBM)
    return pl.pallas_call(
        functools.partial(attend_kernel, kv_dev=kv_dev, slots=slots, choices=choices),
        out_shape=jax.ShapeDtypeStruct(queries.shape, jnp.bfloat16),
        in_specs=[pl.BlockSpec(memory_space=pltpu.SMEM), vmem, vmem, vmem] + [hbm] * (2 * choices),
        out_specs=vmem,
        scratch_shapes=[
            pltpu.VMEM((rest, dim), jnp.bfloat16),
            pltpu.VMEM((rest, dim), jnp.bfloat16),
            pltpu.VMEM((slots * block, dim), jnp.float32),
            pltpu.VMEM((slots * block, dim), jnp.float32),
            pltpu.SemaphoreType.DMA((2, slots - 1)),
        ],
        compiler_params=pltpu.CompilerParams(vmem_limit_bytes=32 * 2**20),
        name="attend",
    )(listed, queries, k_own, v_own, *k_parts, *v_parts)


def others(row, target):
    slots = row.shape[-1]
    own_at = jnp.argmax(row == target[..., None], axis=-1)
    j = jnp.arange(slots - 1)
    return jnp.where(j >= own_at[..., None], row[..., 1:], row[..., :-1])


def climb(own, members):
    same = [own]
    for step in range(1, members // PAIR):
        up = [(s, s + PAIR) for s in range((step - 1) * PAIR, members - PAIR)]
        same.append(lax.ppermute(same[-1], "seq", up))
    crossed = [
        lax.ppermute(part, "seq", [(s, s ^ 1) for s in range(step * PAIR, members)])
        for step, part in enumerate(same)
    ]
    return same[1:] + crossed


def relay(own, chosen, members):
    block, dim = own[0].shape
    stacked = jnp.stack(own).reshape(len(own), members, block // members, dim)
    shares = lax.all_to_all(stacked, "seq", split_axis=1, concat_axis=1, tiled=True)
    wanted = jnp.maximum(others(chosen, jnp.arange(members, dtype=jnp.int32)), 0)
    picked = jnp.take(shares, wanted, axis=1)
    arrived = lax.all_to_all(picked, "seq", split_axis=1, concat_axis=3, tiled=True)
    return arrived.reshape(len(own), wanted.shape[1], block, dim)


def per_device(queries, keys, values, chosen):
    members = lax.axis_size("seq")
    tokens, kv_dev, dim = keys.shape
    slots = chosen.shape[1]
    target = lax.axis_index("seq").astype(jnp.int32)
    listed = others(lax.dynamic_index_in_dim(chosen, target, 0, False), target)
    k_own = keys.reshape(tokens * kv_dev, dim)
    v_own = values.reshape(tokens * kv_dev, dim)
    if members <= MOST_CLIMBED:
        k_parts, v_parts = climb(k_own, members), climb(v_own, members)
        steps = target // PAIR - listed // PAIR
        crossed = (target ^ listed) & 1
        at = steps - 1 + crossed * (members // PAIR)
    else:
        arrived = relay((k_own, v_own), chosen, members)
        k_parts, v_parts = ([arrived[n, j] for j in range(slots - 1)] for n in range(2))
        at = jnp.arange(slots - 1, dtype=jnp.int32)
    at = jnp.where(listed < 0, -1, at)
    return attend(at, queries, k_own, v_own, k_parts, v_parts, kv_dev, slots)


def solution(mesh):
    rows = P(("groups", "seq"), "head", None)
    return jax.shard_map(
        per_device,
        mesh=mesh,
        in_specs=(rows, rows, rows, P("groups", None)),
        out_specs=rows,
        check_vma=False,
    )
```

```python
import functools
import math

import jax
import jax.numpy as jnp
from jax import lax
from jax.experimental import pallas as pl
from jax.experimental.pallas import tpu as pltpu
from jax.sharding import PartitionSpec as P

NO_KEY = -1e30
ROW_CHUNK = 256
PAIR = 2
MOST_CLIMBED = 16


def prepare_kernel(q_ref, k_ref, v_ref, q_out, k_out, v_out, k_wide, v_wide, *, kv_dev):
    tokens, heads, dim = q_ref.shape
    group = heads // kv_dev
    k_wide[...] = k_ref[...].astype(jnp.float32)
    v_wide[...] = v_ref[...].astype(jnp.float32)
    for h in range(kv_dev):
        q = q_ref[:, pl.ds(h * group, group), :].astype(jnp.float32)
        q_out[h] = q.reshape(tokens * group, dim).astype(jnp.bfloat16)
        k_out[h] = k_wide[pl.ds(h, tokens, stride=kv_dev), :].astype(jnp.bfloat16)
        v_out[h] = v_wide[pl.ds(h, tokens, stride=kv_dev), :].astype(jnp.bfloat16)


def prepare(queries, k_own, v_own, kv_dev):
    tokens, heads, dim = queries.shape
    vmem = pl.BlockSpec(memory_space=pltpu.VMEM)
    by_head = jax.ShapeDtypeStruct((kv_dev, tokens, dim), jnp.bfloat16)
    return pl.pallas_call(
        functools.partial(prepare_kernel, kv_dev=kv_dev),
        out_shape=(
            jax.ShapeDtypeStruct((kv_dev, tokens * heads // kv_dev, dim), jnp.bfloat16),
            by_head,
            by_head,
        ),
        in_specs=[vmem] * 3,
        out_specs=(vmem, vmem, vmem),
        scratch_shapes=[pltpu.VMEM(k_own.shape, jnp.float32)] * 2,
        compiler_params=pltpu.CompilerParams(vmem_limit_bytes=32 * 2**20),
        name="prepare",
    )(queries, k_own, v_own)


def attend_kernel(
    listed_ref, q_ref, k_own_ref, v_own_ref, *refs, slots, choices,
):
    k_refs, v_refs = refs[:choices], refs[choices : 2 * choices]
    out_ref, k_buf, v_buf, k_wide, v_wide, sems = refs[2 * choices :]
    kv_dev, tokens, dim = k_own_ref.shape
    group = q_ref.shape[1] // tokens
    block = tokens * kv_dev
    bias = []
    for j in range(slots - 1):
        source = listed_ref[j]
        bias.append(jnp.where(source < 0, NO_KEY, 0.0).astype(jnp.float32))
        for i in range(choices):

            @pl.when(jnp.maximum(source, 0) == i)
            def _start(i=i, j=j):
                for n, (parts, buf) in enumerate(((k_refs, k_buf), (v_refs, v_buf))):
                    pltpu.make_async_copy(
                        parts[i], buf.at[pl.ds(j * block, block), :], sems.at[n, j]
                    ).start()

    for j in range(slots - 1):
        for n, (parts, buf) in enumerate(((k_refs, k_buf), (v_refs, v_buf))):
            pltpu.make_async_copy(
                parts[0], buf.at[pl.ds(j * block, block), :], sems.at[n, j]
            ).wait()
    k_wide[...] = k_buf[...].astype(jnp.float32)
    v_wide[...] = v_buf[...].astype(jnp.float32)

    factor = dim ** (-0.5) * math.log2(math.e)
    rest = (slots - 1) * tokens
    ones = jnp.ones((slots * tokens, dim), jnp.bfloat16)
    chunk_tokens = ROW_CHUNK // group
    for h in range(kv_dev):
        k_h = k_wide[pl.ds(h, rest, stride=kv_dev), :].astype(jnp.bfloat16)
        v_h = v_wide[pl.ds(h, rest, stride=kv_dev), :].astype(jnp.bfloat16)
        k_h = jnp.concatenate([k_own_ref[h], k_h], axis=0)
        v_h = jnp.concatenate([v_own_ref[h], v_h], axis=0)
        v_ones = jnp.concatenate([v_h, ones], axis=1)
        for first in range(0, tokens, chunk_tokens):
            q = q_ref[h, pl.ds(first * group, ROW_CHUNK), :]
            s = lax.dot_general(
                q, k_h, (((1,), (1,)), ((), ())), preferred_element_type=jnp.float32
            )
            row = lax.broadcasted_iota(jnp.int32, (ROW_CHUNK, tokens), 0) // group + first
            key = lax.broadcasted_iota(jnp.int32, (ROW_CHUNK, tokens), 1)
            parts = [jnp.where(key <= row, s[:, :tokens], NO_KEY)]
            for j in range(1, slots):
                parts.append(s[:, j * tokens : (j + 1) * tokens] + bias[j - 1])
            top = parts[0]
            for part in parts[1:]:
                top = jnp.maximum(top, part)
            top = jnp.max(top, axis=1, keepdims=True)
            probs = jnp.concatenate(
                [jnp.exp2((part - top) * factor).astype(jnp.bfloat16) for part in parts], axis=1
            )
            both = jnp.dot(probs, v_ones, preferred_element_type=jnp.float32)
            merged = both[:, :dim] / both[:, dim:]
            out_ref[pl.ds(first, chunk_tokens), pl.ds(h * group, group), :] = (
                merged.reshape(chunk_tokens, group, dim).astype(jnp.bfloat16)
            )


def attend(listed, queries, k_own, v_own, k_parts, v_parts, slots):
    kv_dev, tokens, dim = k_own.shape
    heads = queries.shape[0] * queries.shape[1] // tokens
    rest = (slots - 1) * tokens * kv_dev
    choices = len(k_parts)
    vmem = pl.BlockSpec(memory_space=pltpu.VMEM)
    hbm = pl.BlockSpec(memory_space=pltpu.HBM)
    return pl.pallas_call(
        functools.partial(attend_kernel, slots=slots, choices=choices),
        out_shape=jax.ShapeDtypeStruct((tokens, heads, dim), jnp.bfloat16),
        in_specs=[pl.BlockSpec(memory_space=pltpu.SMEM), vmem, vmem, vmem] + [hbm] * (2 * choices),
        out_specs=vmem,
        scratch_shapes=[
            pltpu.VMEM((rest, dim), jnp.bfloat16),
            pltpu.VMEM((rest, dim), jnp.bfloat16),
            pltpu.VMEM((rest, dim), jnp.float32),
            pltpu.VMEM((rest, dim), jnp.float32),
            pltpu.SemaphoreType.DMA((2, slots - 1)),
        ],
        compiler_params=pltpu.CompilerParams(vmem_limit_bytes=32 * 2**20),
        name="attend",
    )(listed, queries, k_own, v_own, *k_parts, *v_parts)


def others(row, target):
    slots = row.shape[-1]
    own_at = jnp.argmax(row == target[..., None], axis=-1)
    j = jnp.arange(slots - 1)
    return jnp.where(j >= own_at[..., None], row[..., 1:], row[..., :-1])


def climb(own, members):
    up = [(s, (s + PAIR) % members) for s in range(members)]
    across = [(s, s ^ 1) for s in range(members)]
    same = [own]
    for _ in range(1, members // PAIR):
        same.append(lax.ppermute(same[-1], "seq", up))
    return same[1:] + [lax.ppermute(part, "seq", across) for part in same]


def relay(own, chosen, members):
    block, dim = own[0].shape
    stacked = jnp.stack(own).reshape(len(own), members, block // members, dim)
    shares = lax.all_to_all(stacked, "seq", split_axis=1, concat_axis=1, tiled=True)
    wanted = jnp.maximum(others(chosen, jnp.arange(members, dtype=jnp.int32)), 0)
    picked = jnp.take(shares, wanted, axis=1)
    arrived = lax.all_to_all(picked, "seq", split_axis=1, concat_axis=3, tiled=True)
    return arrived.reshape(len(own), wanted.shape[1], block, dim)


def per_device(queries, keys, values, chosen):
    members = lax.axis_size("seq")
    tokens, kv_dev, dim = keys.shape
    slots = chosen.shape[1]
    target = lax.axis_index("seq").astype(jnp.int32)
    listed = others(lax.dynamic_index_in_dim(chosen, target, 0, False), target)
    k_own = keys.reshape(tokens * kv_dev, dim)
    v_own = values.reshape(tokens * kv_dev, dim)
    if members <= MOST_CLIMBED:
        k_parts, v_parts = climb(k_own, members), climb(v_own, members)
        steps = target // PAIR - listed // PAIR
        crossed = (target ^ listed) & 1
        at = steps - 1 + crossed * (members // PAIR)
    else:
        arrived = relay((k_own, v_own), chosen, members)
        k_parts, v_parts = ([arrived[n, j] for j in range(slots - 1)] for n in range(2))
        at = jnp.arange(slots - 1, dtype=jnp.int32)
    at = jnp.where(listed < 0, -1, at)
    ready = prepare(queries, k_own, v_own, kv_dev)
    return attend(at, *ready, k_parts, v_parts, slots)


def solution(mesh):
    rows = P(("groups", "seq"), "head", None)
    return jax.shard_map(
        per_device,
        mesh=mesh,
        in_specs=(rows, rows, rows, P("groups", None)),
        out_specs=rows,
        check_vma=False,
    )
```

```python
import functools
import math

import jax
import jax.numpy as jnp
from jax import lax
from jax.experimental import pallas as pl
from jax.experimental.pallas import tpu as pltpu
from jax.sharding import PartitionSpec as P

NO_KEY = -1e30
ROW_CHUNK = 256
PAIR = 2
MOST_CLIMBED = 16


def prepare_kernel(
    q_hbm, k_hbm, v_hbm, q_out, k_out, v_out, q_ref, k_ref, v_ref, k_wide, v_wide, sems, *, kv_dev
):
    copies = [
        pltpu.make_async_copy(source, here, sems.at[n])
        for n, (source, here) in enumerate(((k_hbm, k_ref), (v_hbm, v_ref), (q_hbm, q_ref)))
    ]
    for copy in copies:
        copy.start()
    tokens, heads, dim = q_ref.shape
    group = heads // kv_dev
    copies[0].wait()
    k_wide[...] = k_ref[...].astype(jnp.float32)
    copies[1].wait()
    v_wide[...] = v_ref[...].astype(jnp.float32)
    for h in range(kv_dev):
        k_out[h] = k_wide[pl.ds(h, tokens, stride=kv_dev), :].astype(jnp.bfloat16)
        v_out[h] = v_wide[pl.ds(h, tokens, stride=kv_dev), :].astype(jnp.bfloat16)
    copies[2].wait()
    for h in range(kv_dev):
        q = q_ref[:, pl.ds(h * group, group), :].astype(jnp.float32)
        q_out[h] = q.reshape(tokens * group, dim).astype(jnp.bfloat16)


def prepare(queries, k_own, v_own, kv_dev):
    tokens, heads, dim = queries.shape
    vmem = pl.BlockSpec(memory_space=pltpu.VMEM)
    hbm = pl.BlockSpec(memory_space=pltpu.HBM)
    by_head = jax.ShapeDtypeStruct((kv_dev, tokens, dim), jnp.bfloat16)
    return pl.pallas_call(
        functools.partial(prepare_kernel, kv_dev=kv_dev),
        out_shape=(
            jax.ShapeDtypeStruct((kv_dev, tokens * heads // kv_dev, dim), jnp.bfloat16),
            by_head,
            by_head,
        ),
        in_specs=[hbm] * 3,
        out_specs=(vmem, vmem, vmem),
        scratch_shapes=[
            pltpu.VMEM(queries.shape, jnp.bfloat16),
            pltpu.VMEM(k_own.shape, jnp.bfloat16),
            pltpu.VMEM(k_own.shape, jnp.bfloat16),
            pltpu.VMEM(k_own.shape, jnp.float32),
            pltpu.VMEM(k_own.shape, jnp.float32),
            pltpu.SemaphoreType.DMA((3,)),
        ],
        compiler_params=pltpu.CompilerParams(vmem_limit_bytes=32 * 2**20),
        name="prepare",
    )(queries, k_own, v_own)


def attend_kernel(
    chosen_ref, q_ref, k_own_ref, v_own_ref, *refs, slots, choices, place,
):
    k_refs, v_refs = refs[:choices], refs[choices : 2 * choices]
    out_ref, k_buf, v_buf, k_wide, v_wide, sems = refs[2 * choices :]
    kv_dev, tokens, dim = k_own_ref.shape
    group = q_ref.shape[1] // tokens
    block = tokens * kv_dev
    target = lax.axis_index("seq").astype(jnp.int32)
    own_at = jnp.int32(0)
    for j in range(1, slots):
        own_at = jnp.where(chosen_ref[target, j] == target, j, own_at)
    bias = []
    for j in range(slots - 1):
        source = chosen_ref[target, jnp.where(j >= own_at, j + 1, j)]
        bias.append(jnp.where(source < 0, NO_KEY, 0.0).astype(jnp.float32))
        at = jnp.where(source < 0, 0, place(j, source, target))
        for i in range(choices):

            @pl.when(at == i)
            def _start(i=i, j=j):
                for n, (parts, buf) in enumerate(((k_refs, k_buf), (v_refs, v_buf))):
                    pltpu.make_async_copy(
                        parts[i], buf.at[pl.ds(j * block, block), :], sems.at[n, j]
                    ).start()

    for j in range(slots - 1):
        for n, (parts, buf) in enumerate(((k_refs, k_buf), (v_refs, v_buf))):
            pltpu.make_async_copy(
                parts[0], buf.at[pl.ds(j * block, block), :], sems.at[n, j]
            ).wait()
    k_wide[...] = k_buf[...].astype(jnp.float32)
    v_wide[...] = v_buf[...].astype(jnp.float32)

    factor = dim ** (-0.5) * math.log2(math.e)
    rest = (slots - 1) * tokens
    ones = jnp.ones((slots * tokens, dim), jnp.bfloat16)
    chunk_tokens = ROW_CHUNK // group
    for h in range(kv_dev):
        k_h = k_wide[pl.ds(h, rest, stride=kv_dev), :].astype(jnp.bfloat16)
        v_h = v_wide[pl.ds(h, rest, stride=kv_dev), :].astype(jnp.bfloat16)
        k_h = jnp.concatenate([k_own_ref[h], k_h], axis=0)
        v_h = jnp.concatenate([v_own_ref[h], v_h], axis=0)
        v_ones = jnp.concatenate([v_h, ones], axis=1)
        for first in range(0, tokens, chunk_tokens):
            q = q_ref[h, pl.ds(first * group, ROW_CHUNK), :]
            s = lax.dot_general(
                q, k_h, (((1,), (1,)), ((), ())), preferred_element_type=jnp.float32
            )
            row = lax.broadcasted_iota(jnp.int32, (ROW_CHUNK, tokens), 0) // group + first
            key = lax.broadcasted_iota(jnp.int32, (ROW_CHUNK, tokens), 1)
            parts = [jnp.where(key <= row, s[:, :tokens], NO_KEY)]
            for j in range(1, slots):
                parts.append(s[:, j * tokens : (j + 1) * tokens] + bias[j - 1])
            top = parts[0]
            for part in parts[1:]:
                top = jnp.maximum(top, part)
            top = jnp.max(top, axis=1, keepdims=True)
            probs = jnp.concatenate(
                [jnp.exp2((part - top) * factor).astype(jnp.bfloat16) for part in parts], axis=1
            )
            both = jnp.dot(probs, v_ones, preferred_element_type=jnp.float32)
            merged = both[:, :dim] / both[:, dim:]
            out_ref[pl.ds(first, chunk_tokens), pl.ds(h * group, group), :] = (
                merged.reshape(chunk_tokens, group, dim).astype(jnp.bfloat16)
            )


def attend(chosen, queries, k_own, v_own, k_parts, v_parts, place):
    slots = chosen.shape[1]
    kv_dev, tokens, dim = k_own.shape
    heads = queries.shape[0] * queries.shape[1] // tokens
    rest = (slots - 1) * tokens * kv_dev
    choices = len(k_parts)
    vmem = pl.BlockSpec(memory_space=pltpu.VMEM)
    hbm = pl.BlockSpec(memory_space=pltpu.HBM)
    return pl.pallas_call(
        functools.partial(attend_kernel, slots=slots, choices=choices, place=place),
        out_shape=jax.ShapeDtypeStruct((tokens, heads, dim), jnp.bfloat16),
        in_specs=[pl.BlockSpec(memory_space=pltpu.SMEM), vmem, vmem, vmem] + [hbm] * (2 * choices),
        out_specs=vmem,
        scratch_shapes=[
            pltpu.VMEM((rest, dim), jnp.bfloat16),
            pltpu.VMEM((rest, dim), jnp.bfloat16),
            pltpu.VMEM((rest, dim), jnp.float32),
            pltpu.VMEM((rest, dim), jnp.float32),
            pltpu.SemaphoreType.DMA((2, slots - 1)),
        ],
        compiler_params=pltpu.CompilerParams(vmem_limit_bytes=32 * 2**20),
        name="attend",
    )(chosen, queries, k_own, v_own, *k_parts, *v_parts)


def others(row, target):
    slots = row.shape[-1]
    own_at = jnp.argmax(row == target[..., None], axis=-1)
    j = jnp.arange(slots - 1)
    return jnp.where(j >= own_at[..., None], row[..., 1:], row[..., :-1])


def climb(k_own, v_own, members):
    up = [(s, (s + PAIR) % members) for s in range(members)]
    across = [(s, s ^ 1) for s in range(members)]
    same, other = [[k_own], [v_own]], [[], []]
    for step in range(members // PAIR):
        last = step == members // PAIR - 1
        for n in range(2):
            if step:
                same[n][-1], other[n][-1] = lax.optimization_barrier((same[n][-1], other[n][-1]))
            here = same[n][-1]
            if not last:
                same[n].append(lax.ppermute(here, "seq", up))
            other[n].append(lax.ppermute(here, "seq", across))
    return [same[n][1:] + other[n] for n in range(2)]


def relay(own, chosen, members):
    block, dim = own[0].shape
    stacked = jnp.stack(own).reshape(len(own), members, block // members, dim)
    shares = lax.all_to_all(stacked, "seq", split_axis=1, concat_axis=1, tiled=True)
    wanted = jnp.maximum(others(chosen, jnp.arange(members, dtype=jnp.int32)), 0)
    picked = jnp.take(shares, wanted, axis=1)
    arrived = lax.all_to_all(picked, "seq", split_axis=1, concat_axis=3, tiled=True)
    return arrived.reshape(len(own), wanted.shape[1], block, dim)


def per_device(queries, keys, values, chosen):
    members = lax.axis_size("seq")
    tokens, kv_dev, dim = keys.shape
    slots = chosen.shape[1]
    k_own = keys.reshape(tokens * kv_dev, dim)
    v_own = values.reshape(tokens * kv_dev, dim)
    if members <= MOST_CLIMBED:
        k_parts, v_parts = climb(k_own, v_own, members)
        queries, _ = lax.optimization_barrier((queries, v_parts[1]))

        def place(slot, source, target):
            return (target >> 1) - (source >> 1) - 1 + ((target ^ source) & 1) * (members // PAIR)

    else:
        arrived = relay((k_own, v_own), chosen, members)
        k_parts, v_parts = ([arrived[n, j] for j in range(slots - 1)] for n in range(2))

        def place(slot, source, target):
            return jnp.int32(slot)

    ready = prepare(queries, k_own, v_own, kv_dev)
    return attend(chosen, *ready, k_parts, v_parts, place)


def solution(mesh):
    rows = P(("groups", "seq"), "head", None)
    return jax.shard_map(
        per_device,
        mesh=mesh,
        in_specs=(rows, rows, rows, P("groups", None)),
        out_specs=rows,
        check_vma=False,
    )
```

```python
import functools
import math

import jax
import jax.numpy as jnp
from jax import lax
from jax.experimental import pallas as pl
from jax.experimental.pallas import tpu as pltpu
from jax.sharding import PartitionSpec as P

NO_KEY = -1e30
ROW_CHUNK = 256
MOST_ROUND = 16


def params():
    return pltpu.CompilerParams(vmem_limit_bytes=40 * 2**20)


def vmem():
    return pl.BlockSpec(memory_space=pltpu.VMEM)


def attend_rows(q, k_h, v_ones, factor, mask, before):
    dim = k_h.shape[1]
    s = lax.dot_general(q, k_h, (((1,), (1,)), ((), ())), preferred_element_type=jnp.float32)
    if mask is not None:
        s = jnp.where(mask, s, NO_KEY)
    top = jnp.max(s, axis=1, keepdims=True)
    if before is not None:
        top = jnp.maximum(before[0], top)
    top = jnp.broadcast_to(top, (q.shape[0], dim))
    probs = jnp.exp2((s - top) * factor).astype(jnp.bfloat16)
    both = jnp.dot(probs, v_ones, preferred_element_type=jnp.float32)
    if before is not None:
        shrink = jnp.exp2((before[0] - top) * factor)
        both = both + before[1] * jnp.concatenate([shrink, shrink], axis=1)
    return top, both


def own_kernel(
    q_hbm, k_hbm, v_hbm, q_out, top_out, both_out, q_ref, k_ref, v_ref, k_wide, v_wide, sems, *, kv_dev
):
    copies = [
        pltpu.make_async_copy(source, here, sems.at[n])
        for n, (source, here) in enumerate(((k_hbm, k_ref), (v_hbm, v_ref), (q_hbm, q_ref)))
    ]
    for copy in copies:
        copy.start()
    tokens, heads, dim = q_ref.shape
    group = heads // kv_dev
    copies[0].wait()
    k_wide[...] = k_ref[...].astype(jnp.float32)
    copies[1].wait()
    v_wide[...] = v_ref[...].astype(jnp.float32)
    copies[2].wait()
    factor = dim ** (-0.5) * math.log2(math.e)
    ones = jnp.ones((tokens, dim), jnp.bfloat16)
    chunk_tokens = ROW_CHUNK // group
    for h in range(kv_dev):
        k_h = k_wide[pl.ds(h, tokens, stride=kv_dev), :].astype(jnp.bfloat16)
        v_h = v_wide[pl.ds(h, tokens, stride=kv_dev), :].astype(jnp.bfloat16)
        v_ones = jnp.concatenate([v_h, ones], axis=1)
        for first in range(0, tokens, chunk_tokens):
            q = q_ref[pl.ds(first, chunk_tokens), pl.ds(h * group, group), :]
            q = q.astype(jnp.float32).reshape(ROW_CHUNK, dim).astype(jnp.bfloat16)
            row = lax.broadcasted_iota(jnp.int32, (ROW_CHUNK, tokens), 0) // group + first
            key = lax.broadcasted_iota(jnp.int32, (ROW_CHUNK, tokens), 1)
            rows = pl.ds(first * group, ROW_CHUNK)
            q_out[h, rows, :] = q
            top_out[h, rows, :], both_out[h, rows, :] = attend_rows(
                q, k_h, v_ones, factor, key <= row, None
            )


def attend_own(queries, k_own, v_own, kv_dev):
    tokens, heads, dim = queries.shape
    rows = tokens * heads // kv_dev
    operands = [pltpu.with_memory_space_constraint(x, pltpu.HBM) for x in (queries, k_own, v_own)]
    return pl.pallas_call(
        functools.partial(own_kernel, kv_dev=kv_dev),
        out_shape=(
            jax.ShapeDtypeStruct((kv_dev, rows, dim), jnp.bfloat16),
            jax.ShapeDtypeStruct((kv_dev, rows, dim), jnp.float32),
            jax.ShapeDtypeStruct((kv_dev, rows, 2 * dim), jnp.float32),
        ),
        in_specs=[pl.BlockSpec(memory_space=pltpu.HBM)] * 3,
        out_specs=(vmem(), vmem(), vmem()),
        scratch_shapes=[
            pltpu.VMEM(queries.shape, jnp.bfloat16),
            pltpu.VMEM(k_own.shape, jnp.bfloat16),
            pltpu.VMEM(k_own.shape, jnp.bfloat16),
            pltpu.VMEM(k_own.shape, jnp.float32),
            pltpu.VMEM(k_own.shape, jnp.float32),
            pltpu.SemaphoreType.DMA((3,)),
        ],
        compiler_params=params(),
        name="attend_own",
    )(*operands)


def listed_kernel(chosen_ref, q_ref, *refs, parts, kv_dev, sources, final):
    k_refs, v_refs = refs[:parts], refs[parts : 2 * parts]
    top_in, both_in = refs[2 * parts : 2 * parts + 2]
    *outs, k_wide, v_wide = refs[2 * parts + 2 :]
    rows_all, dim = q_ref.shape[1:]
    tokens = k_wide.shape[0] // kv_dev
    group = rows_all // tokens
    factor = dim ** (-0.5) * math.log2(math.e)
    ones = jnp.ones((tokens, dim), jnp.bfloat16)
    target = lax.axis_index("seq").astype(jnp.int32)
    chunks = [(h, first) for h in range(kv_dev) for first in range(0, rows_all, ROW_CHUNK)]

    def keep(h, first, top, both):
        rows = pl.ds(first, ROW_CHUNK)
        outs[0][h, rows, :] = top
        outs[1][h, rows, :] = both

    def finish(h, first, top, both):
        del top
        merged = (both[:, :dim] / both[:, dim:]).reshape(ROW_CHUNK // group, group, dim)
        rows = pl.ds(first // group, ROW_CHUNK // group)
        outs[0][rows, pl.ds(h * group, group), :] = merged.astype(jnp.bfloat16)

    def running(h, first):
        rows = pl.ds(first, ROW_CHUNK)
        top_ref, both_ref = (top_in, both_in) if final else outs
        return top_ref[h, rows, :], both_ref[h, rows, :]

    for part, source in enumerate(sources(target)):
        is_listed = chosen_ref[target, 0] == source
        for j in range(1, chosen_ref.shape[1]):
            is_listed |= chosen_ref[target, j] == source

        @pl.when(is_listed)
        def _add(part=part):
            k_wide[...] = k_refs[part][...].astype(jnp.float32)
            v_wide[...] = v_refs[part][...].astype(jnp.float32)
            for h, first in chunks:
                if first == 0:
                    k_h = k_wide[pl.ds(h, tokens, stride=kv_dev), :].astype(jnp.bfloat16)
                    v_h = v_wide[pl.ds(h, tokens, stride=kv_dev), :].astype(jnp.bfloat16)
                    v_ones = jnp.concatenate([v_h, ones], axis=1)
                q = q_ref[h, pl.ds(first, ROW_CHUNK), :]
                added = attend_rows(q, k_h, v_ones, factor, None, running(h, first))
                (finish if final else keep)(h, first, *added)

    if final:

        @pl.when(jnp.logical_not(is_listed))
        def _finish():
            for h, first in chunks:
                finish(h, first, *running(h, first))


def attend_listed(chosen, queries, state, k_parts, v_parts, sources, final):
    kv_dev, rows, dim = queries.shape
    top, both = state
    block = k_parts[0].shape
    parts = len(k_parts)
    tokens = block[0] // kv_dev
    first_state = 2 + 2 * parts
    if final:
        out_shape = jax.ShapeDtypeStruct((tokens, rows * kv_dev // tokens, dim), jnp.bfloat16)
        out_specs, aliases = vmem(), {}
    else:
        out_shape = tuple(jax.ShapeDtypeStruct(x.shape, x.dtype) for x in state)
        out_specs, aliases = (vmem(), vmem()), {first_state: 0, first_state + 1: 1}
    return pl.pallas_call(
        functools.partial(
            listed_kernel, parts=parts, kv_dev=kv_dev, sources=sources, final=final
        ),
        out_shape=out_shape,
        in_specs=[pl.BlockSpec(memory_space=pltpu.SMEM)] + [vmem()] * (3 + 2 * parts),
        out_specs=out_specs,
        input_output_aliases=aliases,
        scratch_shapes=[pltpu.VMEM(block, jnp.float32)] * 2,
        compiler_params=params(),
        name="attend_last" if final else "attend_listed",
    )(chosen, queries, *k_parts, *v_parts, top, both)


def ring_at(place, members):
    back = members - 1 - place
    return jnp.where(place < members // 2, 2 * place, 2 * back + 1)


def ring_place(block, members):
    return jnp.where(block % 2 == 0, block // 2, members - 1 - block // 2)


def listed_along_ring(chosen, queries, k_own, v_own, kv_dev, members):
    ring = list(range(0, members, 2)) + list(range(members - 1, 0, -2))
    ways = [
        [(ring[p], ring[(p + turn) % members]) for p in range(members)] for turn in (1, -1)
    ]

    def send(x, way):
        return lax.ppermute(x, "seq", ways[way])

    def sources_at(distance):
        def sources(target):
            place = ring_place(target, members)
            turns = (-distance, distance) if distance < members // 2 else (distance,)
            return [ring_at(lax.rem(place + turn + members, members), members) for turn in turns]

        return sources

    k_two, v_two = (k_own, k_own), (v_own, v_own)
    state = None
    for distance in range(1, members // 2):
        k_next = tuple(send(x, way) for way, x in enumerate(k_two))
        v_next = tuple(send(x, way) for way, x in enumerate(v_two))
        if distance == 1:
            queries, *state = attend_own(queries, k_own, v_own, kv_dev)
        else:
            state = attend_listed(
                chosen, queries, state, k_two, v_two, sources_at(distance - 1), False
            )
        k_next, state = lax.optimization_barrier((k_next, state))
        k_two, v_two = k_next, lax.optimization_barrier(v_next)
    k_last, v_last = send(k_two[0], 0), send(v_two[1], 1)
    state = attend_listed(
        chosen, queries, state, k_two, v_two, sources_at(members // 2 - 1), False
    )
    return attend_listed(
        chosen, queries, state, [k_last], [v_last], sources_at(members // 2), True
    )


def others(row, target):
    slots = row.shape[-1]
    own_at = jnp.argmax(row == target[..., None], axis=-1)
    j = jnp.arange(slots - 1)
    return jnp.where(j >= own_at[..., None], row[..., 1:], row[..., :-1])


def listed_by_relay(chosen, queries, k_own, v_own, kv_dev, members):
    block, dim = k_own.shape
    stacked = jnp.stack([k_own, v_own]).reshape(2, members, block // members, dim)
    shares = lax.all_to_all(stacked, "seq", split_axis=1, concat_axis=1, tiled=True)
    wanted = others(chosen, jnp.arange(members, dtype=jnp.int32))
    picked = jnp.take(shares, jnp.maximum(wanted, 0), axis=1)
    arrived = lax.all_to_all(picked, "seq", split_axis=1, concat_axis=3, tiled=True)
    arrived = arrived.reshape(2, wanted.shape[1], block, dim)
    k_parts, v_parts = ([arrived[n, j] for j in range(wanted.shape[1])] for n in range(2))
    queries, *state = attend_own(queries, k_own, v_own, kv_dev)
    mine = lax.dynamic_index_in_dim(wanted, lax.axis_index("seq"), 0, True)

    def sources(_):
        return [jnp.int32(j) for j in range(wanted.shape[1])]

    members_listed = jnp.where(mine < 0, -1, jnp.arange(wanted.shape[1], dtype=jnp.int32)[None])
    listed = jnp.broadcast_to(members_listed, wanted.shape)
    last = len(k_parts) - 1
    state = attend_listed(
        listed, queries, state, k_parts[:last], v_parts[:last], lambda _: sources(_)[:last], False
    )
    return attend_listed(
        listed, queries, state, k_parts[last:], v_parts[last:], lambda _: sources(_)[last:], True
    )


def per_device(queries, keys, values, chosen):
    members = lax.axis_size("seq")
    tokens, kv_dev, dim = keys.shape
    k_own = keys.reshape(tokens * kv_dev, dim)
    v_own = values.reshape(tokens * kv_dev, dim)
    attend = listed_along_ring if members <= MOST_ROUND else listed_by_relay
    return attend(chosen, queries, k_own, v_own, kv_dev, members)


def solution(mesh):
    rows = P(("groups", "seq"), "head", None)
    return jax.shard_map(
        per_device,
        mesh=mesh,
        in_specs=(rows, rows, rows, P("groups", None)),
        out_specs=rows,
        check_vma=False,
    )
```

```python
import functools
import math

import jax
import jax.numpy as jnp
from jax import lax
from jax.experimental import pallas as pl
from jax.experimental.pallas import tpu as pltpu
from jax.sharding import PartitionSpec as P

NO_KEY = -1e30
ROW_CHUNK = 256
MOST_ROUND = 16


def params():
    return pltpu.CompilerParams(vmem_limit_bytes=16 * 2**20)


def vmem():
    return pl.BlockSpec(memory_space=pltpu.VMEM)


def prepare_kernel(
    q_hbm, k_hbm, v_hbm, q_out, k_out, v_out, q_ref, k_ref, v_ref, k_wide, v_wide, sems, *, kv_dev
):
    copies = [
        pltpu.make_async_copy(source, here, sems.at[n])
        for n, (source, here) in enumerate(((k_hbm, k_ref), (v_hbm, v_ref), (q_hbm, q_ref)))
    ]
    for copy in copies:
        copy.start()
    tokens, heads, dim = q_ref.shape
    group = heads // kv_dev
    for copy, ref, wide, out in zip(copies, (k_ref, v_ref), (k_wide, v_wide), (k_out, v_out)):
        copy.wait()
        wide[...] = ref[...].astype(jnp.float32)
        for h in range(kv_dev):
            out[h] = wide[pl.ds(h, tokens, stride=kv_dev), :].astype(jnp.bfloat16)
    copies[2].wait()
    for h in range(kv_dev):
        q = q_ref[:, pl.ds(h * group, group), :].astype(jnp.float32)
        q_out[h] = q.reshape(tokens * group, dim).astype(jnp.bfloat16)


def prepare(queries, k_own, v_own, kv_dev):
    tokens, heads, dim = queries.shape
    operands = [pltpu.with_memory_space_constraint(x, pltpu.HBM) for x in (queries, k_own, v_own)]
    by_head = jax.ShapeDtypeStruct((kv_dev, tokens, dim), jnp.bfloat16)
    return pl.pallas_call(
        functools.partial(prepare_kernel, kv_dev=kv_dev),
        out_shape=(
            jax.ShapeDtypeStruct((kv_dev, tokens * heads // kv_dev, dim), jnp.bfloat16),
            by_head,
            by_head,
        ),
        in_specs=[pl.BlockSpec(memory_space=pltpu.HBM)] * 3,
        out_specs=(vmem(), vmem(), vmem()),
        scratch_shapes=[
            pltpu.VMEM(queries.shape, jnp.bfloat16),
            pltpu.VMEM(k_own.shape, jnp.bfloat16),
            pltpu.VMEM(k_own.shape, jnp.bfloat16),
            pltpu.VMEM(k_own.shape, jnp.float32),
            pltpu.VMEM(k_own.shape, jnp.float32),
            pltpu.SemaphoreType.DMA((3,)),
        ],
        compiler_params=params(),
        name="prepare",
    )(*operands)


def gather_listed(chosen_ref, parts, wide, sources):
    target = lax.axis_index("seq").astype(jnp.int32)
    block = parts[0].shape[0]
    most = wide.shape[0] // block
    count = jnp.int32(0)
    for part, source in zip(parts, sources(target)):
        is_listed = chosen_ref[target, 0] == source
        for j in range(1, chosen_ref.shape[1]):
            is_listed |= chosen_ref[target, j] == source
        is_listed &= count < most

        @pl.when(is_listed)
        def _take(part=part, count=count):
            rows = pl.ds(pl.multiple_of(count * block, block), block)
            wide[rows, :] = part[...].astype(jnp.float32)

        count += is_listed.astype(jnp.int32)
    for j in range(most):

        @pl.when(count <= j)
        def _clear(j=j):
            wide[pl.ds(j * block, block), :] = jnp.zeros((block, wide.shape[1]), jnp.float32)

    return count


def weights_kernel(chosen_ref, q_ref, own_ref, *refs, sources):
    *parts, out_ref, wide = refs
    kv_dev, tokens, dim = own_ref.shape
    rows_all = q_ref.shape[1]
    group = rows_all // tokens
    others = wide.shape[0] // (tokens * kv_dev)
    count = gather_listed(chosen_ref, parts, wide, sources)
    bias = [jnp.where(count <= j, NO_KEY, 0.0).astype(jnp.float32) for j in range(others)]
    factor = dim ** (-0.5) * math.log2(math.e)
    for h in range(kv_dev):
        k_h = wide[pl.ds(h, others * tokens, stride=kv_dev), :].astype(jnp.bfloat16)
        k_h = jnp.concatenate([own_ref[h], k_h], axis=0)
        for first in range(0, rows_all, ROW_CHUNK):
            rows = pl.ds(first, ROW_CHUNK)
            s = lax.dot_general(
                q_ref[h, rows, :], k_h, (((1,), (1,)), ((), ())), preferred_element_type=jnp.float32
            )
            row = (lax.broadcasted_iota(jnp.int32, (ROW_CHUNK, tokens), 0) + first) // group
            key = lax.broadcasted_iota(jnp.int32, (ROW_CHUNK, tokens), 1)
            parts_s = [jnp.where(key <= row, s[:, :tokens], NO_KEY)]
            for j in range(others):
                parts_s.append(s[:, (j + 1) * tokens : (j + 2) * tokens] + bias[j])
            top = parts_s[0]
            for part in parts_s[1:]:
                top = jnp.maximum(top, part)
            top = jnp.max(top, axis=1, keepdims=True)
            for j, part in enumerate(parts_s):
                probs = jnp.exp2((part - top) * factor).astype(jnp.bfloat16)
                out_ref[h, rows, pl.ds(j * tokens, tokens)] = probs


def weights(chosen, queries, k_own, k_parts, sources, slots):
    kv_dev, rows, _ = queries.shape
    block, dim = k_parts[0].shape
    return pl.pallas_call(
        functools.partial(weights_kernel, sources=sources),
        out_shape=jax.ShapeDtypeStruct((kv_dev, rows, slots * block // kv_dev), jnp.bfloat16),
        in_specs=[pl.BlockSpec(memory_space=pltpu.SMEM)] + [vmem()] * (2 + len(k_parts)),
        out_specs=vmem(),
        scratch_shapes=[pltpu.VMEM(((slots - 1) * block, dim), jnp.float32)],
        compiler_params=params(),
        name="weights",
    )(chosen, queries, k_own, *k_parts)


def merge_kernel(chosen_ref, weights_ref, own_ref, *refs, sources):
    *parts, out_ref, wide = refs
    kv_dev, tokens, dim = own_ref.shape
    rows_all = weights_ref.shape[1]
    group = rows_all // tokens
    others = wide.shape[0] // (tokens * kv_dev)
    gather_listed(chosen_ref, parts, wide, sources)
    ones = jnp.ones(((others + 1) * tokens, dim), jnp.bfloat16)
    for h in range(kv_dev):
        v_h = wide[pl.ds(h, others * tokens, stride=kv_dev), :].astype(jnp.bfloat16)
        v_ones = jnp.concatenate([jnp.concatenate([own_ref[h], v_h], axis=0), ones], axis=1)
        for first in range(0, rows_all, ROW_CHUNK):
            both = jnp.dot(
                weights_ref[h, pl.ds(first, ROW_CHUNK), :], v_ones, preferred_element_type=jnp.float32
            )
            merged = (both[:, :dim] / both[:, dim:]).reshape(ROW_CHUNK // group, group, dim)
            rows = pl.ds(first // group, ROW_CHUNK // group)
            out_ref[rows, pl.ds(h * group, group), :] = merged.astype(jnp.bfloat16)


def merge(chosen, probs, v_own, v_parts, sources, slots):
    kv_dev, rows, _ = probs.shape
    block, dim = v_parts[0].shape
    tokens = block // kv_dev
    return pl.pallas_call(
        functools.partial(merge_kernel, sources=sources),
        out_shape=jax.ShapeDtypeStruct((tokens, rows * kv_dev // tokens, dim), jnp.bfloat16),
        in_specs=[pl.BlockSpec(memory_space=pltpu.SMEM)] + [vmem()] * (2 + len(v_parts)),
        out_specs=vmem(),
        scratch_shapes=[pltpu.VMEM(((slots - 1) * block, dim), jnp.float32)],
        compiler_params=params(),
        name="merge",
    )(chosen, probs, v_own, *v_parts)


def ring_at(place, members):
    back = members - 1 - place
    return jnp.where(place < members // 2, 2 * place, 2 * back + 1)


def ring_place(block, members):
    return jnp.where(block % 2 == 0, block // 2, members - 1 - block // 2)


def round_the_ring(k_own, v_own, ready, members):
    ring = list(range(0, members, 2)) + list(range(members - 1, 0, -2))
    ways = [
        [(ring[p], ring[(p + turn) % members]) for p in range(members)] for turn in (1, -1)
    ]

    def send(x, way):
        return lax.ppermute(x, "seq", ways[way])

    half = members // 2
    k_two, v_two, k_all, v_all = (k_own, k_own), (v_own, v_own), [], []
    for distance in range(1, half):
        k_two = tuple(send(x, way) for way, x in enumerate(k_two))
        if distance == half - 1:
            forward, k_first = lax.optimization_barrier((v_two[0], k_two[0]))
            v_two, k_two = (forward, v_two[1]), (k_first, k_two[1])
        v_two = tuple(send(x, way) for way, x in enumerate(v_two))
        if distance == 1:
            k_two, ready = lax.optimization_barrier((k_two, ready))
        elif distance < half - 1:
            k_two = lax.optimization_barrier(k_two)
        if distance < half - 1:
            v_two = lax.optimization_barrier(v_two)
        k_all += k_two
        v_all += v_two
    k_all.append(send(k_two[0], 0))
    v_all.append(send(v_two[1], 1))
    return k_all, v_all, ready


def ring_sources(members):
    def sources(target):
        place = ring_place(target, members)
        turns = [turn for far in range(1, members // 2) for turn in (-far, far)] + [members // 2]
        return [ring_at(lax.rem(place + turn + members, members), members) for turn in turns]

    return sources


def others(row, target):
    slots = row.shape[-1]
    own_at = jnp.argmax(row == target[..., None], axis=-1)
    j = jnp.arange(slots - 1)
    return jnp.where(j >= own_at[..., None], row[..., 1:], row[..., :-1])


def relay(k_own, v_own, chosen, members):
    block, dim = k_own.shape
    stacked = jnp.stack([k_own, v_own]).reshape(2, members, block // members, dim)
    shares = lax.all_to_all(stacked, "seq", split_axis=1, concat_axis=1, tiled=True)
    wanted = others(chosen, jnp.arange(members, dtype=jnp.int32))
    picked = jnp.take(shares, jnp.maximum(wanted, 0), axis=1)
    arrived = lax.all_to_all(picked, "seq", split_axis=1, concat_axis=3, tiled=True)
    count = wanted.shape[1]
    k_parts, v_parts = ([arrived[n, 0, j].reshape(block, dim) for j in range(count)] for n in range(2))
    return k_parts, v_parts, jnp.where(wanted < 0, -1, jnp.arange(count, dtype=jnp.int32))


def per_device(queries, keys, values, chosen):
    members = lax.axis_size("seq")
    tokens, kv_dev, dim = keys.shape
    slots = chosen.shape[1]
    k_own = keys.reshape(tokens * kv_dev, dim)
    v_own = values.reshape(tokens * kv_dev, dim)
    ready = prepare(queries, k_own, v_own, kv_dev)
    if members <= MOST_ROUND:
        k_parts, v_parts, ready = round_the_ring(k_own, v_own, ready, members)
        sources = ring_sources(members)
    else:
        k_parts, v_parts, chosen = relay(k_own, v_own, chosen, members)

        def sources(_):
            return [jnp.int32(j) for j in range(slots - 1)]

    q_ready, k_ready, v_ready = ready
    probs = weights(chosen, q_ready, k_ready, k_parts, sources, slots)
    return merge(chosen, probs, v_ready, v_parts, sources, slots)


def solution(mesh):
    rows = P(("groups", "seq"), "head", None)
    return jax.shard_map(
        per_device,
        mesh=mesh,
        in_specs=(rows, rows, rows, P("groups", None)),
        out_specs=rows,
        check_vma=False,
    )
```

```python
import functools
import math

import jax
import jax.numpy as jnp
from jax import lax
from jax.experimental import pallas as pl
from jax.experimental.pallas import tpu as pltpu
from jax.sharding import PartitionSpec as P

NO_KEY = -1e30
ROW_CHUNK = 256
MOST_ROUND = 16


def params():
    return pltpu.CompilerParams(vmem_limit_bytes=16 * 2**20)


def vmem():
    return pl.BlockSpec(memory_space=pltpu.VMEM)


def prepare_kernel(
    chosen_ref, q_hbm, k_hbm, v_hbm, slots_out, q_out, k_out, v_out,
    q_ref, k_ref, v_ref, k_wide, v_wide, sems, *, kv_dev, sources,
):
    copies = [
        pltpu.make_async_copy(source, here, sems.at[n])
        for n, (source, here) in enumerate(((k_hbm, k_ref), (v_hbm, v_ref), (q_hbm, q_ref)))
    ]
    for copy in copies:
        copy.start()
    target = lax.axis_index("seq").astype(jnp.int32)
    count = jnp.int32(0)
    for part, source in enumerate(sources(target)):
        is_listed = chosen_ref[target, 0] == source
        for j in range(1, chosen_ref.shape[1]):
            is_listed |= chosen_ref[target, j] == source
        slots_out[part] = jnp.where(is_listed, count, -1)
        count += is_listed.astype(jnp.int32)
    slots_out[slots_out.shape[0] - 1] = count

    tokens, heads, dim = q_ref.shape
    group = heads // kv_dev
    for copy, ref, wide, out in zip(copies, (k_ref, v_ref), (k_wide, v_wide), (k_out, v_out)):
        copy.wait()
        wide[...] = ref[...].astype(jnp.float32)
        for h in range(kv_dev):
            out[h] = wide[pl.ds(h, tokens, stride=kv_dev), :].astype(jnp.bfloat16)
    copies[2].wait()
    for h in range(kv_dev):
        q = q_ref[:, pl.ds(h * group, group), :].astype(jnp.float32)
        q_out[h] = q.reshape(tokens * group, dim).astype(jnp.bfloat16)


def prepare(chosen, queries, k_own, v_own, kv_dev, sources, parts):
    tokens, heads, dim = queries.shape
    smem = pl.BlockSpec(memory_space=pltpu.SMEM)
    operands = [pltpu.with_memory_space_constraint(x, pltpu.HBM) for x in (queries, k_own, v_own)]
    by_head = jax.ShapeDtypeStruct((kv_dev, tokens, dim), jnp.bfloat16)
    return pl.pallas_call(
        functools.partial(prepare_kernel, kv_dev=kv_dev, sources=sources),
        out_shape=(
            jax.ShapeDtypeStruct((parts + 1,), jnp.int32),
            jax.ShapeDtypeStruct((kv_dev, tokens * heads // kv_dev, dim), jnp.bfloat16),
            by_head,
            by_head,
        ),
        in_specs=[smem] + [pl.BlockSpec(memory_space=pltpu.HBM)] * 3,
        out_specs=(smem, vmem(), vmem(), vmem()),
        scratch_shapes=[
            pltpu.VMEM(queries.shape, jnp.bfloat16),
            pltpu.VMEM(k_own.shape, jnp.bfloat16),
            pltpu.VMEM(k_own.shape, jnp.bfloat16),
            pltpu.VMEM(k_own.shape, jnp.float32),
            pltpu.VMEM(k_own.shape, jnp.float32),
            pltpu.SemaphoreType.DMA((3,)),
        ],
        compiler_params=params(),
        name="prepare",
    )(chosen, *operands)


def gather_listed(slots_ref, parts, wide):
    block = parts[0].shape[0]
    count = slots_ref[len(parts)]
    for i, part in enumerate(parts):
        slot = slots_ref[i]

        @pl.when(slot >= 0)
        def _take(part=part, slot=slot):
            rows = pl.ds(pl.multiple_of(slot * block, block), block)
            wide[rows, :] = part[...].astype(jnp.float32)

    for j in range(wide.shape[0] // block):

        @pl.when(count <= j)
        def _clear(j=j):
            wide[pl.ds(j * block, block), :] = jnp.zeros((block, wide.shape[1]), jnp.float32)

    return count


def weights_kernel(slots_ref, q_ref, own_ref, *refs):
    *parts, out_ref, wide = refs
    kv_dev, tokens, dim = own_ref.shape
    rows_all = q_ref.shape[1]
    group = rows_all // tokens
    others = wide.shape[0] // (tokens * kv_dev)
    count = gather_listed(slots_ref, parts, wide)
    factor = dim ** (-0.5) * math.log2(math.e)

    def fill(bias):
        for h in range(kv_dev):
            k_h = wide[pl.ds(h, others * tokens, stride=kv_dev), :].astype(jnp.bfloat16)
            k_h = jnp.concatenate([own_ref[h], k_h], axis=0)
            for first in range(0, rows_all, ROW_CHUNK):
                rows = pl.ds(first, ROW_CHUNK)
                s = lax.dot_general(
                    q_ref[h, rows, :], k_h, (((1,), (1,)), ((), ())), preferred_element_type=jnp.float32
                )
                row = (lax.broadcasted_iota(jnp.int32, (ROW_CHUNK, tokens), 0) + first) // group
                key = lax.broadcasted_iota(jnp.int32, (ROW_CHUNK, tokens), 1)
                scores = [jnp.where(key <= row, s[:, :tokens], NO_KEY)]
                for j in range(others):
                    score = s[:, (j + 1) * tokens : (j + 2) * tokens]
                    scores.append(score if bias is None else score + bias[j])
                top = scores[0]
                for score in scores[1:]:
                    top = jnp.maximum(top, score)
                top = jnp.max(top, axis=1, keepdims=True)
                for j, score in enumerate(scores):
                    probs = jnp.exp2((score - top) * factor).astype(jnp.bfloat16)
                    out_ref[h, rows, pl.ds(j * tokens, tokens)] = probs

    @pl.when(count == others)
    def _full():
        fill(None)

    @pl.when(count < others)
    def _some():
        fill([jnp.where(count <= j, NO_KEY, 0.0).astype(jnp.float32) for j in range(others)])


def weights(listed, queries, k_own, k_parts, slots):
    kv_dev, rows, _ = queries.shape
    block, dim = k_parts[0].shape
    return pl.pallas_call(
        weights_kernel,
        out_shape=jax.ShapeDtypeStruct((kv_dev, rows, slots * block // kv_dev), jnp.bfloat16),
        in_specs=[pl.BlockSpec(memory_space=pltpu.SMEM)] + [vmem()] * (2 + len(k_parts)),
        out_specs=vmem(),
        scratch_shapes=[pltpu.VMEM(((slots - 1) * block, dim), jnp.float32)],
        compiler_params=params(),
        name="weights",
    )(listed, queries, k_own, *k_parts)


def merge_kernel(slots_ref, weights_ref, own_ref, *refs):
    *parts, out_hbm, wide, values, out_ref, sems = refs
    kv_dev, tokens, dim = own_ref.shape
    group = weights_ref.shape[1] // tokens
    others = wide.shape[0] // (tokens * kv_dev)
    gather_listed(slots_ref, parts, wide)
    ones = jnp.ones(((others + 1) * tokens, dim), jnp.bfloat16)
    for h in range(kv_dev):
        v_h = wide[pl.ds(h, others * tokens, stride=kv_dev), :].astype(jnp.bfloat16)
        v_h = jnp.concatenate([own_ref[h], v_h], axis=0)
        values[h] = jnp.concatenate([v_h, ones], axis=1)
    chunk = ROW_CHUNK // group
    copies = []
    for n in range(tokens // chunk):
        here = pl.ds(n * chunk, chunk)
        for h in range(kv_dev):
            probs = weights_ref[h, pl.ds(n * ROW_CHUNK, ROW_CHUNK), :]
            both = jnp.dot(probs, values[h], preferred_element_type=jnp.float32)
            merged = (both[:, :dim] / both[:, dim:]).reshape(chunk, group, dim)
            out_ref[here, pl.ds(h * group, group), :] = merged.astype(jnp.bfloat16)
        copy = pltpu.make_async_copy(out_ref.at[here], out_hbm.at[here], sems.at[n])
        copy.start()
        copies.append(copy)
    for copy in copies:
        copy.wait()


def merge(listed, probs, v_own, v_parts, slots):
    kv_dev, rows, keys = probs.shape
    block, dim = v_parts[0].shape
    tokens = block // kv_dev
    out = (tokens, rows * kv_dev // tokens, dim)
    return pl.pallas_call(
        merge_kernel,
        out_shape=jax.ShapeDtypeStruct(out, jnp.bfloat16),
        in_specs=[pl.BlockSpec(memory_space=pltpu.SMEM)] + [vmem()] * (2 + len(v_parts)),
        out_specs=pl.BlockSpec(memory_space=pltpu.HBM),
        scratch_shapes=[
            pltpu.VMEM(((slots - 1) * block, dim), jnp.float32),
            pltpu.VMEM((kv_dev, keys, 2 * dim), jnp.bfloat16),
            pltpu.VMEM(out, jnp.bfloat16),
            pltpu.SemaphoreType.DMA((rows // ROW_CHUNK,)),
        ],
        compiler_params=params(),
        name="merge",
    )(listed, probs, v_own, *v_parts)


def ring_at(place, members):
    back = members - 1 - place
    return jnp.where(place < members // 2, 2 * place, 2 * back + 1)


def ring_place(block, members):
    return jnp.where(block % 2 == 0, block // 2, members - 1 - block // 2)


def round_the_ring(k_own, v_own, ready, members):
    ring = list(range(0, members, 2)) + list(range(members - 1, 0, -2))
    ways = [
        [(ring[p], ring[(p + turn) % members]) for p in range(members)] for turn in (1, -1)
    ]

    def send(x, way):
        return lax.ppermute(x, "seq", ways[way])

    half = members // 2
    k_two, v_two, k_all, v_all = (k_own, k_own), (v_own, v_own), [], []
    for distance in range(1, half):
        k_two = tuple(send(x, way) for way, x in enumerate(k_two))
        v_two = tuple(send(x, way) for way, x in enumerate(v_two))
        if distance == 1:
            k_two, ready = lax.optimization_barrier((k_two, ready))
        k_two = lax.optimization_barrier(k_two)
        if distance < half - 1:
            v_two = lax.optimization_barrier(v_two)
        k_all += k_two
        v_all += v_two
    k_all.append(send(k_two[0], 0))
    v_last, _ = lax.optimization_barrier((v_two[1], k_two))
    v_all.append(send(v_last, 1))
    return k_all, v_all, ready


def ring_sources(members):
    def sources(target):
        place = ring_place(target, members)
        turns = [turn for far in range(1, members // 2) for turn in (-far, far)] + [members // 2]
        return [ring_at(lax.rem(place + turn + members, members), members) for turn in turns]

    return sources


def others(row, target):
    slots = row.shape[-1]
    own_at = jnp.argmax(row == target[..., None], axis=-1)
    j = jnp.arange(slots - 1)
    return jnp.where(j >= own_at[..., None], row[..., 1:], row[..., :-1])


def relay(k_own, v_own, chosen, members):
    block, dim = k_own.shape
    stacked = jnp.stack([k_own, v_own]).reshape(2, members, block // members, dim)
    shares = lax.all_to_all(stacked, "seq", split_axis=1, concat_axis=1, tiled=True)
    wanted = others(chosen, jnp.arange(members, dtype=jnp.int32))
    picked = jnp.take(shares, jnp.maximum(wanted, 0), axis=1)
    arrived = lax.all_to_all(picked, "seq", split_axis=1, concat_axis=3, tiled=True)
    count = wanted.shape[1]
    k_parts, v_parts = ([arrived[n, 0, j].reshape(block, dim) for j in range(count)] for n in range(2))
    return k_parts, v_parts, jnp.where(wanted < 0, -1, jnp.arange(count, dtype=jnp.int32))


def per_device(queries, keys, values, chosen):
    members = lax.axis_size("seq")
    tokens, kv_dev, dim = keys.shape
    slots = chosen.shape[1]
    k_own = keys.reshape(tokens * kv_dev, dim)
    v_own = values.reshape(tokens * kv_dev, dim)
    if members <= MOST_ROUND:
        sources = ring_sources(members)
        ready = prepare(chosen, queries, k_own, v_own, kv_dev, sources, members - 1)
        k_parts, v_parts, ready = round_the_ring(k_own, v_own, ready, members)
    else:
        k_parts, v_parts, mine = relay(k_own, v_own, chosen, members)

        def sources(_):
            return [jnp.int32(j) for j in range(slots - 1)]

        ready = prepare(mine, queries, k_own, v_own, kv_dev, sources, slots - 1)
    listed, q_ready, k_ready, v_ready = ready
    probs = weights(listed, q_ready, k_ready, k_parts, slots)
    return merge(listed, probs, v_ready, v_parts, slots)


def solution(mesh):
    rows = P(("groups", "seq"), "head", None)
    return jax.shard_map(
        per_device,
        mesh=mesh,
        in_specs=(rows, rows, rows, P("groups", None)),
        out_specs=rows,
        check_vma=False,
    )
```

```python
import functools
import math

import jax
import jax.numpy as jnp
from jax import lax
from jax.experimental import pallas as pl
from jax.experimental.pallas import tpu as pltpu
from jax.sharding import PartitionSpec as P

NO_KEY = -1e30
ROW_CHUNK = 256
MOST_ROUND = 16


def params():
    return pltpu.CompilerParams(vmem_limit_bytes=16 * 2**20)


def vmem():
    return pl.BlockSpec(memory_space=pltpu.VMEM)


def prepare_kernel(
    lists_hbm, q_hbm, k_hbm, v_hbm, lists_out, q_out, k_out, v_out,
    q_ref, k_ref, v_ref, k_wide, v_wide, sems, *, kv_dev,
):
    whole = ((k_hbm, k_ref), (v_hbm, v_ref), (q_hbm, q_ref), (lists_hbm, lists_out))
    copies = [
        pltpu.make_async_copy(source, here, sems.at[n]) for n, (source, here) in enumerate(whole)
    ]
    for copy in copies:
        copy.start()
    tokens, heads, dim = q_ref.shape
    group = heads // kv_dev
    for copy, ref, wide, out in zip(copies, (k_ref, v_ref), (k_wide, v_wide), (k_out, v_out)):
        copy.wait()
        wide[...] = ref[...].astype(jnp.float32)
        for h in range(kv_dev):
            out[h] = wide[pl.ds(h, tokens, stride=kv_dev), :].astype(jnp.bfloat16)
    copies[2].wait()
    for h in range(kv_dev):
        q = q_ref[:, pl.ds(h * group, group), :].astype(jnp.float32)
        q_out[h] = q.reshape(tokens * group, dim).astype(jnp.bfloat16)
    copies[3].wait()


def prepare(lists, queries, k_own, v_own, kv_dev):
    tokens, heads, dim = queries.shape
    operands = [
        pltpu.with_memory_space_constraint(x, pltpu.HBM) for x in (lists, queries, k_own, v_own)
    ]
    by_head = jax.ShapeDtypeStruct((kv_dev, tokens, dim), jnp.bfloat16)
    return pl.pallas_call(
        functools.partial(prepare_kernel, kv_dev=kv_dev),
        out_shape=(
            jax.ShapeDtypeStruct(lists.shape, lists.dtype),
            jax.ShapeDtypeStruct((kv_dev, tokens * heads // kv_dev, dim), jnp.bfloat16),
            by_head,
            by_head,
        ),
        in_specs=[pl.BlockSpec(memory_space=pltpu.HBM)] * 4,
        out_specs=(vmem(), vmem(), vmem(), vmem()),
        scratch_shapes=[
            pltpu.VMEM(queries.shape, jnp.bfloat16),
            pltpu.VMEM(k_own.shape, jnp.bfloat16),
            pltpu.VMEM(k_own.shape, jnp.bfloat16),
            pltpu.VMEM(k_own.shape, jnp.float32),
            pltpu.VMEM(k_own.shape, jnp.float32),
            pltpu.SemaphoreType.DMA((4,)),
        ],
        compiler_params=params(),
        name="prepare",
    )(*operands)


def gather_listed(lists_ref, parts, wide, sources):
    target = lax.axis_index("seq").astype(jnp.int32)
    block = parts[0].shape[0]
    listed = [lists_ref[j, target] for j in range(lists_ref.shape[0])]
    count = jnp.int32(0)
    for part, source in zip(parts, sources(target)):
        is_listed = functools.reduce(jnp.logical_or, [entry == source for entry in listed])

        @pl.when(is_listed)
        def _take(part=part, count=count):
            rows = pl.ds(pl.multiple_of(count * block, block), block)
            wide[rows, :] = part[...].astype(jnp.float32)

        count += is_listed.astype(jnp.int32)
    for j in range(wide.shape[0] // block):

        @pl.when(count <= j)
        def _clear(j=j):
            wide[pl.ds(j * block, block), :] = jnp.zeros((block, wide.shape[1]), jnp.float32)

    return count


def weights_kernel(lists_ref, q_ref, own_ref, *refs, sources):
    *parts, out_ref, wide = refs
    kv_dev, tokens, dim = own_ref.shape
    rows_all = q_ref.shape[1]
    group = rows_all // tokens
    others = wide.shape[0] // (tokens * kv_dev)
    count = gather_listed(lists_ref, parts, wide, sources)
    factor = dim ** (-0.5) * math.log2(math.e)

    def fill(bias):
        for h in range(kv_dev):
            k_h = wide[pl.ds(h, others * tokens, stride=kv_dev), :].astype(jnp.bfloat16)
            k_h = jnp.concatenate([own_ref[h], k_h], axis=0)
            for first in range(0, rows_all, ROW_CHUNK):
                rows = pl.ds(first, ROW_CHUNK)
                s = lax.dot_general(
                    q_ref[h, rows, :], k_h, (((1,), (1,)), ((), ())), preferred_element_type=jnp.float32
                )
                row = (lax.broadcasted_iota(jnp.int32, (ROW_CHUNK, tokens), 0) + first) // group
                key = lax.broadcasted_iota(jnp.int32, (ROW_CHUNK, tokens), 1)
                scores = [jnp.where(key <= row, s[:, :tokens], NO_KEY)]
                for j in range(others):
                    score = s[:, (j + 1) * tokens : (j + 2) * tokens]
                    scores.append(score if bias is None else score + bias[j])
                top = scores[0]
                for score in scores[1:]:
                    top = jnp.maximum(top, score)
                top = jnp.max(top, axis=1, keepdims=True)
                for j, score in enumerate(scores):
                    probs = jnp.exp2((score - top) * factor).astype(jnp.bfloat16)
                    out_ref[h, rows, pl.ds(j * tokens, tokens)] = probs

    @pl.when(count == others)
    def _full():
        fill(None)

    @pl.when(count < others)
    def _some():
        fill([jnp.where(count <= j, NO_KEY, 0.0).astype(jnp.float32) for j in range(others)])


def weights(lists, queries, k_own, k_parts, sources):
    slots = lists.shape[0]
    kv_dev, rows, _ = queries.shape
    block, dim = k_parts[0].shape
    return pl.pallas_call(
        functools.partial(weights_kernel, sources=sources),
        out_shape=jax.ShapeDtypeStruct((kv_dev, rows, slots * block // kv_dev), jnp.bfloat16),
        in_specs=[pl.BlockSpec(memory_space=pltpu.SMEM)] + [vmem()] * (2 + len(k_parts)),
        out_specs=vmem(),
        scratch_shapes=[pltpu.VMEM(((slots - 1) * block, dim), jnp.float32)],
        compiler_params=params(),
        name="weights",
    )(lists, queries, k_own, *k_parts)


def merge_kernel(lists_ref, weights_ref, own_ref, *refs, sources):
    *parts, out_hbm, wide, values, out_ref, sems = refs
    kv_dev, tokens, dim = own_ref.shape
    group = weights_ref.shape[1] // tokens
    others = wide.shape[0] // (tokens * kv_dev)
    gather_listed(lists_ref, parts, wide, sources)
    ones = jnp.ones(((others + 1) * tokens, dim), jnp.bfloat16)
    for h in range(kv_dev):
        v_h = wide[pl.ds(h, others * tokens, stride=kv_dev), :].astype(jnp.bfloat16)
        v_h = jnp.concatenate([own_ref[h], v_h], axis=0)
        values[h] = jnp.concatenate([v_h, ones], axis=1)
    chunk = ROW_CHUNK // group
    copies = []
    for n in range(tokens // chunk):
        here = pl.ds(n * chunk, chunk)
        for h in range(kv_dev):
            probs = weights_ref[h, pl.ds(n * ROW_CHUNK, ROW_CHUNK), :]
            both = jnp.dot(probs, values[h], preferred_element_type=jnp.float32)
            merged = (both[:, :dim] / both[:, dim:]).reshape(chunk, group, dim)
            out_ref[here, pl.ds(h * group, group), :] = merged.astype(jnp.bfloat16)
        copy = pltpu.make_async_copy(out_ref.at[here], out_hbm.at[here], sems.at[n])
        copy.start()
        copies.append(copy)
    for copy in copies:
        copy.wait()


def merge(lists, probs, v_own, v_parts, sources):
    slots = lists.shape[0]
    kv_dev, rows, keys = probs.shape
    block, dim = v_parts[0].shape
    tokens = block // kv_dev
    out = (tokens, rows * kv_dev // tokens, dim)
    return pl.pallas_call(
        functools.partial(merge_kernel, sources=sources),
        out_shape=jax.ShapeDtypeStruct(out, jnp.bfloat16),
        in_specs=[pl.BlockSpec(memory_space=pltpu.SMEM)] + [vmem()] * (2 + len(v_parts)),
        out_specs=pl.BlockSpec(memory_space=pltpu.HBM),
        scratch_shapes=[
            pltpu.VMEM(((slots - 1) * block, dim), jnp.float32),
            pltpu.VMEM((kv_dev, keys, 2 * dim), jnp.bfloat16),
            pltpu.VMEM(out, jnp.bfloat16),
            pltpu.SemaphoreType.DMA((rows // ROW_CHUNK,)),
        ],
        compiler_params=params(),
        name="merge",
    )(lists, probs, v_own, *v_parts)


def ring_at(place, members):
    back = members - 1 - place
    return jnp.where(place < members // 2, 2 * place, 2 * back + 1)


def ring_place(block, members):
    return jnp.where(block % 2 == 0, block // 2, members - 1 - block // 2)


def round_the_ring(k_own, v_own, members):
    ring = list(range(0, members, 2)) + list(range(members - 1, 0, -2))
    ways = [
        [(ring[p], ring[(p + turn) % members]) for p in range(members)] for turn in (1, -1)
    ]

    def send(x, way):
        return lax.ppermute(x, "seq", ways[way])

    half = members // 2
    k_two, v_two, k_all, v_all = (k_own, k_own), (v_own, v_own), [], []
    for distance in range(1, half):
        k_two = tuple(send(x, way) for way, x in enumerate(k_two))
        v_two = tuple(send(x, way) for way, x in enumerate(v_two))
        k_two = lax.optimization_barrier(k_two)
        if distance < half - 1:
            v_two = lax.optimization_barrier(v_two)
        k_all += k_two
        v_all += v_two
    k_all.append(send(k_two[0], 0))
    v_last, _ = lax.optimization_barrier((v_two[1], k_two))
    v_all.append(send(v_last, 1))
    return k_all, v_all, k_two


def ring_sources(members):
    def sources(target):
        place = ring_place(target, members)
        turns = [turn for far in range(1, members // 2) for turn in (-far, far)] + [members // 2]
        return [ring_at(lax.rem(place + turn + members, members), members) for turn in turns]

    return sources


def others(row, target):
    slots = row.shape[-1]
    own_at = jnp.argmax(row == target[..., None], axis=-1)
    j = jnp.arange(slots - 1)
    return jnp.where(j >= own_at[..., None], row[..., 1:], row[..., :-1])


def relay(k_own, v_own, chosen, members):
    block, dim = k_own.shape
    stacked = jnp.stack([k_own, v_own]).reshape(2, members, block // members, dim)
    shares = lax.all_to_all(stacked, "seq", split_axis=1, concat_axis=1, tiled=True)
    wanted = others(chosen, jnp.arange(members, dtype=jnp.int32))
    picked = jnp.take(shares, jnp.maximum(wanted, 0), axis=1)
    arrived = lax.all_to_all(picked, "seq", split_axis=1, concat_axis=3, tiled=True)
    count = wanted.shape[1]
    k_parts, v_parts = ([arrived[n, 0, j].reshape(block, dim) for j in range(count)] for n in range(2))
    return k_parts, v_parts, jnp.where(wanted < 0, -1, jnp.arange(count, dtype=jnp.int32))


def per_device(queries, keys, values, chosen):
    members = lax.axis_size("seq")
    tokens, kv_dev, dim = keys.shape
    slots = chosen.shape[1]
    k_own = keys.reshape(tokens * kv_dev, dim)
    v_own = values.reshape(tokens * kv_dev, dim)
    if members <= MOST_ROUND:
        sources = ring_sources(members)
        k_parts, v_parts, before = round_the_ring(k_own, v_own, members)
        queries, _ = lax.optimization_barrier((queries, before))
    else:
        k_parts, v_parts, chosen = relay(k_own, v_own, chosen, members)

        def sources(_):
            return [jnp.int32(j) for j in range(slots - 1)]

    lists, q_ready, k_ready, v_ready = prepare(chosen.T, queries, k_own, v_own, kv_dev)
    probs = weights(lists, q_ready, k_ready, k_parts, sources)
    return merge(lists, probs, v_ready, v_parts, sources)


def solution(mesh):
    rows = P(("groups", "seq"), "head", None)
    return jax.shard_map(
        per_device,
        mesh=mesh,
        in_specs=(rows, rows, rows, P("groups", None)),
        out_specs=rows,
        check_vma=False,
    )
```

```python
import functools
import math

import jax
import jax.numpy as jnp
from jax import lax
from jax.experimental import pallas as pl
from jax.experimental.pallas import tpu as pltpu
from jax.sharding import PartitionSpec as P

NO_KEY = -1e30
ROW_CHUNK = 256
MOST_ROUND = 16
HEADS_OUT = 16


def params():
    return pltpu.CompilerParams(vmem_limit_bytes=16 * 2**20)


def vmem():
    return pl.BlockSpec(memory_space=pltpu.VMEM)


def prepare_kernel(
    lists_hbm, q_hbm, k_hbm, v_hbm, lists_out, q_out, k_out, v_out,
    q_ref, k_ref, v_ref, k_wide, v_wide, sems, *, kv_dev,
):
    whole = ((k_hbm, k_ref), (v_hbm, v_ref), (q_hbm, q_ref), (lists_hbm, lists_out))
    copies = [
        pltpu.make_async_copy(source, here, sems.at[n]) for n, (source, here) in enumerate(whole)
    ]
    for copy in copies:
        copy.start()
    tokens, heads, dim = q_ref.shape
    group = heads // kv_dev
    for copy, ref, wide, out in zip(copies, (k_ref, v_ref), (k_wide, v_wide), (k_out, v_out)):
        copy.wait()
        wide[...] = ref[...].astype(jnp.float32)
        for h in range(kv_dev):
            out[h] = wide[pl.ds(h, tokens, stride=kv_dev), :].astype(jnp.bfloat16)
    copies[2].wait()
    for h in range(kv_dev):
        q = q_ref[:, pl.ds(h * group, group), :].astype(jnp.float32)
        q_out[h] = q.reshape(tokens * group, dim).astype(jnp.bfloat16)
    copies[3].wait()


def prepare(lists, queries, k_own, v_own, kv_dev):
    tokens, heads, dim = queries.shape
    operands = [
        pltpu.with_memory_space_constraint(x, pltpu.HBM) for x in (lists, queries, k_own, v_own)
    ]
    by_head = jax.ShapeDtypeStruct((kv_dev, tokens, dim), jnp.bfloat16)
    return pl.pallas_call(
        functools.partial(prepare_kernel, kv_dev=kv_dev),
        out_shape=(
            jax.ShapeDtypeStruct(lists.shape, lists.dtype),
            jax.ShapeDtypeStruct((kv_dev, tokens * heads // kv_dev, dim), jnp.bfloat16),
            by_head,
            by_head,
        ),
        in_specs=[pl.BlockSpec(memory_space=pltpu.HBM)] * 4,
        out_specs=(vmem(), vmem(), vmem(), vmem()),
        scratch_shapes=[
            pltpu.VMEM(queries.shape, jnp.bfloat16),
            pltpu.VMEM(k_own.shape, jnp.bfloat16),
            pltpu.VMEM(k_own.shape, jnp.bfloat16),
            pltpu.VMEM(k_own.shape, jnp.float32),
            pltpu.VMEM(k_own.shape, jnp.float32),
            pltpu.SemaphoreType.DMA((4,)),
        ],
        compiler_params=params(),
        name="prepare",
    )(*operands)


def is_listed(lists_ref, target, source):
    same = [lists_ref[j, target] == source for j in range(lists_ref.shape[0])]
    return functools.reduce(jnp.logical_or, same)


def by_head(wide, h, kv_dev, keys):
    return wide[pl.ds(h, keys, stride=kv_dev), :].astype(jnp.bfloat16)


def with_ones(values):
    return jnp.concatenate([values, jnp.ones_like(values)], axis=1)


def put_out(out_ref, h, first, both, group):
    rows, dim = both.shape[0], both.shape[1] // 2
    merged = (both[:, :dim] / both[:, dim:]).reshape(rows // group, group, dim)
    tokens = pl.ds(first // group, rows // group)
    out_ref[tokens, pl.ds(h * group, group), :] = merged.astype(jnp.bfloat16)


def send_out(out_ref, out_hbm, sems, h, group):
    done = (h + 1) * group
    if done % HEADS_OUT:
        return []
    heads = pl.ds(done - HEADS_OUT, HEADS_OUT)
    copy = pltpu.make_async_copy(
        out_ref.at[:, heads, :], out_hbm.at[:, heads, :], sems.at[done // HEADS_OUT - 1]
    )
    copy.start()
    return [copy]


def attend_kernel(lists_ref, q_ref, k_own_ref, v_own_ref, *refs, parts, sources, last):
    k_parts, v_parts = refs[:parts], refs[parts : 2 * parts]
    out_hbm, *state, k_wide, v_wide, out_ref, sems = refs[2 * parts :]
    kv_dev, tokens, dim = k_own_ref.shape
    rows_all = q_ref.shape[1]
    group = rows_all // tokens
    block = tokens * kv_dev
    most = k_wide.shape[0] // block
    factor = dim ** (-0.5) * math.log2(math.e)
    target = lax.axis_index("seq").astype(jnp.int32)

    count = jnp.int32(0)
    for source, k_part, v_part in zip(sources(target), k_parts, v_parts):
        take = is_listed(lists_ref, target, source)

        @pl.when(take)
        def _take(k_part=k_part, v_part=v_part, count=count):
            rows = pl.ds(pl.multiple_of(count * block, block), block)
            k_wide[rows, :] = k_part[...].astype(jnp.float32)
            v_wide[rows, :] = v_part[...].astype(jnp.float32)

        count += take.astype(jnp.int32)

    def run(others, final):
        copies = []
        for h in range(kv_dev):
            k_h, v_h = k_own_ref[h], v_own_ref[h]
            if others:
                keys = others * tokens
                k_h = jnp.concatenate([k_h, by_head(k_wide, h, kv_dev, keys)], axis=0)
                v_h = jnp.concatenate([v_h, by_head(v_wide, h, kv_dev, keys)], axis=0)
            v_h = with_ones(v_h)
            for first in range(0, rows_all, ROW_CHUNK):
                rows = pl.ds(first, ROW_CHUNK)
                s = lax.dot_general(
                    q_ref[h, rows, :], k_h, (((1,), (1,)), ((), ())), preferred_element_type=jnp.float32
                )
                row = (lax.broadcasted_iota(jnp.int32, (ROW_CHUNK, tokens), 0) + first) // group
                key = lax.broadcasted_iota(jnp.int32, (ROW_CHUNK, tokens), 1)
                scores = [jnp.where(key <= row, s[:, :tokens], NO_KEY)]
                scores += [s[:, (j + 1) * tokens : (j + 2) * tokens] for j in range(others)]
                top = jnp.max(functools.reduce(jnp.maximum, scores), axis=1, keepdims=True)
                probs = [jnp.exp2((score - top) * factor).astype(jnp.bfloat16) for score in scores]
                both = jnp.dot(
                    jnp.concatenate(probs, axis=1), v_h, preferred_element_type=jnp.float32
                )
                if final:
                    put_out(out_ref, h, first, both, group)
                else:
                    state[0][h, rows, :] = jnp.broadcast_to(top, (ROW_CHUNK, dim))
                    state[1][h, rows, :] = both
            if final:
                copies += send_out(out_ref, out_hbm, sems, h, group)
        for copy in copies:
            copy.wait()

    unfinished = False if last is None else is_listed(lists_ref, target, last(target))
    for others in range(most + 1):

        @pl.when(jnp.logical_and(count == others, jnp.logical_not(unfinished)))
        def _whole(others=others):
            run(others, True)

        if last is not None and others < most:

            @pl.when(jnp.logical_and(count == others, unfinished))
            def _part(others=others):
                run(others, False)


def attend(lists, queries, k_own, v_own, k_parts, v_parts, sources, last):
    kv_dev, rows, dim = queries.shape
    tokens = k_own.shape[1]
    rest = (lists.shape[0] - 1) * tokens * kv_dev
    out = jax.ShapeDtypeStruct((tokens, rows * kv_dev // tokens, dim), jnp.bfloat16)
    state = [] if last is None else [
        jax.ShapeDtypeStruct((kv_dev, rows, wide), jnp.float32) for wide in (dim, 2 * dim)
    ]
    hbm, smem = (pl.BlockSpec(memory_space=space) for space in (pltpu.HBM, pltpu.SMEM))
    return pl.pallas_call(
        functools.partial(attend_kernel, parts=len(k_parts), sources=sources, last=last),
        out_shape=(out, *state),
        in_specs=[smem] + [vmem()] * (3 + 2 * len(k_parts)),
        out_specs=(hbm, *(vmem() for _ in state)),
        scratch_shapes=[
            pltpu.VMEM((rest, dim), jnp.float32),
            pltpu.VMEM((rest, dim), jnp.float32),
            pltpu.VMEM(out.shape, jnp.bfloat16),
            pltpu.SemaphoreType.DMA((out.shape[1] // HEADS_OUT,)),
        ],
        compiler_params=params(),
        name="attend",
    )(lists, queries, k_own, v_own, *k_parts, *v_parts)


def last_kernel(
    lists_ref, q_ref, top_ref, both_ref, k_ref, v_ref, _, out_hbm, k_wide, v_wide, out_ref, sems, *, last
):
    kv_dev, rows_all, dim = q_ref.shape
    tokens = k_ref.shape[0] // kv_dev
    group = rows_all // tokens
    factor = dim ** (-0.5) * math.log2(math.e)
    target = lax.axis_index("seq").astype(jnp.int32)

    @pl.when(is_listed(lists_ref, target, last(target)))
    def _add():
        k_wide[...] = k_ref[...].astype(jnp.float32)
        v_wide[...] = v_ref[...].astype(jnp.float32)
        copies = []
        for h in range(kv_dev):
            k_h = by_head(k_wide, h, kv_dev, tokens)
            v_h = with_ones(by_head(v_wide, h, kv_dev, tokens))
            for first in range(0, rows_all, ROW_CHUNK):
                rows = pl.ds(first, ROW_CHUNK)
                s = lax.dot_general(
                    q_ref[h, rows, :], k_h, (((1,), (1,)), ((), ())), preferred_element_type=jnp.float32
                )
                before = top_ref[h, rows, :]
                top = jnp.maximum(before, jnp.max(s, axis=1, keepdims=True))
                probs = jnp.exp2((s - top) * factor).astype(jnp.bfloat16)
                shrink = jnp.exp2((before - top) * factor)
                both = jnp.dot(probs, v_h, preferred_element_type=jnp.float32)
                both += both_ref[h, rows, :] * jnp.concatenate([shrink, shrink], axis=1)
                put_out(out_ref, h, first, both, group)
            copies += send_out(out_ref, out_hbm, sems, h, group)
        for copy in copies:
            copy.wait()


def attend_last(lists, queries, state, k_last, v_last, out, last):
    top, both = state
    hbm, smem = (pl.BlockSpec(memory_space=space) for space in (pltpu.HBM, pltpu.SMEM))
    return pl.pallas_call(
        functools.partial(last_kernel, last=last),
        out_shape=jax.ShapeDtypeStruct(out.shape, out.dtype),
        in_specs=[smem] + [vmem()] * 5 + [hbm],
        out_specs=hbm,
        input_output_aliases={6: 0},
        scratch_shapes=[
            pltpu.VMEM(k_last.shape, jnp.float32),
            pltpu.VMEM(k_last.shape, jnp.float32),
            pltpu.VMEM(out.shape, jnp.bfloat16),
            pltpu.SemaphoreType.DMA((out.shape[1] // HEADS_OUT,)),
        ],
        compiler_params=params(),
        name="attend_last",
    )(lists, queries, top, both, k_last, v_last, out)


def ring_at(place, members):
    back = members - 1 - place
    return jnp.where(place < members // 2, 2 * place, 2 * back + 1)


def ring_place(block, members):
    return jnp.where(block % 2 == 0, block // 2, members - 1 - block // 2)


def round_the_ring(k_own, v_own, ready, members):
    ring = list(range(0, members, 2)) + list(range(members - 1, 0, -2))
    ways = [
        [(ring[p], ring[(p + turn) % members]) for p in range(members)] for turn in (1, -1)
    ]

    def send(x, way):
        return lax.ppermute(x, "seq", ways[way])

    half = members // 2
    k_two, v_two, k_all, v_all = [k_own, k_own], [v_own, v_own], [], []
    for distance in range(1, half):
        ahead = send(k_two[0], 0), send(v_two[1], 1)
        behind = send(v_two[0], 0), send(k_two[1], 1)
        if distance == 1:
            ahead, ready = lax.optimization_barrier((ahead, ready))
        ahead = lax.optimization_barrier(ahead)
        behind = lax.optimization_barrier(behind)
        k_two, v_two = [ahead[0], behind[1]], [behind[0], ahead[1]]
        k_all += k_two
        v_all += v_two
    return k_all, v_all, send(k_two[0], 0), send(v_two[1], 1), ready


def ring_sources(members):
    def at(target, turn):
        place = lax.rem(ring_place(target, members) + turn + members, members)
        return ring_at(place, members)

    def sources(target):
        return [at(target, turn) for far in range(1, members // 2) for turn in (-far, far)]

    return sources, lambda target: at(target, members // 2)


def others(row, target):
    slots = row.shape[-1]
    own_at = jnp.argmax(row == target[..., None], axis=-1)
    j = jnp.arange(slots - 1)
    return jnp.where(j >= own_at[..., None], row[..., 1:], row[..., :-1])


def relay(k_own, v_own, chosen, members):
    block, dim = k_own.shape
    stacked = jnp.stack([k_own, v_own]).reshape(2, members, block // members, dim)
    shares = lax.all_to_all(stacked, "seq", split_axis=1, concat_axis=1, tiled=True)
    wanted = others(chosen, jnp.arange(members, dtype=jnp.int32))
    picked = jnp.take(shares, jnp.maximum(wanted, 0), axis=1)
    arrived = lax.all_to_all(picked, "seq", split_axis=1, concat_axis=3, tiled=True)
    count = wanted.shape[1]
    k_parts, v_parts = ([arrived[n, 0, j].reshape(block, dim) for j in range(count)] for n in range(2))
    return k_parts, v_parts, jnp.where(wanted < 0, -1, jnp.arange(count, dtype=jnp.int32))


def per_device(queries, keys, values, chosen):
    members = lax.axis_size("seq")
    tokens, kv_dev, dim = keys.shape
    k_own = keys.reshape(tokens * kv_dev, dim)
    v_own = values.reshape(tokens * kv_dev, dim)
    if members <= MOST_ROUND:
        ready = prepare(chosen.T, queries, k_own, v_own, kv_dev)
        k_parts, v_parts, k_last, v_last, ready = round_the_ring(k_own, v_own, ready, members)
        lists, q_ready, k_ready, v_ready = ready
        sources, last = ring_sources(members)
        out, *state = attend(lists, q_ready, k_ready, v_ready, k_parts, v_parts, sources, last)
        return attend_last(lists, q_ready, state, k_last, v_last, out, last)

    k_parts, v_parts, mine = relay(k_own, v_own, chosen, members)
    lists, *ready = prepare(mine.T, queries, k_own, v_own, kv_dev)

    def sources(_):
        return [jnp.int32(j) for j in range(len(k_parts))]

    lists = jnp.concatenate([lists, jnp.full_like(lists[:1], -1)])
    return attend(lists, *ready, k_parts, v_parts, sources, None)[0]


def solution(mesh):
    rows = P(("groups", "seq"), "head", None)
    return jax.shard_map(
        per_device,
        mesh=mesh,
        in_specs=(rows, rows, rows, P("groups", None)),
        out_specs=rows,
        check_vma=False,
    )
```

```python
import functools
import math

import jax
import jax.numpy as jnp
from jax import lax
from jax.experimental import pallas as pl
from jax.experimental.pallas import tpu as pltpu
from jax.sharding import PartitionSpec as P

NO_KEY = -1e30
ROW_CHUNK = 256
MOST_ROUND = 16
HEADS_OUT = 16
KEY_TILE = 256


def params():
    return pltpu.CompilerParams(vmem_limit_bytes=16 * 2**20)


def vmem():
    return pl.BlockSpec(memory_space=pltpu.VMEM)


def prepare_kernel(
    lists_hbm, q_hbm, k_hbm, v_hbm, lists_out, q_out, k_out, v_out,
    q_ref, k_ref, v_ref, k_wide, v_wide, sems, *, kv_dev,
):
    whole = ((k_hbm, k_ref), (v_hbm, v_ref), (q_hbm, q_ref), (lists_hbm, lists_out))
    copies = [
        pltpu.make_async_copy(source, here, sems.at[n]) for n, (source, here) in enumerate(whole)
    ]
    for copy in copies:
        copy.start()
    tokens, heads, dim = q_ref.shape
    group = heads // kv_dev
    for copy, ref, wide, out in zip(copies, (k_ref, v_ref), (k_wide, v_wide), (k_out, v_out)):
        copy.wait()
        wide[...] = ref[...].astype(jnp.float32)
        for h in range(kv_dev):
            out[h] = wide[pl.ds(h, tokens, stride=kv_dev), :].astype(jnp.bfloat16)
    copies[2].wait()
    for h in range(kv_dev):
        q = q_ref[:, pl.ds(h * group, group), :].astype(jnp.float32)
        q_out[h] = q.reshape(tokens * group, dim).astype(jnp.bfloat16)
    copies[3].wait()


def prepare(lists, queries, k_own, v_own, kv_dev):
    tokens, heads, dim = queries.shape
    operands = [
        pltpu.with_memory_space_constraint(x, pltpu.HBM) for x in (lists, queries, k_own, v_own)
    ]
    by_head = jax.ShapeDtypeStruct((kv_dev, tokens, dim), jnp.bfloat16)
    return pl.pallas_call(
        functools.partial(prepare_kernel, kv_dev=kv_dev),
        out_shape=(
            jax.ShapeDtypeStruct(lists.shape, lists.dtype),
            jax.ShapeDtypeStruct((kv_dev, tokens * heads // kv_dev, dim), jnp.bfloat16),
            by_head,
            by_head,
        ),
        in_specs=[pl.BlockSpec(memory_space=pltpu.HBM)] * 4,
        out_specs=(vmem(), vmem(), vmem(), vmem()),
        scratch_shapes=[
            pltpu.VMEM(queries.shape, jnp.bfloat16),
            pltpu.VMEM(k_own.shape, jnp.bfloat16),
            pltpu.VMEM(k_own.shape, jnp.bfloat16),
            pltpu.VMEM(k_own.shape, jnp.float32),
            pltpu.VMEM(k_own.shape, jnp.float32),
            pltpu.SemaphoreType.DMA((4,)),
        ],
        compiler_params=params(),
        name="prepare",
    )(*operands)


def is_listed(lists_ref, target, source):
    same = [lists_ref[j, target] == source for j in range(lists_ref.shape[0])]
    return functools.reduce(jnp.logical_or, same)


def by_head(wide, h, kv_dev, keys):
    return wide[pl.ds(h, keys, stride=kv_dev), :].astype(jnp.bfloat16)


def pad_keys(x, axis):
    missing = -x.shape[axis] % KEY_TILE
    if not missing:
        return x
    shape = x.shape[:axis] + (missing,) + x.shape[axis + 1 :]
    return jnp.concatenate([x, jnp.zeros(shape, x.dtype)], axis=axis)


def with_ones(values):
    return pad_keys(jnp.concatenate([values, jnp.ones_like(values)], axis=1), 0)


def scores_of(q, keys):
    return lax.dot_general(q, keys, (((1,), (1,)), ((), ())), preferred_element_type=jnp.float32)


def put_out(out_ref, h, first, both, group):
    rows, dim = both.shape[0], both.shape[1] // 2
    merged = (both[:, :dim] / both[:, dim:]).reshape(rows // group, group, dim)
    tokens = pl.ds(first // group, rows // group)
    out_ref[tokens, pl.ds(h * group, group), :] = merged.astype(jnp.bfloat16)


def send_out(out_ref, out_hbm, sems, h, group):
    done = (h + 1) * group
    if done % HEADS_OUT:
        return []
    heads = pl.ds(done - HEADS_OUT, HEADS_OUT)
    copy = pltpu.make_async_copy(
        out_ref.at[:, heads, :], out_hbm.at[:, heads, :], sems.at[done // HEADS_OUT - 1]
    )
    copy.start()
    return [copy]


def attend_kernel(lists_ref, q_ref, k_own_ref, v_own_ref, *refs, parts, sources, last):
    k_parts, v_parts = refs[:parts], refs[parts : 2 * parts]
    out_hbm, *state, k_wide, v_wide, out_ref, sems = refs[2 * parts :]
    kv_dev, tokens, dim = k_own_ref.shape
    rows_all = q_ref.shape[1]
    group = rows_all // tokens
    block = tokens * kv_dev
    most = k_wide.shape[0] // block
    factor = dim ** (-0.5) * math.log2(math.e)
    target = lax.axis_index("seq").astype(jnp.int32)

    count = jnp.int32(0)
    for source, k_part, v_part in zip(sources(target), k_parts, v_parts):
        take = is_listed(lists_ref, target, source)

        @pl.when(take)
        def _take(k_part=k_part, v_part=v_part, count=count):
            rows = pl.ds(pl.multiple_of(count * block, block), block)
            k_wide[rows, :] = k_part[...].astype(jnp.float32)
            v_wide[rows, :] = v_part[...].astype(jnp.float32)

        count += take.astype(jnp.int32)

    def run(others, final):
        copies = []
        for h in range(kv_dev):
            k_h, v_h = k_own_ref[h], v_own_ref[h]
            if others:
                keys = others * tokens
                k_h = jnp.concatenate([k_h, by_head(k_wide, h, kv_dev, keys)], axis=0)
                v_h = jnp.concatenate([v_h, by_head(v_wide, h, kv_dev, keys)], axis=0)
            k_h, v_h = pad_keys(k_h, 0), with_ones(v_h)
            for first in range(0, rows_all, ROW_CHUNK):
                rows = pl.ds(first, ROW_CHUNK)
                s = scores_of(q_ref[h, rows, :], k_h)
                row = (lax.broadcasted_iota(jnp.int32, (ROW_CHUNK, tokens), 0) + first) // group
                key = lax.broadcasted_iota(jnp.int32, (ROW_CHUNK, tokens), 1)
                scores = [jnp.where(key <= row, s[:, :tokens], NO_KEY)]
                scores += [s[:, (j + 1) * tokens : (j + 2) * tokens] for j in range(others)]
                top = jnp.max(functools.reduce(jnp.maximum, scores), axis=1, keepdims=True)
                probs = [jnp.exp2((score - top) * factor).astype(jnp.bfloat16) for score in scores]
                probs = pad_keys(jnp.concatenate(probs, axis=1), 1)
                both = jnp.dot(probs, v_h, preferred_element_type=jnp.float32)
                if final:
                    put_out(out_ref, h, first, both, group)
                else:
                    state[0][h, rows, :] = jnp.broadcast_to(top, (ROW_CHUNK, dim))
                    state[1][h, rows, :] = both
            if final:
                copies += send_out(out_ref, out_hbm, sems, h, group)
        for copy in copies:
            copy.wait()

    unfinished = False if last is None else is_listed(lists_ref, target, last(target))
    for others in range(most + 1):

        @pl.when(jnp.logical_and(count == others, jnp.logical_not(unfinished)))
        def _whole(others=others):
            run(others, True)

        if last is not None and others < most:

            @pl.when(jnp.logical_and(count == others, unfinished))
            def _part(others=others):
                run(others, False)


def attend(lists, queries, k_own, v_own, k_parts, v_parts, sources, last):
    kv_dev, rows, dim = queries.shape
    tokens = k_own.shape[1]
    rest = (lists.shape[0] - 1) * tokens * kv_dev
    out = jax.ShapeDtypeStruct((tokens, rows * kv_dev // tokens, dim), jnp.bfloat16)
    state = [] if last is None else [
        jax.ShapeDtypeStruct((kv_dev, rows, wide), jnp.float32) for wide in (dim, 2 * dim)
    ]
    hbm, smem = (pl.BlockSpec(memory_space=space) for space in (pltpu.HBM, pltpu.SMEM))
    return pl.pallas_call(
        functools.partial(attend_kernel, parts=len(k_parts), sources=sources, last=last),
        out_shape=(out, *state),
        in_specs=[smem] + [vmem()] * (3 + 2 * len(k_parts)),
        out_specs=(hbm, *(vmem() for _ in state)),
        scratch_shapes=[
            pltpu.VMEM((rest, dim), jnp.float32),
            pltpu.VMEM((rest, dim), jnp.float32),
            pltpu.VMEM(out.shape, jnp.bfloat16),
            pltpu.SemaphoreType.DMA((out.shape[1] // HEADS_OUT,)),
        ],
        compiler_params=params(),
        name="attend",
    )(lists, queries, k_own, v_own, *k_parts, *v_parts)


def last_kernel(
    lists_ref, q_ref, top_ref, both_ref, k_ref, v_ref, _, out_hbm, k_wide, v_wide, out_ref, sems, *, last
):
    kv_dev, rows_all, dim = q_ref.shape
    tokens = k_ref.shape[0] // kv_dev
    group = rows_all // tokens
    factor = dim ** (-0.5) * math.log2(math.e)
    target = lax.axis_index("seq").astype(jnp.int32)

    @pl.when(is_listed(lists_ref, target, last(target)))
    def _add():
        k_wide[...] = k_ref[...].astype(jnp.float32)
        v_wide[...] = v_ref[...].astype(jnp.float32)
        copies = []
        for h in range(kv_dev):
            k_h = pad_keys(by_head(k_wide, h, kv_dev, tokens), 0)
            v_h = with_ones(by_head(v_wide, h, kv_dev, tokens))
            for first in range(0, rows_all, ROW_CHUNK):
                rows = pl.ds(first, ROW_CHUNK)
                s = scores_of(q_ref[h, rows, :], k_h)[:, :tokens]
                before = top_ref[h, rows, :]
                top = jnp.maximum(before, jnp.max(s, axis=1, keepdims=True))
                probs = pad_keys(jnp.exp2((s - top) * factor).astype(jnp.bfloat16), 1)
                shrink = jnp.exp2((before - top) * factor)
                both = jnp.dot(probs, v_h, preferred_element_type=jnp.float32)
                both += both_ref[h, rows, :] * jnp.concatenate([shrink, shrink], axis=1)
                put_out(out_ref, h, first, both, group)
            copies += send_out(out_ref, out_hbm, sems, h, group)
        for copy in copies:
            copy.wait()


def attend_last(lists, queries, state, k_last, v_last, out, last):
    top, both = state
    hbm, smem = (pl.BlockSpec(memory_space=space) for space in (pltpu.HBM, pltpu.SMEM))
    return pl.pallas_call(
        functools.partial(last_kernel, last=last),
        out_shape=jax.ShapeDtypeStruct(out.shape, out.dtype),
        in_specs=[smem] + [vmem()] * 5 + [hbm],
        out_specs=hbm,
        input_output_aliases={6: 0},
        scratch_shapes=[
            pltpu.VMEM(k_last.shape, jnp.float32),
            pltpu.VMEM(k_last.shape, jnp.float32),
            pltpu.VMEM(out.shape, jnp.bfloat16),
            pltpu.SemaphoreType.DMA((out.shape[1] // HEADS_OUT,)),
        ],
        compiler_params=params(),
        name="attend_last",
    )(lists, queries, top, both, k_last, v_last, out)


def ring_at(place, members):
    back = members - 1 - place
    return jnp.where(place < members // 2, 2 * place, 2 * back + 1)


def ring_place(block, members):
    return jnp.where(block % 2 == 0, block // 2, members - 1 - block // 2)


def round_the_ring(k_own, v_own, ready, members):
    ring = list(range(0, members, 2)) + list(range(members - 1, 0, -2))
    ways = [
        [(ring[p], ring[(p + turn) % members]) for p in range(members)] for turn in (1, -1)
    ]

    def send(x, way):
        return lax.ppermute(x, "seq", ways[way])

    half = members // 2
    k_two, v_two, k_all, v_all = [k_own, k_own], [v_own, v_own], [], []
    for distance in range(1, half):
        ahead = send(k_two[0], 0), send(v_two[1], 1)
        behind = send(v_two[0], 0), send(k_two[1], 1)
        if distance == 1:
            ahead, ready = lax.optimization_barrier((ahead, ready))
        ahead = lax.optimization_barrier(ahead)
        behind = lax.optimization_barrier(behind)
        k_two, v_two = [ahead[0], behind[1]], [behind[0], ahead[1]]
        k_all += k_two
        v_all += v_two
    return k_all, v_all, send(k_two[0], 0), send(v_two[1], 1), ready


def ring_sources(members):
    def at(target, turn):
        place = lax.rem(ring_place(target, members) + turn + members, members)
        return ring_at(place, members)

    def sources(target):
        return [at(target, turn) for far in range(1, members // 2) for turn in (-far, far)]

    return sources, lambda target: at(target, members // 2)


def others(row, target):
    slots = row.shape[-1]
    own_at = jnp.argmax(row == target[..., None], axis=-1)
    j = jnp.arange(slots - 1)
    return jnp.where(j >= own_at[..., None], row[..., 1:], row[..., :-1])


def relay(k_own, v_own, chosen, members):
    block, dim = k_own.shape
    stacked = jnp.stack([k_own, v_own]).reshape(2, members, block // members, dim)
    shares = lax.all_to_all(stacked, "seq", split_axis=1, concat_axis=1, tiled=True)
    wanted = others(chosen, jnp.arange(members, dtype=jnp.int32))
    picked = jnp.take(shares, jnp.maximum(wanted, 0), axis=1)
    arrived = lax.all_to_all(picked, "seq", split_axis=1, concat_axis=3, tiled=True)
    count = wanted.shape[1]
    k_parts, v_parts = ([arrived[n, 0, j].reshape(block, dim) for j in range(count)] for n in range(2))
    return k_parts, v_parts, jnp.where(wanted < 0, -1, jnp.arange(count, dtype=jnp.int32))


def per_device(queries, keys, values, chosen):
    members = lax.axis_size("seq")
    tokens, kv_dev, dim = keys.shape
    k_own = keys.reshape(tokens * kv_dev, dim)
    v_own = values.reshape(tokens * kv_dev, dim)
    if members <= MOST_ROUND:
        ready = prepare(chosen.T, queries, k_own, v_own, kv_dev)
        k_parts, v_parts, k_last, v_last, ready = round_the_ring(k_own, v_own, ready, members)
        lists, q_ready, k_ready, v_ready = ready
        sources, last = ring_sources(members)
        out, *state = attend(lists, q_ready, k_ready, v_ready, k_parts, v_parts, sources, last)
        return attend_last(lists, q_ready, state, k_last, v_last, out, last)

    k_parts, v_parts, mine = relay(k_own, v_own, chosen, members)
    lists, *ready = prepare(mine.T, queries, k_own, v_own, kv_dev)

    def sources(_):
        return [jnp.int32(j) for j in range(len(k_parts))]

    lists = jnp.concatenate([lists, jnp.full_like(lists[:1], -1)])
    return attend(lists, *ready, k_parts, v_parts, sources, None)[0]


def solution(mesh):
    rows = P(("groups", "seq"), "head", None)
    return jax.shard_map(
        per_device,
        mesh=mesh,
        in_specs=(rows, rows, rows, P("groups", None)),
        out_specs=rows,
        check_vma=False,
    )
```

```python
import functools
import math

import jax
import jax.numpy as jnp
from jax import lax
from jax.experimental import pallas as pl
from jax.experimental.pallas import tpu as pltpu
from jax.sharding import PartitionSpec as P

NO_KEY = -1e30
ROW_CHUNK = 256
MOST_ROUND = 16


def params():
    return pltpu.CompilerParams(vmem_limit_bytes=16 * 2**20)


def vmem():
    return pl.BlockSpec(memory_space=pltpu.VMEM)


def prepare_kernel(
    lists_hbm, q_hbm, k_hbm, v_hbm, lists_out, q_out, k_out, v_out,
    q_ref, k_ref, v_ref, k_wide, v_wide, sems, *, kv_dev,
):
    whole = ((k_hbm, k_ref), (v_hbm, v_ref), (q_hbm, q_ref), (lists_hbm, lists_out))
    copies = [
        pltpu.make_async_copy(source, here, sems.at[n]) for n, (source, here) in enumerate(whole)
    ]
    for copy in copies:
        copy.start()
    tokens, heads, dim = q_ref.shape
    group = heads // kv_dev
    for copy, ref, wide, out in zip(copies, (k_ref, v_ref), (k_wide, v_wide), (k_out, v_out)):
        copy.wait()
        wide[...] = ref[...].astype(jnp.float32)
        for h in range(kv_dev):
            out[h] = wide[pl.ds(h, tokens, stride=kv_dev), :].astype(jnp.bfloat16)
    copies[2].wait()
    for h in range(kv_dev):
        q = q_ref[:, pl.ds(h * group, group), :].astype(jnp.float32)
        q_out[h] = q.reshape(tokens * group, dim).astype(jnp.bfloat16)
    copies[3].wait()


def prepare(lists, queries, k_own, v_own, kv_dev):
    tokens, heads, dim = queries.shape
    operands = [
        pltpu.with_memory_space_constraint(x, pltpu.HBM) for x in (lists, queries, k_own, v_own)
    ]
    by_head = jax.ShapeDtypeStruct((kv_dev, tokens, dim), jnp.bfloat16)
    return pl.pallas_call(
        functools.partial(prepare_kernel, kv_dev=kv_dev),
        out_shape=(
            jax.ShapeDtypeStruct(lists.shape, lists.dtype),
            jax.ShapeDtypeStruct((kv_dev, tokens * heads // kv_dev, dim), jnp.bfloat16),
            by_head,
            by_head,
        ),
        in_specs=[pl.BlockSpec(memory_space=pltpu.HBM)] * 4,
        out_specs=(vmem(), vmem(), vmem(), vmem()),
        scratch_shapes=[
            pltpu.VMEM(queries.shape, jnp.bfloat16),
            pltpu.VMEM(k_own.shape, jnp.bfloat16),
            pltpu.VMEM(k_own.shape, jnp.bfloat16),
            pltpu.VMEM(k_own.shape, jnp.float32),
            pltpu.VMEM(k_own.shape, jnp.float32),
            pltpu.SemaphoreType.DMA((4,)),
        ],
        compiler_params=params(),
        name="prepare",
    )(*operands)


def is_listed(lists_ref, target, source):
    same = [lists_ref[j, target] == source for j in range(lists_ref.shape[0])]
    return functools.reduce(jnp.logical_or, same)


def by_head(wide, h, kv_dev, keys):
    return wide[pl.ds(h, keys, stride=kv_dev), :].astype(jnp.bfloat16)


def with_ones(values):
    return jnp.concatenate([values, jnp.ones_like(values)], axis=1)


def scores_of(q, keys):
    return lax.dot_general(q, keys, (((1,), (1,)), ((), ())), preferred_element_type=jnp.float32)


def put_out(out_ref, h, first, both, group):
    rows, dim = both.shape[0], both.shape[1] // 2
    merged = (both[:, :dim] / both[:, dim:]).reshape(rows // group, group, dim)
    tokens = pl.ds(first // group, rows // group)
    out_ref[tokens, pl.ds(h * group, group), :] = merged.astype(jnp.bfloat16)


def over_rows(rows_all, body, out_ref, out_hbm, sems, sends):
    chunks = rows_all // ROW_CHUNK
    tokens = out_ref.shape[0] // chunks

    def copy(n):
        here = pl.ds(pl.multiple_of(n * tokens, tokens), tokens)
        return pltpu.make_async_copy(out_ref.at[here], out_hbm.at[here], sems.at[n])

    def step(n, carry):
        body(pl.multiple_of(n * ROW_CHUNK, ROW_CHUNK))
        if sends:
            copy(n).start()
        return carry

    lax.fori_loop(0, chunks, step, 0)
    if sends:
        for n in range(chunks):
            copy(n).wait()


def attend_kernel(lists_ref, q_ref, k_own_ref, v_own_ref, *refs, parts, sources, last):
    k_parts, v_parts = refs[:parts], refs[parts : 2 * parts]
    out_hbm, *state, k_wide, v_wide, k_ready, v_ready, out_ref, sems = refs[2 * parts :]
    kv_dev, tokens, dim = k_own_ref.shape
    rows_all = q_ref.shape[1]
    group = rows_all // tokens
    block = tokens * kv_dev
    most = k_wide.shape[0] // block
    factor = dim ** (-0.5) * math.log2(math.e)
    target = lax.axis_index("seq").astype(jnp.int32)

    count = jnp.int32(0)
    for source, k_part, v_part in zip(sources(target), k_parts, v_parts):
        take = is_listed(lists_ref, target, source)

        @pl.when(take)
        def _take(k_part=k_part, v_part=v_part, count=count):
            rows = pl.ds(pl.multiple_of(count * block, block), block)
            k_wide[rows, :] = k_part[...].astype(jnp.float32)
            v_wide[rows, :] = v_part[...].astype(jnp.float32)

        count += take.astype(jnp.int32)

    def run(others, final):
        keys = (others + 1) * tokens
        for h in range(kv_dev):
            k_h, v_h = k_own_ref[h], v_own_ref[h]
            if others:
                k_h = jnp.concatenate([k_h, by_head(k_wide, h, kv_dev, others * tokens)], axis=0)
                v_h = jnp.concatenate([v_h, by_head(v_wide, h, kv_dev, others * tokens)], axis=0)
            k_ready[h, pl.ds(0, keys), :] = k_h
            v_ready[h, pl.ds(0, keys), :] = with_ones(v_h)

        def rows_from(first):
            rows = pl.ds(first, ROW_CHUNK)
            row = (lax.broadcasted_iota(jnp.int32, (ROW_CHUNK, tokens), 0) + first) // group
            key = lax.broadcasted_iota(jnp.int32, (ROW_CHUNK, tokens), 1)
            for h in range(kv_dev):
                s = scores_of(q_ref[h, rows, :], k_ready[h, pl.ds(0, keys), :])
                scores = [jnp.where(key <= row, s[:, :tokens], NO_KEY)]
                scores += [s[:, (j + 1) * tokens : (j + 2) * tokens] for j in range(others)]
                top = jnp.max(functools.reduce(jnp.maximum, scores), axis=1, keepdims=True)
                probs = [jnp.exp2((score - top) * factor).astype(jnp.bfloat16) for score in scores]
                probs = jnp.concatenate(probs, axis=1)
                both = jnp.dot(
                    probs, v_ready[h, pl.ds(0, keys), :], preferred_element_type=jnp.float32
                )
                if final:
                    put_out(out_ref, h, first, both, group)
                else:
                    state[0][h, rows, :] = jnp.broadcast_to(top, (ROW_CHUNK, dim))
                    state[1][h, rows, :] = both

        over_rows(rows_all, rows_from, out_ref, out_hbm, sems, final)

    unfinished = False if last is None else is_listed(lists_ref, target, last(target))
    for others in range(most + 1):

        @pl.when(jnp.logical_and(count == others, jnp.logical_not(unfinished)))
        def _whole(others=others):
            run(others, True)

        if last is not None and others < most:

            @pl.when(jnp.logical_and(count == others, unfinished))
            def _part(others=others):
                run(others, False)


def attend(lists, queries, k_own, v_own, k_parts, v_parts, sources, last):
    kv_dev, rows, dim = queries.shape
    tokens = k_own.shape[1]
    slots = lists.shape[0]
    rest = (slots - 1) * tokens * kv_dev
    out = jax.ShapeDtypeStruct((tokens, rows * kv_dev // tokens, dim), jnp.bfloat16)
    state = [] if last is None else [
        jax.ShapeDtypeStruct((kv_dev, rows, wide), jnp.float32) for wide in (dim, 2 * dim)
    ]
    hbm, smem = (pl.BlockSpec(memory_space=space) for space in (pltpu.HBM, pltpu.SMEM))
    return pl.pallas_call(
        functools.partial(attend_kernel, parts=len(k_parts), sources=sources, last=last),
        out_shape=(out, *state),
        in_specs=[smem] + [vmem()] * (3 + 2 * len(k_parts)),
        out_specs=(hbm, *(vmem() for _ in state)),
        scratch_shapes=[
            pltpu.VMEM((rest, dim), jnp.float32),
            pltpu.VMEM((rest, dim), jnp.float32),
            pltpu.VMEM((kv_dev, slots * tokens, dim), jnp.bfloat16),
            pltpu.VMEM((kv_dev, slots * tokens, 2 * dim), jnp.bfloat16),
            pltpu.VMEM(out.shape, jnp.bfloat16),
            pltpu.SemaphoreType.DMA((rows // ROW_CHUNK,)),
        ],
        compiler_params=params(),
        name="attend",
    )(lists, queries, k_own, v_own, *k_parts, *v_parts)


def last_kernel(
    lists_ref, q_ref, top_ref, both_ref, k_ref, v_ref, _, out_hbm,
    k_wide, v_wide, k_ready, v_ready, out_ref, sems, *, last,
):
    kv_dev, rows_all, dim = q_ref.shape
    tokens = k_ref.shape[0] // kv_dev
    group = rows_all // tokens
    factor = dim ** (-0.5) * math.log2(math.e)
    target = lax.axis_index("seq").astype(jnp.int32)

    def rows_from(first):
        rows = pl.ds(first, ROW_CHUNK)
        for h in range(kv_dev):
            s = scores_of(q_ref[h, rows, :], k_ready[h])
            before = top_ref[h, rows, :]
            top = jnp.maximum(before, jnp.max(s, axis=1, keepdims=True))
            probs = jnp.exp2((s - top) * factor).astype(jnp.bfloat16)
            shrink = jnp.exp2((before - top) * factor)
            both = jnp.dot(probs, v_ready[h], preferred_element_type=jnp.float32)
            both += both_ref[h, rows, :] * jnp.concatenate([shrink, shrink], axis=1)
            put_out(out_ref, h, first, both, group)

    @pl.when(is_listed(lists_ref, target, last(target)))
    def _add():
        k_wide[...] = k_ref[...].astype(jnp.float32)
        v_wide[...] = v_ref[...].astype(jnp.float32)
        for h in range(kv_dev):
            k_ready[h] = by_head(k_wide, h, kv_dev, tokens)
            v_ready[h] = with_ones(by_head(v_wide, h, kv_dev, tokens))
        over_rows(rows_all, rows_from, out_ref, out_hbm, sems, True)


def attend_last(lists, queries, state, k_last, v_last, out, last):
    top, both = state
    kv_dev, rows, dim = queries.shape
    tokens = out.shape[0]
    hbm, smem = (pl.BlockSpec(memory_space=space) for space in (pltpu.HBM, pltpu.SMEM))
    return pl.pallas_call(
        functools.partial(last_kernel, last=last),
        out_shape=jax.ShapeDtypeStruct(out.shape, out.dtype),
        in_specs=[smem] + [vmem()] * 5 + [hbm],
        out_specs=hbm,
        input_output_aliases={6: 0},
        scratch_shapes=[
            pltpu.VMEM(k_last.shape, jnp.float32),
            pltpu.VMEM(k_last.shape, jnp.float32),
            pltpu.VMEM((kv_dev, tokens, dim), jnp.bfloat16),
            pltpu.VMEM((kv_dev, tokens, 2 * dim), jnp.bfloat16),
            pltpu.VMEM(out.shape, jnp.bfloat16),
            pltpu.SemaphoreType.DMA((rows // ROW_CHUNK,)),
        ],
        compiler_params=params(),
        name="attend_last",
    )(lists, queries, top, both, k_last, v_last, out)


def ring_at(place, members):
    back = members - 1 - place
    return jnp.where(place < members // 2, 2 * place, 2 * back + 1)


def ring_place(block, members):
    return jnp.where(block % 2 == 0, block // 2, members - 1 - block // 2)


def round_the_ring(k_own, v_own, ready, members):
    ring = list(range(0, members, 2)) + list(range(members - 1, 0, -2))
    ways = [
        [(ring[p], ring[(p + turn) % members]) for p in range(members)] for turn in (1, -1)
    ]

    def send(x, way):
        return lax.ppermute(x, "seq", ways[way])

    half = members // 2
    k_two, v_two, k_all, v_all = [k_own, k_own], [v_own, v_own], [], []
    for distance in range(1, half):
        ahead = send(k_two[0], 0), send(v_two[1], 1)
        behind = send(v_two[0], 0), send(k_two[1], 1)
        if distance == 1:
            ahead, ready = lax.optimization_barrier((ahead, ready))
        ahead = lax.optimization_barrier(ahead)
        behind = lax.optimization_barrier(behind)
        k_two, v_two = [ahead[0], behind[1]], [behind[0], ahead[1]]
        k_all += k_two
        v_all += v_two
    return k_all, v_all, send(k_two[0], 0), send(v_two[1], 1), ready


def ring_sources(members):
    def at(target, turn):
        place = lax.rem(ring_place(target, members) + turn + members, members)
        return ring_at(place, members)

    def sources(target):
        return [at(target, turn) for far in range(1, members // 2) for turn in (-far, far)]

    return sources, lambda target: at(target, members // 2)


def others(row, target):
    slots = row.shape[-1]
    own_at = jnp.argmax(row == target[..., None], axis=-1)
    j = jnp.arange(slots - 1)
    return jnp.where(j >= own_at[..., None], row[..., 1:], row[..., :-1])


def relay(k_own, v_own, chosen, members):
    block, dim = k_own.shape
    stacked = jnp.stack([k_own, v_own]).reshape(2, members, block // members, dim)
    shares = lax.all_to_all(stacked, "seq", split_axis=1, concat_axis=1, tiled=True)
    wanted = others(chosen, jnp.arange(members, dtype=jnp.int32))
    picked = jnp.take(shares, jnp.maximum(wanted, 0), axis=1)
    arrived = lax.all_to_all(picked, "seq", split_axis=1, concat_axis=3, tiled=True)
    count = wanted.shape[1]
    k_parts, v_parts = ([arrived[n, 0, j].reshape(block, dim) for j in range(count)] for n in range(2))
    return k_parts, v_parts, jnp.where(wanted < 0, -1, jnp.arange(count, dtype=jnp.int32))


def per_device(queries, keys, values, chosen):
    members = lax.axis_size("seq")
    tokens, kv_dev, dim = keys.shape
    k_own = keys.reshape(tokens * kv_dev, dim)
    v_own = values.reshape(tokens * kv_dev, dim)
    if members <= MOST_ROUND:
        ready = prepare(chosen.T, queries, k_own, v_own, kv_dev)
        k_parts, v_parts, k_last, v_last, ready = round_the_ring(k_own, v_own, ready, members)
        lists, q_ready, k_ready, v_ready = ready
        sources, last = ring_sources(members)
        out, *state = attend(lists, q_ready, k_ready, v_ready, k_parts, v_parts, sources, last)
        return attend_last(lists, q_ready, state, k_last, v_last, out, last)

    k_parts, v_parts, mine = relay(k_own, v_own, chosen, members)
    lists, *ready = prepare(mine.T, queries, k_own, v_own, kv_dev)

    def sources(_):
        return [jnp.int32(j) for j in range(len(k_parts))]

    lists = jnp.concatenate([lists, jnp.full_like(lists[:1], -1)])
    return attend(lists, *ready, k_parts, v_parts, sources, None)[0]


def solution(mesh):
    rows = P(("groups", "seq"), "head", None)
    return jax.shard_map(
        per_device,
        mesh=mesh,
        in_specs=(rows, rows, rows, P("groups", None)),
        out_specs=rows,
        check_vma=False,
    )
```

```python
import functools
import math

import jax
import jax.numpy as jnp
from jax import lax
from jax.experimental import pallas as pl
from jax.experimental.pallas import tpu as pltpu
from jax.sharding import PartitionSpec as P

NO_KEY = -1e30
ROW_CHUNK = 256
MOST_ROUND = 16
HEADS_OUT = 16


def params():
    return pltpu.CompilerParams(vmem_limit_bytes=16 * 2**20)


def vmem():
    return pl.BlockSpec(memory_space=pltpu.VMEM)


def prepare_kernel(
    lists_hbm, q_hbm, k_hbm, v_hbm, lists_out, q_out, k_out, v_out,
    q_ref, k_ref, v_ref, k_wide, v_wide, sems, *, kv_dev,
):
    whole = ((k_hbm, k_ref), (v_hbm, v_ref), (q_hbm, q_ref), (lists_hbm, lists_out))
    copies = [
        pltpu.make_async_copy(source, here, sems.at[n]) for n, (source, here) in enumerate(whole)
    ]
    for copy in copies:
        copy.start()
    tokens, heads, dim = q_ref.shape
    group = heads // kv_dev
    for copy, ref, wide, out in zip(copies, (k_ref, v_ref), (k_wide, v_wide), (k_out, v_out)):
        copy.wait()
        wide[...] = ref[...].astype(jnp.float32)
        for h in range(kv_dev):
            out[h] = wide[pl.ds(h, tokens, stride=kv_dev), :].astype(jnp.bfloat16)
    copies[2].wait()
    for h in range(kv_dev):
        q = q_ref[:, pl.ds(h * group, group), :].astype(jnp.float32)
        q_out[h] = q.reshape(tokens * group, dim).astype(jnp.bfloat16)
    copies[3].wait()


def prepare(lists, queries, k_own, v_own, kv_dev):
    tokens, heads, dim = queries.shape
    operands = [
        pltpu.with_memory_space_constraint(x, pltpu.HBM) for x in (lists, queries, k_own, v_own)
    ]
    by_head = jax.ShapeDtypeStruct((kv_dev, tokens, dim), jnp.bfloat16)
    return pl.pallas_call(
        functools.partial(prepare_kernel, kv_dev=kv_dev),
        out_shape=(
            jax.ShapeDtypeStruct(lists.shape, lists.dtype),
            jax.ShapeDtypeStruct((kv_dev, tokens * heads // kv_dev, dim), jnp.bfloat16),
            by_head,
            by_head,
        ),
        in_specs=[pl.BlockSpec(memory_space=pltpu.HBM)] * 4,
        out_specs=(vmem(), vmem(), vmem(), vmem()),
        scratch_shapes=[
            pltpu.VMEM(queries.shape, jnp.bfloat16),
            pltpu.VMEM(k_own.shape, jnp.bfloat16),
            pltpu.VMEM(k_own.shape, jnp.bfloat16),
            pltpu.VMEM(k_own.shape, jnp.float32),
            pltpu.VMEM(k_own.shape, jnp.float32),
            pltpu.SemaphoreType.DMA((4,)),
        ],
        compiler_params=params(),
        name="prepare",
    )(*operands)


def is_listed(lists_ref, target, source):
    same = [lists_ref[j, target] == source for j in range(lists_ref.shape[0])]
    return functools.reduce(jnp.logical_or, same)


def by_head(wide, h, kv_dev, keys):
    return wide[pl.ds(h, keys, stride=kv_dev), :].astype(jnp.bfloat16)


def with_ones(values):
    return jnp.concatenate([values, jnp.ones_like(values)], axis=1)


def put_out(out_ref, h, first, both, group):
    rows, dim = both.shape[0], both.shape[1] // 2
    merged = (both[:, :dim] * pl.reciprocal(both[:, dim:])).reshape(rows // group, group, dim)
    tokens = pl.ds(first // group, rows // group)
    out_ref[tokens, pl.ds(h * group, group), :] = merged.astype(jnp.bfloat16)


def send_out(out_ref, out_hbm, sems, h, group):
    done = (h + 1) * group
    if done % HEADS_OUT:
        return []
    heads = pl.ds(done - HEADS_OUT, HEADS_OUT)
    copy = pltpu.make_async_copy(
        out_ref.at[:, heads, :], out_hbm.at[:, heads, :], sems.at[done // HEADS_OUT - 1]
    )
    copy.start()
    return [copy]


def chunks_of(kv_dev, rows_all):
    return [(h, first) for h in range(kv_dev) for first in range(0, rows_all, ROW_CHUNK)]


def in_turns(stages, jobs):
    held = {}
    for turn in range(len(jobs) + len(stages) - 1):
        for n, stage in enumerate(stages):
            at = turn - n
            if 0 <= at < len(jobs):
                held[at] = stage(jobs[at], held.get(at))
        held.pop(turn - len(stages) + 1, None)


def scores_of(q, keys):
    return lax.dot_general(q, keys, (((1,), (1,)), ((), ())), preferred_element_type=jnp.float32)


def attend_kernel(lists_ref, q_ref, k_own_ref, v_own_ref, *refs, parts, sources, last):
    k_parts, v_parts = refs[:parts], refs[parts : 2 * parts]
    out_hbm, *state, k_wide, v_wide, out_ref, sems = refs[2 * parts :]
    kv_dev, tokens, dim = k_own_ref.shape
    rows_all = q_ref.shape[1]
    group = rows_all // tokens
    block = tokens * kv_dev
    most = k_wide.shape[0] // block
    factor = dim ** (-0.5) * math.log2(math.e)
    target = lax.axis_index("seq").astype(jnp.int32)

    count = jnp.int32(0)
    for source, k_part, v_part in zip(sources(target), k_parts, v_parts):
        take = is_listed(lists_ref, target, source)

        @pl.when(take)
        def _take(k_part=k_part, v_part=v_part, count=count):
            rows = pl.ds(pl.multiple_of(count * block, block), block)
            k_wide[rows, :] = k_part[...].astype(jnp.float32)
            v_wide[rows, :] = v_part[...].astype(jnp.float32)

        count += take.astype(jnp.int32)

    def run(others, final):
        keys = (others + 1) * tokens
        copies = []
        k_ready, v_ready = [], []
        for h in range(kv_dev):
            k_h, v_h = k_own_ref[h], v_own_ref[h]
            if others:
                k_h = jnp.concatenate([k_h, by_head(k_wide, h, kv_dev, keys - tokens)], axis=0)
                v_h = jnp.concatenate([v_h, by_head(v_wide, h, kv_dev, keys - tokens)], axis=0)
            k_ready.append(k_h)
            v_ready.append(with_ones(v_h))

        def score(job, _):
            h, first = job
            return scores_of(q_ref[h, pl.ds(first, ROW_CHUNK), :], k_ready[h])

        def weigh(job, s):
            first = job[1]
            row = (lax.broadcasted_iota(jnp.int32, (ROW_CHUNK, tokens), 0) + first) // group
            key = lax.broadcasted_iota(jnp.int32, (ROW_CHUNK, tokens), 1)
            scores = [jnp.where(key <= row, s[:, :tokens], NO_KEY)]
            scores += [s[:, (j + 1) * tokens : (j + 2) * tokens] for j in range(others)]
            top = jnp.max(functools.reduce(jnp.maximum, scores), axis=1, keepdims=True)
            probs = [jnp.exp2((part - top) * factor).astype(jnp.bfloat16) for part in scores]
            return jnp.concatenate(probs, axis=1), top

        def add_up(job, weighed):
            h, first = job
            probs, top = weighed
            both = jnp.dot(probs, v_ready[h], preferred_element_type=jnp.float32)
            if final:
                put_out(out_ref, h, first, both, group)
                if first + ROW_CHUNK == rows_all:
                    copies.extend(send_out(out_ref, out_hbm, sems, h, group))
            else:
                rows = pl.ds(first, ROW_CHUNK)
                state[0][h, rows, :] = jnp.broadcast_to(top, (ROW_CHUNK, dim))
                state[1][h, rows, :] = both

        in_turns([score, weigh, add_up], chunks_of(kv_dev, rows_all))
        for copy in copies:
            copy.wait()

    unfinished = False if last is None else is_listed(lists_ref, target, last(target))
    for others in range(most + 1):

        @pl.when(jnp.logical_and(count == others, jnp.logical_not(unfinished)))
        def _whole(others=others):
            run(others, True)

        if last is not None and others < most:

            @pl.when(jnp.logical_and(count == others, unfinished))
            def _part(others=others):
                run(others, False)


def attend(lists, queries, k_own, v_own, k_parts, v_parts, sources, last):
    kv_dev, rows, dim = queries.shape
    tokens = k_own.shape[1]
    rest = (lists.shape[0] - 1) * tokens * kv_dev
    out = jax.ShapeDtypeStruct((tokens, rows * kv_dev // tokens, dim), jnp.bfloat16)
    state = [] if last is None else [
        jax.ShapeDtypeStruct((kv_dev, rows, wide), jnp.float32) for wide in (dim, 2 * dim)
    ]
    hbm, smem = (pl.BlockSpec(memory_space=space) for space in (pltpu.HBM, pltpu.SMEM))
    return pl.pallas_call(
        functools.partial(attend_kernel, parts=len(k_parts), sources=sources, last=last),
        out_shape=(out, *state),
        in_specs=[smem] + [vmem()] * (3 + 2 * len(k_parts)),
        out_specs=(hbm, *(vmem() for _ in state)),
        scratch_shapes=[
            pltpu.VMEM((rest, dim), jnp.float32),
            pltpu.VMEM((rest, dim), jnp.float32),
            pltpu.VMEM(out.shape, jnp.bfloat16),
            pltpu.SemaphoreType.DMA((out.shape[1] // HEADS_OUT,)),
        ],
        compiler_params=params(),
        name="attend",
    )(lists, queries, k_own, v_own, *k_parts, *v_parts)


def last_kernel(
    lists_ref, q_ref, top_ref, both_ref, k_ref, v_ref, _, out_hbm, k_wide, v_wide, out_ref, sems, *, last
):
    kv_dev, rows_all, dim = q_ref.shape
    tokens = k_ref.shape[0] // kv_dev
    group = rows_all // tokens
    factor = dim ** (-0.5) * math.log2(math.e)
    target = lax.axis_index("seq").astype(jnp.int32)

    @pl.when(is_listed(lists_ref, target, last(target)))
    def _add():
        k_wide[...] = k_ref[...].astype(jnp.float32)
        v_wide[...] = v_ref[...].astype(jnp.float32)
        k_ready = [by_head(k_wide, h, kv_dev, tokens) for h in range(kv_dev)]
        v_ready = [with_ones(by_head(v_wide, h, kv_dev, tokens)) for h in range(kv_dev)]
        copies = []

        def score(job, _):
            h, first = job
            return scores_of(q_ref[h, pl.ds(first, ROW_CHUNK), :], k_ready[h])

        def weigh(job, s):
            h, first = job
            before = top_ref[h, pl.ds(first, ROW_CHUNK), :]
            top = jnp.maximum(before, jnp.max(s, axis=1, keepdims=True))
            shrink = jnp.exp2((before - top) * factor)
            return jnp.exp2((s - top) * factor).astype(jnp.bfloat16), shrink

        def add_up(job, weighed):
            h, first = job
            probs, shrink = weighed
            both = jnp.dot(probs, v_ready[h], preferred_element_type=jnp.float32)
            both += both_ref[h, pl.ds(first, ROW_CHUNK), :] * jnp.concatenate([shrink, shrink], axis=1)
            put_out(out_ref, h, first, both, group)
            if first + ROW_CHUNK == rows_all:
                copies.extend(send_out(out_ref, out_hbm, sems, h, group))

        in_turns([score, weigh, add_up], chunks_of(kv_dev, rows_all))
        for copy in copies:
            copy.wait()


def attend_last(lists, queries, state, k_last, v_last, out, last):
    top, both = state
    hbm, smem = (pl.BlockSpec(memory_space=space) for space in (pltpu.HBM, pltpu.SMEM))
    return pl.pallas_call(
        functools.partial(last_kernel, last=last),
        out_shape=jax.ShapeDtypeStruct(out.shape, out.dtype),
        in_specs=[smem] + [vmem()] * 5 + [hbm],
        out_specs=hbm,
        input_output_aliases={6: 0},
        scratch_shapes=[
            pltpu.VMEM(k_last.shape, jnp.float32),
            pltpu.VMEM(k_last.shape, jnp.float32),
            pltpu.VMEM(out.shape, jnp.bfloat16),
            pltpu.SemaphoreType.DMA((out.shape[1] // HEADS_OUT,)),
        ],
        compiler_params=params(),
        name="attend_last",
    )(lists, queries, top, both, k_last, v_last, out)


def ring_at(place, members):
    back = members - 1 - place
    return jnp.where(place < members // 2, 2 * place, 2 * back + 1)


def ring_place(block, members):
    return jnp.where(block % 2 == 0, block // 2, members - 1 - block // 2)


def round_the_ring(k_own, v_own, ready, members):
    ring = list(range(0, members, 2)) + list(range(members - 1, 0, -2))
    ways = [
        [(ring[p], ring[(p + turn) % members]) for p in range(members)] for turn in (1, -1)
    ]

    def send(x, way):
        return lax.ppermute(x, "seq", ways[way])

    half = members // 2
    k_two, v_two, k_all, v_all = [k_own, k_own], [v_own, v_own], [], []
    for distance in range(1, half):
        ahead = send(k_two[0], 0), send(v_two[1], 1)
        behind = send(v_two[0], 0), send(k_two[1], 1)
        if distance == 1:
            ahead, ready = lax.optimization_barrier((ahead, ready))
        ahead = lax.optimization_barrier(ahead)
        behind = lax.optimization_barrier(behind)
        k_two, v_two = [ahead[0], behind[1]], [behind[0], ahead[1]]
        k_all += k_two
        v_all += v_two
    return k_all, v_all, send(k_two[0], 0), send(v_two[1], 1), ready


def ring_sources(members):
    def at(target, turn):
        place = lax.rem(ring_place(target, members) + turn + members, members)
        return ring_at(place, members)

    def sources(target):
        return [at(target, turn) for far in range(1, members // 2) for turn in (-far, far)]

    return sources, lambda target: at(target, members // 2)


def others(row, target):
    slots = row.shape[-1]
    own_at = jnp.argmax(row == target[..., None], axis=-1)
    j = jnp.arange(slots - 1)
    return jnp.where(j >= own_at[..., None], row[..., 1:], row[..., :-1])


def relay(k_own, v_own, chosen, members):
    block, dim = k_own.shape
    stacked = jnp.stack([k_own, v_own]).reshape(2, members, block // members, dim)
    shares = lax.all_to_all(stacked, "seq", split_axis=1, concat_axis=1, tiled=True)
    wanted = others(chosen, jnp.arange(members, dtype=jnp.int32))
    picked = jnp.take(shares, jnp.maximum(wanted, 0), axis=1)
    arrived = lax.all_to_all(picked, "seq", split_axis=1, concat_axis=3, tiled=True)
    count = wanted.shape[1]
    k_parts, v_parts = ([arrived[n, 0, j].reshape(block, dim) for j in range(count)] for n in range(2))
    return k_parts, v_parts, jnp.where(wanted < 0, -1, jnp.arange(count, dtype=jnp.int32))


def per_device(queries, keys, values, chosen):
    members = lax.axis_size("seq")
    tokens, kv_dev, dim = keys.shape
    k_own = keys.reshape(tokens * kv_dev, dim)
    v_own = values.reshape(tokens * kv_dev, dim)
    if members <= MOST_ROUND:
        ready = prepare(chosen.T, queries, k_own, v_own, kv_dev)
        k_parts, v_parts, k_last, v_last, ready = round_the_ring(k_own, v_own, ready, members)
        lists, q_ready, k_ready, v_ready = ready
        sources, last = ring_sources(members)
        out, *state = attend(lists, q_ready, k_ready, v_ready, k_parts, v_parts, sources, last)
        return attend_last(lists, q_ready, state, k_last, v_last, out, last)

    k_parts, v_parts, mine = relay(k_own, v_own, chosen, members)
    lists, *ready = prepare(mine.T, queries, k_own, v_own, kv_dev)

    def sources(_):
        return [jnp.int32(j) for j in range(len(k_parts))]

    lists = jnp.concatenate([lists, jnp.full_like(lists[:1], -1)])
    return attend(lists, *ready, k_parts, v_parts, sources, None)[0]


def solution(mesh):
    rows = P(("groups", "seq"), "head", None)
    return jax.shard_map(
        per_device,
        mesh=mesh,
        in_specs=(rows, rows, rows, P("groups", None)),
        out_specs=rows,
        check_vma=False,
    )
```

```python
import functools
import math

import jax
import jax.numpy as jnp
from jax import lax
from jax.experimental import pallas as pl
from jax.experimental.pallas import tpu as pltpu
from jax.sharding import PartitionSpec as P

NO_KEY = -1e30
ROW_CHUNK = 256
ROUND = (8, 12, 16)
HEADS_OUT = 16


def params():
    return pltpu.CompilerParams(vmem_limit_bytes=16 * 2**20)


def vmem():
    return pl.BlockSpec(memory_space=pltpu.VMEM)


def prepare_kernel(
    lists_hbm, q_hbm, k_hbm, v_hbm, lists_out, q_out, k_out, v_out,
    q_ref, k_ref, v_ref, k_wide, v_wide, sems, *, kv_dev,
):
    whole = ((k_hbm, k_ref), (v_hbm, v_ref), (q_hbm, q_ref), (lists_hbm, lists_out))
    copies = [
        pltpu.make_async_copy(source, here, sems.at[n]) for n, (source, here) in enumerate(whole)
    ]
    for copy in copies:
        copy.start()
    tokens, heads, dim = q_ref.shape
    group = heads // kv_dev
    for copy, ref, wide, out in zip(copies, (k_ref, v_ref), (k_wide, v_wide), (k_out, v_out)):
        copy.wait()
        wide[...] = ref[...].astype(jnp.float32)
        for h in range(kv_dev):
            out[h] = wide[pl.ds(h, tokens, stride=kv_dev), :].astype(jnp.bfloat16)
    copies[2].wait()
    for h in range(kv_dev):
        q = q_ref[:, pl.ds(h * group, group), :].astype(jnp.float32)
        q_out[h] = q.reshape(tokens * group, dim).astype(jnp.bfloat16)
    copies[3].wait()


def prepare(lists, queries, k_own, v_own, kv_dev):
    tokens, heads, dim = queries.shape
    operands = [
        pltpu.with_memory_space_constraint(x, pltpu.HBM) for x in (lists, queries, k_own, v_own)
    ]
    by_head = jax.ShapeDtypeStruct((kv_dev, tokens, dim), jnp.bfloat16)
    return pl.pallas_call(
        functools.partial(prepare_kernel, kv_dev=kv_dev),
        out_shape=(
            jax.ShapeDtypeStruct(lists.shape, lists.dtype),
            jax.ShapeDtypeStruct((kv_dev, tokens * heads // kv_dev, dim), jnp.bfloat16),
            by_head,
            by_head,
        ),
        in_specs=[pl.BlockSpec(memory_space=pltpu.HBM)] * 4,
        out_specs=(vmem(), vmem(), vmem(), vmem()),
        scratch_shapes=[
            pltpu.VMEM(queries.shape, jnp.bfloat16),
            pltpu.VMEM(k_own.shape, jnp.bfloat16),
            pltpu.VMEM(k_own.shape, jnp.bfloat16),
            pltpu.VMEM(k_own.shape, jnp.float32),
            pltpu.VMEM(k_own.shape, jnp.float32),
            pltpu.SemaphoreType.DMA((4,)),
        ],
        compiler_params=params(),
        name="prepare",
    )(*operands)


def listed_bits(lists_ref, code):
    target = lax.axis_index("seq").astype(jnp.int32)
    entries = lists_ref[...]
    mine = lax.broadcasted_iota(jnp.int32, entries.shape, 1) == target
    bits = jnp.left_shift(1, code(jnp.maximum(entries, 0), target)).astype(jnp.float32)
    return jnp.sum(jnp.where(jnp.logical_and(mine, entries >= 0), bits, 0.0)).astype(jnp.int32)


def has(bits, code):
    return jnp.bitwise_and(lax.shift_right_logical(bits, jnp.int32(code)), 1) == 1


def by_head(wide, h, kv_dev, keys):
    return wide[pl.ds(h, keys, stride=kv_dev), :].astype(jnp.bfloat16)


def with_ones(values):
    return jnp.concatenate([values, jnp.ones_like(values)], axis=1)


def put_out(out_ref, h, first, both, group):
    rows, dim = both.shape[0], both.shape[1] // 2
    merged = (both[:, :dim] * pl.reciprocal(both[:, dim:])).reshape(rows // group, group, dim)
    tokens = pl.ds(first // group, rows // group)
    out_ref[tokens, pl.ds(h * group, group), :] = merged.astype(jnp.bfloat16)


def send_out(out_ref, out_hbm, sems, h, group):
    done = (h + 1) * group
    if done % HEADS_OUT:
        return []
    heads = pl.ds(done - HEADS_OUT, HEADS_OUT)
    copy = pltpu.make_async_copy(
        out_ref.at[:, heads, :], out_hbm.at[:, heads, :], sems.at[done // HEADS_OUT - 1]
    )
    copy.start()
    return [copy]


def chunks_of(kv_dev, rows_all):
    return [(h, first) for h in range(kv_dev) for first in range(0, rows_all, ROW_CHUNK)]


def in_turns(stages, jobs):
    held = {}
    for turn in range(len(jobs) + len(stages) - 1):
        for n, stage in enumerate(stages):
            at = turn - n
            if 0 <= at < len(jobs):
                held[at] = stage(jobs[at], held.get(at))
        held.pop(turn - len(stages) + 1, None)


def scores_of(q, keys):
    return lax.dot_general(q, keys, (((1,), (1,)), ((), ())), preferred_element_type=jnp.float32)


def attend_kernel(lists_ref, q_ref, k_own_ref, v_own_ref, *refs, codes, code, last):
    parts = len(codes)
    k_parts, v_parts = refs[:parts], refs[parts : 2 * parts]
    out_hbm, *state, k_wide, v_wide, out_ref, sems = refs[2 * parts :]
    kv_dev, tokens, dim = k_own_ref.shape
    rows_all = q_ref.shape[1]
    group = rows_all // tokens
    block = tokens * kv_dev
    most = k_wide.shape[0] // block
    factor = dim ** (-0.5) * math.log2(math.e)

    bits = listed_bits(lists_ref, code)
    count = jnp.int32(0)
    for part_code, k_part, v_part in zip(codes, k_parts, v_parts):
        take = has(bits, part_code)

        @pl.when(take)
        def _take(k_part=k_part, v_part=v_part, count=count):
            rows = pl.ds(pl.multiple_of(count * block, block), block)
            k_wide[rows, :] = k_part[...].astype(jnp.float32)
            v_wide[rows, :] = v_part[...].astype(jnp.float32)

        count += take.astype(jnp.int32)

    def run(others, final):
        keys = (others + 1) * tokens
        copies = []
        k_ready, v_ready = [], []
        for h in range(kv_dev):
            k_h, v_h = k_own_ref[h], v_own_ref[h]
            if others:
                k_h = jnp.concatenate([k_h, by_head(k_wide, h, kv_dev, keys - tokens)], axis=0)
                v_h = jnp.concatenate([v_h, by_head(v_wide, h, kv_dev, keys - tokens)], axis=0)
            k_ready.append(k_h)
            v_ready.append(with_ones(v_h))

        def score(job, _):
            h, first = job
            return scores_of(q_ref[h, pl.ds(first, ROW_CHUNK), :], k_ready[h])

        def weigh(job, s):
            first = job[1]
            row = (lax.broadcasted_iota(jnp.int32, (ROW_CHUNK, tokens), 0) + first) // group
            key = lax.broadcasted_iota(jnp.int32, (ROW_CHUNK, tokens), 1)
            scores = [jnp.where(key <= row, s[:, :tokens], NO_KEY)]
            scores += [s[:, (j + 1) * tokens : (j + 2) * tokens] for j in range(others)]
            top = jnp.max(functools.reduce(jnp.maximum, scores), axis=1, keepdims=True)
            probs = [jnp.exp2((part - top) * factor).astype(jnp.bfloat16) for part in scores]
            return jnp.concatenate(probs, axis=1), top

        def add_up(job, weighed):
            h, first = job
            probs, top = weighed
            both = jnp.dot(probs, v_ready[h], preferred_element_type=jnp.float32)
            if final:
                put_out(out_ref, h, first, both, group)
                if first + ROW_CHUNK == rows_all:
                    copies.extend(send_out(out_ref, out_hbm, sems, h, group))
            else:
                rows = pl.ds(first, ROW_CHUNK)
                state[0][h, rows, :] = jnp.broadcast_to(top, (ROW_CHUNK, dim))
                state[1][h, rows, :] = both

        in_turns([score, weigh, add_up], chunks_of(kv_dev, rows_all))
        for copy in copies:
            copy.wait()

    unfinished = False if last is None else has(bits, last)
    for others in range(most + 1):

        @pl.when(jnp.logical_and(count == others, jnp.logical_not(unfinished)))
        def _whole(others=others):
            run(others, True)

        if last is not None and others < most:

            @pl.when(jnp.logical_and(count == others, unfinished))
            def _part(others=others):
                run(others, False)


def attend(lists, queries, k_own, v_own, k_parts, v_parts, codes, code, last):
    kv_dev, rows, dim = queries.shape
    tokens = k_own.shape[1]
    rest = (lists.shape[0] - 1) * tokens * kv_dev
    out = jax.ShapeDtypeStruct((tokens, rows * kv_dev // tokens, dim), jnp.bfloat16)
    state = [] if last is None else [
        jax.ShapeDtypeStruct((kv_dev, rows, wide), jnp.float32) for wide in (dim, 2 * dim)
    ]
    hbm = pl.BlockSpec(memory_space=pltpu.HBM)
    return pl.pallas_call(
        functools.partial(attend_kernel, codes=codes, code=code, last=last),
        out_shape=(out, *state),
        in_specs=[vmem()] * (4 + 2 * len(k_parts)),
        out_specs=(hbm, *(vmem() for _ in state)),
        scratch_shapes=[
            pltpu.VMEM((rest, dim), jnp.float32),
            pltpu.VMEM((rest, dim), jnp.float32),
            pltpu.VMEM(out.shape, jnp.bfloat16),
            pltpu.SemaphoreType.DMA((out.shape[1] // HEADS_OUT,)),
        ],
        compiler_params=params(),
        name="attend",
    )(lists, queries, k_own, v_own, *k_parts, *v_parts)


def last_kernel(
    lists_ref, q_ref, top_ref, both_ref, k_ref, v_ref, _, out_hbm, k_wide, v_wide, out_ref, sems, *, code, last
):
    kv_dev, rows_all, dim = q_ref.shape
    tokens = k_ref.shape[0] // kv_dev
    group = rows_all // tokens
    factor = dim ** (-0.5) * math.log2(math.e)

    @pl.when(has(listed_bits(lists_ref, code), last))
    def _add():
        k_wide[...] = k_ref[...].astype(jnp.float32)
        v_wide[...] = v_ref[...].astype(jnp.float32)
        k_ready = [by_head(k_wide, h, kv_dev, tokens) for h in range(kv_dev)]
        v_ready = [with_ones(by_head(v_wide, h, kv_dev, tokens)) for h in range(kv_dev)]
        copies = []

        def score(job, _):
            h, first = job
            return scores_of(q_ref[h, pl.ds(first, ROW_CHUNK), :], k_ready[h])

        def weigh(job, s):
            h, first = job
            before = top_ref[h, pl.ds(first, ROW_CHUNK), :]
            top = jnp.maximum(before, jnp.max(s, axis=1, keepdims=True))
            shrink = jnp.exp2((before - top) * factor)
            return jnp.exp2((s - top) * factor).astype(jnp.bfloat16), shrink

        def add_up(job, weighed):
            h, first = job
            probs, shrink = weighed
            both = jnp.dot(probs, v_ready[h], preferred_element_type=jnp.float32)
            both += both_ref[h, pl.ds(first, ROW_CHUNK), :] * jnp.concatenate([shrink, shrink], axis=1)
            put_out(out_ref, h, first, both, group)
            if first + ROW_CHUNK == rows_all:
                copies.extend(send_out(out_ref, out_hbm, sems, h, group))

        in_turns([score, weigh, add_up], chunks_of(kv_dev, rows_all))
        for copy in copies:
            copy.wait()


def attend_last(lists, queries, state, k_last, v_last, out, code, last):
    top, both = state
    hbm = pl.BlockSpec(memory_space=pltpu.HBM)
    return pl.pallas_call(
        functools.partial(last_kernel, code=code, last=last),
        out_shape=jax.ShapeDtypeStruct(out.shape, out.dtype),
        in_specs=[vmem()] * 6 + [hbm],
        out_specs=hbm,
        input_output_aliases={6: 0},
        scratch_shapes=[
            pltpu.VMEM(k_last.shape, jnp.float32),
            pltpu.VMEM(k_last.shape, jnp.float32),
            pltpu.VMEM(out.shape, jnp.bfloat16),
            pltpu.SemaphoreType.DMA((out.shape[1] // HEADS_OUT,)),
        ],
        compiler_params=params(),
        name="attend_last",
    )(lists, queries, top, both, k_last, v_last, out)


def ring_place(block, members):
    return jnp.where((block & 1) == 0, block >> 1, members - 1 - (block >> 1))


def ring_code(members):
    def code(block, target):
        ahead = ring_place(block, members) - ring_place(target, members)
        return jnp.where(ahead < 0, ahead + members, ahead)

    return code


def ring_steps(members):
    half = members // 2
    first, final = half // 2, half // 2 + half - 1
    still = {p: p for p in range(members)}
    forward = {p: (p + 1) % members for p in range(members)}
    backward = {p: (p - 1) % members for p in range(members)}
    forward_late = {**still, **{p: p + 1 for p in range(first - 1, final)}, final: first - 1}
    backward_late = {**still, **{p: p - 1 for p in range(first + 2, final + 3)}}
    backward_late.update({p: p - 1 for p in range(2, first + 2)})
    backward_late[1] = final + 2
    forward_last = {**still, **{p: p + 1 for p in range(first, final)}, final: first}
    backward_last = {**still, **{p: p - 1 for p in range(first + 1, final + 1)}, first: final}
    return (forward, backward), (forward_late, backward_late), (forward_last, backward_last)


def round_the_ring(k_own, v_own, ready, members):
    ring = list(range(0, members, 2)) + list(range(members - 1, 0, -2))
    steps, late, final = ring_steps(members)

    def send(x, step):
        return lax.ppermute(x, "seq", [(ring[p], ring[to]) for p, to in sorted(step.items())])

    half = members // 2
    k_two, v_two, k_all, v_all = [k_own, k_own], [v_own, v_own], [], []
    for distance in range(1, half):
        forward, backward = late if distance == half - 1 else steps
        ahead = send(k_two[0], forward), send(v_two[1], backward)
        behind = send(v_two[0], forward), send(k_two[1], backward)
        if distance == 1:
            ahead, ready = lax.optimization_barrier((ahead, ready))
        ahead = lax.optimization_barrier(ahead)
        behind = lax.optimization_barrier(behind)
        k_two, v_two = [ahead[0], behind[1]], [behind[0], ahead[1]]
        k_all += k_two
        v_all += v_two
    here = ring_place(lax.axis_index("seq").astype(jnp.int32), members)
    k_last = jnp.where(here == half // 2 + half - 1, k_all[1], k_two[0])
    v_last = jnp.where(here == half // 2, v_all[0], v_two[1])
    return k_all, v_all, send(k_last, final[0]), send(v_last, final[1]), ready


def others(row, target):
    slots = row.shape[-1]
    own_at = jnp.argmax(row == target[..., None], axis=-1)
    j = jnp.arange(slots - 1)
    return jnp.where(j >= own_at[..., None], row[..., 1:], row[..., :-1])


def relay(k_own, v_own, chosen, members):
    block, dim = k_own.shape
    stacked = jnp.stack([k_own, v_own]).reshape(2, members, block // members, dim)
    shares = lax.all_to_all(stacked, "seq", split_axis=1, concat_axis=1, tiled=True)
    wanted = others(chosen, jnp.arange(members, dtype=jnp.int32))
    picked = jnp.take(shares, jnp.maximum(wanted, 0), axis=1)
    arrived = lax.all_to_all(picked, "seq", split_axis=1, concat_axis=3, tiled=True)
    count = wanted.shape[1]
    k_parts, v_parts = ([arrived[n, 0, j].reshape(block, dim) for j in range(count)] for n in range(2))
    return k_parts, v_parts, jnp.where(wanted < 0, -1, jnp.arange(count, dtype=jnp.int32))


def per_device(queries, keys, values, chosen):
    members = lax.axis_size("seq")
    tokens, kv_dev, dim = keys.shape
    k_own = keys.reshape(tokens * kv_dev, dim)
    v_own = values.reshape(tokens * kv_dev, dim)
    if members in ROUND:
        ready = prepare(chosen.T, queries, k_own, v_own, kv_dev)
        k_parts, v_parts, k_last, v_last, ready = round_the_ring(k_own, v_own, ready, members)
        lists, q_ready, k_ready, v_ready = ready
        half, code = members // 2, ring_code(members)
        codes = [turn for far in range(1, half) for turn in (members - far, far)]
        out, *state = attend(
            lists, q_ready, k_ready, v_ready, k_parts, v_parts, codes, code, half
        )
        return attend_last(lists, q_ready, state, k_last, v_last, out, code, half)

    k_parts, v_parts, mine = relay(k_own, v_own, chosen, members)
    lists, *ready = prepare(mine.T, queries, k_own, v_own, kv_dev)
    lists = jnp.concatenate([lists, jnp.full_like(lists[:1], -1)])
    codes = list(range(len(k_parts)))
    return attend(lists, *ready, k_parts, v_parts, codes, lambda block, _: block, None)[0]


def solution(mesh):
    rows = P(("groups", "seq"), "head", None)
    return jax.shard_map(
        per_device,
        mesh=mesh,
        in_specs=(rows, rows, rows, P("groups", None)),
        out_specs=rows,
        check_vma=False,
    )
```

```python
import functools
import math

import jax
import jax.numpy as jnp
from jax import lax
from jax.experimental import pallas as pl
from jax.experimental.pallas import tpu as pltpu
from jax.sharding import PartitionSpec as P

NO_KEY = -1e30
ROW_CHUNK = 256
ROUND = (8, 16)
HEADS_OUT = 16


def params():
    return pltpu.CompilerParams(vmem_limit_bytes=16 * 2**20)


def vmem():
    return pl.BlockSpec(memory_space=pltpu.VMEM)


def prepare_kernel(
    lists_hbm, q_hbm, k_hbm, v_hbm, lists_out, q_out, k_out, v_out,
    q_ref, k_ref, v_ref, k_wide, v_wide, sems, *, kv_dev,
):
    whole = ((k_hbm, k_ref), (v_hbm, v_ref), (q_hbm, q_ref), (lists_hbm, lists_out))
    copies = [
        pltpu.make_async_copy(source, here, sems.at[n]) for n, (source, here) in enumerate(whole)
    ]
    for copy in copies:
        copy.start()
    tokens, heads, dim = q_ref.shape
    group = heads // kv_dev
    for copy, ref, wide, out in zip(copies, (k_ref, v_ref), (k_wide, v_wide), (k_out, v_out)):
        copy.wait()
        wide[...] = ref[...].astype(jnp.float32)
        for h in range(kv_dev):
            out[h] = wide[pl.ds(h, tokens, stride=kv_dev), :].astype(jnp.bfloat16)
    copies[2].wait()
    for h in range(kv_dev):
        q = q_ref[:, pl.ds(h * group, group), :].astype(jnp.float32)
        q_out[h] = q.reshape(tokens * group, dim).astype(jnp.bfloat16)
    copies[3].wait()


def prepare(lists, queries, k_own, v_own, kv_dev):
    tokens, heads, dim = queries.shape
    operands = [
        pltpu.with_memory_space_constraint(x, pltpu.HBM) for x in (lists, queries, k_own, v_own)
    ]
    by_head = jax.ShapeDtypeStruct((kv_dev, tokens, dim), jnp.bfloat16)
    return pl.pallas_call(
        functools.partial(prepare_kernel, kv_dev=kv_dev),
        out_shape=(
            jax.ShapeDtypeStruct(lists.shape, lists.dtype),
            jax.ShapeDtypeStruct((kv_dev, tokens * heads // kv_dev, dim), jnp.bfloat16),
            by_head,
            by_head,
        ),
        in_specs=[pl.BlockSpec(memory_space=pltpu.HBM)] * 4,
        out_specs=(vmem(), vmem(), vmem(), vmem()),
        scratch_shapes=[
            pltpu.VMEM(queries.shape, jnp.bfloat16),
            pltpu.VMEM(k_own.shape, jnp.bfloat16),
            pltpu.VMEM(k_own.shape, jnp.bfloat16),
            pltpu.VMEM(k_own.shape, jnp.float32),
            pltpu.VMEM(k_own.shape, jnp.float32),
            pltpu.SemaphoreType.DMA((4,)),
        ],
        compiler_params=params(),
        name="prepare",
    )(*operands)


def listed_bits(lists_ref, code):
    target = lax.axis_index("seq").astype(jnp.int32)
    entries = lists_ref[...]
    mine = lax.broadcasted_iota(jnp.int32, entries.shape, 1) == target
    bits = jnp.left_shift(1, code(jnp.maximum(entries, 0), target)).astype(jnp.float32)
    return jnp.sum(jnp.where(jnp.logical_and(mine, entries >= 0), bits, 0.0)).astype(jnp.int32)


def has(bits, code):
    return jnp.bitwise_and(lax.shift_right_logical(bits, jnp.int32(code)), 1) == 1


def by_head(wide, h, kv_dev, keys):
    return wide[pl.ds(h, keys, stride=kv_dev), :].astype(jnp.bfloat16)


def with_ones(values):
    return jnp.concatenate([values, jnp.ones_like(values)], axis=1)


def put_out(out_ref, h, first, both, group):
    rows, dim = both.shape[0], both.shape[1] // 2
    merged = (both[:, :dim] * pl.reciprocal(both[:, dim:])).reshape(rows // group, group, dim)
    tokens = pl.ds(first // group, rows // group)
    out_ref[tokens, pl.ds(h * group, group), :] = merged.astype(jnp.bfloat16)


def send_out(out_ref, out_hbm, sems, h, group):
    done = (h + 1) * group
    if done % HEADS_OUT:
        return []
    heads = pl.ds(done - HEADS_OUT, HEADS_OUT)
    copy = pltpu.make_async_copy(
        out_ref.at[:, heads, :], out_hbm.at[:, heads, :], sems.at[done // HEADS_OUT - 1]
    )
    copy.start()
    return [copy]


def chunks_of(kv_dev, rows_all):
    return [(h, first) for h in range(kv_dev) for first in range(0, rows_all, ROW_CHUNK)]


def in_turns(stages, jobs):
    held = {}
    for turn in range(len(jobs) + len(stages) - 1):
        for n, stage in enumerate(stages):
            at = turn - n
            if 0 <= at < len(jobs):
                held[at] = stage(jobs[at], held.get(at))
        held.pop(turn - len(stages) + 1, None)


def scores_of(q, keys):
    return lax.dot_general(q, keys, (((1,), (1,)), ((), ())), preferred_element_type=jnp.float32)


def attend_kernel(lists_ref, q_ref, k_own_ref, v_own_ref, *refs, codes, code, last):
    parts = len(codes)
    k_parts, v_parts = refs[:parts], refs[parts : 2 * parts]
    out_hbm, *state, k_wide, v_wide, out_ref, sems = refs[2 * parts :]
    kv_dev, tokens, dim = k_own_ref.shape
    rows_all = q_ref.shape[1]
    group = rows_all // tokens
    block = tokens * kv_dev
    most = k_wide.shape[0] // block
    factor = dim ** (-0.5) * math.log2(math.e)

    bits = listed_bits(lists_ref, code)
    count = jnp.int32(0)
    for part_code, k_part, v_part in zip(codes, k_parts, v_parts):
        take = has(bits, part_code)

        @pl.when(take)
        def _take(k_part=k_part, v_part=v_part, count=count):
            rows = pl.ds(pl.multiple_of(count * block, block), block)
            k_wide[rows, :] = k_part[...].astype(jnp.float32)
            v_wide[rows, :] = v_part[...].astype(jnp.float32)

        count += take.astype(jnp.int32)

    def run(others, final):
        keys = (others + 1) * tokens
        copies = []
        k_ready, v_ready = [], []
        for h in range(kv_dev):
            k_h, v_h = k_own_ref[h], v_own_ref[h]
            if others:
                k_h = jnp.concatenate([k_h, by_head(k_wide, h, kv_dev, keys - tokens)], axis=0)
                v_h = jnp.concatenate([v_h, by_head(v_wide, h, kv_dev, keys - tokens)], axis=0)
            k_ready.append(k_h)
            v_ready.append(with_ones(v_h))

        def score(job, _):
            h, first = job
            return scores_of(q_ref[h, pl.ds(first, ROW_CHUNK), :], k_ready[h])

        def weigh(job, s):
            first = job[1]
            row = (lax.broadcasted_iota(jnp.int32, (ROW_CHUNK, tokens), 0) + first) // group
            key = lax.broadcasted_iota(jnp.int32, (ROW_CHUNK, tokens), 1)
            scores = [jnp.where(key <= row, s[:, :tokens], NO_KEY)]
            scores += [s[:, (j + 1) * tokens : (j + 2) * tokens] for j in range(others)]
            top = jnp.max(functools.reduce(jnp.maximum, scores), axis=1, keepdims=True)
            probs = [jnp.exp2((part - top) * factor).astype(jnp.bfloat16) for part in scores]
            return jnp.concatenate(probs, axis=1), top

        def add_up(job, weighed):
            h, first = job
            probs, top = weighed
            both = jnp.dot(probs, v_ready[h], preferred_element_type=jnp.float32)
            if final:
                put_out(out_ref, h, first, both, group)
                if first + ROW_CHUNK == rows_all:
                    copies.extend(send_out(out_ref, out_hbm, sems, h, group))
            else:
                rows = pl.ds(first, ROW_CHUNK)
                state[0][h, rows, :] = jnp.broadcast_to(top, (ROW_CHUNK, dim))
                state[1][h, rows, :] = both

        in_turns([score, weigh, add_up], chunks_of(kv_dev, rows_all))
        for copy in copies:
            copy.wait()

    unfinished = False if last is None else has(bits, last)
    for others in range(most + 1):

        @pl.when(jnp.logical_and(count == others, jnp.logical_not(unfinished)))
        def _whole(others=others):
            run(others, True)

        if last is not None and others < most:

            @pl.when(jnp.logical_and(count == others, unfinished))
            def _part(others=others):
                run(others, False)


def attend(lists, queries, k_own, v_own, k_parts, v_parts, codes, code, last):
    kv_dev, rows, dim = queries.shape
    tokens = k_own.shape[1]
    rest = (lists.shape[0] - 1) * tokens * kv_dev
    out = jax.ShapeDtypeStruct((tokens, rows * kv_dev // tokens, dim), jnp.bfloat16)
    state = [] if last is None else [
        jax.ShapeDtypeStruct((kv_dev, rows, wide), jnp.float32) for wide in (dim, 2 * dim)
    ]
    hbm = pl.BlockSpec(memory_space=pltpu.HBM)
    return pl.pallas_call(
        functools.partial(attend_kernel, codes=codes, code=code, last=last),
        out_shape=(out, *state),
        in_specs=[vmem()] * (4 + 2 * len(k_parts)),
        out_specs=(hbm, *(vmem() for _ in state)),
        scratch_shapes=[
            pltpu.VMEM((rest, dim), jnp.float32),
            pltpu.VMEM((rest, dim), jnp.float32),
            pltpu.VMEM(out.shape, jnp.bfloat16),
            pltpu.SemaphoreType.DMA((out.shape[1] // HEADS_OUT,)),
        ],
        compiler_params=params(),
        name="attend",
    )(lists, queries, k_own, v_own, *k_parts, *v_parts)


def last_kernel(
    lists_ref, q_ref, top_ref, both_ref, k_ref, v_ref, _, out_hbm, k_wide, v_wide, out_ref, sems, *, code, last
):
    kv_dev, rows_all, dim = q_ref.shape
    tokens = k_ref.shape[0] // kv_dev
    group = rows_all // tokens
    factor = dim ** (-0.5) * math.log2(math.e)

    @pl.when(has(listed_bits(lists_ref, code), last))
    def _add():
        k_wide[...] = k_ref[...].astype(jnp.float32)
        v_wide[...] = v_ref[...].astype(jnp.float32)
        k_ready = [by_head(k_wide, h, kv_dev, tokens) for h in range(kv_dev)]
        v_ready = [with_ones(by_head(v_wide, h, kv_dev, tokens)) for h in range(kv_dev)]
        copies = []

        def score(job, _):
            h, first = job
            return scores_of(q_ref[h, pl.ds(first, ROW_CHUNK), :], k_ready[h])

        def weigh(job, s):
            h, first = job
            before = top_ref[h, pl.ds(first, ROW_CHUNK), :]
            top = jnp.maximum(before, jnp.max(s, axis=1, keepdims=True))
            shrink = jnp.exp2((before - top) * factor)
            return jnp.exp2((s - top) * factor).astype(jnp.bfloat16), shrink

        def add_up(job, weighed):
            h, first = job
            probs, shrink = weighed
            both = jnp.dot(probs, v_ready[h], preferred_element_type=jnp.float32)
            both += both_ref[h, pl.ds(first, ROW_CHUNK), :] * jnp.concatenate([shrink, shrink], axis=1)
            put_out(out_ref, h, first, both, group)
            if first + ROW_CHUNK == rows_all:
                copies.extend(send_out(out_ref, out_hbm, sems, h, group))

        in_turns([score, weigh, add_up], chunks_of(kv_dev, rows_all))
        for copy in copies:
            copy.wait()


def attend_last(lists, queries, state, k_last, v_last, out, code, last):
    top, both = state
    hbm = pl.BlockSpec(memory_space=pltpu.HBM)
    return pl.pallas_call(
        functools.partial(last_kernel, code=code, last=last),
        out_shape=jax.ShapeDtypeStruct(out.shape, out.dtype),
        in_specs=[vmem()] * 6 + [hbm],
        out_specs=hbm,
        input_output_aliases={6: 0},
        scratch_shapes=[
            pltpu.VMEM(k_last.shape, jnp.float32),
            pltpu.VMEM(k_last.shape, jnp.float32),
            pltpu.VMEM(out.shape, jnp.bfloat16),
            pltpu.SemaphoreType.DMA((out.shape[1] // HEADS_OUT,)),
        ],
        compiler_params=params(),
        name="attend_last",
    )(lists, queries, top, both, k_last, v_last, out)


def ring_place(block, members):
    return jnp.where((block & 1) == 0, block >> 1, members - 1 - (block >> 1))


def ring_code(members):
    def code(block, target):
        ahead = ring_place(block, members) - ring_place(target, members)
        return jnp.where(ahead < 0, ahead + members, ahead)

    return code


def ring_steps(members):
    first, final = members // 4, 3 * members // 4 - 1
    forward = {p: (p + 1) % members for p in range(members)}
    backward = {p: (p - 1) % members for p in range(members)}
    low = [p for p in range(members) if not first <= p <= final]
    last_forward = {p: members - 1 - p for p in low}
    last_backward = {p: p ^ 1 for p in low}
    last_forward.update({p: p + 1 for p in range(first, final)})
    last_backward.update({p: p - 1 for p in range(first + 1, final + 1)})
    last_forward[final], last_backward[first] = first, final
    return forward, backward, last_forward, last_backward


def round_the_ring(k_own, v_own, ready, members):
    ring = list(range(0, members, 2)) + list(range(members - 1, 0, -2))
    forward, backward, last_forward, last_backward = ring_steps(members)

    def send(x, step):
        return lax.ppermute(x, "seq", [(ring[p], ring[to]) for p, to in sorted(step.items())])

    half = members // 2
    k_two, v_two, k_all, v_all = [k_own, k_own], [v_own, v_own], [], []
    for distance in range(1, half):
        ahead = send(k_two[0], forward), send(v_two[1], backward)
        behind = send(v_two[0], forward), send(k_two[1], backward)
        if distance == 1:
            ahead, ready = lax.optimization_barrier((ahead, ready))
        ahead = lax.optimization_barrier(ahead)
        behind = lax.optimization_barrier(behind)
        k_two, v_two = [ahead[0], behind[1]], [behind[0], ahead[1]]
        k_all += k_two
        v_all += v_two
    here = ring_place(lax.axis_index("seq").astype(jnp.int32), members)
    k_last = jnp.where(here == 3 * members // 4 - 1, k_all[1], k_two[0])
    v_last = jnp.where(here == members // 4, v_all[0], v_two[1])
    return k_all, v_all, send(k_last, last_forward), send(v_last, last_backward), ready


def others(row, target):
    slots = row.shape[-1]
    own_at = jnp.argmax(row == target[..., None], axis=-1)
    j = jnp.arange(slots - 1)
    return jnp.where(j >= own_at[..., None], row[..., 1:], row[..., :-1])


def relay(k_own, v_own, chosen, members):
    block, dim = k_own.shape
    stacked = jnp.stack([k_own, v_own]).reshape(2, members, block // members, dim)
    shares = lax.all_to_all(stacked, "seq", split_axis=1, concat_axis=1, tiled=True)
    wanted = others(chosen, jnp.arange(members, dtype=jnp.int32))
    picked = jnp.take(shares, jnp.maximum(wanted, 0), axis=1)
    arrived = lax.all_to_all(picked, "seq", split_axis=1, concat_axis=3, tiled=True)
    count = wanted.shape[1]
    k_parts, v_parts = ([arrived[n, 0, j].reshape(block, dim) for j in range(count)] for n in range(2))
    return k_parts, v_parts, jnp.where(wanted < 0, -1, jnp.arange(count, dtype=jnp.int32))


def per_device(queries, keys, values, chosen):
    members = lax.axis_size("seq")
    tokens, kv_dev, dim = keys.shape
    k_own = keys.reshape(tokens * kv_dev, dim)
    v_own = values.reshape(tokens * kv_dev, dim)
    if members in ROUND:
        ready = prepare(chosen.T, queries, k_own, v_own, kv_dev)
        k_parts, v_parts, k_last, v_last, ready = round_the_ring(k_own, v_own, ready, members)
        lists, q_ready, k_ready, v_ready = ready
        half, code = members // 2, ring_code(members)
        codes = [turn for far in range(1, half) for turn in (members - far, far)]
        out, *state = attend(
            lists, q_ready, k_ready, v_ready, k_parts, v_parts, codes, code, half
        )
        return attend_last(lists, q_ready, state, k_last, v_last, out, code, half)

    k_parts, v_parts, mine = relay(k_own, v_own, chosen, members)
    lists, *ready = prepare(mine.T, queries, k_own, v_own, kv_dev)
    lists = jnp.concatenate([lists, jnp.full_like(lists[:1], -1)])
    codes = list(range(len(k_parts)))
    return attend(lists, *ready, k_parts, v_parts, codes, lambda block, _: block, None)[0]


def solution(mesh):
    rows = P(("groups", "seq"), "head", None)
    return jax.shard_map(
        per_device,
        mesh=mesh,
        in_specs=(rows, rows, rows, P("groups", None)),
        out_specs=rows,
        check_vma=False,
    )
```

```python
import functools
import math

import jax
import jax.numpy as jnp
from jax import lax
from jax.experimental import pallas as pl
from jax.experimental.pallas import tpu as pltpu
from jax.sharding import PartitionSpec as P

NO_KEY = -1e30
ROW_CHUNK = 512
ROUND = (8, 16)
HEADS_OUT = 16


def params():
    return pltpu.CompilerParams(vmem_limit_bytes=16 * 2**20)


def vmem():
    return pl.BlockSpec(memory_space=pltpu.VMEM)


def prepare_kernel(
    lists_hbm, q_hbm, k_hbm, v_hbm, lists_out, q_out, k_out, v_out,
    q_ref, k_ref, v_ref, k_wide, v_wide, sems, *, kv_dev,
):
    whole = ((k_hbm, k_ref), (v_hbm, v_ref), (q_hbm, q_ref), (lists_hbm, lists_out))
    copies = [
        pltpu.make_async_copy(source, here, sems.at[n]) for n, (source, here) in enumerate(whole)
    ]
    for copy in copies:
        copy.start()
    tokens, heads, dim = q_ref.shape
    group = heads // kv_dev
    for copy, ref, wide, out in zip(copies, (k_ref, v_ref), (k_wide, v_wide), (k_out, v_out)):
        copy.wait()
        wide[...] = ref[...].astype(jnp.float32)
        for h in range(kv_dev):
            out[h] = wide[pl.ds(h, tokens, stride=kv_dev), :].astype(jnp.bfloat16)
    copies[2].wait()
    for h in range(kv_dev):
        q = q_ref[:, pl.ds(h * group, group), :].astype(jnp.float32)
        q_out[h] = q.reshape(tokens * group, dim).astype(jnp.bfloat16)
    copies[3].wait()


def prepare(lists, queries, k_own, v_own, kv_dev):
    tokens, heads, dim = queries.shape
    operands = [
        pltpu.with_memory_space_constraint(x, pltpu.HBM) for x in (lists, queries, k_own, v_own)
    ]
    by_head = jax.ShapeDtypeStruct((kv_dev, tokens, dim), jnp.bfloat16)
    return pl.pallas_call(
        functools.partial(prepare_kernel, kv_dev=kv_dev),
        out_shape=(
            jax.ShapeDtypeStruct(lists.shape, lists.dtype),
            jax.ShapeDtypeStruct((kv_dev, tokens * heads // kv_dev, dim), jnp.bfloat16),
            by_head,
            by_head,
        ),
        in_specs=[pl.BlockSpec(memory_space=pltpu.HBM)] * 4,
        out_specs=(vmem(), vmem(), vmem(), vmem()),
        scratch_shapes=[
            pltpu.VMEM(queries.shape, jnp.bfloat16),
            pltpu.VMEM(k_own.shape, jnp.bfloat16),
            pltpu.VMEM(k_own.shape, jnp.bfloat16),
            pltpu.VMEM(k_own.shape, jnp.float32),
            pltpu.VMEM(k_own.shape, jnp.float32),
            pltpu.SemaphoreType.DMA((4,)),
        ],
        compiler_params=params(),
        name="prepare",
    )(*operands)


def listed_bits(lists_ref, code):
    target = lax.axis_index("seq").astype(jnp.int32)
    entries = lists_ref[...]
    mine = lax.broadcasted_iota(jnp.int32, entries.shape, 1) == target
    bits = jnp.left_shift(1, code(jnp.maximum(entries, 0), target)).astype(jnp.float32)
    return jnp.sum(jnp.where(jnp.logical_and(mine, entries >= 0), bits, 0.0)).astype(jnp.int32)


def has(bits, code):
    return jnp.bitwise_and(lax.shift_right_logical(bits, jnp.int32(code)), 1) == 1


def by_head(wide, h, kv_dev, keys):
    return wide[pl.ds(h, keys, stride=kv_dev), :].astype(jnp.bfloat16)


def with_ones(values):
    return jnp.concatenate([values, jnp.ones_like(values)], axis=1)


def put_out(out_ref, h, first, both, group):
    rows, dim = both.shape[0], both.shape[1] // 2
    merged = (both[:, :dim] * pl.reciprocal(both[:, dim:])).reshape(rows // group, group, dim)
    tokens = pl.ds(first // group, rows // group)
    out_ref[tokens, pl.ds(h * group, group), :] = merged.astype(jnp.bfloat16)


def send_out(out_ref, out_hbm, sems, h, group):
    done = (h + 1) * group
    if done % HEADS_OUT:
        return []
    heads = pl.ds(done - HEADS_OUT, HEADS_OUT)
    copy = pltpu.make_async_copy(
        out_ref.at[:, heads, :], out_hbm.at[:, heads, :], sems.at[done // HEADS_OUT - 1]
    )
    copy.start()
    return [copy]


def chunks_of(kv_dev, rows_all):
    return [(h, first) for h in range(kv_dev) for first in range(0, rows_all, ROW_CHUNK)]


def in_turns(stages, jobs):
    held = {}
    for turn in range(len(jobs) + len(stages) - 1):
        for n, stage in enumerate(stages):
            at = turn - n
            if 0 <= at < len(jobs):
                held[at] = stage(jobs[at], held.get(at))
        held.pop(turn - len(stages) + 1, None)


def scores_of(q, keys):
    return lax.dot_general(q, keys, (((1,), (1,)), ((), ())), preferred_element_type=jnp.float32)


def attend_kernel(lists_ref, q_ref, k_own_ref, v_own_ref, *refs, codes, code, last):
    parts = len(codes)
    k_parts, v_parts = refs[:parts], refs[parts : 2 * parts]
    out_hbm, *state, k_wide, v_wide, out_ref, sems = refs[2 * parts :]
    kv_dev, tokens, dim = k_own_ref.shape
    rows_all = q_ref.shape[1]
    group = rows_all // tokens
    block = tokens * kv_dev
    most = k_wide.shape[0] // block
    factor = dim ** (-0.5) * math.log2(math.e)

    bits = listed_bits(lists_ref, code)
    count = jnp.int32(0)
    for part_code, k_part, v_part in zip(codes, k_parts, v_parts):
        take = has(bits, part_code)

        @pl.when(take)
        def _take(k_part=k_part, v_part=v_part, count=count):
            rows = pl.ds(pl.multiple_of(count * block, block), block)
            k_wide[rows, :] = k_part[...].astype(jnp.float32)
            v_wide[rows, :] = v_part[...].astype(jnp.float32)

        count += take.astype(jnp.int32)

    def run(others, final):
        keys = (others + 1) * tokens
        copies = []
        k_ready, v_ready = [], []
        for h in range(kv_dev):
            k_h, v_h = k_own_ref[h], v_own_ref[h]
            if others:
                k_h = jnp.concatenate([k_h, by_head(k_wide, h, kv_dev, keys - tokens)], axis=0)
                v_h = jnp.concatenate([v_h, by_head(v_wide, h, kv_dev, keys - tokens)], axis=0)
            k_ready.append(k_h)
            v_ready.append(with_ones(v_h))

        def score(job, _):
            h, first = job
            return scores_of(q_ref[h, pl.ds(first, ROW_CHUNK), :], k_ready[h])

        def weigh(job, s):
            first = job[1]
            row = (lax.broadcasted_iota(jnp.int32, (ROW_CHUNK, tokens), 0) + first) // group
            key = lax.broadcasted_iota(jnp.int32, (ROW_CHUNK, tokens), 1)
            scores = [jnp.where(key <= row, s[:, :tokens], NO_KEY)]
            scores += [s[:, (j + 1) * tokens : (j + 2) * tokens] for j in range(others)]
            top = jnp.max(functools.reduce(jnp.maximum, scores), axis=1, keepdims=True)
            probs = [jnp.exp2((part - top) * factor).astype(jnp.bfloat16) for part in scores]
            return jnp.concatenate(probs, axis=1), top

        def add_up(job, weighed):
            h, first = job
            probs, top = weighed
            both = jnp.dot(probs, v_ready[h], preferred_element_type=jnp.float32)
            if final:
                put_out(out_ref, h, first, both, group)
                if first + ROW_CHUNK == rows_all:
                    copies.extend(send_out(out_ref, out_hbm, sems, h, group))
            else:
                rows = pl.ds(first, ROW_CHUNK)
                state[0][h, rows, :] = jnp.broadcast_to(top, (ROW_CHUNK, dim))
                state[1][h, rows, :] = both

        in_turns([score, weigh, add_up], chunks_of(kv_dev, rows_all))
        for copy in copies:
            copy.wait()

    unfinished = False if last is None else has(bits, last)
    for others in range(most + 1):

        @pl.when(jnp.logical_and(count == others, jnp.logical_not(unfinished)))
        def _whole(others=others):
            run(others, True)

        if last is not None and others < most:

            @pl.when(jnp.logical_and(count == others, unfinished))
            def _part(others=others):
                run(others, False)


def attend(lists, queries, k_own, v_own, k_parts, v_parts, codes, code, last):
    kv_dev, rows, dim = queries.shape
    tokens = k_own.shape[1]
    rest = (lists.shape[0] - 1) * tokens * kv_dev
    out = jax.ShapeDtypeStruct((tokens, rows * kv_dev // tokens, dim), jnp.bfloat16)
    state = [] if last is None else [
        jax.ShapeDtypeStruct((kv_dev, rows, wide), jnp.float32) for wide in (dim, 2 * dim)
    ]
    hbm = pl.BlockSpec(memory_space=pltpu.HBM)
    return pl.pallas_call(
        functools.partial(attend_kernel, codes=codes, code=code, last=last),
        out_shape=(out, *state),
        in_specs=[vmem()] * (4 + 2 * len(k_parts)),
        out_specs=(hbm, *(vmem() for _ in state)),
        scratch_shapes=[
            pltpu.VMEM((rest, dim), jnp.float32),
            pltpu.VMEM((rest, dim), jnp.float32),
            pltpu.VMEM(out.shape, jnp.bfloat16),
            pltpu.SemaphoreType.DMA((out.shape[1] // HEADS_OUT,)),
        ],
        compiler_params=params(),
        name="attend",
    )(lists, queries, k_own, v_own, *k_parts, *v_parts)


def last_kernel(
    lists_ref, q_ref, top_ref, both_ref, k_ref, v_ref, _, out_hbm, k_wide, v_wide, out_ref, sems, *, code, last
):
    kv_dev, rows_all, dim = q_ref.shape
    tokens = k_ref.shape[0] // kv_dev
    group = rows_all // tokens
    factor = dim ** (-0.5) * math.log2(math.e)

    @pl.when(has(listed_bits(lists_ref, code), last))
    def _add():
        k_wide[...] = k_ref[...].astype(jnp.float32)
        v_wide[...] = v_ref[...].astype(jnp.float32)
        k_ready = [by_head(k_wide, h, kv_dev, tokens) for h in range(kv_dev)]
        v_ready = [with_ones(by_head(v_wide, h, kv_dev, tokens)) for h in range(kv_dev)]
        copies = []

        def score(job, _):
            h, first = job
            return scores_of(q_ref[h, pl.ds(first, ROW_CHUNK), :], k_ready[h])

        def weigh(job, s):
            h, first = job
            before = top_ref[h, pl.ds(first, ROW_CHUNK), :]
            top = jnp.maximum(before, jnp.max(s, axis=1, keepdims=True))
            shrink = jnp.exp2((before - top) * factor)
            return jnp.exp2((s - top) * factor).astype(jnp.bfloat16), shrink

        def add_up(job, weighed):
            h, first = job
            probs, shrink = weighed
            both = jnp.dot(probs, v_ready[h], preferred_element_type=jnp.float32)
            both += both_ref[h, pl.ds(first, ROW_CHUNK), :] * jnp.concatenate([shrink, shrink], axis=1)
            put_out(out_ref, h, first, both, group)
            if first + ROW_CHUNK == rows_all:
                copies.extend(send_out(out_ref, out_hbm, sems, h, group))

        in_turns([score, weigh, add_up], chunks_of(kv_dev, rows_all))
        for copy in copies:
            copy.wait()


def attend_last(lists, queries, state, k_last, v_last, out, code, last):
    top, both = state
    hbm = pl.BlockSpec(memory_space=pltpu.HBM)
    return pl.pallas_call(
        functools.partial(last_kernel, code=code, last=last),
        out_shape=jax.ShapeDtypeStruct(out.shape, out.dtype),
        in_specs=[vmem()] * 6 + [hbm],
        out_specs=hbm,
        input_output_aliases={6: 0},
        scratch_shapes=[
            pltpu.VMEM(k_last.shape, jnp.float32),
            pltpu.VMEM(k_last.shape, jnp.float32),
            pltpu.VMEM(out.shape, jnp.bfloat16),
            pltpu.SemaphoreType.DMA((out.shape[1] // HEADS_OUT,)),
        ],
        compiler_params=params(),
        name="attend_last",
    )(lists, queries, top, both, k_last, v_last, out)


def ring_place(block, members):
    return jnp.where((block & 1) == 0, block >> 1, members - 1 - (block >> 1))


def ring_code(members):
    def code(block, target):
        ahead = ring_place(block, members) - ring_place(target, members)
        return jnp.where(ahead < 0, ahead + members, ahead)

    return code


def ring_steps(members):
    first, final = members // 4, 3 * members // 4 - 1
    forward = {p: (p + 1) % members for p in range(members)}
    backward = {p: (p - 1) % members for p in range(members)}
    low = [p for p in range(members) if not first <= p <= final]
    last_forward = {p: members - 1 - p for p in low}
    last_backward = {p: p ^ 1 for p in low}
    last_forward.update({p: p + 1 for p in range(first, final)})
    last_backward.update({p: p - 1 for p in range(first + 1, final + 1)})
    last_forward[final], last_backward[first] = first, final
    return forward, backward, last_forward, last_backward


def round_the_ring(k_own, v_own, ready, members):
    ring = list(range(0, members, 2)) + list(range(members - 1, 0, -2))
    forward, backward, last_forward, last_backward = ring_steps(members)

    def send(x, step):
        return lax.ppermute(x, "seq", [(ring[p], ring[to]) for p, to in sorted(step.items())])

    half = members // 2
    k_two, v_two, k_all, v_all = [k_own, k_own], [v_own, v_own], [], []
    for distance in range(1, half):
        ahead = send(k_two[0], forward), send(v_two[1], backward)
        behind = send(v_two[0], forward), send(k_two[1], backward)
        if distance == 1:
            ahead, ready = lax.optimization_barrier((ahead, ready))
        ahead = lax.optimization_barrier(ahead)
        behind = lax.optimization_barrier(behind)
        k_two, v_two = [ahead[0], behind[1]], [behind[0], ahead[1]]
        k_all += k_two
        v_all += v_two
    here = ring_place(lax.axis_index("seq").astype(jnp.int32), members)
    k_last = jnp.where(here == 3 * members // 4 - 1, k_all[1], k_two[0])
    v_last = jnp.where(here == members // 4, v_all[0], v_two[1])
    return k_all, v_all, send(k_last, last_forward), send(v_last, last_backward), ready


def others(row, target):
    slots = row.shape[-1]
    own_at = jnp.argmax(row == target[..., None], axis=-1)
    j = jnp.arange(slots - 1)
    return jnp.where(j >= own_at[..., None], row[..., 1:], row[..., :-1])


def relay(k_own, v_own, chosen, members):
    block, dim = k_own.shape
    stacked = jnp.stack([k_own, v_own]).reshape(2, members, block // members, dim)
    shares = lax.all_to_all(stacked, "seq", split_axis=1, concat_axis=1, tiled=True)
    wanted = others(chosen, jnp.arange(members, dtype=jnp.int32))
    picked = jnp.take(shares, jnp.maximum(wanted, 0), axis=1)
    arrived = lax.all_to_all(picked, "seq", split_axis=1, concat_axis=3, tiled=True)
    count = wanted.shape[1]
    k_parts, v_parts = ([arrived[n, 0, j].reshape(block, dim) for j in range(count)] for n in range(2))
    return k_parts, v_parts, jnp.where(wanted < 0, -1, jnp.arange(count, dtype=jnp.int32))


def per_device(queries, keys, values, chosen):
    members = lax.axis_size("seq")
    tokens, kv_dev, dim = keys.shape
    k_own = keys.reshape(tokens * kv_dev, dim)
    v_own = values.reshape(tokens * kv_dev, dim)
    if members in ROUND:
        ready = prepare(chosen.T, queries, k_own, v_own, kv_dev)
        k_parts, v_parts, k_last, v_last, ready = round_the_ring(k_own, v_own, ready, members)
        lists, q_ready, k_ready, v_ready = ready
        half, code = members // 2, ring_code(members)
        codes = [turn for far in range(1, half) for turn in (members - far, far)]
        out, *state = attend(
            lists, q_ready, k_ready, v_ready, k_parts, v_parts, codes, code, half
        )
        return attend_last(lists, q_ready, state, k_last, v_last, out, code, half)

    k_parts, v_parts, mine = relay(k_own, v_own, chosen, members)
    lists, *ready = prepare(mine.T, queries, k_own, v_own, kv_dev)
    lists = jnp.concatenate([lists, jnp.full_like(lists[:1], -1)])
    codes = list(range(len(k_parts)))
    return attend(lists, *ready, k_parts, v_parts, codes, lambda block, _: block, None)[0]


def solution(mesh):
    rows = P(("groups", "seq"), "head", None)
    return jax.shard_map(
        per_device,
        mesh=mesh,
        in_specs=(rows, rows, rows, P("groups", None)),
        out_specs=rows,
        check_vma=False,
    )
```

```python
import functools
import math

import jax
import jax.numpy as jnp
from jax import lax
from jax.experimental import pallas as pl
from jax.experimental.pallas import tpu as pltpu
from jax.sharding import PartitionSpec as P

NO_KEY = -1e30
ROW_CHUNK = 512
LARGEST = 64.0
ROUND = (8, 16)
HEADS_OUT = 16


def params():
    return pltpu.CompilerParams(vmem_limit_bytes=16 * 2**20)


def vmem():
    return pl.BlockSpec(memory_space=pltpu.VMEM)


def listed_bits(lists_ref, code):
    target = lax.axis_index("seq").astype(jnp.int32)
    entries = lists_ref[...]
    mine = lax.broadcasted_iota(jnp.int32, entries.shape, 1) == target
    bits = jnp.left_shift(1, code(jnp.maximum(entries, 0), target)).astype(jnp.float32)
    return jnp.sum(jnp.where(jnp.logical_and(mine, entries >= 0), bits, 0.0)).astype(jnp.int32)


def has(bits, code):
    return jnp.bitwise_and(lax.shift_right_logical(bits, jnp.int32(code)), 1) == 1


def by_head(wide, h, kv_dev, keys):
    return wide[pl.ds(h, keys, stride=kv_dev), :].astype(jnp.bfloat16)


def with_ones(values):
    return jnp.concatenate([values, jnp.ones_like(values)], axis=1)


def put_out(out_ref, h, first, both, group):
    rows, dim = both.shape[0], both.shape[1] // 2
    merged = (both[:, :dim] * pl.reciprocal(both[:, dim:])).reshape(rows // group, group, dim)
    tokens = pl.ds(first // group, rows // group)
    out_ref[tokens, pl.ds(h * group, group), :] = merged.astype(jnp.bfloat16)


def send_out(out_ref, out_hbm, sems, h, group):
    done = (h + 1) * group
    if done % HEADS_OUT:
        return []
    heads = pl.ds(done - HEADS_OUT, HEADS_OUT)
    copy = pltpu.make_async_copy(
        out_ref.at[:, heads, :], out_hbm.at[:, heads, :], sems.at[done // HEADS_OUT - 1]
    )
    copy.start()
    return [copy]


def chunks_of(kv_dev, rows_all):
    return [(h, first) for h in range(kv_dev) for first in range(0, rows_all, ROW_CHUNK)]


def in_turns(stages, jobs):
    held = {}
    for turn in range(len(jobs) + len(stages) - 1):
        for n, stage in enumerate(stages):
            at = turn - n
            if 0 <= at < len(jobs):
                held[at] = stage(jobs[at], held.get(at))
        held.pop(turn - len(stages) + 1, None)


def scores_of(q, keys):
    return lax.dot_general(q, keys, (((1,), (1,)), ((), ())), preferred_element_type=jnp.float32)


def own_kernel(
    lists_hbm, q_hbm, k_hbm, v_hbm, lists_out, q_out, top_out, both_out,
    q_ref, k_ref, v_ref, k_wide, v_wide, sems, *, kv_dev,
):
    whole = ((k_hbm, k_ref), (v_hbm, v_ref), (q_hbm, q_ref), (lists_hbm, lists_out))
    copies = [
        pltpu.make_async_copy(source, here, sems.at[n]) for n, (source, here) in enumerate(whole)
    ]
    for copy in copies:
        copy.start()
    tokens, heads, dim = q_ref.shape
    group = heads // kv_dev
    factor = dim ** (-0.5) * math.log2(math.e)
    copies[0].wait()
    k_wide[...] = k_ref[...].astype(jnp.float32)
    copies[1].wait()
    v_wide[...] = v_ref[...].astype(jnp.float32)
    k_ready = [by_head(k_wide, h, kv_dev, tokens) for h in range(kv_dev)]
    v_ready = [with_ones(by_head(v_wide, h, kv_dev, tokens)) for h in range(kv_dev)]
    copies[2].wait()

    def score(job, _):
        h, first = job
        here = pl.ds(first // group, ROW_CHUNK // group)
        q = q_ref[here, pl.ds(h * group, group), :].astype(jnp.float32)
        q = q.reshape(ROW_CHUNK, dim).astype(jnp.bfloat16)
        q_out[h, pl.ds(first, ROW_CHUNK), :] = q
        return scores_of(q, k_ready[h])

    def weigh(job, s):
        row = (lax.broadcasted_iota(jnp.int32, s.shape, 0) + job[1]) // group
        s = jnp.where(lax.broadcasted_iota(jnp.int32, s.shape, 1) <= row, s, NO_KEY)
        top = jnp.max(s, axis=1, keepdims=True)
        return jnp.exp2((s - top) * factor).astype(jnp.bfloat16), top

    def add_up(job, weighed):
        h, first = job
        probs, top = weighed
        rows = pl.ds(first, ROW_CHUNK)
        top_out[h, rows, :] = jnp.broadcast_to(top, (ROW_CHUNK, dim))
        both_out[h, rows, :] = jnp.dot(probs, v_ready[h], preferred_element_type=jnp.float32)

    in_turns([score, weigh, add_up], chunks_of(kv_dev, tokens * group))
    copies[3].wait()


def attend_own(lists, queries, k_own, v_own, kv_dev):
    tokens, heads, dim = queries.shape
    rows = tokens * heads // kv_dev
    operands = [
        pltpu.with_memory_space_constraint(x, pltpu.HBM) for x in (lists, queries, k_own, v_own)
    ]
    return pl.pallas_call(
        functools.partial(own_kernel, kv_dev=kv_dev),
        out_shape=(
            jax.ShapeDtypeStruct(lists.shape, lists.dtype),
            jax.ShapeDtypeStruct((kv_dev, rows, dim), jnp.bfloat16),
            jax.ShapeDtypeStruct((kv_dev, rows, dim), jnp.float32),
            jax.ShapeDtypeStruct((kv_dev, rows, 2 * dim), jnp.float32),
        ),
        in_specs=[pl.BlockSpec(memory_space=pltpu.HBM)] * 4,
        out_specs=(vmem(), vmem(), vmem(), vmem()),
        scratch_shapes=[
            pltpu.VMEM(queries.shape, jnp.bfloat16),
            pltpu.VMEM(k_own.shape, jnp.bfloat16),
            pltpu.VMEM(k_own.shape, jnp.bfloat16),
            pltpu.VMEM(k_own.shape, jnp.float32),
            pltpu.VMEM(k_own.shape, jnp.float32),
            pltpu.SemaphoreType.DMA((4,)),
        ],
        compiler_params=params(),
        name="attend_own",
    )(*operands)


def listed_kernel(lists_ref, q_ref, top_ref, both_ref, *refs, codes, code, last, done):
    parts = len(codes)
    k_parts, v_parts = refs[:parts], refs[parts : 2 * parts]
    outs = refs[2 * parts + done :]
    out_hbm, *state, k_wide, v_wide, out_ref, sems = outs
    kv_dev, rows_all, dim = q_ref.shape
    block = k_parts[0].shape[0]
    tokens = block // kv_dev
    group = rows_all // tokens
    most = k_wide.shape[0] // block
    factor = dim ** (-0.5) * math.log2(math.e)

    bits = listed_bits(lists_ref, code)
    count = jnp.int32(0)
    for part_code, k_part, v_part in zip(codes, k_parts, v_parts):
        take = has(bits, part_code)

        @pl.when(take)
        def _take(k_part=k_part, v_part=v_part, count=count):
            rows = pl.ds(pl.multiple_of(count * block, block), block)
            k_wide[rows, :] = k_part[...].astype(jnp.float32)
            v_wide[rows, :] = v_part[...].astype(jnp.float32)

        count += take.astype(jnp.int32)

    def keep(h, first, top, both):
        rows = pl.ds(first, ROW_CHUNK)
        state[0][h, rows, :] = top
        state[1][h, rows, :] = both

    def run(others, final):
        keys = others * tokens
        copies, shifts = [], []
        k_ready = [by_head(k_wide, h, kv_dev, keys) for h in range(kv_dev if others else 0)]
        v_ready = [with_ones(by_head(v_wide, h, kv_dev, keys)) for h in range(kv_dev if others else 0)]

        def blocks_of(s):
            return [s[:, j * tokens : (j + 1) * tokens] for j in range(others)]

        def score(job, _):
            h, first = job
            return scores_of(q_ref[h, pl.ds(first, ROW_CHUNK), :], k_ready[h]) if others else None

        def weigh(job, s):
            if not others:
                return None
            h, first = job
            top = top_ref[h, pl.ds(first, ROW_CHUNK), :]
            shifted = [(part - top) * factor for part in blocks_of(s)]
            largest = functools.reduce(jnp.maximum, shifted)
            shifts.append(jnp.max(largest.reshape(ROW_CHUNK // 8, 8, tokens), axis=0))
            return jnp.concatenate([jnp.exp2(part).astype(jnp.bfloat16) for part in shifted], axis=1)

        def add_up(job, probs):
            h, first = job
            rows = pl.ds(first, ROW_CHUNK)
            both = both_ref[h, rows, :]
            if others:
                both += jnp.dot(probs, v_ready[h], preferred_element_type=jnp.float32)
            if not final:
                keep(h, first, top_ref[h, rows, :], both)
                return
            put_out(out_ref, h, first, both, group)
            if first + ROW_CHUNK == rows_all:
                copies.extend(send_out(out_ref, out_hbm, sems, h, group))

        in_turns([score, weigh, add_up], chunks_of(kv_dev, rows_all))
        for copy in copies:
            copy.wait()
        if not others:
            return

        @pl.when(jnp.max(functools.reduce(jnp.maximum, shifts)) > LARGEST)
        def _rescale():
            def chunk(n, carry):
                first = pl.multiple_of(n * ROW_CHUNK, ROW_CHUNK)
                rows = pl.ds(first, ROW_CHUNK)
                for h in range(kv_dev):
                    scores = blocks_of(scores_of(q_ref[h, rows, :], k_ready[h]))
                    before = top_ref[h, rows, :]
                    top = jnp.max(functools.reduce(jnp.maximum, scores), axis=1, keepdims=True)
                    top = jnp.maximum(before, top)
                    probs = [jnp.exp2((part - top) * factor).astype(jnp.bfloat16) for part in scores]
                    shrink = jnp.exp2((before - top) * factor)
                    both = both_ref[h, rows, :] * jnp.concatenate([shrink, shrink], axis=1)
                    both += jnp.dot(
                        jnp.concatenate(probs, axis=1), v_ready[h], preferred_element_type=jnp.float32
                    )
                    if final:
                        put_out(out_ref, h, first, both, group)
                    else:
                        keep(h, first, top, both)
                return carry

            lax.fori_loop(0, rows_all // ROW_CHUNK, chunk, 0)
            if final:
                for h in range(kv_dev):
                    for copy in send_out(out_ref, out_hbm, sems, h, group):
                        copy.wait()

    unfinished = False if last is None else has(bits, last)
    for others in range(int(done), most + 1):

        @pl.when(jnp.logical_and(count == others, jnp.logical_not(unfinished)))
        def _whole(others=others):
            run(others, True)

        if last is not None and others < most:

            @pl.when(jnp.logical_and(count == others, unfinished))
            def _part(others=others):
                run(others, False)


def attend_listed(lists, queries, state, k_parts, v_parts, codes, code, last=None, out=None):
    kv_dev, rows, dim = queries.shape
    block = k_parts[0].shape[0]
    most = min(len(codes), lists.shape[0] - 1)
    made = jax.ShapeDtypeStruct((block // kv_dev, rows * kv_dev**2 // block, dim), jnp.bfloat16)
    kept = [] if last is None else [jax.ShapeDtypeStruct(x.shape, x.dtype) for x in state]
    done = [] if out is None else [out]
    hbm = pl.BlockSpec(memory_space=pltpu.HBM)
    operands = [lists, queries, *state, *k_parts, *v_parts]
    return pl.pallas_call(
        functools.partial(listed_kernel, codes=codes, code=code, last=last, done=bool(done)),
        out_shape=(made, *kept),
        in_specs=[vmem()] * len(operands) + [hbm] * len(done),
        out_specs=(hbm, *(vmem() for _ in kept)),
        input_output_aliases={len(operands): 0} if done else {},
        scratch_shapes=[
            pltpu.VMEM((most * block, dim), jnp.float32),
            pltpu.VMEM((most * block, dim), jnp.float32),
            pltpu.VMEM(made.shape, jnp.bfloat16),
            pltpu.SemaphoreType.DMA((made.shape[1] // HEADS_OUT,)),
        ],
        compiler_params=params(),
        name="attend_last" if done else "attend_listed",
    )(*operands, *done)


def ring_place(block, members):
    return jnp.where((block & 1) == 0, block >> 1, members - 1 - (block >> 1))


def ring_code(members):
    def code(block, target):
        ahead = ring_place(block, members) - ring_place(target, members)
        return jnp.where(ahead < 0, ahead + members, ahead)

    return code


def ring_steps(members):
    first, final = members // 4, 3 * members // 4 - 1
    forward = {p: (p + 1) % members for p in range(members)}
    backward = {p: (p - 1) % members for p in range(members)}
    low = [p for p in range(members) if not first <= p <= final]
    last_forward = {p: members - 1 - p for p in low}
    last_backward = {p: p ^ 1 for p in low}
    last_forward.update({p: p + 1 for p in range(first, final)})
    last_backward.update({p: p - 1 for p in range(first + 1, final + 1)})
    last_forward[final], last_backward[first] = first, final
    return forward, backward, last_forward, last_backward


def round_the_ring(k_own, v_own, ready, members):
    ring = list(range(0, members, 2)) + list(range(members - 1, 0, -2))
    forward, backward, last_forward, last_backward = ring_steps(members)

    def send(x, step):
        return lax.ppermute(x, "seq", [(ring[p], ring[to]) for p, to in sorted(step.items())])

    half = members // 2
    k_two, v_two, k_all, v_all = [k_own, k_own], [v_own, v_own], [], []
    for distance in range(1, half):
        ahead = send(k_two[0], forward), send(v_two[1], backward)
        behind = send(v_two[0], forward), send(k_two[1], backward)
        if distance == 1:
            ahead, ready = lax.optimization_barrier((ahead, ready))
        if distance < half - 1:
            ahead = lax.optimization_barrier(ahead)
        behind = lax.optimization_barrier(behind)
        k_two, v_two = [ahead[0], behind[1]], [behind[0], ahead[1]]
        k_all += k_two
        v_all += v_two
    here = ring_place(lax.axis_index("seq").astype(jnp.int32), members)
    k_last = jnp.where(here == 3 * members // 4 - 1, k_all[1], k_two[0])
    v_last = jnp.where(here == members // 4, v_all[0], v_two[1])
    return k_all, v_all, send(k_last, last_forward), send(v_last, last_backward), ready


def others(row, target):
    slots = row.shape[-1]
    own_at = jnp.argmax(row == target[..., None], axis=-1)
    j = jnp.arange(slots - 1)
    return jnp.where(j >= own_at[..., None], row[..., 1:], row[..., :-1])


def relay(k_own, v_own, chosen, members):
    block, dim = k_own.shape
    stacked = jnp.stack([k_own, v_own]).reshape(2, members, block // members, dim)
    shares = lax.all_to_all(stacked, "seq", split_axis=1, concat_axis=1, tiled=True)
    wanted = others(chosen, jnp.arange(members, dtype=jnp.int32))
    picked = jnp.take(shares, jnp.maximum(wanted, 0), axis=1)
    arrived = lax.all_to_all(picked, "seq", split_axis=1, concat_axis=3, tiled=True)
    count = wanted.shape[1]
    k_parts, v_parts = ([arrived[n, 0, j].reshape(block, dim) for j in range(count)] for n in range(2))
    return k_parts, v_parts, jnp.where(wanted < 0, -1, jnp.arange(count, dtype=jnp.int32))


def per_device(queries, keys, values, chosen):
    members = lax.axis_size("seq")
    tokens, kv_dev, dim = keys.shape
    k_own = keys.reshape(tokens * kv_dev, dim)
    v_own = values.reshape(tokens * kv_dev, dim)
    if members in ROUND:
        ready = attend_own(chosen.T, queries, k_own, v_own, kv_dev)
        k_parts, v_parts, k_last, v_last, ready = round_the_ring(k_own, v_own, ready, members)
        lists, queries, *state = ready
        half, code = members // 2, ring_code(members)
        codes = [turn for far in range(1, half) for turn in (members - far, far)]
        out, *state = attend_listed(lists, queries, state, k_parts, v_parts, codes, code, last=half)
        return attend_listed(lists, queries, state, [k_last], [v_last], [half], code, out=out)[0]

    k_parts, v_parts, mine = relay(k_own, v_own, chosen, members)
    lists, queries, *state = attend_own(mine.T, queries, k_own, v_own, kv_dev)
    lists = jnp.concatenate([lists, jnp.full_like(lists[:1], -1)])
    codes = list(range(len(k_parts)))
    return attend_listed(
        lists, queries, state, k_parts, v_parts, codes, lambda block, _: block
    )[0]


def solution(mesh):
    rows = P(("groups", "seq"), "head", None)
    return jax.shard_map(
        per_device,
        mesh=mesh,
        in_specs=(rows, rows, rows, P("groups", None)),
        out_specs=rows,
        check_vma=False,
    )
```

```python
import functools
import math

import jax
import jax.numpy as jnp
from jax import lax
from jax.experimental import pallas as pl
from jax.experimental.pallas import tpu as pltpu
from jax.sharding import PartitionSpec as P

NO_KEY = -1e30
ROW_CHUNK = 256
LARGEST = 64.0
ROUND = (8, 16)


def params():
    return pltpu.CompilerParams(vmem_limit_bytes=16 * 2**20)


def vmem():
    return pl.BlockSpec(memory_space=pltpu.VMEM)


def prepare_kernel(
    lists_hbm, q_hbm, k_hbm, v_hbm, lists_out, q_out, k_out, v_out,
    q_ref, k_ref, v_ref, k_wide, v_wide, sems, *, kv_dev,
):
    whole = ((k_hbm, k_ref), (v_hbm, v_ref), (q_hbm, q_ref), (lists_hbm, lists_out))
    copies = [
        pltpu.make_async_copy(source, here, sems.at[n]) for n, (source, here) in enumerate(whole)
    ]
    for copy in copies:
        copy.start()
    tokens, heads, dim = q_ref.shape
    group = heads // kv_dev
    for copy, ref, wide, out in zip(copies, (k_ref, v_ref), (k_wide, v_wide), (k_out, v_out)):
        copy.wait()
        wide[...] = ref[...].astype(jnp.float32)
        for h in range(kv_dev):
            out[h] = wide[pl.ds(h, tokens, stride=kv_dev), :].astype(jnp.bfloat16)
    copies[2].wait()
    for h in range(kv_dev):
        q = q_ref[:, pl.ds(h * group, group), :].astype(jnp.float32)
        q_out[h] = q.reshape(tokens * group, dim).astype(jnp.bfloat16)
    copies[3].wait()


def prepare(lists, queries, k_own, v_own, kv_dev):
    tokens, heads, dim = queries.shape
    operands = [
        pltpu.with_memory_space_constraint(x, pltpu.HBM) for x in (lists, queries, k_own, v_own)
    ]
    by_head = jax.ShapeDtypeStruct((kv_dev, tokens, dim), jnp.bfloat16)
    return pl.pallas_call(
        functools.partial(prepare_kernel, kv_dev=kv_dev),
        out_shape=(
            jax.ShapeDtypeStruct(lists.shape, lists.dtype),
            jax.ShapeDtypeStruct((kv_dev, tokens * heads // kv_dev, dim), jnp.bfloat16),
            by_head,
            by_head,
        ),
        in_specs=[pl.BlockSpec(memory_space=pltpu.HBM)] * 4,
        out_specs=(vmem(), vmem(), vmem(), vmem()),
        scratch_shapes=[
            pltpu.VMEM(queries.shape, jnp.bfloat16),
            pltpu.VMEM(k_own.shape, jnp.bfloat16),
            pltpu.VMEM(k_own.shape, jnp.bfloat16),
            pltpu.VMEM(k_own.shape, jnp.float32),
            pltpu.VMEM(k_own.shape, jnp.float32),
            pltpu.SemaphoreType.DMA((4,)),
        ],
        compiler_params=params(),
        name="prepare",
    )(*operands)


def listed_bits(lists_ref, code):
    target = lax.axis_index("seq").astype(jnp.int32)
    entries = lists_ref[...]
    mine = lax.broadcasted_iota(jnp.int32, entries.shape, 1) == target
    bits = jnp.left_shift(1, code(jnp.maximum(entries, 0), target)).astype(jnp.float32)
    return jnp.sum(jnp.where(jnp.logical_and(mine, entries >= 0), bits, 0.0)).astype(jnp.int32)


def has(bits, code):
    return jnp.bitwise_and(lax.shift_right_logical(bits, jnp.int32(code)), 1) == 1


def by_head(wide, h, kv_dev, keys):
    return wide[pl.ds(h, keys, stride=kv_dev), :].astype(jnp.bfloat16)


def with_ones(values):
    return jnp.concatenate([values, jnp.ones_like(values)], axis=1)


class Output:
    def __init__(self, out_ref, out_hbm, sems, kv_dev, group):
        self.out_ref, self.out_hbm, self.sems = out_ref, out_hbm, sems
        self.kv_dev, self.group, self.copies, self.before = kv_dev, group, [], None

    def put(self, h, first, both):
        rows, dim = both.shape[0], both.shape[1] // 2
        merged = both[:, :dim] * pl.reciprocal(both[:, dim:])
        merged = merged.reshape(rows // self.group, self.group, dim)
        if h % 2 == 0:
            self.before = merged
            return
        here = pl.ds(first // self.group, rows // self.group)
        heads = pl.ds((h - 1) * self.group, 2 * self.group)
        two = jnp.concatenate([self.before, merged], axis=1)
        self.out_ref[here, heads, :] = two.astype(jnp.bfloat16)
        if h + 1 == self.kv_dev:
            self.copies.append(
                pltpu.make_async_copy(
                    self.out_ref.at[here], self.out_hbm.at[here], self.sems.at[len(self.copies)]
                )
            )
            self.copies[-1].start()

    def wait(self):
        for copy in self.copies:
            copy.wait()


def chunks_of(kv_dev, rows_all):
    return [(h, first) for first in range(0, rows_all, ROW_CHUNK) for h in range(kv_dev)]


def in_turns(stages, jobs):
    held = {}
    for turn in range(len(jobs) + len(stages) - 1):
        for n, stage in enumerate(stages):
            at = turn - n
            if 0 <= at < len(jobs):
                held[at] = stage(jobs[at], held.get(at))
        held.pop(turn - len(stages) + 1, None)


def scores_of(q, keys):
    return lax.dot_general(q, keys, (((1,), (1,)), ((), ())), preferred_element_type=jnp.float32)


def attend_kernel(lists_ref, q_ref, k_own_ref, v_own_ref, *refs, codes, code, last):
    parts = len(codes)
    k_parts, v_parts = refs[:parts], refs[parts : 2 * parts]
    out_hbm, *state, k_wide, v_wide, out_ref, sems = refs[2 * parts :]
    kv_dev, tokens, dim = k_own_ref.shape
    rows_all = q_ref.shape[1]
    group = rows_all // tokens
    block = tokens * kv_dev
    most = k_wide.shape[0] // block
    factor = dim ** (-0.5) * math.log2(math.e)

    bits = listed_bits(lists_ref, code)
    count = jnp.int32(0)
    for part_code, k_part, v_part in zip(codes, k_parts, v_parts):
        take = has(bits, part_code)

        @pl.when(take)
        def _take(k_part=k_part, v_part=v_part, count=count):
            rows = pl.ds(pl.multiple_of(count * block, block), block)
            k_wide[rows, :] = k_part[...].astype(jnp.float32)
            v_wide[rows, :] = v_part[...].astype(jnp.float32)

        count += take.astype(jnp.int32)

    def run(others, final):
        keys = (others + 1) * tokens
        output = Output(out_ref, out_hbm, sems, kv_dev, group)
        k_ready, v_ready = [], []
        for h in range(kv_dev):
            k_h, v_h = k_own_ref[h], v_own_ref[h]
            if others:
                k_h = jnp.concatenate([k_h, by_head(k_wide, h, kv_dev, keys - tokens)], axis=0)
                v_h = jnp.concatenate([v_h, by_head(v_wide, h, kv_dev, keys - tokens)], axis=0)
            k_ready.append(k_h)
            v_ready.append(with_ones(v_h))

        def score(job, _):
            h, first = job
            return scores_of(q_ref[h, pl.ds(first, ROW_CHUNK), :], k_ready[h])

        def weigh(job, s):
            first = job[1]
            row = (lax.broadcasted_iota(jnp.int32, (ROW_CHUNK, tokens), 0) + first) // group
            key = lax.broadcasted_iota(jnp.int32, (ROW_CHUNK, tokens), 1)
            scores = [jnp.where(key <= row, s[:, :tokens], NO_KEY)]
            scores += [s[:, (j + 1) * tokens : (j + 2) * tokens] for j in range(others)]
            top = jnp.max(functools.reduce(jnp.maximum, scores), axis=1, keepdims=True)
            probs = [jnp.exp2((part - top) * factor).astype(jnp.bfloat16) for part in scores]
            return jnp.concatenate(probs, axis=1), top

        def add_up(job, weighed):
            h, first = job
            probs, top = weighed
            both = jnp.dot(probs, v_ready[h], preferred_element_type=jnp.float32)
            if final:
                output.put(h, first, both)
            else:
                rows = pl.ds(first, ROW_CHUNK)
                state[0][h, rows, :] = jnp.broadcast_to(top, (ROW_CHUNK, dim))
                state[1][h, rows, :] = both

        in_turns([score, weigh, add_up], chunks_of(kv_dev, rows_all))
        output.wait()

    unfinished = False if last is None else has(bits, last)
    for others in range(most + 1):

        @pl.when(jnp.logical_and(count == others, jnp.logical_not(unfinished)))
        def _whole(others=others):
            run(others, True)

        if last is not None and others < most:

            @pl.when(jnp.logical_and(count == others, unfinished))
            def _part(others=others):
                run(others, False)


def attend(lists, queries, k_own, v_own, k_parts, v_parts, codes, code, last):
    kv_dev, rows, dim = queries.shape
    tokens = k_own.shape[1]
    rest = (lists.shape[0] - 1) * tokens * kv_dev
    out = jax.ShapeDtypeStruct((tokens, rows * kv_dev // tokens, dim), jnp.bfloat16)
    state = [] if last is None else [
        jax.ShapeDtypeStruct((kv_dev, rows, wide), jnp.float32) for wide in (dim, 2 * dim)
    ]
    hbm = pl.BlockSpec(memory_space=pltpu.HBM)
    return pl.pallas_call(
        functools.partial(attend_kernel, codes=codes, code=code, last=last),
        out_shape=(out, *state),
        in_specs=[vmem()] * (4 + 2 * len(k_parts)),
        out_specs=(hbm, *(vmem() for _ in state)),
        scratch_shapes=[
            pltpu.VMEM((rest, dim), jnp.float32),
            pltpu.VMEM((rest, dim), jnp.float32),
            pltpu.VMEM(out.shape, jnp.bfloat16),
            pltpu.SemaphoreType.DMA((rows // ROW_CHUNK,)),
        ],
        compiler_params=params(),
        name="attend",
    )(lists, queries, k_own, v_own, *k_parts, *v_parts)


def last_kernel(
    lists_ref, q_ref, top_ref, both_ref, k_ref, v_ref, _, out_hbm, k_wide, v_wide, out_ref, sems, *, code, last
):
    kv_dev, rows_all, dim = q_ref.shape
    tokens = k_ref.shape[0] // kv_dev
    group = rows_all // tokens
    factor = dim ** (-0.5) * math.log2(math.e)

    @pl.when(has(listed_bits(lists_ref, code), last))
    def _add():
        k_wide[...] = k_ref[...].astype(jnp.float32)
        v_wide[...] = v_ref[...].astype(jnp.float32)
        k_ready = [by_head(k_wide, h, kv_dev, tokens) for h in range(kv_dev)]
        v_ready = [with_ones(by_head(v_wide, h, kv_dev, tokens)) for h in range(kv_dev)]
        jobs = chunks_of(kv_dev, rows_all)
        output = Output(out_ref, out_hbm, sems, kv_dev, group)
        shifts = []

        def score(job, _):
            h, first = job
            return scores_of(q_ref[h, pl.ds(first, ROW_CHUNK), :], k_ready[h])

        def weigh(job, s):
            h, first = job
            shifted = (s - top_ref[h, pl.ds(first, ROW_CHUNK), :]) * factor
            shifts.append(jnp.max(shifted.reshape(ROW_CHUNK // 8, 8, tokens), axis=0))
            return jnp.exp2(shifted).astype(jnp.bfloat16)

        def add_up(job, probs):
            h, first = job
            both = jnp.dot(probs, v_ready[h], preferred_element_type=jnp.float32)
            output.put(h, first, both + both_ref[h, pl.ds(first, ROW_CHUNK), :])

        in_turns([score, weigh, add_up], jobs)
        output.wait()

        @pl.when(jnp.max(functools.reduce(jnp.maximum, shifts)) > LARGEST)
        def _rescale():
            again = Output(out_ref, out_hbm, sems, kv_dev, group)
            for h, first in jobs:
                rows = pl.ds(first, ROW_CHUNK)
                s = scores_of(q_ref[h, rows, :], k_ready[h])
                before = top_ref[h, rows, :]
                top = jnp.maximum(before, jnp.max(s, axis=1, keepdims=True))
                probs = jnp.exp2((s - top) * factor).astype(jnp.bfloat16)
                shrink = jnp.exp2((before - top) * factor)
                both = both_ref[h, rows, :] * jnp.concatenate([shrink, shrink], axis=1)
                both += jnp.dot(probs, v_ready[h], preferred_element_type=jnp.float32)
                again.put(h, first, both)
            again.wait()


def attend_last(lists, queries, state, k_last, v_last, out, code, last):
    top, both = state
    hbm = pl.BlockSpec(memory_space=pltpu.HBM)
    return pl.pallas_call(
        functools.partial(last_kernel, code=code, last=last),
        out_shape=jax.ShapeDtypeStruct(out.shape, out.dtype),
        in_specs=[vmem()] * 6 + [hbm],
        out_specs=hbm,
        input_output_aliases={6: 0},
        scratch_shapes=[
            pltpu.VMEM(k_last.shape, jnp.float32),
            pltpu.VMEM(k_last.shape, jnp.float32),
            pltpu.VMEM(out.shape, jnp.bfloat16),
            pltpu.SemaphoreType.DMA((queries.shape[1] // ROW_CHUNK,)),
        ],
        compiler_params=params(),
        name="attend_last",
    )(lists, queries, top, both, k_last, v_last, out)


def ring_place(block, members):
    return jnp.where((block & 1) == 0, block >> 1, members - 1 - (block >> 1))


def ring_code(members):
    def code(block, target):
        ahead = ring_place(block, members) - ring_place(target, members)
        return jnp.where(ahead < 0, ahead + members, ahead)

    return code


def ring_steps(members):
    first, final = members // 4, 3 * members // 4 - 1
    forward = {p: (p + 1) % members for p in range(members)}
    backward = {p: (p - 1) % members for p in range(members)}
    low = [p for p in range(members) if not first <= p <= final]
    last_forward = {p: members - 1 - p for p in low}
    last_backward = {p: p ^ 1 for p in low}
    last_forward.update({p: p + 1 for p in range(first, final)})
    last_backward.update({p: p - 1 for p in range(first + 1, final + 1)})
    last_forward[final], last_backward[first] = first, final
    return forward, backward, last_forward, last_backward


def round_the_ring(k_own, v_own, ready, members):
    ring = list(range(0, members, 2)) + list(range(members - 1, 0, -2))
    forward, backward, last_forward, last_backward = ring_steps(members)

    def send(x, step):
        return lax.ppermute(x, "seq", [(ring[p], ring[to]) for p, to in sorted(step.items())])

    half = members // 2
    k_two, v_two, k_all, v_all = [k_own, k_own], [v_own, v_own], [], []
    for distance in range(1, half):
        ahead = send(k_two[0], forward), send(v_two[1], backward)
        behind = send(v_two[0], forward), send(k_two[1], backward)
        if distance == 1:
            ahead, ready = lax.optimization_barrier((ahead, ready))
        if distance < half - 1:
            ahead = lax.optimization_barrier(ahead)
        behind = lax.optimization_barrier(behind)
        k_two, v_two = [ahead[0], behind[1]], [behind[0], ahead[1]]
        k_all += k_two
        v_all += v_two
    here = ring_place(lax.axis_index("seq").astype(jnp.int32), members)
    k_last = jnp.where(here == 3 * members // 4 - 1, k_all[1], k_two[0])
    v_last = jnp.where(here == members // 4, v_all[0], v_two[1])
    return k_all, v_all, send(k_last, last_forward), send(v_last, last_backward), ready


def others(row, target):
    slots = row.shape[-1]
    own_at = jnp.argmax(row == target[..., None], axis=-1)
    j = jnp.arange(slots - 1)
    return jnp.where(j >= own_at[..., None], row[..., 1:], row[..., :-1])


def relay(k_own, v_own, chosen, members):
    block, dim = k_own.shape
    stacked = jnp.stack([k_own, v_own]).reshape(2, members, block // members, dim)
    shares = lax.all_to_all(stacked, "seq", split_axis=1, concat_axis=1, tiled=True)
    wanted = others(chosen, jnp.arange(members, dtype=jnp.int32))
    picked = jnp.take(shares, jnp.maximum(wanted, 0), axis=1)
    arrived = lax.all_to_all(picked, "seq", split_axis=1, concat_axis=3, tiled=True)
    count = wanted.shape[1]
    k_parts, v_parts = ([arrived[n, 0, j].reshape(block, dim) for j in range(count)] for n in range(2))
    return k_parts, v_parts, jnp.where(wanted < 0, -1, jnp.arange(count, dtype=jnp.int32))


def per_device(queries, keys, values, chosen):
    members = lax.axis_size("seq")
    tokens, kv_dev, dim = keys.shape
    k_own = keys.reshape(tokens * kv_dev, dim)
    v_own = values.reshape(tokens * kv_dev, dim)
    if members in ROUND:
        ready = prepare(chosen.T, queries, k_own, v_own, kv_dev)
        k_parts, v_parts, k_last, v_last, ready = round_the_ring(k_own, v_own, ready, members)
        lists, q_ready, k_ready, v_ready = ready
        half, code = members // 2, ring_code(members)
        codes = [turn for far in range(1, half) for turn in (members - far, far)]
        out, *state = attend(
            lists, q_ready, k_ready, v_ready, k_parts, v_parts, codes, code, half
        )
        return attend_last(lists, q_ready, state, k_last, v_last, out, code, half)

    k_parts, v_parts, mine = relay(k_own, v_own, chosen, members)
    lists, *ready = prepare(mine.T, queries, k_own, v_own, kv_dev)
    lists = jnp.concatenate([lists, jnp.full_like(lists[:1], -1)])
    codes = list(range(len(k_parts)))
    return attend(lists, *ready, k_parts, v_parts, codes, lambda block, _: block, None)[0]


def solution(mesh):
    rows = P(("groups", "seq"), "head", None)
    return jax.shard_map(
        per_device,
        mesh=mesh,
        in_specs=(rows, rows, rows, P("groups", None)),
        out_specs=rows,
        check_vma=False,
    )
```

```python
import functools
import math

import jax
import jax.numpy as jnp
from jax import lax
from jax.experimental import pallas as pl
from jax.experimental.pallas import tpu as pltpu
from jax.sharding import PartitionSpec as P

NO_KEY = -1e30
ROW_CHUNK = 256
LARGEST = 64.0
ROUND = (8, 16)


def params():
    return pltpu.CompilerParams(vmem_limit_bytes=16 * 2**20)


def vmem():
    return pl.BlockSpec(memory_space=pltpu.VMEM)


def prepare_kernel(*refs, kv_dev, turn):
    n_in = 4
    lists_hbm, q_hbm, k_hbm, v_hbm = refs[:n_in]
    rest = refs[n_in:]
    made = rest[: len(rest) - 10]
    outs = rest[len(made) : len(made) + 4]
    lists_out, q_out, k_out, v_out = outs
    q_ref, k_ref, v_ref, k_wide, v_wide, sems = rest[len(made) + 4 :]

    def work():
        whole = ((k_hbm, k_ref), (v_hbm, v_ref), (q_hbm, q_ref), (lists_hbm, lists_out))
        copies = [
            pltpu.make_async_copy(source, here, sems.at[n])
            for n, (source, here) in enumerate(whole)
        ]
        for copy in copies:
            copy.start()
        tokens, heads, dim = q_ref.shape
        group = heads // kv_dev
        for copy, ref, wide, out in zip(copies, (k_ref, v_ref), (k_wide, v_wide), (k_out, v_out)):
            copy.wait()
            wide[...] = ref[...].astype(jnp.float32)
            for h in range(kv_dev):
                out[h] = wide[pl.ds(h, tokens, stride=kv_dev), :].astype(jnp.bfloat16)
        copies[2].wait()
        for h in range(kv_dev):
            q = q_ref[:, pl.ds(h * group, group), :].astype(jnp.float32)
            q_out[h] = q.reshape(tokens * group, dim).astype(jnp.bfloat16)
        copies[3].wait()

    if turn is None:
        work()
        return
    mine = lax.rem(lax.axis_index("head"), turn[1]) == turn[0]
    pl.when(mine)(work)
    if made:

        @pl.when(jnp.logical_not(mine))
        def _take_over():
            for before, out in zip(made, outs):
                out[...] = before[...]


def prepare(lists, queries, k_own, v_own, kv_dev, turn=None, made=()):
    tokens, heads, dim = queries.shape
    operands = [
        pltpu.with_memory_space_constraint(x, pltpu.HBM) for x in (lists, queries, k_own, v_own)
    ]
    by_head = jax.ShapeDtypeStruct((kv_dev, tokens, dim), jnp.bfloat16)
    return pl.pallas_call(
        functools.partial(prepare_kernel, kv_dev=kv_dev, turn=turn),
        out_shape=(
            jax.ShapeDtypeStruct(lists.shape, lists.dtype),
            jax.ShapeDtypeStruct((kv_dev, tokens * heads // kv_dev, dim), jnp.bfloat16),
            by_head,
            by_head,
        ),
        in_specs=[pl.BlockSpec(memory_space=pltpu.HBM)] * 4 + [vmem()] * len(made),
        out_specs=(vmem(), vmem(), vmem(), vmem()),
        scratch_shapes=[
            pltpu.VMEM(queries.shape, jnp.bfloat16),
            pltpu.VMEM(k_own.shape, jnp.bfloat16),
            pltpu.VMEM(k_own.shape, jnp.bfloat16),
            pltpu.VMEM(k_own.shape, jnp.float32),
            pltpu.VMEM(k_own.shape, jnp.float32),
            pltpu.SemaphoreType.DMA((4,)),
        ],
        compiler_params=params(),
        name="prepare",
    )(*operands, *made)


def listed_bits(lists_ref, code):
    target = lax.axis_index("seq").astype(jnp.int32)
    entries = lists_ref[...]
    mine = lax.broadcasted_iota(jnp.int32, entries.shape, 1) == target
    bits = jnp.left_shift(1, code(jnp.maximum(entries, 0), target)).astype(jnp.float32)
    return jnp.sum(jnp.where(jnp.logical_and(mine, entries >= 0), bits, 0.0)).astype(jnp.int32)


def has(bits, code):
    return jnp.bitwise_and(lax.shift_right_logical(bits, jnp.int32(code)), 1) == 1


def by_head(wide, h, kv_dev, keys):
    return wide[pl.ds(h, keys, stride=kv_dev), :].astype(jnp.bfloat16)


def with_ones(values):
    return jnp.concatenate([values, jnp.ones_like(values)], axis=1)


class Output:
    def __init__(self, out_ref, out_hbm, sems, kv_dev, group):
        self.out_ref, self.out_hbm, self.sems = out_ref, out_hbm, sems
        self.kv_dev, self.group, self.copies, self.before = kv_dev, group, [], None

    def put(self, h, first, both):
        rows, dim = both.shape[0], both.shape[1] // 2
        merged = both[:, :dim] * pl.reciprocal(both[:, dim:])
        merged = merged.reshape(rows // self.group, self.group, dim)
        if h % 2 == 0:
            self.before = merged
            return
        here = pl.ds(first // self.group, rows // self.group)
        heads = pl.ds((h - 1) * self.group, 2 * self.group)
        two = jnp.concatenate([self.before, merged], axis=1)
        self.out_ref[here, heads, :] = two.astype(jnp.bfloat16)
        if h + 1 == self.kv_dev:
            self.copies.append(
                pltpu.make_async_copy(
                    self.out_ref.at[here], self.out_hbm.at[here], self.sems.at[len(self.copies)]
                )
            )
            self.copies[-1].start()

    def wait(self):
        for copy in self.copies:
            copy.wait()


def chunks_of(kv_dev, rows_all):
    return [(h, first) for first in range(0, rows_all, ROW_CHUNK) for h in range(kv_dev)]


def in_turns(stages, jobs):
    held = {}
    for turn in range(len(jobs) + len(stages) - 1):
        for n, stage in enumerate(stages):
            at = turn - n
            if 0 <= at < len(jobs):
                held[at] = stage(jobs[at], held.get(at))
        held.pop(turn - len(stages) + 1, None)


def scores_of(q, keys):
    return lax.dot_general(q, keys, (((1,), (1,)), ((), ())), preferred_element_type=jnp.float32)


def attend_kernel(lists_ref, q_ref, k_own_ref, v_own_ref, *refs, codes, code, last):
    parts = len(codes)
    k_parts, v_parts = refs[:parts], refs[parts : 2 * parts]
    out_hbm, *state, k_wide, v_wide, out_ref, sems = refs[2 * parts :]
    kv_dev, tokens, dim = k_own_ref.shape
    rows_all = q_ref.shape[1]
    group = rows_all // tokens
    block = tokens * kv_dev
    most = k_wide.shape[0] // block
    factor = dim ** (-0.5) * math.log2(math.e)

    bits = listed_bits(lists_ref, code)
    count = jnp.int32(0)
    for part_code, k_part, v_part in zip(codes, k_parts, v_parts):
        take = has(bits, part_code)

        @pl.when(take)
        def _take(k_part=k_part, v_part=v_part, count=count):
            rows = pl.ds(pl.multiple_of(count * block, block), block)
            k_wide[rows, :] = k_part[...].astype(jnp.float32)
            v_wide[rows, :] = v_part[...].astype(jnp.float32)

        count += take.astype(jnp.int32)

    def run(others, final):
        keys = (others + 1) * tokens
        output = Output(out_ref, out_hbm, sems, kv_dev, group)
        k_ready, v_ready = [], []
        for h in range(kv_dev):
            k_h, v_h = k_own_ref[h], v_own_ref[h]
            if others:
                k_h = jnp.concatenate([k_h, by_head(k_wide, h, kv_dev, keys - tokens)], axis=0)
                v_h = jnp.concatenate([v_h, by_head(v_wide, h, kv_dev, keys - tokens)], axis=0)
            k_ready.append(k_h)
            v_ready.append(with_ones(v_h))

        def score(job, _):
            h, first = job
            return scores_of(q_ref[h, pl.ds(first, ROW_CHUNK), :], k_ready[h])

        def weigh(job, s):
            first = job[1]
            row = (lax.broadcasted_iota(jnp.int32, (ROW_CHUNK, tokens), 0) + first) // group
            key = lax.broadcasted_iota(jnp.int32, (ROW_CHUNK, tokens), 1)
            scores = [jnp.where(key <= row, s[:, :tokens], NO_KEY)]
            scores += [s[:, (j + 1) * tokens : (j + 2) * tokens] for j in range(others)]
            top = jnp.max(functools.reduce(jnp.maximum, scores), axis=1, keepdims=True)
            probs = [jnp.exp2((part - top) * factor).astype(jnp.bfloat16) for part in scores]
            return jnp.concatenate(probs, axis=1), top

        def add_up(job, weighed):
            h, first = job
            probs, top = weighed
            both = jnp.dot(probs, v_ready[h], preferred_element_type=jnp.float32)
            if final:
                output.put(h, first, both)
            else:
                rows = pl.ds(first, ROW_CHUNK)
                state[0][h, rows, :] = jnp.broadcast_to(top, (ROW_CHUNK, dim))
                state[1][h, rows, :] = both

        in_turns([score, weigh, add_up], chunks_of(kv_dev, rows_all))
        output.wait()

    unfinished = False if last is None else has(bits, last)
    for others in range(most + 1):

        @pl.when(jnp.logical_and(count == others, jnp.logical_not(unfinished)))
        def _whole(others=others):
            run(others, True)

        if last is not None and others < most:

            @pl.when(jnp.logical_and(count == others, unfinished))
            def _part(others=others):
                run(others, False)


def attend(lists, queries, k_own, v_own, k_parts, v_parts, codes, code, last):
    kv_dev, rows, dim = queries.shape
    tokens = k_own.shape[1]
    rest = (lists.shape[0] - 1) * tokens * kv_dev
    out = jax.ShapeDtypeStruct((tokens, rows * kv_dev // tokens, dim), jnp.bfloat16)
    state = [] if last is None else [
        jax.ShapeDtypeStruct((kv_dev, rows, wide), jnp.float32) for wide in (dim, 2 * dim)
    ]
    hbm = pl.BlockSpec(memory_space=pltpu.HBM)
    return pl.pallas_call(
        functools.partial(attend_kernel, codes=codes, code=code, last=last),
        out_shape=(out, *state),
        in_specs=[vmem()] * (4 + 2 * len(k_parts)),
        out_specs=(hbm, *(vmem() for _ in state)),
        scratch_shapes=[
            pltpu.VMEM((rest, dim), jnp.float32),
            pltpu.VMEM((rest, dim), jnp.float32),
            pltpu.VMEM(out.shape, jnp.bfloat16),
            pltpu.SemaphoreType.DMA((rows // ROW_CHUNK,)),
        ],
        compiler_params=params(),
        name="attend",
    )(lists, queries, k_own, v_own, *k_parts, *v_parts)


def last_kernel(
    lists_ref, q_ref, top_ref, both_ref, k_ref, v_ref, _, out_hbm, k_wide, v_wide, out_ref, sems, *, code, last
):
    kv_dev, rows_all, dim = q_ref.shape
    tokens = k_ref.shape[0] // kv_dev
    group = rows_all // tokens
    factor = dim ** (-0.5) * math.log2(math.e)

    @pl.when(has(listed_bits(lists_ref, code), last))
    def _add():
        k_wide[...] = k_ref[...].astype(jnp.float32)
        v_wide[...] = v_ref[...].astype(jnp.float32)
        k_ready = [by_head(k_wide, h, kv_dev, tokens) for h in range(kv_dev)]
        v_ready = [with_ones(by_head(v_wide, h, kv_dev, tokens)) for h in range(kv_dev)]
        jobs = chunks_of(kv_dev, rows_all)
        output = Output(out_ref, out_hbm, sems, kv_dev, group)
        shifts = []

        def score(job, _):
            h, first = job
            return scores_of(q_ref[h, pl.ds(first, ROW_CHUNK), :], k_ready[h])

        def weigh(job, s):
            h, first = job
            shifted = (s - top_ref[h, pl.ds(first, ROW_CHUNK), :]) * factor
            shifts.append(jnp.max(shifted.reshape(ROW_CHUNK // 8, 8, tokens), axis=0))
            return jnp.exp2(shifted).astype(jnp.bfloat16)

        def add_up(job, probs):
            h, first = job
            both = jnp.dot(probs, v_ready[h], preferred_element_type=jnp.float32)
            output.put(h, first, both + both_ref[h, pl.ds(first, ROW_CHUNK), :])

        in_turns([score, weigh, add_up], jobs)
        output.wait()

        @pl.when(jnp.max(functools.reduce(jnp.maximum, shifts)) > LARGEST)
        def _rescale():
            again = Output(out_ref, out_hbm, sems, kv_dev, group)
            for h, first in jobs:
                rows = pl.ds(first, ROW_CHUNK)
                s = scores_of(q_ref[h, rows, :], k_ready[h])
                before = top_ref[h, rows, :]
                top = jnp.maximum(before, jnp.max(s, axis=1, keepdims=True))
                probs = jnp.exp2((s - top) * factor).astype(jnp.bfloat16)
                shrink = jnp.exp2((before - top) * factor)
                both = both_ref[h, rows, :] * jnp.concatenate([shrink, shrink], axis=1)
                both += jnp.dot(probs, v_ready[h], preferred_element_type=jnp.float32)
                again.put(h, first, both)
            again.wait()


def attend_last(lists, queries, state, k_last, v_last, out, code, last):
    top, both = state
    hbm = pl.BlockSpec(memory_space=pltpu.HBM)
    return pl.pallas_call(
        functools.partial(last_kernel, code=code, last=last),
        out_shape=jax.ShapeDtypeStruct(out.shape, out.dtype),
        in_specs=[vmem()] * 6 + [hbm],
        out_specs=hbm,
        input_output_aliases={6: 0},
        scratch_shapes=[
            pltpu.VMEM(k_last.shape, jnp.float32),
            pltpu.VMEM(k_last.shape, jnp.float32),
            pltpu.VMEM(out.shape, jnp.bfloat16),
            pltpu.SemaphoreType.DMA((queries.shape[1] // ROW_CHUNK,)),
        ],
        compiler_params=params(),
        name="attend_last",
    )(lists, queries, top, both, k_last, v_last, out)


def ring_place(block, members):
    return jnp.where((block & 1) == 0, block >> 1, members - 1 - (block >> 1))


def ring_code(members):
    def code(block, target):
        ahead = ring_place(block, members) - ring_place(target, members)
        return jnp.where(ahead < 0, ahead + members, ahead)

    return code


def ring_steps(members):
    first, final = members // 4, 3 * members // 4 - 1
    forward = {p: (p + 1) % members for p in range(members)}
    backward = {p: (p - 1) % members for p in range(members)}
    low = [p for p in range(members) if not first <= p <= final]
    last_forward = {p: members - 1 - p for p in low}
    last_backward = {p: p ^ 1 for p in low}
    last_forward.update({p: p + 1 for p in range(first, final)})
    last_backward.update({p: p - 1 for p in range(first + 1, final + 1)})
    last_forward[final], last_backward[first] = first, final
    return forward, backward, last_forward, last_backward


def round_the_ring(k_own, v_own, ready, members):
    ring = list(range(0, members, 2)) + list(range(members - 1, 0, -2))
    forward, backward, last_forward, last_backward = ring_steps(members)

    def send(x, step):
        return lax.ppermute(x, "seq", [(ring[p], ring[to]) for p, to in sorted(step.items())])

    half = members // 2
    k_two, v_two, k_all, v_all = [k_own, k_own], [v_own, v_own], [], []
    for distance in range(1, half):
        ahead = send(k_two[0], forward), send(v_two[1], backward)
        behind = send(v_two[0], forward), send(k_two[1], backward)
        if distance == 1:
            ahead, ready = lax.optimization_barrier((ahead, ready))
        if distance < half - 1:
            ahead = lax.optimization_barrier(ahead)
        behind = lax.optimization_barrier(behind)
        k_two, v_two = [ahead[0], behind[1]], [behind[0], ahead[1]]
        k_all += k_two
        v_all += v_two
    here = ring_place(lax.axis_index("seq").astype(jnp.int32), members)
    k_last = jnp.where(here == 3 * members // 4 - 1, k_all[1], k_two[0])
    v_last = jnp.where(here == members // 4, v_all[0], v_two[1])
    return k_all, v_all, send(k_last, last_forward), send(v_last, last_backward), ready


def others(row, target):
    slots = row.shape[-1]
    own_at = jnp.argmax(row == target[..., None], axis=-1)
    j = jnp.arange(slots - 1)
    return jnp.where(j >= own_at[..., None], row[..., 1:], row[..., :-1])


def relay(k_own, v_own, chosen, members):
    block, dim = k_own.shape
    stacked = jnp.stack([k_own, v_own]).reshape(2, members, block // members, dim)
    shares = lax.all_to_all(stacked, "seq", split_axis=1, concat_axis=1, tiled=True)
    wanted = others(chosen, jnp.arange(members, dtype=jnp.int32))
    picked = jnp.take(shares, jnp.maximum(wanted, 0), axis=1)
    arrived = lax.all_to_all(picked, "seq", split_axis=1, concat_axis=3, tiled=True)
    count = wanted.shape[1]
    k_parts, v_parts = ([arrived[n, 0, j].reshape(block, dim) for j in range(count)] for n in range(2))
    return k_parts, v_parts, jnp.where(wanted < 0, -1, jnp.arange(count, dtype=jnp.int32))


def per_device(queries, keys, values, chosen):
    members = lax.axis_size("seq")
    tokens, kv_dev, dim = keys.shape
    k_own = keys.reshape(tokens * kv_dev, dim)
    v_own = values.reshape(tokens * kv_dev, dim)
    if members in ROUND:
        own = chosen.T, queries, k_own, v_own, kv_dev
        made = prepare(*own, turn=(1, 2))
        k_own, v_own, made = lax.optimization_barrier((k_own, v_own, made))
        ready = prepare(*own, turn=(0, 2), made=made)
        k_parts, v_parts, k_last, v_last, ready = round_the_ring(k_own, v_own, ready, members)
        lists, q_ready, k_ready, v_ready = ready
        half, code = members // 2, ring_code(members)
        codes = [turn for far in range(1, half) for turn in (members - far, far)]
        out, *state = attend(
            lists, q_ready, k_ready, v_ready, k_parts, v_parts, codes, code, half
        )
        return attend_last(lists, q_ready, state, k_last, v_last, out, code, half)

    k_parts, v_parts, mine = relay(k_own, v_own, chosen, members)
    lists, *ready = prepare(mine.T, queries, k_own, v_own, kv_dev)
    lists = jnp.concatenate([lists, jnp.full_like(lists[:1], -1)])
    codes = list(range(len(k_parts)))
    return attend(lists, *ready, k_parts, v_parts, codes, lambda block, _: block, None)[0]


def solution(mesh):
    rows = P(("groups", "seq"), "head", None)
    return jax.shard_map(
        per_device,
        mesh=mesh,
        in_specs=(rows, rows, rows, P("groups", None)),
        out_specs=rows,
        check_vma=False,
    )
```

```python
import functools
import math

import jax
import jax.numpy as jnp
from jax import lax
from jax.experimental import pallas as pl
from jax.experimental.pallas import tpu as pltpu
from jax.sharding import PartitionSpec as P

NO_KEY = -1e30
ROW_CHUNK = 256
LARGEST = 64.0
ROUND = (8,)


def params():
    return pltpu.CompilerParams(vmem_limit_bytes=16 * 2**20)


def vmem():
    return pl.BlockSpec(memory_space=pltpu.VMEM)


def prepare_kernel(
    lists_hbm, q_hbm, k_hbm, v_hbm, lists_out, q_out, k_out, v_out,
    q_ref, k_ref, v_ref, k_wide, v_wide, sems, *, kv_dev,
):
    whole = ((k_hbm, k_ref), (v_hbm, v_ref), (q_hbm, q_ref), (lists_hbm, lists_out))
    copies = [
        pltpu.make_async_copy(source, here, sems.at[n]) for n, (source, here) in enumerate(whole)
    ]
    for copy in copies:
        copy.start()
    tokens, heads, dim = q_ref.shape
    group = heads // kv_dev
    for copy, ref, wide, out in zip(copies, (k_ref, v_ref), (k_wide, v_wide), (k_out, v_out)):
        copy.wait()
        wide[...] = ref[...].astype(jnp.float32)
        for h in range(kv_dev):
            out[h] = wide[pl.ds(h, tokens, stride=kv_dev), :].astype(jnp.bfloat16)
    copies[2].wait()
    for h in range(kv_dev):
        q = q_ref[:, pl.ds(h * group, group), :].astype(jnp.float32)
        q_out[h] = q.reshape(tokens * group, dim).astype(jnp.bfloat16)
    copies[3].wait()


def prepare(lists, queries, k_own, v_own, kv_dev):
    tokens, heads, dim = queries.shape
    operands = [
        pltpu.with_memory_space_constraint(x, pltpu.HBM) for x in (lists, queries, k_own, v_own)
    ]
    by_head = jax.ShapeDtypeStruct((kv_dev, tokens, dim), jnp.bfloat16)
    return pl.pallas_call(
        functools.partial(prepare_kernel, kv_dev=kv_dev),
        out_shape=(
            jax.ShapeDtypeStruct(lists.shape, lists.dtype),
            jax.ShapeDtypeStruct((kv_dev, tokens * heads // kv_dev, dim), jnp.bfloat16),
            by_head,
            by_head,
        ),
        in_specs=[pl.BlockSpec(memory_space=pltpu.HBM)] * 4,
        out_specs=(vmem(), vmem(), vmem(), vmem()),
        scratch_shapes=[
            pltpu.VMEM(queries.shape, jnp.bfloat16),
            pltpu.VMEM(k_own.shape, jnp.bfloat16),
            pltpu.VMEM(k_own.shape, jnp.bfloat16),
            pltpu.VMEM(k_own.shape, jnp.float32),
            pltpu.VMEM(k_own.shape, jnp.float32),
            pltpu.SemaphoreType.DMA((4,)),
        ],
        compiler_params=params(),
        name="prepare",
    )(*operands)


def listed_bits(lists_ref, code):
    target = lax.axis_index("seq").astype(jnp.int32)
    entries = lists_ref[...]
    mine = lax.broadcasted_iota(jnp.int32, entries.shape, 1) == target
    bits = jnp.left_shift(1, code(jnp.maximum(entries, 0), target)).astype(jnp.float32)
    return jnp.sum(jnp.where(jnp.logical_and(mine, entries >= 0), bits, 0.0)).astype(jnp.int32)


def has(bits, code):
    return jnp.bitwise_and(lax.shift_right_logical(bits, jnp.int32(code)), 1) == 1


def by_head(wide, h, kv_dev, keys):
    return wide[pl.ds(h, keys, stride=kv_dev), :].astype(jnp.bfloat16)


def with_ones(values):
    return jnp.concatenate([values, jnp.ones_like(values)], axis=1)


class Output:
    def __init__(self, out_ref, out_hbm, sems, kv_dev, group):
        self.out_ref, self.out_hbm, self.sems = out_ref, out_hbm, sems
        self.kv_dev, self.group, self.copies, self.before = kv_dev, group, [], None

    def put(self, h, first, both):
        rows, dim = both.shape[0], both.shape[1] // 2
        merged = both[:, :dim] * pl.reciprocal(both[:, dim:])
        merged = merged.reshape(rows // self.group, self.group, dim)
        if h % 2 == 0:
            self.before = merged
            return
        here = pl.ds(first // self.group, rows // self.group)
        heads = pl.ds((h - 1) * self.group, 2 * self.group)
        two = jnp.concatenate([self.before, merged], axis=1)
        self.out_ref[here, heads, :] = two.astype(jnp.bfloat16)
        if h + 1 == self.kv_dev:
            self.copies.append(
                pltpu.make_async_copy(
                    self.out_ref.at[here], self.out_hbm.at[here], self.sems.at[len(self.copies)]
                )
            )
            self.copies[-1].start()

    def wait(self):
        for copy in self.copies:
            copy.wait()


def chunks_of(kv_dev, rows_all):
    return [(h, first) for first in range(0, rows_all, ROW_CHUNK) for h in range(kv_dev)]


def in_turns(stages, jobs):
    held = {}
    for turn in range(len(jobs) + len(stages) - 1):
        for n, stage in enumerate(stages):
            at = turn - n
            if 0 <= at < len(jobs):
                held[at] = stage(jobs[at], held.get(at))
        held.pop(turn - len(stages) + 1, None)


def scores_of(q, keys):
    return lax.dot_general(q, keys, (((1,), (1,)), ((), ())), preferred_element_type=jnp.float32)


def attend_kernel(lists_ref, q_ref, k_own_ref, v_own_ref, *refs, codes, code, last):
    parts = len(codes)
    k_parts, v_parts = refs[:parts], refs[parts : 2 * parts]
    out_hbm, *state, k_wide, v_wide, out_ref, sems = refs[2 * parts :]
    kv_dev, tokens, dim = k_own_ref.shape
    rows_all = q_ref.shape[1]
    group = rows_all // tokens
    block = tokens * kv_dev
    most = k_wide.shape[0] // block
    factor = dim ** (-0.5) * math.log2(math.e)

    bits = listed_bits(lists_ref, code)
    count = jnp.int32(0)
    for part_code, k_part, v_part in zip(codes, k_parts, v_parts):
        take = has(bits, part_code)

        @pl.when(take)
        def _take(k_part=k_part, v_part=v_part, count=count):
            rows = pl.ds(pl.multiple_of(count * block, block), block)
            k_wide[rows, :] = k_part[...].astype(jnp.float32)
            v_wide[rows, :] = v_part[...].astype(jnp.float32)

        count += take.astype(jnp.int32)

    def run(others, final):
        keys = (others + 1) * tokens
        output = Output(out_ref, out_hbm, sems, kv_dev, group)
        k_ready, v_ready = [], []
        for h in range(kv_dev):
            k_h, v_h = k_own_ref[h], v_own_ref[h]
            if others:
                k_h = jnp.concatenate([k_h, by_head(k_wide, h, kv_dev, keys - tokens)], axis=0)
                v_h = jnp.concatenate([v_h, by_head(v_wide, h, kv_dev, keys - tokens)], axis=0)
            k_ready.append(k_h)
            v_ready.append(with_ones(v_h))

        def score(job, _):
            h, first = job
            return scores_of(q_ref[h, pl.ds(first, ROW_CHUNK), :], k_ready[h])

        def weigh(job, s):
            first = job[1]
            row = (lax.broadcasted_iota(jnp.int32, (ROW_CHUNK, tokens), 0) + first) // group
            key = lax.broadcasted_iota(jnp.int32, (ROW_CHUNK, tokens), 1)
            scores = [jnp.where(key <= row, s[:, :tokens], NO_KEY)]
            scores += [s[:, (j + 1) * tokens : (j + 2) * tokens] for j in range(others)]
            top = jnp.max(functools.reduce(jnp.maximum, scores), axis=1, keepdims=True)
            probs = [jnp.exp2((part - top) * factor).astype(jnp.bfloat16) for part in scores]
            return jnp.concatenate(probs, axis=1), top

        def add_up(job, weighed):
            h, first = job
            probs, top = weighed
            both = jnp.dot(probs, v_ready[h], preferred_element_type=jnp.float32)
            if final:
                output.put(h, first, both)
            else:
                rows = pl.ds(first, ROW_CHUNK)
                state[0][h, rows, :] = jnp.broadcast_to(top, (ROW_CHUNK, dim))
                state[1][h, rows, :] = both

        in_turns([score, weigh, add_up], chunks_of(kv_dev, rows_all))
        output.wait()

    unfinished = False if last is None else has(bits, last)
    for others in range(most + 1):

        @pl.when(jnp.logical_and(count == others, jnp.logical_not(unfinished)))
        def _whole(others=others):
            run(others, True)

        if last is not None and others < most:

            @pl.when(jnp.logical_and(count == others, unfinished))
            def _part(others=others):
                run(others, False)


def attend(lists, queries, k_own, v_own, k_parts, v_parts, codes, code, last):
    kv_dev, rows, dim = queries.shape
    tokens = k_own.shape[1]
    rest = (lists.shape[0] - 1) * tokens * kv_dev
    out = jax.ShapeDtypeStruct((tokens, rows * kv_dev // tokens, dim), jnp.bfloat16)
    state = [] if last is None else [
        jax.ShapeDtypeStruct((kv_dev, rows, wide), jnp.float32) for wide in (dim, 2 * dim)
    ]
    hbm = pl.BlockSpec(memory_space=pltpu.HBM)
    return pl.pallas_call(
        functools.partial(attend_kernel, codes=codes, code=code, last=last),
        out_shape=(out, *state),
        in_specs=[vmem()] * (4 + 2 * len(k_parts)),
        out_specs=(hbm, *(vmem() for _ in state)),
        scratch_shapes=[
            pltpu.VMEM((rest, dim), jnp.float32),
            pltpu.VMEM((rest, dim), jnp.float32),
            pltpu.VMEM(out.shape, jnp.bfloat16),
            pltpu.SemaphoreType.DMA((rows // ROW_CHUNK,)),
        ],
        compiler_params=params(),
        name="attend",
    )(lists, queries, k_own, v_own, *k_parts, *v_parts)


def last_kernel(
    lists_ref, q_ref, top_ref, both_ref, k_ref, v_ref, _, out_hbm, k_wide, v_wide, out_ref, sems, *, code, last
):
    kv_dev, rows_all, dim = q_ref.shape
    tokens = k_ref.shape[0] // kv_dev
    group = rows_all // tokens
    factor = dim ** (-0.5) * math.log2(math.e)

    @pl.when(has(listed_bits(lists_ref, code), last))
    def _add():
        k_wide[...] = k_ref[...].astype(jnp.float32)
        v_wide[...] = v_ref[...].astype(jnp.float32)
        k_ready = [by_head(k_wide, h, kv_dev, tokens) for h in range(kv_dev)]
        v_ready = [with_ones(by_head(v_wide, h, kv_dev, tokens)) for h in range(kv_dev)]
        jobs = chunks_of(kv_dev, rows_all)
        output = Output(out_ref, out_hbm, sems, kv_dev, group)
        shifts = []

        def score(job, _):
            h, first = job
            return scores_of(q_ref[h, pl.ds(first, ROW_CHUNK), :], k_ready[h])

        def weigh(job, s):
            h, first = job
            shifted = (s - top_ref[h, pl.ds(first, ROW_CHUNK), :]) * factor
            shifts.append(jnp.max(shifted.reshape(ROW_CHUNK // 8, 8, tokens), axis=0))
            return jnp.exp2(shifted).astype(jnp.bfloat16)

        def add_up(job, probs):
            h, first = job
            both = jnp.dot(probs, v_ready[h], preferred_element_type=jnp.float32)
            output.put(h, first, both + both_ref[h, pl.ds(first, ROW_CHUNK), :])

        in_turns([score, weigh, add_up], jobs)
        output.wait()

        @pl.when(jnp.max(functools.reduce(jnp.maximum, shifts)) > LARGEST)
        def _rescale():
            again = Output(out_ref, out_hbm, sems, kv_dev, group)
            for h, first in jobs:
                rows = pl.ds(first, ROW_CHUNK)
                s = scores_of(q_ref[h, rows, :], k_ready[h])
                before = top_ref[h, rows, :]
                top = jnp.maximum(before, jnp.max(s, axis=1, keepdims=True))
                probs = jnp.exp2((s - top) * factor).astype(jnp.bfloat16)
                shrink = jnp.exp2((before - top) * factor)
                both = both_ref[h, rows, :] * jnp.concatenate([shrink, shrink], axis=1)
                both += jnp.dot(probs, v_ready[h], preferred_element_type=jnp.float32)
                again.put(h, first, both)
            again.wait()


def attend_last(lists, queries, state, k_last, v_last, out, code, last):
    top, both = state
    hbm = pl.BlockSpec(memory_space=pltpu.HBM)
    return pl.pallas_call(
        functools.partial(last_kernel, code=code, last=last),
        out_shape=jax.ShapeDtypeStruct(out.shape, out.dtype),
        in_specs=[vmem()] * 6 + [hbm],
        out_specs=hbm,
        input_output_aliases={6: 0},
        scratch_shapes=[
            pltpu.VMEM(k_last.shape, jnp.float32),
            pltpu.VMEM(k_last.shape, jnp.float32),
            pltpu.VMEM(out.shape, jnp.bfloat16),
            pltpu.SemaphoreType.DMA((queries.shape[1] // ROW_CHUNK,)),
        ],
        compiler_params=params(),
        name="attend_last",
    )(lists, queries, top, both, k_last, v_last, out)


def ring_place(block, members):
    return jnp.where((block & 1) == 0, block >> 1, members - 1 - (block >> 1))


def ring_code(members):
    def code(block, target):
        ahead = ring_place(block, members) - ring_place(target, members)
        return jnp.where(ahead < 0, ahead + members, ahead)

    return code


LAST_KEYS = {1: 3, 2: 5, 3: 4, 4: 6, 5: 2, 6: 1}, {1: 2, 2: 0, 3: 4, 5: 1}
LAST_VALUES = {1: 6, 2: 5, 3: 1, 4: 3, 5: 2, 6: 4}, {2: 0, 4: 4, 5: 1, 6: 3}


def round_the_ring(k_own, v_own, ready, members):
    ring = list(range(0, members, 2)) + list(range(members - 1, 0, -2))
    cores = lax.axis_size("head")
    here = ring_place(lax.axis_index("seq").astype(jnp.int32), members)

    def send(x, turn):
        return lax.ppermute(x, "seq", [(ring[p], ring[(p + turn) % members]) for p in range(members)])

    def send_last(parts, plan):
        steps, whats = plan
        x = parts[-1]
        for place, what in whats.items():
            x = jnp.where(here == place, parts[what], x)
        pairs = []
        for p in range(members):
            for core in range(cores):
                to = (steps[p], core) if p in steps else (p, (core + 1) % cores)
                pairs.append((ring[p] * cores + core, ring[to[0]] * cores + to[1]))
        return lax.ppermute(x, ("seq", "head"), pairs)

    half = members // 2
    k_two, v_two, k_all, v_all = [k_own, k_own], [v_own, v_own], [], []
    for distance in range(1, half):
        ahead = send(k_two[0], 1), send(v_two[1], -1)
        behind = send(v_two[0], 1), send(k_two[1], -1)
        if distance == 1:
            ahead, ready = lax.optimization_barrier((ahead, ready))
        if distance < half - 1:
            ahead = lax.optimization_barrier(ahead)
        behind = lax.optimization_barrier(behind)
        k_two, v_two = [ahead[0], behind[1]], [behind[0], ahead[1]]
        k_all += k_two
        v_all += v_two
    k_last = send_last(k_all[:-1], LAST_KEYS)
    v_last = send_last(v_all[:-2] + v_all[-1:], LAST_VALUES)
    return k_all, v_all, k_last, v_last, ready


def others(row, target):
    slots = row.shape[-1]
    own_at = jnp.argmax(row == target[..., None], axis=-1)
    j = jnp.arange(slots - 1)
    return jnp.where(j >= own_at[..., None], row[..., 1:], row[..., :-1])


def relay(k_own, v_own, chosen, members):
    block, dim = k_own.shape
    stacked = jnp.stack([k_own, v_own]).reshape(2, members, block // members, dim)
    shares = lax.all_to_all(stacked, "seq", split_axis=1, concat_axis=1, tiled=True)
    wanted = others(chosen, jnp.arange(members, dtype=jnp.int32))
    picked = jnp.take(shares, jnp.maximum(wanted, 0), axis=1)
    arrived = lax.all_to_all(picked, "seq", split_axis=1, concat_axis=3, tiled=True)
    count = wanted.shape[1]
    k_parts, v_parts = ([arrived[n, 0, j].reshape(block, dim) for j in range(count)] for n in range(2))
    return k_parts, v_parts, jnp.where(wanted < 0, -1, jnp.arange(count, dtype=jnp.int32))


def per_device(queries, keys, values, chosen):
    members = lax.axis_size("seq")
    tokens, kv_dev, dim = keys.shape
    k_own = keys.reshape(tokens * kv_dev, dim)
    v_own = values.reshape(tokens * kv_dev, dim)
    if members in ROUND:
        ready = prepare(chosen.T, queries, k_own, v_own, kv_dev)
        k_parts, v_parts, k_last, v_last, ready = round_the_ring(k_own, v_own, ready, members)
        lists, q_ready, k_ready, v_ready = ready
        half, code = members // 2, ring_code(members)
        codes = [turn for far in range(1, half) for turn in (members - far, far)]
        out, *state = attend(
            lists, q_ready, k_ready, v_ready, k_parts, v_parts, codes, code, half
        )
        return attend_last(lists, q_ready, state, k_last, v_last, out, code, half)

    k_parts, v_parts, mine = relay(k_own, v_own, chosen, members)
    lists, *ready = prepare(mine.T, queries, k_own, v_own, kv_dev)
    lists = jnp.concatenate([lists, jnp.full_like(lists[:1], -1)])
    codes = list(range(len(k_parts)))
    return attend(lists, *ready, k_parts, v_parts, codes, lambda block, _: block, None)[0]


def solution(mesh):
    rows = P(("groups", "seq"), "head", None)
    return jax.shard_map(
        per_device,
        mesh=mesh,
        in_specs=(rows, rows, rows, P("groups", None)),
        out_specs=rows,
        check_vma=False,
    )
```

```python
import functools
import math

import jax
import jax.numpy as jnp
from jax import lax
from jax.experimental import pallas as pl
from jax.experimental.pallas import tpu as pltpu
from jax.sharding import PartitionSpec as P

NO_KEY = -1e30
ROW_CHUNK = 256
LARGEST = 64.0
ROUND = (8,)


def params():
    return pltpu.CompilerParams(vmem_limit_bytes=16 * 2**20)


def vmem():
    return pl.BlockSpec(memory_space=pltpu.VMEM)


def prepare_kernel(
    lists_hbm, q_hbm, k_hbm, v_hbm, lists_out, q_out, k_out, v_out,
    q_ref, k_ref, v_ref, k_wide, v_wide, sems, *, kv_dev,
):
    whole = ((k_hbm, k_ref), (v_hbm, v_ref), (q_hbm, q_ref), (lists_hbm, lists_out))
    copies = [
        pltpu.make_async_copy(source, here, sems.at[n]) for n, (source, here) in enumerate(whole)
    ]
    for copy in copies:
        copy.start()
    tokens, heads, dim = q_ref.shape
    group = heads // kv_dev
    for copy, ref, wide, out in zip(copies, (k_ref, v_ref), (k_wide, v_wide), (k_out, v_out)):
        copy.wait()
        wide[...] = ref[...].astype(jnp.float32)
        for h in range(kv_dev):
            out[h] = wide[pl.ds(h, tokens, stride=kv_dev), :].astype(jnp.bfloat16)
    copies[2].wait()
    for h in range(kv_dev):
        q = q_ref[:, pl.ds(h * group, group), :].astype(jnp.float32)
        q_out[h] = q.reshape(tokens * group, dim).astype(jnp.bfloat16)
    copies[3].wait()


def prepare(lists, queries, k_own, v_own, kv_dev):
    tokens, heads, dim = queries.shape
    operands = [
        pltpu.with_memory_space_constraint(x, pltpu.HBM) for x in (lists, queries, k_own, v_own)
    ]
    by_head = jax.ShapeDtypeStruct((kv_dev, tokens, dim), jnp.bfloat16)
    return pl.pallas_call(
        functools.partial(prepare_kernel, kv_dev=kv_dev),
        out_shape=(
            jax.ShapeDtypeStruct(lists.shape, lists.dtype),
            jax.ShapeDtypeStruct((kv_dev, tokens * heads // kv_dev, dim), jnp.bfloat16),
            by_head,
            by_head,
        ),
        in_specs=[pl.BlockSpec(memory_space=pltpu.HBM)] * 4,
        out_specs=(vmem(), vmem(), vmem(), vmem()),
        scratch_shapes=[
            pltpu.VMEM(queries.shape, jnp.bfloat16),
            pltpu.VMEM(k_own.shape, jnp.bfloat16),
            pltpu.VMEM(k_own.shape, jnp.bfloat16),
            pltpu.VMEM(k_own.shape, jnp.float32),
            pltpu.VMEM(k_own.shape, jnp.float32),
            pltpu.SemaphoreType.DMA((4,)),
        ],
        compiler_params=params(),
        name="prepare",
    )(*operands)


def listed_bits(lists_ref, code):
    target = lax.axis_index("seq").astype(jnp.int32)
    entries = lists_ref[...]
    mine = lax.broadcasted_iota(jnp.int32, entries.shape, 1) == target
    bits = jnp.left_shift(1, code(jnp.maximum(entries, 0), target)).astype(jnp.float32)
    return jnp.sum(jnp.where(jnp.logical_and(mine, entries >= 0), bits, 0.0)).astype(jnp.int32)


def has(bits, code):
    return jnp.bitwise_and(lax.shift_right_logical(bits, jnp.int32(code)), 1) == 1


def by_head(wide, h, kv_dev, keys):
    return wide[pl.ds(h, keys, stride=kv_dev), :].astype(jnp.bfloat16)


def with_ones(values):
    return jnp.concatenate([values, jnp.ones_like(values)], axis=1)


class Output:
    def __init__(self, out_ref, out_hbm, sems, kv_dev, group):
        self.out_ref, self.out_hbm, self.sems = out_ref, out_hbm, sems
        self.kv_dev, self.group, self.copies, self.before = kv_dev, group, [], None

    def put(self, h, first, both):
        rows, dim = both.shape[0], both.shape[1] // 2
        merged = both[:, :dim] * pl.reciprocal(both[:, dim:])
        merged = merged.reshape(rows // self.group, self.group, dim)
        if h % 2 == 0:
            self.before = merged
            return
        here = pl.ds(first // self.group, rows // self.group)
        heads = pl.ds((h - 1) * self.group, 2 * self.group)
        two = jnp.concatenate([self.before, merged], axis=1)
        self.out_ref[here, heads, :] = two.astype(jnp.bfloat16)
        if h + 1 == self.kv_dev:
            self.copies.append(
                pltpu.make_async_copy(
                    self.out_ref.at[here], self.out_hbm.at[here], self.sems.at[len(self.copies)]
                )
            )
            self.copies[-1].start()

    def wait(self):
        for copy in self.copies:
            copy.wait()


def chunks_of(kv_dev, rows_all):
    return [(h, first) for first in range(0, rows_all, ROW_CHUNK) for h in range(kv_dev)]


def in_turns(stages, jobs):
    held = {}
    for turn in range(len(jobs) + len(stages) - 1):
        for n, stage in enumerate(stages):
            at = turn - n
            if 0 <= at < len(jobs):
                held[at] = stage(jobs[at], held.get(at))
        held.pop(turn - len(stages) + 1, None)


def scores_of(q, keys):
    return lax.dot_general(q, keys, (((1,), (1,)), ((), ())), preferred_element_type=jnp.float32)


def attend_kernel(lists_ref, q_ref, k_own_ref, v_own_ref, *refs, codes, code, last):
    parts = len(codes)
    k_parts, v_parts = refs[:parts], refs[parts : 2 * parts]
    out_hbm, *state, k_wide, v_wide, out_ref, sems = refs[2 * parts :]
    kv_dev, tokens, dim = k_own_ref.shape
    rows_all = q_ref.shape[1]
    group = rows_all // tokens
    block = tokens * kv_dev
    most = k_wide.shape[0] // block
    factor = dim ** (-0.5) * math.log2(math.e)

    bits = listed_bits(lists_ref, code)
    count = jnp.int32(0)
    for part_code, k_part, v_part in zip(codes, k_parts, v_parts):
        take = has(bits, part_code)

        @pl.when(take)
        def _take(k_part=k_part, v_part=v_part, count=count):
            rows = pl.ds(pl.multiple_of(count * block, block), block)
            k_wide[rows, :] = k_part[...].astype(jnp.float32)
            v_wide[rows, :] = v_part[...].astype(jnp.float32)

        count += take.astype(jnp.int32)

    def run(others, final):
        keys = (others + 1) * tokens
        output = Output(out_ref, out_hbm, sems, kv_dev, group)
        k_ready, v_ready = [], []
        for h in range(kv_dev):
            k_h, v_h = k_own_ref[h], v_own_ref[h]
            if others:
                k_h = jnp.concatenate([k_h, by_head(k_wide, h, kv_dev, keys - tokens)], axis=0)
                v_h = jnp.concatenate([v_h, by_head(v_wide, h, kv_dev, keys - tokens)], axis=0)
            k_ready.append(k_h)
            v_ready.append(with_ones(v_h))

        past = lax.broadcasted_iota(jnp.int32, (ROW_CHUNK, tokens), 0)
        past -= group * lax.broadcasted_iota(jnp.int32, (ROW_CHUNK, tokens), 1)

        def score(job, _):
            h, first = job
            return scores_of(q_ref[h, pl.ds(first, ROW_CHUNK), :], k_ready[h])

        def weigh(job, s):
            first = job[1]
            scores = [jnp.where(past >= -first, s[:, :tokens], NO_KEY)]
            scores += [s[:, (j + 1) * tokens : (j + 2) * tokens] for j in range(others)]
            top = jnp.max(functools.reduce(jnp.maximum, scores), axis=1, keepdims=True)
            probs = [jnp.exp2((part - top) * factor).astype(jnp.bfloat16) for part in scores]
            return jnp.concatenate(probs, axis=1), top

        def add_up(job, weighed):
            h, first = job
            probs, top = weighed
            both = jnp.dot(probs, v_ready[h], preferred_element_type=jnp.float32)
            if final:
                output.put(h, first, both)
            else:
                rows = pl.ds(first, ROW_CHUNK)
                state[0][h, rows, :] = jnp.broadcast_to(top, (ROW_CHUNK, dim))
                state[1][h, rows, :] = both

        in_turns([score, weigh, add_up], chunks_of(kv_dev, rows_all))
        output.wait()

    unfinished = False if last is None else has(bits, last)
    for others in range(most + 1):

        @pl.when(jnp.logical_and(count == others, jnp.logical_not(unfinished)))
        def _whole(others=others):
            run(others, True)

        if last is not None and others < most:

            @pl.when(jnp.logical_and(count == others, unfinished))
            def _part(others=others):
                run(others, False)


def attend(lists, queries, k_own, v_own, k_parts, v_parts, codes, code, last):
    kv_dev, rows, dim = queries.shape
    tokens = k_own.shape[1]
    rest = (lists.shape[0] - 1) * tokens * kv_dev
    out = jax.ShapeDtypeStruct((tokens, rows * kv_dev // tokens, dim), jnp.bfloat16)
    state = [] if last is None else [
        jax.ShapeDtypeStruct((kv_dev, rows, wide), jnp.float32) for wide in (dim, 2 * dim)
    ]
    hbm = pl.BlockSpec(memory_space=pltpu.HBM)
    return pl.pallas_call(
        functools.partial(attend_kernel, codes=codes, code=code, last=last),
        out_shape=(out, *state),
        in_specs=[vmem()] * (4 + 2 * len(k_parts)),
        out_specs=(hbm, *(vmem() for _ in state)),
        scratch_shapes=[
            pltpu.VMEM((rest, dim), jnp.float32),
            pltpu.VMEM((rest, dim), jnp.float32),
            pltpu.VMEM(out.shape, jnp.bfloat16),
            pltpu.SemaphoreType.DMA((rows // ROW_CHUNK,)),
        ],
        compiler_params=params(),
        name="attend",
    )(lists, queries, k_own, v_own, *k_parts, *v_parts)


def last_kernel(
    lists_ref, q_ref, top_ref, both_ref, k_ref, v_ref, _, out_hbm, k_wide, v_wide, out_ref, sems, *, code, last
):
    kv_dev, rows_all, dim = q_ref.shape
    tokens = k_ref.shape[0] // kv_dev
    group = rows_all // tokens
    factor = dim ** (-0.5) * math.log2(math.e)

    @pl.when(has(listed_bits(lists_ref, code), last))
    def _add():
        k_wide[...] = k_ref[...].astype(jnp.float32)
        v_wide[...] = v_ref[...].astype(jnp.float32)
        k_ready = [by_head(k_wide, h, kv_dev, tokens) for h in range(kv_dev)]
        v_ready = [with_ones(by_head(v_wide, h, kv_dev, tokens)) for h in range(kv_dev)]
        jobs = chunks_of(kv_dev, rows_all)
        output = Output(out_ref, out_hbm, sems, kv_dev, group)
        shifts = []

        def score(job, _):
            h, first = job
            return scores_of(q_ref[h, pl.ds(first, ROW_CHUNK), :], k_ready[h])

        def weigh(job, s):
            h, first = job
            shifted = (s - top_ref[h, pl.ds(first, ROW_CHUNK), :]) * factor
            shifts.append(jnp.max(shifted.reshape(ROW_CHUNK // 8, 8, tokens), axis=0))
            return jnp.exp2(shifted).astype(jnp.bfloat16)

        def add_up(job, probs):
            h, first = job
            both = jnp.dot(probs, v_ready[h], preferred_element_type=jnp.float32)
            output.put(h, first, both + both_ref[h, pl.ds(first, ROW_CHUNK), :])

        in_turns([score, weigh, add_up], jobs)
        output.wait()

        @pl.when(jnp.max(functools.reduce(jnp.maximum, shifts)) > LARGEST)
        def _rescale():
            again = Output(out_ref, out_hbm, sems, kv_dev, group)
            for h, first in jobs:
                rows = pl.ds(first, ROW_CHUNK)
                s = scores_of(q_ref[h, rows, :], k_ready[h])
                before = top_ref[h, rows, :]
                top = jnp.maximum(before, jnp.max(s, axis=1, keepdims=True))
                probs = jnp.exp2((s - top) * factor).astype(jnp.bfloat16)
                shrink = jnp.exp2((before - top) * factor)
                both = both_ref[h, rows, :] * jnp.concatenate([shrink, shrink], axis=1)
                both += jnp.dot(probs, v_ready[h], preferred_element_type=jnp.float32)
                again.put(h, first, both)
            again.wait()


def attend_last(lists, queries, state, k_last, v_last, out, code, last):
    top, both = state
    hbm = pl.BlockSpec(memory_space=pltpu.HBM)
    return pl.pallas_call(
        functools.partial(last_kernel, code=code, last=last),
        out_shape=jax.ShapeDtypeStruct(out.shape, out.dtype),
        in_specs=[vmem()] * 6 + [hbm],
        out_specs=hbm,
        input_output_aliases={6: 0},
        scratch_shapes=[
            pltpu.VMEM(k_last.shape, jnp.float32),
            pltpu.VMEM(k_last.shape, jnp.float32),
            pltpu.VMEM(out.shape, jnp.bfloat16),
            pltpu.SemaphoreType.DMA((queries.shape[1] // ROW_CHUNK,)),
        ],
        compiler_params=params(),
        name="attend_last",
    )(lists, queries, top, both, k_last, v_last, out)


def ring_place(block, members):
    return jnp.where((block & 1) == 0, block >> 1, members - 1 - (block >> 1))


def ring_code(members):
    def code(block, target):
        ahead = ring_place(block, members) - ring_place(target, members)
        return jnp.where(ahead < 0, ahead + members, ahead)

    return code


LAST_KEYS = {1: 2, 2: 3, 3: 4, 4: 5, 5: 6, 6: 1}, {}
LAST_VALUES = {1: 6, 2: 5, 3: 1, 4: 3, 5: 2, 6: 4}, {2: 0, 4: 4, 5: 1, 6: 3}


def round_the_ring(k_own, v_own, ready, members):
    ring = list(range(0, members, 2)) + list(range(members - 1, 0, -2))
    cores = lax.axis_size("head")
    here = ring_place(lax.axis_index("seq").astype(jnp.int32), members)

    def send(x, turn):
        return lax.ppermute(x, "seq", [(ring[p], ring[(p + turn) % members]) for p in range(members)])

    def send_last(parts, plan):
        steps, whats = plan
        x = parts[-1]
        for place, what in whats.items():
            x = jnp.where(here == place, parts[what], x)
        pairs = []
        for p in range(members):
            for core in range(cores):
                to = (steps[p], core) if p in steps else (p, (core + 1) % cores)
                pairs.append((ring[p] * cores + core, ring[to[0]] * cores + to[1]))
        return lax.ppermute(x, ("seq", "head"), pairs)

    half = members // 2
    k_two, v_two, k_all, v_all = [k_own, k_own], [v_own, v_own], [], []
    for distance in range(1, half):
        ahead = send(k_two[0], 1), send(v_two[1], -1)
        behind = send(v_two[0], 1), send(k_two[1], -1)
        if distance == 1:
            ahead, ready = lax.optimization_barrier((ahead, ready))
        if distance < half - 1:
            ahead = lax.optimization_barrier(ahead)
        behind = lax.optimization_barrier(behind)
        k_two, v_two = [ahead[0], behind[1]], [behind[0], ahead[1]]
        k_all += k_two
        v_all += v_two
    k_last = send_last(k_all[:-1], LAST_KEYS)
    v_last = send_last(v_all[:-2] + v_all[-1:], LAST_VALUES)
    return k_all, v_all, k_last, v_last, ready


def others(row, target):
    slots = row.shape[-1]
    own_at = jnp.argmax(row == target[..., None], axis=-1)
    j = jnp.arange(slots - 1)
    return jnp.where(j >= own_at[..., None], row[..., 1:], row[..., :-1])


def relay(k_own, v_own, chosen, members):
    block, dim = k_own.shape
    stacked = jnp.stack([k_own, v_own]).reshape(2, members, block // members, dim)
    shares = lax.all_to_all(stacked, "seq", split_axis=1, concat_axis=1, tiled=True)
    wanted = others(chosen, jnp.arange(members, dtype=jnp.int32))
    picked = jnp.take(shares, jnp.maximum(wanted, 0), axis=1)
    arrived = lax.all_to_all(picked, "seq", split_axis=1, concat_axis=3, tiled=True)
    count = wanted.shape[1]
    k_parts, v_parts = ([arrived[n, 0, j].reshape(block, dim) for j in range(count)] for n in range(2))
    return k_parts, v_parts, jnp.where(wanted < 0, -1, jnp.arange(count, dtype=jnp.int32))


def per_device(queries, keys, values, chosen):
    members = lax.axis_size("seq")
    tokens, kv_dev, dim = keys.shape
    k_own = keys.reshape(tokens * kv_dev, dim)
    v_own = values.reshape(tokens * kv_dev, dim)
    if members in ROUND:
        ready = prepare(chosen.T, queries, k_own, v_own, kv_dev)
        k_parts, v_parts, k_last, v_last, ready = round_the_ring(k_own, v_own, ready, members)
        lists, q_ready, k_ready, v_ready = ready
        half, code = members // 2, ring_code(members)
        codes = [turn for far in range(1, half) for turn in (members - far, far)]
        out, *state = attend(
            lists, q_ready, k_ready, v_ready, k_parts, v_parts, codes, code, half
        )
        return attend_last(lists, q_ready, state, k_last, v_last, out, code, half)

    k_parts, v_parts, mine = relay(k_own, v_own, chosen, members)
    lists, *ready = prepare(mine.T, queries, k_own, v_own, kv_dev)
    lists = jnp.concatenate([lists, jnp.full_like(lists[:1], -1)])
    codes = list(range(len(k_parts)))
    return attend(lists, *ready, k_parts, v_parts, codes, lambda block, _: block, None)[0]


def solution(mesh):
    rows = P(("groups", "seq"), "head", None)
    return jax.shard_map(
        per_device,
        mesh=mesh,
        in_specs=(rows, rows, rows, P("groups", None)),
        out_specs=rows,
        check_vma=False,
    )
```

```python
import functools
import math

import jax
import jax.numpy as jnp
from jax import lax
from jax.experimental import pallas as pl
from jax.experimental.pallas import tpu as pltpu
from jax.sharding import PartitionSpec as P

NO_KEY = -1e30
ROW_CHUNK = 256
LARGEST = 64.0
ROUND = (8,)


def params():
    return pltpu.CompilerParams(vmem_limit_bytes=16 * 2**20)


def vmem():
    return pl.BlockSpec(memory_space=pltpu.VMEM)


def prepare_kernel(
    lists_hbm, q_hbm, k_hbm, v_hbm, lists_out, q_out, k_out, v_out,
    q_ref, k_ref, v_ref, k_wide, v_wide, sems, *, kv_dev,
):
    whole = ((k_hbm, k_ref), (v_hbm, v_ref), (q_hbm, q_ref), (lists_hbm, lists_out))
    copies = [
        pltpu.make_async_copy(source, here, sems.at[n]) for n, (source, here) in enumerate(whole)
    ]
    for copy in copies:
        copy.start()
    tokens, heads, dim = q_ref.shape
    group = heads // kv_dev
    for copy, ref, wide, out in zip(copies, (k_ref, v_ref), (k_wide, v_wide), (k_out, v_out)):
        copy.wait()
        wide[...] = ref[...].astype(jnp.float32)
        for h in range(kv_dev):
            out[h] = wide[pl.ds(h, tokens, stride=kv_dev), :].astype(jnp.bfloat16)
    copies[2].wait()
    for h in range(kv_dev):
        q = q_ref[:, pl.ds(h * group, group), :].astype(jnp.float32)
        q_out[h] = q.reshape(tokens * group, dim).astype(jnp.bfloat16)
    copies[3].wait()


def prepare(lists, queries, k_own, v_own, kv_dev):
    tokens, heads, dim = queries.shape
    operands = [
        pltpu.with_memory_space_constraint(x, pltpu.HBM) for x in (lists, queries, k_own, v_own)
    ]
    by_head = jax.ShapeDtypeStruct((kv_dev, tokens, dim), jnp.bfloat16)
    return pl.pallas_call(
        functools.partial(prepare_kernel, kv_dev=kv_dev),
        out_shape=(
            jax.ShapeDtypeStruct(lists.shape, lists.dtype),
            jax.ShapeDtypeStruct((kv_dev, tokens * heads // kv_dev, dim), jnp.bfloat16),
            by_head,
            by_head,
        ),
        in_specs=[pl.BlockSpec(memory_space=pltpu.HBM)] * 4,
        out_specs=(vmem(), vmem(), vmem(), vmem()),
        scratch_shapes=[
            pltpu.VMEM(queries.shape, jnp.bfloat16),
            pltpu.VMEM(k_own.shape, jnp.bfloat16),
            pltpu.VMEM(k_own.shape, jnp.bfloat16),
            pltpu.VMEM(k_own.shape, jnp.float32),
            pltpu.VMEM(k_own.shape, jnp.float32),
            pltpu.SemaphoreType.DMA((4,)),
        ],
        compiler_params=params(),
        name="prepare",
    )(*operands)


def listed_bits(lists_ref, code):
    target = lax.axis_index("seq").astype(jnp.int32)
    entries = lists_ref[...]
    mine = lax.broadcasted_iota(jnp.int32, entries.shape, 1) == target
    bits = jnp.left_shift(1, code(jnp.maximum(entries, 0), target)).astype(jnp.float32)
    return jnp.sum(jnp.where(jnp.logical_and(mine, entries >= 0), bits, 0.0)).astype(jnp.int32)


def has(bits, code):
    return jnp.bitwise_and(lax.shift_right_logical(bits, jnp.int32(code)), 1) == 1


def by_head(wide, h, kv_dev, keys):
    return wide[pl.ds(h, keys, stride=kv_dev), :].astype(jnp.bfloat16)


def with_ones(values):
    return jnp.concatenate([values, jnp.ones_like(values)], axis=1)


class Output:
    def __init__(self, out_ref, out_hbm, sems, kv_dev, group):
        self.out_ref, self.out_hbm, self.sems = out_ref, out_hbm, sems
        self.kv_dev, self.group, self.copies, self.before = kv_dev, group, [], None

    def put(self, h, first, both):
        rows, dim = both.shape[0], both.shape[1] // 2
        merged = both[:, :dim] * pl.reciprocal(both[:, dim:])
        merged = merged.reshape(rows // self.group, self.group, dim)
        if h % 2 == 0:
            self.before = merged
            return
        here = pl.ds(first // self.group, rows // self.group)
        heads = pl.ds((h - 1) * self.group, 2 * self.group)
        two = jnp.concatenate([self.before, merged], axis=1)
        self.out_ref[here, heads, :] = two.astype(jnp.bfloat16)
        if h + 1 == self.kv_dev:
            self.copies.append(
                pltpu.make_async_copy(
                    self.out_ref.at[here], self.out_hbm.at[here], self.sems.at[len(self.copies)]
                )
            )
            self.copies[-1].start()

    def wait(self):
        for copy in self.copies:
            copy.wait()


def chunks_of(kv_dev, rows_all):
    return [(h, first) for first in range(0, rows_all, ROW_CHUNK) for h in range(kv_dev)]


def in_turns(stages, jobs):
    held = {}
    for turn in range(len(jobs) + len(stages) - 1):
        for n, stage in enumerate(stages):
            at = turn - n
            if 0 <= at < len(jobs):
                held[at] = stage(jobs[at], held.get(at))
        held.pop(turn - len(stages) + 1, None)


def scores_of(q, keys):
    return lax.dot_general(q, keys, (((1,), (1,)), ((), ())), preferred_element_type=jnp.float32)


def attend_kernel(lists_ref, q_ref, k_own_ref, v_own_ref, *refs, codes, code, last):
    parts = len(codes)
    k_parts, v_parts = refs[:parts], refs[parts : 2 * parts]
    out_hbm, *state, k_wide, v_wide, out_ref, sems = refs[2 * parts :]
    kv_dev, tokens, dim = k_own_ref.shape
    rows_all = q_ref.shape[1]
    group = rows_all // tokens
    block = tokens * kv_dev
    most = k_wide.shape[0] // block
    factor = dim ** (-0.5) * math.log2(math.e)

    bits = listed_bits(lists_ref, code)
    count = jnp.int32(0)
    for part_code, k_part, v_part in zip(codes, k_parts, v_parts):
        take = has(bits, part_code)

        @pl.when(take)
        def _take(k_part=k_part, v_part=v_part, count=count):
            rows = pl.ds(pl.multiple_of(count * block, block), block)
            k_wide[rows, :] = k_part[...].astype(jnp.float32)
            v_wide[rows, :] = v_part[...].astype(jnp.float32)

        count += take.astype(jnp.int32)

    def run(others, final):
        keys = (others + 1) * tokens
        output = Output(out_ref, out_hbm, sems, kv_dev, group)
        k_ready, v_ready = [], []
        for h in range(kv_dev):
            k_h, v_h = k_own_ref[h], v_own_ref[h]
            if others:
                k_h = jnp.concatenate([k_h, by_head(k_wide, h, kv_dev, keys - tokens)], axis=0)
                v_h = jnp.concatenate([v_h, by_head(v_wide, h, kv_dev, keys - tokens)], axis=0)
            k_ready.append(k_h)
            v_ready.append(with_ones(v_h))

        past = lax.broadcasted_iota(jnp.int32, (ROW_CHUNK, tokens), 0)
        past -= group * lax.broadcasted_iota(jnp.int32, (ROW_CHUNK, tokens), 1)

        def score(job, _):
            h, first = job
            return scores_of(q_ref[h, pl.ds(first, ROW_CHUNK), :], k_ready[h])

        def weigh(job, s):
            first = job[1]
            scores = [jnp.where(past >= -first, s[:, :tokens], NO_KEY)]
            scores += [s[:, (j + 1) * tokens : (j + 2) * tokens] for j in range(others)]
            top = jnp.max(functools.reduce(jnp.maximum, scores), axis=1, keepdims=True)
            probs = [jnp.exp2((part - top) * factor).astype(jnp.bfloat16) for part in scores]
            return jnp.concatenate(probs, axis=1), top

        def add_up(job, weighed):
            h, first = job
            probs, top = weighed
            both = jnp.dot(probs, v_ready[h], preferred_element_type=jnp.float32)
            if final:
                output.put(h, first, both)
            else:
                rows = pl.ds(first, ROW_CHUNK)
                state[0][h, rows, :] = jnp.broadcast_to(top, (ROW_CHUNK, dim))
                state[1][h, rows, :] = both

        in_turns([score, weigh, add_up], chunks_of(kv_dev, rows_all))
        output.wait()

    unfinished = False if last is None else has(bits, last)
    for others in range(most + 1):

        @pl.when(jnp.logical_and(count == others, jnp.logical_not(unfinished)))
        def _whole(others=others):
            run(others, True)

        if last is not None and others < most:

            @pl.when(jnp.logical_and(count == others, unfinished))
            def _part(others=others):
                run(others, False)


def attend(lists, queries, k_own, v_own, k_parts, v_parts, codes, code, last):
    kv_dev, rows, dim = queries.shape
    tokens = k_own.shape[1]
    rest = (lists.shape[0] - 1) * tokens * kv_dev
    out = jax.ShapeDtypeStruct((tokens, rows * kv_dev // tokens, dim), jnp.bfloat16)
    state = [] if last is None else [
        jax.ShapeDtypeStruct((kv_dev, rows, wide), jnp.float32) for wide in (dim, 2 * dim)
    ]
    hbm = pl.BlockSpec(memory_space=pltpu.HBM)
    return pl.pallas_call(
        functools.partial(attend_kernel, codes=codes, code=code, last=last),
        out_shape=(out, *state),
        in_specs=[vmem()] * (4 + 2 * len(k_parts)),
        out_specs=(hbm, *(vmem() for _ in state)),
        scratch_shapes=[
            pltpu.VMEM((rest, dim), jnp.float32),
            pltpu.VMEM((rest, dim), jnp.float32),
            pltpu.VMEM(out.shape, jnp.bfloat16),
            pltpu.SemaphoreType.DMA((rows // ROW_CHUNK,)),
        ],
        compiler_params=params(),
        name="attend",
    )(lists, queries, k_own, v_own, *k_parts, *v_parts)


def last_kernel(
    lists_ref, q_ref, top_ref, both_ref, k_ref, v_ref, _, out_hbm, k_wide, v_wide, out_ref, sems, *, code, last
):
    kv_dev, rows_all, dim = q_ref.shape
    tokens = k_ref.shape[0] // kv_dev
    group = rows_all // tokens
    factor = dim ** (-0.5) * math.log2(math.e)

    @pl.when(has(listed_bits(lists_ref, code), last))
    def _add():
        k_wide[...] = k_ref[...].astype(jnp.float32)
        v_wide[...] = v_ref[...].astype(jnp.float32)
        k_ready = [by_head(k_wide, h, kv_dev, tokens) for h in range(kv_dev)]
        v_ready = [with_ones(by_head(v_wide, h, kv_dev, tokens)) for h in range(kv_dev)]
        jobs = chunks_of(kv_dev, rows_all)
        output = Output(out_ref, out_hbm, sems, kv_dev, group)
        shifts = []

        def score(job, _):
            h, first = job
            return scores_of(q_ref[h, pl.ds(first, ROW_CHUNK), :], k_ready[h])

        def weigh(job, s):
            h, first = job
            shifted = (s - top_ref[h, pl.ds(first, ROW_CHUNK), :]) * factor
            shifts.append(jnp.max(shifted.reshape(ROW_CHUNK // 8, 8, tokens), axis=0))
            return jnp.exp2(shifted).astype(jnp.bfloat16)

        def add_up(job, probs):
            h, first = job
            both = jnp.dot(probs, v_ready[h], preferred_element_type=jnp.float32)
            output.put(h, first, both + both_ref[h, pl.ds(first, ROW_CHUNK), :])

        in_turns([score, weigh, add_up], jobs)
        output.wait()

        @pl.when(jnp.max(functools.reduce(jnp.maximum, shifts)) > LARGEST)
        def _rescale():
            again = Output(out_ref, out_hbm, sems, kv_dev, group)
            for h, first in jobs:
                rows = pl.ds(first, ROW_CHUNK)
                s = scores_of(q_ref[h, rows, :], k_ready[h])
                before = top_ref[h, rows, :]
                top = jnp.maximum(before, jnp.max(s, axis=1, keepdims=True))
                probs = jnp.exp2((s - top) * factor).astype(jnp.bfloat16)
                shrink = jnp.exp2((before - top) * factor)
                both = both_ref[h, rows, :] * jnp.concatenate([shrink, shrink], axis=1)
                both += jnp.dot(probs, v_ready[h], preferred_element_type=jnp.float32)
                again.put(h, first, both)
            again.wait()


def attend_last(lists, queries, state, k_last, v_last, out, code, last):
    top, both = state
    hbm = pl.BlockSpec(memory_space=pltpu.HBM)
    return pl.pallas_call(
        functools.partial(last_kernel, code=code, last=last),
        out_shape=jax.ShapeDtypeStruct(out.shape, out.dtype),
        in_specs=[vmem()] * 6 + [hbm],
        out_specs=hbm,
        input_output_aliases={6: 0},
        scratch_shapes=[
            pltpu.VMEM(k_last.shape, jnp.float32),
            pltpu.VMEM(k_last.shape, jnp.float32),
            pltpu.VMEM(out.shape, jnp.bfloat16),
            pltpu.SemaphoreType.DMA((queries.shape[1] // ROW_CHUNK,)),
        ],
        compiler_params=params(),
        name="attend_last",
    )(lists, queries, top, both, k_last, v_last, out)


def ring_place(block, members):
    return jnp.where((block & 1) == 0, block >> 1, members - 1 - (block >> 1))


def ring_code(members):
    def code(block, target):
        ahead = ring_place(block, members) - ring_place(target, members)
        return jnp.where(ahead < 0, ahead + members, ahead)

    return code


LAST_KEYS = {1: 2, 2: 3, 3: 4, 4: 5, 5: 6, 6: 1}, {}
LAST_VALUES = {1: 6, 2: 5, 3: 1, 4: 3, 5: 2, 6: 4}, {2: 0, 4: 4, 5: 1, 6: 3}


def round_the_ring(k_own, v_own, ready, members):
    ring = list(range(0, members, 2)) + list(range(members - 1, 0, -2))
    cores = lax.axis_size("head")
    here = ring_place(lax.axis_index("seq").astype(jnp.int32), members)

    def send(x, turn):
        return lax.ppermute(x, "seq", [(ring[p], ring[(p + turn) % members]) for p in range(members)])

    def send_last(parts, plan):
        steps, whats = plan
        x = parts[-1]
        for place, what in whats.items():
            x = jnp.where(here == place, parts[what], x)
        pairs = []
        for p in range(members):
            for core in range(cores):
                to = (steps[p], core) if p in steps else (p, (core + 1) % cores)
                pairs.append((ring[p] * cores + core, ring[to[0]] * cores + to[1]))
        return lax.ppermute(x, ("seq", "head"), pairs)

    half = members // 2
    k_two, v_two, k_all, v_all = [k_own, k_own], [v_own, v_own], [], []
    for distance in range(1, half):
        ahead = send(k_two[0], 1), send(v_two[1], -1)
        if distance == 1:
            k_two[1], v_two[0], ready = lax.optimization_barrier((k_two[1], v_two[0], ready))
        behind = send(v_two[0], 1), send(k_two[1], -1)
        ahead = lax.optimization_barrier(ahead)
        behind = lax.optimization_barrier(behind)
        k_two, v_two = [ahead[0], behind[1]], [behind[0], ahead[1]]
        k_all += k_two
        v_all += v_two
    k_last = send_last(k_all[:-1], LAST_KEYS)
    v_last = send_last(v_all[:-2] + v_all[-1:], LAST_VALUES)
    return k_all, v_all, k_last, v_last, ready


def others(row, target):
    slots = row.shape[-1]
    own_at = jnp.argmax(row == target[..., None], axis=-1)
    j = jnp.arange(slots - 1)
    return jnp.where(j >= own_at[..., None], row[..., 1:], row[..., :-1])


def relay(k_own, v_own, chosen, members):
    block, dim = k_own.shape
    stacked = jnp.stack([k_own, v_own]).reshape(2, members, block // members, dim)
    shares = lax.all_to_all(stacked, "seq", split_axis=1, concat_axis=1, tiled=True)
    wanted = others(chosen, jnp.arange(members, dtype=jnp.int32))
    picked = jnp.take(shares, jnp.maximum(wanted, 0), axis=1)
    arrived = lax.all_to_all(picked, "seq", split_axis=1, concat_axis=3, tiled=True)
    count = wanted.shape[1]
    k_parts, v_parts = ([arrived[n, 0, j].reshape(block, dim) for j in range(count)] for n in range(2))
    return k_parts, v_parts, jnp.where(wanted < 0, -1, jnp.arange(count, dtype=jnp.int32))


def per_device(queries, keys, values, chosen):
    members = lax.axis_size("seq")
    tokens, kv_dev, dim = keys.shape
    k_own = keys.reshape(tokens * kv_dev, dim)
    v_own = values.reshape(tokens * kv_dev, dim)
    if members in ROUND:
        ready = prepare(chosen.T, queries, k_own, v_own, kv_dev)
        k_parts, v_parts, k_last, v_last, ready = round_the_ring(k_own, v_own, ready, members)
        lists, q_ready, k_ready, v_ready = ready
        half, code = members // 2, ring_code(members)
        codes = [turn for far in range(1, half) for turn in (members - far, far)]
        out, *state = attend(
            lists, q_ready, k_ready, v_ready, k_parts, v_parts, codes, code, half
        )
        return attend_last(lists, q_ready, state, k_last, v_last, out, code, half)

    k_parts, v_parts, mine = relay(k_own, v_own, chosen, members)
    lists, *ready = prepare(mine.T, queries, k_own, v_own, kv_dev)
    lists = jnp.concatenate([lists, jnp.full_like(lists[:1], -1)])
    codes = list(range(len(k_parts)))
    return attend(lists, *ready, k_parts, v_parts, codes, lambda block, _: block, None)[0]


def solution(mesh):
    rows = P(("groups", "seq"), "head", None)
    return jax.shard_map(
        per_device,
        mesh=mesh,
        in_specs=(rows, rows, rows, P("groups", None)),
        out_specs=rows,
        check_vma=False,
    )
```

```python
import functools
import math

import jax
import jax.numpy as jnp
from jax import lax
from jax.experimental import pallas as pl
from jax.experimental.pallas import tpu as pltpu
from jax.sharding import PartitionSpec as P

NO_KEY = -1e30
ROW_CHUNK = 128
LARGEST = 64.0
ROUND = (8,)


def params():
    return pltpu.CompilerParams(vmem_limit_bytes=16 * 2**20)


def vmem():
    return pl.BlockSpec(memory_space=pltpu.VMEM)


def prepare_kernel(
    lists_hbm, q_hbm, k_hbm, v_hbm, lists_out, q_out, k_out, v_out,
    q_ref, k_ref, v_ref, k_wide, v_wide, sems, *, kv_dev,
):
    whole = ((k_hbm, k_ref), (v_hbm, v_ref), (q_hbm, q_ref), (lists_hbm, lists_out))
    copies = [
        pltpu.make_async_copy(source, here, sems.at[n]) for n, (source, here) in enumerate(whole)
    ]
    for copy in copies:
        copy.start()
    tokens, heads, dim = q_ref.shape
    group = heads // kv_dev
    for copy, ref, wide, out in zip(copies, (k_ref, v_ref), (k_wide, v_wide), (k_out, v_out)):
        copy.wait()
        wide[...] = ref[...].astype(jnp.float32)
        for h in range(kv_dev):
            out[h] = wide[pl.ds(h, tokens, stride=kv_dev), :].astype(jnp.bfloat16)
    copies[2].wait()
    for h in range(kv_dev):
        q = q_ref[:, pl.ds(h * group, group), :].astype(jnp.float32)
        q_out[h] = q.reshape(tokens * group, dim).astype(jnp.bfloat16)
    copies[3].wait()


def prepare(lists, queries, k_own, v_own, kv_dev):
    tokens, heads, dim = queries.shape
    operands = [
        pltpu.with_memory_space_constraint(x, pltpu.HBM) for x in (lists, queries, k_own, v_own)
    ]
    by_head = jax.ShapeDtypeStruct((kv_dev, tokens, dim), jnp.bfloat16)
    return pl.pallas_call(
        functools.partial(prepare_kernel, kv_dev=kv_dev),
        out_shape=(
            jax.ShapeDtypeStruct(lists.shape, lists.dtype),
            jax.ShapeDtypeStruct((kv_dev, tokens * heads // kv_dev, dim), jnp.bfloat16),
            by_head,
            by_head,
        ),
        in_specs=[pl.BlockSpec(memory_space=pltpu.HBM)] * 4,
        out_specs=(vmem(), vmem(), vmem(), vmem()),
        scratch_shapes=[
            pltpu.VMEM(queries.shape, jnp.bfloat16),
            pltpu.VMEM(k_own.shape, jnp.bfloat16),
            pltpu.VMEM(k_own.shape, jnp.bfloat16),
            pltpu.VMEM(k_own.shape, jnp.float32),
            pltpu.VMEM(k_own.shape, jnp.float32),
            pltpu.SemaphoreType.DMA((4,)),
        ],
        compiler_params=params(),
        name="prepare",
    )(*operands)


def listed_bits(lists_ref, code):
    target = lax.axis_index("seq").astype(jnp.int32)
    entries = lists_ref[...]
    mine = lax.broadcasted_iota(jnp.int32, entries.shape, 1) == target
    bits = jnp.left_shift(1, code(jnp.maximum(entries, 0), target)).astype(jnp.float32)
    return jnp.sum(jnp.where(jnp.logical_and(mine, entries >= 0), bits, 0.0)).astype(jnp.int32)


def has(bits, code):
    return jnp.bitwise_and(lax.shift_right_logical(bits, jnp.int32(code)), 1) == 1


def by_head(wide, h, kv_dev, keys):
    return wide[pl.ds(h, keys, stride=kv_dev), :].astype(jnp.bfloat16)


def with_ones(values):
    return jnp.concatenate([values, jnp.ones_like(values)], axis=1)


class Once(dict):
    def __init__(self, make):
        super().__init__()
        self.make = make

    def __missing__(self, h):
        self[h] = self.make(h)
        return self[h]


class Output:
    def __init__(self, out_ref, out_hbm, sems, kv_dev, group):
        self.out_ref, self.out_hbm, self.sems = out_ref, out_hbm, sems
        self.kv_dev, self.group, self.copies, self.before = kv_dev, group, [], None

    def put(self, h, first, both):
        rows, dim = both.shape[0], both.shape[1] // 2
        merged = both[:, :dim] * pl.reciprocal(both[:, dim:])
        merged = merged.reshape(rows // self.group, self.group, dim)
        if h % 2 == 0:
            self.before = merged
            return
        here = pl.ds(first // self.group, rows // self.group)
        heads = pl.ds((h - 1) * self.group, 2 * self.group)
        two = jnp.concatenate([self.before, merged], axis=1)
        self.out_ref[here, heads, :] = two.astype(jnp.bfloat16)
        if h + 1 == self.kv_dev:
            self.copies.append(
                pltpu.make_async_copy(
                    self.out_ref.at[here], self.out_hbm.at[here], self.sems.at[len(self.copies)]
                )
            )
            self.copies[-1].start()

    def wait(self):
        for copy in self.copies:
            copy.wait()


def chunks_of(kv_dev, rows_all):
    return [(h, first) for first in range(0, rows_all, ROW_CHUNK) for h in range(kv_dev)]


def in_turns(stages, jobs):
    held = {}
    for turn in range(len(jobs) + len(stages) - 1):
        for n, stage in enumerate(stages):
            at = turn - n
            if 0 <= at < len(jobs):
                held[at] = stage(jobs[at], held.get(at))
        held.pop(turn - len(stages) + 1, None)


def scores_of(q, keys):
    return lax.dot_general(q, keys, (((1,), (1,)), ((), ())), preferred_element_type=jnp.float32)


def attend_kernel(lists_ref, q_ref, k_own_ref, v_own_ref, *refs, codes, code, last):
    parts = len(codes)
    k_parts, v_parts = refs[:parts], refs[parts : 2 * parts]
    out_hbm, *state, k_wide, v_wide, out_ref, sems = refs[2 * parts :]
    kv_dev, tokens, dim = k_own_ref.shape
    rows_all = q_ref.shape[1]
    group = rows_all // tokens
    block = tokens * kv_dev
    most = k_wide.shape[0] // block
    factor = dim ** (-0.5) * math.log2(math.e)

    bits = listed_bits(lists_ref, code)
    count = jnp.int32(0)
    for part_code, k_part, v_part in zip(codes, k_parts, v_parts):
        take = has(bits, part_code)

        @pl.when(take)
        def _take(k_part=k_part, v_part=v_part, count=count):
            rows = pl.ds(pl.multiple_of(count * block, block), block)
            k_wide[rows, :] = k_part[...].astype(jnp.float32)
            v_wide[rows, :] = v_part[...].astype(jnp.float32)

        count += take.astype(jnp.int32)

    def run(others, final):
        keys = (others + 1) * tokens
        output = Output(out_ref, out_hbm, sems, kv_dev, group)

        def keys_of(h):
            if not others:
                return k_own_ref[h]
            return jnp.concatenate([k_own_ref[h], by_head(k_wide, h, kv_dev, keys - tokens)], axis=0)

        def values_of(h):
            if not others:
                return with_ones(v_own_ref[h])
            rest = by_head(v_wide, h, kv_dev, keys - tokens)
            return with_ones(jnp.concatenate([v_own_ref[h], rest], axis=0))

        k_ready, v_ready = Once(keys_of), Once(values_of)
        past = lax.broadcasted_iota(jnp.int32, (ROW_CHUNK, tokens), 0)
        past -= group * lax.broadcasted_iota(jnp.int32, (ROW_CHUNK, tokens), 1)

        def score(job, _):
            h, first = job
            return scores_of(q_ref[h, pl.ds(first, ROW_CHUNK), :], k_ready[h])

        def weigh(job, s):
            first = job[1]
            scores = [jnp.where(past >= -first, s[:, :tokens], NO_KEY)]
            scores += [s[:, (j + 1) * tokens : (j + 2) * tokens] for j in range(others)]
            top = jnp.max(functools.reduce(jnp.maximum, scores), axis=1, keepdims=True)
            probs = [jnp.exp2((part - top) * factor).astype(jnp.bfloat16) for part in scores]
            return jnp.concatenate(probs, axis=1), top

        def add_up(job, weighed):
            h, first = job
            probs, top = weighed
            both = jnp.dot(probs, v_ready[h], preferred_element_type=jnp.float32)
            if final:
                output.put(h, first, both)
            else:
                rows = pl.ds(first, ROW_CHUNK)
                state[0][h, rows, :] = jnp.broadcast_to(top, (ROW_CHUNK, dim))
                state[1][h, rows, :] = both

        in_turns([score, weigh, add_up], chunks_of(kv_dev, rows_all))
        output.wait()

    unfinished = False if last is None else has(bits, last)
    for others in range(most + 1):

        @pl.when(jnp.logical_and(count == others, jnp.logical_not(unfinished)))
        def _whole(others=others):
            run(others, True)

        if last is not None and others < most:

            @pl.when(jnp.logical_and(count == others, unfinished))
            def _part(others=others):
                run(others, False)


def attend(lists, queries, k_own, v_own, k_parts, v_parts, codes, code, last):
    kv_dev, rows, dim = queries.shape
    tokens = k_own.shape[1]
    rest = (lists.shape[0] - 1) * tokens * kv_dev
    out = jax.ShapeDtypeStruct((tokens, rows * kv_dev // tokens, dim), jnp.bfloat16)
    state = [] if last is None else [
        jax.ShapeDtypeStruct((kv_dev, rows, wide), jnp.float32) for wide in (dim, 2 * dim)
    ]
    hbm = pl.BlockSpec(memory_space=pltpu.HBM)
    return pl.pallas_call(
        functools.partial(attend_kernel, codes=codes, code=code, last=last),
        out_shape=(out, *state),
        in_specs=[vmem()] * (4 + 2 * len(k_parts)),
        out_specs=(hbm, *(vmem() for _ in state)),
        scratch_shapes=[
            pltpu.VMEM((rest, dim), jnp.float32),
            pltpu.VMEM((rest, dim), jnp.float32),
            pltpu.VMEM(out.shape, jnp.bfloat16),
            pltpu.SemaphoreType.DMA((rows // ROW_CHUNK,)),
        ],
        compiler_params=params(),
        name="attend",
    )(lists, queries, k_own, v_own, *k_parts, *v_parts)


def last_kernel(
    lists_ref, q_ref, top_ref, both_ref, k_ref, v_ref, _, out_hbm, k_wide, v_wide, out_ref, sems, *, code, last
):
    kv_dev, rows_all, dim = q_ref.shape
    tokens = k_ref.shape[0] // kv_dev
    group = rows_all // tokens
    factor = dim ** (-0.5) * math.log2(math.e)

    @pl.when(has(listed_bits(lists_ref, code), last))
    def _add():
        k_wide[...] = k_ref[...].astype(jnp.float32)
        v_wide[...] = v_ref[...].astype(jnp.float32)
        k_ready = Once(lambda h: by_head(k_wide, h, kv_dev, tokens))
        v_ready = Once(lambda h: with_ones(by_head(v_wide, h, kv_dev, tokens)))
        jobs = chunks_of(kv_dev, rows_all)
        output = Output(out_ref, out_hbm, sems, kv_dev, group)
        shifts = []

        def score(job, _):
            h, first = job
            return scores_of(q_ref[h, pl.ds(first, ROW_CHUNK), :], k_ready[h])

        def weigh(job, s):
            h, first = job
            shifted = (s - top_ref[h, pl.ds(first, ROW_CHUNK), :]) * factor
            shifts.append(jnp.max(shifted.reshape(ROW_CHUNK // 8, 8, tokens), axis=0))
            return jnp.exp2(shifted).astype(jnp.bfloat16)

        def add_up(job, probs):
            h, first = job
            both = jnp.dot(probs, v_ready[h], preferred_element_type=jnp.float32)
            output.put(h, first, both + both_ref[h, pl.ds(first, ROW_CHUNK), :])

        in_turns([score, weigh, add_up], jobs)
        output.wait()

        @pl.when(jnp.max(functools.reduce(jnp.maximum, shifts)) > LARGEST)
        def _rescale():
            again = Output(out_ref, out_hbm, sems, kv_dev, group)
            for h, first in jobs:
                rows = pl.ds(first, ROW_CHUNK)
                s = scores_of(q_ref[h, rows, :], k_ready[h])
                before = top_ref[h, rows, :]
                top = jnp.maximum(before, jnp.max(s, axis=1, keepdims=True))
                probs = jnp.exp2((s - top) * factor).astype(jnp.bfloat16)
                shrink = jnp.exp2((before - top) * factor)
                both = both_ref[h, rows, :] * jnp.concatenate([shrink, shrink], axis=1)
                both += jnp.dot(probs, v_ready[h], preferred_element_type=jnp.float32)
                again.put(h, first, both)
            again.wait()


def attend_last(lists, queries, state, k_last, v_last, out, code, last):
    top, both = state
    hbm = pl.BlockSpec(memory_space=pltpu.HBM)
    return pl.pallas_call(
        functools.partial(last_kernel, code=code, last=last),
        out_shape=jax.ShapeDtypeStruct(out.shape, out.dtype),
        in_specs=[vmem()] * 6 + [hbm],
        out_specs=hbm,
        input_output_aliases={6: 0},
        scratch_shapes=[
            pltpu.VMEM(k_last.shape, jnp.float32),
            pltpu.VMEM(k_last.shape, jnp.float32),
            pltpu.VMEM(out.shape, jnp.bfloat16),
            pltpu.SemaphoreType.DMA((queries.shape[1] // ROW_CHUNK,)),
        ],
        compiler_params=params(),
        name="attend_last",
    )(lists, queries, top, both, k_last, v_last, out)


def ring_place(block, members):
    return jnp.where((block & 1) == 0, block >> 1, members - 1 - (block >> 1))


def ring_code(members):
    def code(block, target):
        ahead = ring_place(block, members) - ring_place(target, members)
        return jnp.where(ahead < 0, ahead + members, ahead)

    return code


LAST_KEYS = {1: 2, 2: 3, 3: 4, 4: 5, 5: 6, 6: 1}, {}
LAST_VALUES = {1: 6, 2: 5, 3: 1, 4: 3, 5: 2, 6: 4}, {2: 0, 4: 4, 5: 1, 6: 3}


def round_the_ring(k_own, v_own, ready, members):
    ring = list(range(0, members, 2)) + list(range(members - 1, 0, -2))
    cores = lax.axis_size("head")
    here = ring_place(lax.axis_index("seq").astype(jnp.int32), members)

    def send(x, turn):
        return lax.ppermute(x, "seq", [(ring[p], ring[(p + turn) % members]) for p in range(members)])

    def send_last(parts, plan):
        steps, whats = plan
        x = parts[-1]
        for place, what in whats.items():
            x = jnp.where(here == place, parts[what], x)
        pairs = []
        for p in range(members):
            for core in range(cores):
                to = (steps[p], core) if p in steps else (p, (core + 1) % cores)
                pairs.append((ring[p] * cores + core, ring[to[0]] * cores + to[1]))
        return lax.ppermute(x, ("seq", "head"), pairs)

    half = members // 2
    k_two, v_two, k_all, v_all = [k_own, k_own], [v_own, v_own], [], []
    for distance in range(1, half):
        ahead = send(k_two[0], 1), send(v_two[1], -1)
        if distance == 1:
            k_two[1], v_two[0], ready = lax.optimization_barrier((k_two[1], v_two[0], ready))
        behind = send(v_two[0], 1), send(k_two[1], -1)
        ahead = lax.optimization_barrier(ahead)
        behind = lax.optimization_barrier(behind)
        k_two, v_two = [ahead[0], behind[1]], [behind[0], ahead[1]]
        k_all += k_two
        v_all += v_two
    k_last = send_last(k_all[:-1], LAST_KEYS)
    v_last = send_last(v_all[:-2] + v_all[-1:], LAST_VALUES)
    return k_all, v_all, k_last, v_last, ready


def others(row, target):
    slots = row.shape[-1]
    own_at = jnp.argmax(row == target[..., None], axis=-1)
    j = jnp.arange(slots - 1)
    return jnp.where(j >= own_at[..., None], row[..., 1:], row[..., :-1])


def relay(k_own, v_own, chosen, members):
    block, dim = k_own.shape
    stacked = jnp.stack([k_own, v_own]).reshape(2, members, block // members, dim)
    shares = lax.all_to_all(stacked, "seq", split_axis=1, concat_axis=1, tiled=True)
    wanted = others(chosen, jnp.arange(members, dtype=jnp.int32))
    picked = jnp.take(shares, jnp.maximum(wanted, 0), axis=1)
    arrived = lax.all_to_all(picked, "seq", split_axis=1, concat_axis=3, tiled=True)
    count = wanted.shape[1]
    k_parts, v_parts = ([arrived[n, 0, j].reshape(block, dim) for j in range(count)] for n in range(2))
    return k_parts, v_parts, jnp.where(wanted < 0, -1, jnp.arange(count, dtype=jnp.int32))


def per_device(queries, keys, values, chosen):
    members = lax.axis_size("seq")
    tokens, kv_dev, dim = keys.shape
    k_own = keys.reshape(tokens * kv_dev, dim)
    v_own = values.reshape(tokens * kv_dev, dim)
    if members in ROUND:
        ready = prepare(chosen.T, queries, k_own, v_own, kv_dev)
        k_parts, v_parts, k_last, v_last, ready = round_the_ring(k_own, v_own, ready, members)
        lists, q_ready, k_ready, v_ready = ready
        half, code = members // 2, ring_code(members)
        codes = [turn for far in range(1, half) for turn in (members - far, far)]
        out, *state = attend(
            lists, q_ready, k_ready, v_ready, k_parts, v_parts, codes, code, half
        )
        return attend_last(lists, q_ready, state, k_last, v_last, out, code, half)

    k_parts, v_parts, mine = relay(k_own, v_own, chosen, members)
    lists, *ready = prepare(mine.T, queries, k_own, v_own, kv_dev)
    lists = jnp.concatenate([lists, jnp.full_like(lists[:1], -1)])
    codes = list(range(len(k_parts)))
    return attend(lists, *ready, k_parts, v_parts, codes, lambda block, _: block, None)[0]


def solution(mesh):
    rows = P(("groups", "seq"), "head", None)
    return jax.shard_map(
        per_device,
        mesh=mesh,
        in_specs=(rows, rows, rows, P("groups", None)),
        out_specs=rows,
        check_vma=False,
    )
```

```python
import functools
import math

import jax
import jax.numpy as jnp
from jax import lax
from jax.experimental import pallas as pl
from jax.experimental.pallas import tpu as pltpu
from jax.sharding import PartitionSpec as P

NO_KEY = -1e30
LARGEST = 64.0
ROUND = (8,)


def params():
    return pltpu.CompilerParams(vmem_limit_bytes=16 * 2**20)


def vmem():
    return pl.BlockSpec(memory_space=pltpu.VMEM)


def prepare_kernel(
    lists_hbm, q_hbm, k_hbm, v_hbm, lists_out, q_out, k_out, v_out,
    q_ref, k_ref, v_ref, k_wide, v_wide, sems, *, kv_dev,
):
    whole = ((k_hbm, k_ref), (v_hbm, v_ref), (q_hbm, q_ref), (lists_hbm, lists_out))
    copies = [
        pltpu.make_async_copy(source, here, sems.at[n]) for n, (source, here) in enumerate(whole)
    ]
    for copy in copies:
        copy.start()
    tokens, heads, dim = q_ref.shape
    group = heads // kv_dev
    for copy, ref, wide, out in zip(copies, (k_ref, v_ref), (k_wide, v_wide), (k_out, v_out)):
        copy.wait()
        wide[...] = ref[...].astype(jnp.float32)
        for h in range(kv_dev):
            out[h] = wide[pl.ds(h, tokens, stride=kv_dev), :].astype(jnp.bfloat16)
    copies[2].wait()
    for h in range(kv_dev):
        q = q_ref[:, pl.ds(h * group, group), :].astype(jnp.float32)
        q_out[h] = q.reshape(tokens * group, dim).astype(jnp.bfloat16)
    copies[3].wait()


def prepare(lists, queries, k_own, v_own, kv_dev):
    tokens, heads, dim = queries.shape
    operands = [
        pltpu.with_memory_space_constraint(x, pltpu.HBM) for x in (lists, queries, k_own, v_own)
    ]
    by_head = jax.ShapeDtypeStruct((kv_dev, tokens, dim), jnp.bfloat16)
    return pl.pallas_call(
        functools.partial(prepare_kernel, kv_dev=kv_dev),
        out_shape=(
            jax.ShapeDtypeStruct(lists.shape, lists.dtype),
            jax.ShapeDtypeStruct((kv_dev, tokens * heads // kv_dev, dim), jnp.bfloat16),
            by_head,
            by_head,
        ),
        in_specs=[pl.BlockSpec(memory_space=pltpu.HBM)] * 4,
        out_specs=(vmem(), vmem(), vmem(), vmem()),
        scratch_shapes=[
            pltpu.VMEM(queries.shape, jnp.bfloat16),
            pltpu.VMEM(k_own.shape, jnp.bfloat16),
            pltpu.VMEM(k_own.shape, jnp.bfloat16),
            pltpu.VMEM(k_own.shape, jnp.float32),
            pltpu.VMEM(k_own.shape, jnp.float32),
            pltpu.SemaphoreType.DMA((4,)),
        ],
        compiler_params=params(),
        name="prepare",
    )(*operands)


def listed_bits(lists_ref, code):
    target = lax.axis_index("seq").astype(jnp.int32)
    entries = lists_ref[...]
    mine = lax.broadcasted_iota(jnp.int32, entries.shape, 1) == target
    bits = jnp.left_shift(1, code(jnp.maximum(entries, 0), target)).astype(jnp.float32)
    return jnp.sum(jnp.where(jnp.logical_and(mine, entries >= 0), bits, 0.0)).astype(jnp.int32)


def has(bits, code):
    return jnp.bitwise_and(lax.shift_right_logical(bits, jnp.int32(code)), 1) == 1


def by_head(wide, h, kv_dev, keys):
    return wide[pl.ds(h, keys, stride=kv_dev), :].astype(jnp.bfloat16)


def with_ones(values):
    return jnp.concatenate([values, jnp.ones_like(values)], axis=1)


class Once(dict):
    def __init__(self, make):
        super().__init__()
        self.make = make

    def __missing__(self, h):
        self[h] = self.make(h)
        return self[h]


class Output:
    def __init__(self, out_ref, out_hbm, sems, kv_dev, group):
        self.out_ref, self.out_hbm, self.sems = out_ref, out_hbm, sems
        self.kv_dev, self.group, self.copies, self.before = kv_dev, group, [], None

    def put(self, h, first, both):
        rows, dim = both.shape[0], both.shape[1] // 2
        merged = both[:, :dim] * pl.reciprocal(both[:, dim:])
        merged = merged.reshape(rows // self.group, self.group, dim)
        if h % 2 == 0:
            self.before = merged
            return
        here = pl.ds(first // self.group, rows // self.group)
        heads = pl.ds((h - 1) * self.group, 2 * self.group)
        two = jnp.concatenate([self.before, merged], axis=1)
        self.out_ref[here, heads, :] = two.astype(jnp.bfloat16)
        if h + 1 == self.kv_dev:
            self.copies.append(
                pltpu.make_async_copy(
                    self.out_ref.at[here], self.out_hbm.at[here], self.sems.at[len(self.copies)]
                )
            )
            self.copies[-1].start()

    def wait(self):
        for copy in self.copies:
            copy.wait()


def row_chunk(blocks):
    return 512 if blocks % 2 else 256


def chunks_of(kv_dev, rows_all, chunk):
    return [(h, first) for first in range(0, rows_all, chunk) for h in range(kv_dev)]


def in_turns(stages, jobs):
    held = {}
    for turn in range(len(jobs) + len(stages) - 1):
        for n, stage in enumerate(stages):
            at = turn - n
            if 0 <= at < len(jobs):
                held[at] = stage(jobs[at], held.get(at))
        held.pop(turn - len(stages) + 1, None)


def scores_of(q, keys):
    return lax.dot_general(q, keys, (((1,), (1,)), ((), ())), preferred_element_type=jnp.float32)


def attend_kernel(lists_ref, q_ref, k_own_ref, v_own_ref, *refs, codes, code, last):
    parts = len(codes)
    k_parts, v_parts = refs[:parts], refs[parts : 2 * parts]
    out_hbm, *state, k_wide, v_wide, out_ref, sems = refs[2 * parts :]
    kv_dev, tokens, dim = k_own_ref.shape
    rows_all = q_ref.shape[1]
    group = rows_all // tokens
    block = tokens * kv_dev
    most = k_wide.shape[0] // block
    factor = dim ** (-0.5) * math.log2(math.e)

    bits = listed_bits(lists_ref, code)
    count = jnp.int32(0)
    for part_code, k_part, v_part in zip(codes, k_parts, v_parts):
        take = has(bits, part_code)

        @pl.when(take)
        def _take(k_part=k_part, v_part=v_part, count=count):
            rows = pl.ds(pl.multiple_of(count * block, block), block)
            k_wide[rows, :] = k_part[...].astype(jnp.float32)
            v_wide[rows, :] = v_part[...].astype(jnp.float32)

        count += take.astype(jnp.int32)

    def run(others, final):
        keys = (others + 1) * tokens
        chunk = row_chunk(others + 1)
        output = Output(out_ref, out_hbm, sems, kv_dev, group)

        def keys_of(h):
            if not others:
                return k_own_ref[h]
            return jnp.concatenate([k_own_ref[h], by_head(k_wide, h, kv_dev, keys - tokens)], axis=0)

        def values_of(h):
            if not others:
                return with_ones(v_own_ref[h])
            rest = by_head(v_wide, h, kv_dev, keys - tokens)
            return with_ones(jnp.concatenate([v_own_ref[h], rest], axis=0))

        k_ready, v_ready = Once(keys_of), Once(values_of)
        past = lax.broadcasted_iota(jnp.int32, (chunk, tokens), 0)
        past -= group * lax.broadcasted_iota(jnp.int32, (chunk, tokens), 1)

        def score(job, _):
            h, first = job
            return scores_of(q_ref[h, pl.ds(first, chunk), :], k_ready[h])

        def weigh(job, s):
            first = job[1]
            scores = [jnp.where(past >= -first, s[:, :tokens], NO_KEY)]
            scores += [s[:, (j + 1) * tokens : (j + 2) * tokens] for j in range(others)]
            top = jnp.max(functools.reduce(jnp.maximum, scores), axis=1, keepdims=True)
            probs = [jnp.exp2((part - top) * factor).astype(jnp.bfloat16) for part in scores]
            return jnp.concatenate(probs, axis=1), top

        def add_up(job, weighed):
            h, first = job
            probs, top = weighed
            both = jnp.dot(probs, v_ready[h], preferred_element_type=jnp.float32)
            if final:
                output.put(h, first, both)
            else:
                rows = pl.ds(first, chunk)
                state[0][h, rows, :] = jnp.broadcast_to(top, (chunk, dim))
                state[1][h, rows, :] = both

        in_turns([score, weigh, add_up], chunks_of(kv_dev, rows_all, chunk))
        output.wait()

    unfinished = False if last is None else has(bits, last)
    for others in range(most + 1):

        @pl.when(jnp.logical_and(count == others, jnp.logical_not(unfinished)))
        def _whole(others=others):
            run(others, True)

        if last is not None and others < most:

            @pl.when(jnp.logical_and(count == others, unfinished))
            def _part(others=others):
                run(others, False)


def attend(lists, queries, k_own, v_own, k_parts, v_parts, codes, code, last):
    kv_dev, rows, dim = queries.shape
    tokens = k_own.shape[1]
    rest = (lists.shape[0] - 1) * tokens * kv_dev
    out = jax.ShapeDtypeStruct((tokens, rows * kv_dev // tokens, dim), jnp.bfloat16)
    state = [] if last is None else [
        jax.ShapeDtypeStruct((kv_dev, rows, wide), jnp.float32) for wide in (dim, 2 * dim)
    ]
    hbm = pl.BlockSpec(memory_space=pltpu.HBM)
    return pl.pallas_call(
        functools.partial(attend_kernel, codes=codes, code=code, last=last),
        out_shape=(out, *state),
        in_specs=[vmem()] * (4 + 2 * len(k_parts)),
        out_specs=(hbm, *(vmem() for _ in state)),
        scratch_shapes=[
            pltpu.VMEM((rest, dim), jnp.float32),
            pltpu.VMEM((rest, dim), jnp.float32),
            pltpu.VMEM(out.shape, jnp.bfloat16),
            pltpu.SemaphoreType.DMA((rows // row_chunk(0),)),
        ],
        compiler_params=params(),
        name="attend",
    )(lists, queries, k_own, v_own, *k_parts, *v_parts)


def last_kernel(
    lists_ref, q_ref, top_ref, both_ref, k_ref, v_ref, _, out_hbm, k_wide, v_wide, out_ref, sems, *, code, last
):
    kv_dev, rows_all, dim = q_ref.shape
    tokens = k_ref.shape[0] // kv_dev
    group = rows_all // tokens
    factor = dim ** (-0.5) * math.log2(math.e)

    @pl.when(has(listed_bits(lists_ref, code), last))
    def _add():
        k_wide[...] = k_ref[...].astype(jnp.float32)
        v_wide[...] = v_ref[...].astype(jnp.float32)
        k_ready = Once(lambda h: by_head(k_wide, h, kv_dev, tokens))
        v_ready = Once(lambda h: with_ones(by_head(v_wide, h, kv_dev, tokens)))
        chunk = row_chunk(1)
        jobs = chunks_of(kv_dev, rows_all, chunk)
        output = Output(out_ref, out_hbm, sems, kv_dev, group)
        shifts = []

        def score(job, _):
            h, first = job
            return scores_of(q_ref[h, pl.ds(first, chunk), :], k_ready[h])

        def weigh(job, s):
            h, first = job
            shifted = (s - top_ref[h, pl.ds(first, chunk), :]) * factor
            shifts.append(jnp.max(shifted.reshape(chunk // 8, 8, tokens), axis=0))
            return jnp.exp2(shifted).astype(jnp.bfloat16)

        def add_up(job, probs):
            h, first = job
            both = jnp.dot(probs, v_ready[h], preferred_element_type=jnp.float32)
            output.put(h, first, both + both_ref[h, pl.ds(first, chunk), :])

        in_turns([score, weigh, add_up], jobs)
        output.wait()

        @pl.when(jnp.max(functools.reduce(jnp.maximum, shifts)) > LARGEST)
        def _rescale():
            again = Output(out_ref, out_hbm, sems, kv_dev, group)
            for h, first in jobs:
                rows = pl.ds(first, chunk)
                s = scores_of(q_ref[h, rows, :], k_ready[h])
                before = top_ref[h, rows, :]
                top = jnp.maximum(before, jnp.max(s, axis=1, keepdims=True))
                probs = jnp.exp2((s - top) * factor).astype(jnp.bfloat16)
                shrink = jnp.exp2((before - top) * factor)
                both = both_ref[h, rows, :] * jnp.concatenate([shrink, shrink], axis=1)
                both += jnp.dot(probs, v_ready[h], preferred_element_type=jnp.float32)
                again.put(h, first, both)
            again.wait()


def attend_last(lists, queries, state, k_last, v_last, out, code, last):
    top, both = state
    hbm = pl.BlockSpec(memory_space=pltpu.HBM)
    return pl.pallas_call(
        functools.partial(last_kernel, code=code, last=last),
        out_shape=jax.ShapeDtypeStruct(out.shape, out.dtype),
        in_specs=[vmem()] * 6 + [hbm],
        out_specs=hbm,
        input_output_aliases={6: 0},
        scratch_shapes=[
            pltpu.VMEM(k_last.shape, jnp.float32),
            pltpu.VMEM(k_last.shape, jnp.float32),
            pltpu.VMEM(out.shape, jnp.bfloat16),
            pltpu.SemaphoreType.DMA((queries.shape[1] // row_chunk(0),)),
        ],
        compiler_params=params(),
        name="attend_last",
    )(lists, queries, top, both, k_last, v_last, out)


def ring_place(block, members):
    return jnp.where((block & 1) == 0, block >> 1, members - 1 - (block >> 1))


def ring_code(members):
    def code(block, target):
        ahead = ring_place(block, members) - ring_place(target, members)
        return jnp.where(ahead < 0, ahead + members, ahead)

    return code


LAST_KEYS = {1: 2, 2: 3, 3: 4, 4: 5, 5: 6, 6: 1}, {}
LAST_VALUES = {1: 6, 2: 5, 3: 1, 4: 3, 5: 2, 6: 4}, {2: 0, 4: 4, 5: 1, 6: 3}


def round_the_ring(k_own, v_own, ready, members):
    ring = list(range(0, members, 2)) + list(range(members - 1, 0, -2))
    cores = lax.axis_size("head")
    here = ring_place(lax.axis_index("seq").astype(jnp.int32), members)

    def send(x, turn):
        return lax.ppermute(x, "seq", [(ring[p], ring[(p + turn) % members]) for p in range(members)])

    def send_last(parts, plan):
        steps, whats = plan
        x = parts[-1]
        for place, what in whats.items():
            x = jnp.where(here == place, parts[what], x)
        pairs = []
        for p in range(members):
            for core in range(cores):
                to = (steps[p], core) if p in steps else (p, (core + 1) % cores)
                pairs.append((ring[p] * cores + core, ring[to[0]] * cores + to[1]))
        return lax.ppermute(x, ("seq", "head"), pairs)

    half = members // 2
    k_two, v_two, k_all, v_all = [k_own, k_own], [v_own, v_own], [], []
    for distance in range(1, half):
        ahead = send(k_two[0], 1), send(v_two[1], -1)
        if distance == 1:
            k_two[1], v_two[0], ready = lax.optimization_barrier((k_two[1], v_two[0], ready))
        behind = send(v_two[0], 1), send(k_two[1], -1)
        ahead = lax.optimization_barrier(ahead)
        behind = lax.optimization_barrier(behind)
        k_two, v_two = [ahead[0], behind[1]], [behind[0], ahead[1]]
        k_all += k_two
        v_all += v_two
    k_last = send_last(k_all[:-1], LAST_KEYS)
    v_last = send_last(v_all[:-2] + v_all[-1:], LAST_VALUES)
    return k_all, v_all, k_last, v_last, ready


def others(row, target):
    slots = row.shape[-1]
    own_at = jnp.argmax(row == target[..., None], axis=-1)
    j = jnp.arange(slots - 1)
    return jnp.where(j >= own_at[..., None], row[..., 1:], row[..., :-1])


def relay(k_own, v_own, chosen, members):
    block, dim = k_own.shape
    stacked = jnp.stack([k_own, v_own]).reshape(2, members, block // members, dim)
    shares = lax.all_to_all(stacked, "seq", split_axis=1, concat_axis=1, tiled=True)
    wanted = others(chosen, jnp.arange(members, dtype=jnp.int32))
    picked = jnp.take(shares, jnp.maximum(wanted, 0), axis=1)
    arrived = lax.all_to_all(picked, "seq", split_axis=1, concat_axis=3, tiled=True)
    count = wanted.shape[1]
    k_parts, v_parts = ([arrived[n, 0, j].reshape(block, dim) for j in range(count)] for n in range(2))
    return k_parts, v_parts, jnp.where(wanted < 0, -1, jnp.arange(count, dtype=jnp.int32))


def per_device(queries, keys, values, chosen):
    members = lax.axis_size("seq")
    tokens, kv_dev, dim = keys.shape
    k_own = keys.reshape(tokens * kv_dev, dim)
    v_own = values.reshape(tokens * kv_dev, dim)
    if members in ROUND:
        ready = prepare(chosen.T, queries, k_own, v_own, kv_dev)
        k_parts, v_parts, k_last, v_last, ready = round_the_ring(k_own, v_own, ready, members)
        lists, q_ready, k_ready, v_ready = ready
        half, code = members // 2, ring_code(members)
        codes = [turn for far in range(1, half) for turn in (members - far, far)]
        out, *state = attend(
            lists, q_ready, k_ready, v_ready, k_parts, v_parts, codes, code, half
        )
        return attend_last(lists, q_ready, state, k_last, v_last, out, code, half)

    k_parts, v_parts, mine = relay(k_own, v_own, chosen, members)
    lists, *ready = prepare(mine.T, queries, k_own, v_own, kv_dev)
    lists = jnp.concatenate([lists, jnp.full_like(lists[:1], -1)])
    codes = list(range(len(k_parts)))
    return attend(lists, *ready, k_parts, v_parts, codes, lambda block, _: block, None)[0]


def solution(mesh):
    rows = P(("groups", "seq"), "head", None)
    return jax.shard_map(
        per_device,
        mesh=mesh,
        in_specs=(rows, rows, rows, P("groups", None)),
        out_specs=rows,
        check_vma=False,
    )
```

```python
import functools
import math

import jax
import jax.numpy as jnp
from jax import lax
from jax.experimental import pallas as pl
from jax.experimental.pallas import tpu as pltpu
from jax.sharding import PartitionSpec as P

NO_KEY = -1e30
ROW_CHUNK = 256
LARGEST = 64.0
ROUND = (8,)


def params():
    return pltpu.CompilerParams(vmem_limit_bytes=16 * 2**20)


def vmem():
    return pl.BlockSpec(memory_space=pltpu.VMEM)


def prepare_kernel(
    lists_hbm, q_hbm, k_hbm, v_hbm, lists_out, q_out, k_out, v_out,
    q_ref, k_ref, v_ref, k_wide, v_wide, sems, *, kv_dev,
):
    whole = ((k_hbm, k_ref), (v_hbm, v_ref), (q_hbm, q_ref), (lists_hbm, lists_out))
    copies = [
        pltpu.make_async_copy(source, here, sems.at[n]) for n, (source, here) in enumerate(whole)
    ]
    for copy in copies:
        copy.start()
    tokens, heads, dim = q_ref.shape
    group = heads // kv_dev
    for copy, ref, wide, out in zip(copies, (k_ref, v_ref), (k_wide, v_wide), (k_out, v_out)):
        copy.wait()
        wide[...] = ref[...].astype(jnp.float32)
        for h in range(kv_dev):
            out[h] = wide[pl.ds(h, tokens, stride=kv_dev), :].astype(jnp.bfloat16)
    copies[2].wait()
    for h in range(kv_dev):
        q = q_ref[:, pl.ds(h * group, group), :].astype(jnp.float32)
        q_out[h] = q.reshape(tokens * group, dim).astype(jnp.bfloat16)
    copies[3].wait()


def prepare(lists, queries, k_own, v_own, kv_dev):
    tokens, heads, dim = queries.shape
    operands = [
        pltpu.with_memory_space_constraint(x, pltpu.HBM) for x in (lists, queries, k_own, v_own)
    ]
    by_head = jax.ShapeDtypeStruct((kv_dev, tokens, dim), jnp.bfloat16)
    return pl.pallas_call(
        functools.partial(prepare_kernel, kv_dev=kv_dev),
        out_shape=(
            jax.ShapeDtypeStruct(lists.shape, lists.dtype),
            jax.ShapeDtypeStruct((kv_dev, tokens * heads // kv_dev, dim), jnp.bfloat16),
            by_head,
            by_head,
        ),
        in_specs=[pl.BlockSpec(memory_space=pltpu.HBM)] * 4,
        out_specs=(vmem(), vmem(), vmem(), vmem()),
        scratch_shapes=[
            pltpu.VMEM(queries.shape, jnp.bfloat16),
            pltpu.VMEM(k_own.shape, jnp.bfloat16),
            pltpu.VMEM(k_own.shape, jnp.bfloat16),
            pltpu.VMEM(k_own.shape, jnp.float32),
            pltpu.VMEM(k_own.shape, jnp.float32),
            pltpu.SemaphoreType.DMA((4,)),
        ],
        compiler_params=params(),
        name="prepare",
    )(*operands)


def listed_bits(lists_ref, code):
    target = lax.axis_index("seq").astype(jnp.int32)
    entries = lists_ref[...]
    mine = lax.broadcasted_iota(jnp.int32, entries.shape, 1) == target
    bits = jnp.left_shift(1, code(jnp.maximum(entries, 0), target)).astype(jnp.float32)
    return jnp.sum(jnp.where(jnp.logical_and(mine, entries >= 0), bits, 0.0)).astype(jnp.int32)


def has(bits, code):
    return jnp.bitwise_and(lax.shift_right_logical(bits, jnp.int32(code)), 1) == 1


def by_head(wide, h, kv_dev, keys):
    return wide[pl.ds(h, keys, stride=kv_dev), :].astype(jnp.bfloat16)


def with_ones(values):
    return jnp.concatenate([values, jnp.ones_like(values)], axis=1)


class Output:
    def __init__(self, out_ref, out_hbm, sems, kv_dev, group):
        self.out_ref, self.out_hbm, self.sems = out_ref, out_hbm, sems
        self.kv_dev, self.group, self.copies, self.before = kv_dev, group, [], None

    def put(self, h, first, both):
        rows, dim = both.shape[0], both.shape[1] // 2
        merged = both[:, :dim] * pl.reciprocal(both[:, dim:])
        merged = merged.reshape(rows // self.group, self.group, dim)
        if h % 2 == 0:
            self.before = merged
            return
        here = pl.ds(first // self.group, rows // self.group)
        heads = pl.ds((h - 1) * self.group, 2 * self.group)
        two = jnp.concatenate([self.before, merged], axis=1)
        self.out_ref[here, heads, :] = two.astype(jnp.bfloat16)
        if h + 1 == self.kv_dev:
            self.copies.append(
                pltpu.make_async_copy(
                    self.out_ref.at[here], self.out_hbm.at[here], self.sems.at[len(self.copies)]
                )
            )
            self.copies[-1].start()

    def wait(self):
        for copy in self.copies:
            copy.wait()


def chunks_of(kv_dev, rows_all):
    return [(h, first) for first in range(0, rows_all, ROW_CHUNK) for h in range(kv_dev)]


def in_turns(stages, jobs):
    held = {}
    for turn in range(len(jobs) + len(stages) - 1):
        for n, stage in enumerate(stages):
            at = turn - n
            if 0 <= at < len(jobs):
                held[at] = stage(jobs[at], held.get(at))
        held.pop(turn - len(stages) + 1, None)


def scores_of(q, keys):
    return lax.dot_general(q, keys, (((1,), (1,)), ((), ())), preferred_element_type=jnp.float32)


def attend_kernel(lists_ref, q_ref, k_own_ref, v_own_ref, *refs, codes, code, last):
    parts = len(codes)
    k_parts, v_parts = refs[:parts], refs[parts : 2 * parts]
    out_hbm, *state, k_wide, v_wide, out_ref, sems = refs[2 * parts :]
    kv_dev, tokens, dim = k_own_ref.shape
    rows_all = q_ref.shape[1]
    group = rows_all // tokens
    block = tokens * kv_dev
    most = k_wide.shape[0] // block
    factor = dim ** (-0.5) * math.log2(math.e)

    bits = listed_bits(lists_ref, code)
    count = jnp.int32(0)
    for part_code, k_part, v_part in zip(codes, k_parts, v_parts):
        take = has(bits, part_code)

        @pl.when(take)
        def _take(k_part=k_part, v_part=v_part, count=count):
            rows = pl.ds(pl.multiple_of(count * block, block), block)
            k_wide[rows, :] = k_part[...].astype(jnp.float32)
            v_wide[rows, :] = v_part[...].astype(jnp.float32)

        count += take.astype(jnp.int32)

    def run(others, final):
        keys = (others + 1) * tokens
        output = Output(out_ref, out_hbm, sems, kv_dev, group)
        k_ready, v_ready = [], []
        for h in range(kv_dev):
            k_h, v_h = k_own_ref[h], v_own_ref[h]
            if others:
                k_h = jnp.concatenate([k_h, by_head(k_wide, h, kv_dev, keys - tokens)], axis=0)
                v_h = jnp.concatenate([v_h, by_head(v_wide, h, kv_dev, keys - tokens)], axis=0)
            k_ready.append(k_h)
            v_ready.append(with_ones(v_h))

        past = lax.broadcasted_iota(jnp.int32, (ROW_CHUNK, tokens), 0)
        past -= group * lax.broadcasted_iota(jnp.int32, (ROW_CHUNK, tokens), 1)

        def score(job, _):
            h, first = job
            return scores_of(q_ref[h, pl.ds(first, ROW_CHUNK), :], k_ready[h])

        def weigh(job, s):
            first = job[1]
            scores = [jnp.where(past >= -first, s[:, :tokens], NO_KEY)]
            scores += [s[:, (j + 1) * tokens : (j + 2) * tokens] for j in range(others)]
            top = jnp.max(functools.reduce(jnp.maximum, scores), axis=1, keepdims=True)
            probs = [jnp.exp2((part - top) * factor).astype(jnp.bfloat16) for part in scores]
            return jnp.concatenate(probs, axis=1), top

        def add_up(job, weighed):
            h, first = job
            probs, top = weighed
            both = jnp.dot(probs, v_ready[h], preferred_element_type=jnp.float32)
            if final:
                output.put(h, first, both)
            else:
                rows = pl.ds(first, ROW_CHUNK)
                state[0][h, rows, :] = jnp.broadcast_to(top, (ROW_CHUNK, dim))
                state[1][h, rows, :] = both

        in_turns([score, weigh, add_up], chunks_of(kv_dev, rows_all))
        output.wait()

    unfinished = False if last is None else has(bits, last)
    for others in range(most + 1):

        @pl.when(jnp.logical_and(count == others, jnp.logical_not(unfinished)))
        def _whole(others=others):
            run(others, True)

        if last is not None and others < most:

            @pl.when(jnp.logical_and(count == others, unfinished))
            def _part(others=others):
                run(others, False)


def attend(lists, queries, k_own, v_own, k_parts, v_parts, codes, code, last):
    kv_dev, rows, dim = queries.shape
    tokens = k_own.shape[1]
    rest = (lists.shape[0] - 1) * tokens * kv_dev
    out = jax.ShapeDtypeStruct((tokens, rows * kv_dev // tokens, dim), jnp.bfloat16)
    state = [] if last is None else [
        jax.ShapeDtypeStruct((kv_dev, rows, wide), jnp.float32) for wide in (dim, 2 * dim)
    ]
    hbm = pl.BlockSpec(memory_space=pltpu.HBM)
    return pl.pallas_call(
        functools.partial(attend_kernel, codes=codes, code=code, last=last),
        out_shape=(out, *state),
        in_specs=[vmem()] * (4 + 2 * len(k_parts)),
        out_specs=(hbm, *(vmem() for _ in state)),
        scratch_shapes=[
            pltpu.VMEM((rest, dim), jnp.float32),
            pltpu.VMEM((rest, dim), jnp.float32),
            pltpu.VMEM(out.shape, jnp.bfloat16),
            pltpu.SemaphoreType.DMA((rows // ROW_CHUNK,)),
        ],
        compiler_params=params(),
        name="attend",
    )(lists, queries, k_own, v_own, *k_parts, *v_parts)


def last_kernel(
    lists_ref, q_ref, top_ref, both_ref, k_ref, v_ref, _, out_hbm, k_wide, v_wide, out_ref, sems, *, code, last
):
    kv_dev, rows_all, dim = q_ref.shape
    tokens = k_ref.shape[0] // kv_dev
    group = rows_all // tokens
    factor = dim ** (-0.5) * math.log2(math.e)

    @pl.when(has(listed_bits(lists_ref, code), last))
    def _add():
        k_wide[...] = k_ref[...].astype(jnp.float32)
        v_wide[...] = v_ref[...].astype(jnp.float32)
        k_ready = [by_head(k_wide, h, kv_dev, tokens) for h in range(kv_dev)]
        v_ready = [with_ones(by_head(v_wide, h, kv_dev, tokens)) for h in range(kv_dev)]
        jobs = chunks_of(kv_dev, rows_all)
        output = Output(out_ref, out_hbm, sems, kv_dev, group)
        shifts = []

        def score(job, _):
            h, first = job
            return scores_of(q_ref[h, pl.ds(first, ROW_CHUNK), :], k_ready[h])

        def weigh(job, s):
            h, first = job
            shifted = (s - top_ref[h, pl.ds(first, ROW_CHUNK), :]) * factor
            shifts.append(jnp.max(shifted.reshape(ROW_CHUNK // 8, 8, tokens), axis=0))
            return jnp.exp2(shifted).astype(jnp.bfloat16)

        def add_up(job, probs):
            h, first = job
            both = jnp.dot(probs, v_ready[h], preferred_element_type=jnp.float32)
            output.put(h, first, both + both_ref[h, pl.ds(first, ROW_CHUNK), :])

        in_turns([score, weigh, add_up], jobs)
        output.wait()

        @pl.when(jnp.max(functools.reduce(jnp.maximum, shifts)) > LARGEST)
        def _rescale():
            again = Output(out_ref, out_hbm, sems, kv_dev, group)
            for h, first in jobs:
                rows = pl.ds(first, ROW_CHUNK)
                s = scores_of(q_ref[h, rows, :], k_ready[h])
                before = top_ref[h, rows, :]
                top = jnp.maximum(before, jnp.max(s, axis=1, keepdims=True))
                probs = jnp.exp2((s - top) * factor).astype(jnp.bfloat16)
                shrink = jnp.exp2((before - top) * factor)
                both = both_ref[h, rows, :] * jnp.concatenate([shrink, shrink], axis=1)
                both += jnp.dot(probs, v_ready[h], preferred_element_type=jnp.float32)
                again.put(h, first, both)
            again.wait()


def attend_last(lists, queries, state, k_last, v_last, out, code, last):
    top, both = state
    hbm = pl.BlockSpec(memory_space=pltpu.HBM)
    return pl.pallas_call(
        functools.partial(last_kernel, code=code, last=last),
        out_shape=jax.ShapeDtypeStruct(out.shape, out.dtype),
        in_specs=[vmem()] * 6 + [hbm],
        out_specs=hbm,
        input_output_aliases={6: 0},
        scratch_shapes=[
            pltpu.VMEM(k_last.shape, jnp.float32),
            pltpu.VMEM(k_last.shape, jnp.float32),
            pltpu.VMEM(out.shape, jnp.bfloat16),
            pltpu.SemaphoreType.DMA((queries.shape[1] // ROW_CHUNK,)),
        ],
        compiler_params=params(),
        name="attend_last",
    )(lists, queries, top, both, k_last, v_last, out)


def ring_place(block, members):
    return jnp.where((block & 1) == 0, block >> 1, members - 1 - (block >> 1))


def ring_code(members):
    def code(block, target):
        ahead = ring_place(block, members) - ring_place(target, members)
        return jnp.where(ahead < 0, ahead + members, ahead)

    return code


LAST_KEYS = {1: 2, 2: 3, 3: 4, 4: 5, 5: 6, 6: 1}, {}
LAST_VALUES = {1: 6, 2: 5, 3: 1, 4: 3, 5: 2, 6: 4}, {2: 0, 4: 4, 5: 1, 6: 3}


def round_the_ring(k_own, v_own, ready, members):
    ring = list(range(0, members, 2)) + list(range(members - 1, 0, -2))
    cores = lax.axis_size("head")
    here = ring_place(lax.axis_index("seq").astype(jnp.int32), members)

    def send(x, turn):
        return lax.ppermute(x, "seq", [(ring[p], ring[(p + turn) % members]) for p in range(members)])

    def send_last(parts, plan):
        steps, whats = plan
        x = parts[-1]
        for place, what in whats.items():
            x = jnp.where(here == place, parts[what], x)
        pairs = []
        for p in range(members):
            for core in range(cores):
                to = (steps[p], core) if p in steps else (p, (core + 1) % cores)
                pairs.append((ring[p] * cores + core, ring[to[0]] * cores + to[1]))
        return lax.ppermute(x, ("seq", "head"), pairs)

    half = members // 2
    k_two, v_two, k_all, v_all = [k_own, k_own], [v_own, v_own], [], []
    for distance in range(1, half):
        ahead = send(k_two[0], 1), send(v_two[1], -1)
        if distance == 1:
            k_two[1], v_two[0], ready = lax.optimization_barrier((k_two[1], v_two[0], ready))
        behind = send(v_two[0], 1), send(k_two[1], -1)
        ahead = lax.optimization_barrier(ahead)
        k_two, v_two = [ahead[0], behind[1]], [behind[0], ahead[1]]
        k_all += k_two
        v_all += v_two
    k_last = send_last(k_all[:-1], LAST_KEYS)
    v_last = send_last(v_all[:-2] + v_all[-1:], LAST_VALUES)
    return k_all, v_all, k_last, v_last, ready


def others(row, target):
    slots = row.shape[-1]
    own_at = jnp.argmax(row == target[..., None], axis=-1)
    j = jnp.arange(slots - 1)
    return jnp.where(j >= own_at[..., None], row[..., 1:], row[..., :-1])


def relay(k_own, v_own, chosen, members):
    block, dim = k_own.shape
    stacked = jnp.stack([k_own, v_own]).reshape(2, members, block // members, dim)
    shares = lax.all_to_all(stacked, "seq", split_axis=1, concat_axis=1, tiled=True)
    wanted = others(chosen, jnp.arange(members, dtype=jnp.int32))
    picked = jnp.take(shares, jnp.maximum(wanted, 0), axis=1)
    arrived = lax.all_to_all(picked, "seq", split_axis=1, concat_axis=3, tiled=True)
    count = wanted.shape[1]
    k_parts, v_parts = ([arrived[n, 0, j].reshape(block, dim) for j in range(count)] for n in range(2))
    return k_parts, v_parts, jnp.where(wanted < 0, -1, jnp.arange(count, dtype=jnp.int32))


def per_device(queries, keys, values, chosen):
    members = lax.axis_size("seq")
    tokens, kv_dev, dim = keys.shape
    k_own = keys.reshape(tokens * kv_dev, dim)
    v_own = values.reshape(tokens * kv_dev, dim)
    if members in ROUND:
        ready = prepare(chosen.T, queries, k_own, v_own, kv_dev)
        k_parts, v_parts, k_last, v_last, ready = round_the_ring(k_own, v_own, ready, members)
        lists, q_ready, k_ready, v_ready = ready
        half, code = members // 2, ring_code(members)
        codes = [turn for far in range(1, half) for turn in (members - far, far)]
        out, *state = attend(
            lists, q_ready, k_ready, v_ready, k_parts, v_parts, codes, code, half
        )
        return attend_last(lists, q_ready, state, k_last, v_last, out, code, half)

    k_parts, v_parts, mine = relay(k_own, v_own, chosen, members)
    lists, *ready = prepare(mine.T, queries, k_own, v_own, kv_dev)
    lists = jnp.concatenate([lists, jnp.full_like(lists[:1], -1)])
    codes = list(range(len(k_parts)))
    return attend(lists, *ready, k_parts, v_parts, codes, lambda block, _: block, None)[0]


def solution(mesh):
    rows = P(("groups", "seq"), "head", None)
    return jax.shard_map(
        per_device,
        mesh=mesh,
        in_specs=(rows, rows, rows, P("groups", None)),
        out_specs=rows,
        check_vma=False,
    )
```

```python
import functools
import math

import jax
import jax.numpy as jnp
from jax import lax
from jax.experimental import pallas as pl
from jax.experimental.pallas import tpu as pltpu
from jax.sharding import PartitionSpec as P

NO_KEY = -1e30
LARGEST = 64.0
ROUND = (8,)


def params():
    return pltpu.CompilerParams(vmem_limit_bytes=16 * 2**20)


def vmem():
    return pl.BlockSpec(memory_space=pltpu.VMEM)


def prepare_kernel(
    lists_hbm, q_hbm, k_hbm, v_hbm, lists_out, q_out, k_out, v_out,
    q_ref, k_ref, v_ref, k_wide, v_wide, sems, *, kv_dev,
):
    whole = ((k_hbm, k_ref), (v_hbm, v_ref), (q_hbm, q_ref), (lists_hbm, lists_out))
    copies = [
        pltpu.make_async_copy(source, here, sems.at[n]) for n, (source, here) in enumerate(whole)
    ]
    for copy in copies:
        copy.start()
    tokens, heads, dim = q_ref.shape
    group = heads // kv_dev
    for copy, ref, wide, out in zip(copies, (k_ref, v_ref), (k_wide, v_wide), (k_out, v_out)):
        copy.wait()
        wide[...] = ref[...].astype(jnp.float32)
        for h in range(kv_dev):
            out[h] = wide[pl.ds(h, tokens, stride=kv_dev), :].astype(jnp.bfloat16)
    copies[2].wait()
    for h in range(kv_dev):
        q = q_ref[:, pl.ds(h * group, group), :].astype(jnp.float32)
        q_out[h] = q.reshape(tokens * group, dim).astype(jnp.bfloat16)
    copies[3].wait()


def prepare(lists, queries, k_own, v_own, kv_dev):
    tokens, heads, dim = queries.shape
    operands = [
        pltpu.with_memory_space_constraint(x, pltpu.HBM) for x in (lists, queries, k_own, v_own)
    ]
    by_head = jax.ShapeDtypeStruct((kv_dev, tokens, dim), jnp.bfloat16)
    return pl.pallas_call(
        functools.partial(prepare_kernel, kv_dev=kv_dev),
        out_shape=(
            jax.ShapeDtypeStruct(lists.shape, lists.dtype),
            jax.ShapeDtypeStruct((kv_dev, tokens * heads // kv_dev, dim), jnp.bfloat16),
            by_head,
            by_head,
        ),
        in_specs=[pl.BlockSpec(memory_space=pltpu.HBM)] * 4,
        out_specs=(vmem(), vmem(), vmem(), vmem()),
        scratch_shapes=[
            pltpu.VMEM(queries.shape, jnp.bfloat16),
            pltpu.VMEM(k_own.shape, jnp.bfloat16),
            pltpu.VMEM(k_own.shape, jnp.bfloat16),
            pltpu.VMEM(k_own.shape, jnp.float32),
            pltpu.VMEM(k_own.shape, jnp.float32),
            pltpu.SemaphoreType.DMA((4,)),
        ],
        compiler_params=params(),
        name="prepare",
    )(*operands)


def listed_bits(lists_ref, code):
    target = lax.axis_index("seq").astype(jnp.int32)
    entries = lists_ref[...]
    mine = lax.broadcasted_iota(jnp.int32, entries.shape, 1) == target
    bits = jnp.left_shift(1, code(jnp.maximum(entries, 0), target)).astype(jnp.float32)
    return jnp.sum(jnp.where(jnp.logical_and(mine, entries >= 0), bits, 0.0)).astype(jnp.int32)


def has(bits, code):
    return jnp.bitwise_and(lax.shift_right_logical(bits, jnp.int32(code)), 1) == 1


def by_head(wide, h, kv_dev, keys):
    return wide[pl.ds(h, keys, stride=kv_dev), :].astype(jnp.bfloat16)


def with_ones(values):
    return jnp.concatenate([values, jnp.ones_like(values)], axis=1)


class Once(dict):
    def __init__(self, make):
        super().__init__()
        self.make = make

    def __missing__(self, h):
        self[h] = self.make(h)
        return self[h]


class Output:
    def __init__(self, out_ref, out_hbm, sems, kv_dev, group):
        self.out_ref, self.out_hbm, self.sems = out_ref, out_hbm, sems
        self.kv_dev, self.group, self.copies, self.before = kv_dev, group, [], None

    def put(self, h, first, both):
        rows, dim = both.shape[0], both.shape[1] // 2
        merged = both[:, :dim] * pl.reciprocal(both[:, dim:])
        merged = merged.reshape(rows // self.group, self.group, dim)
        if h % 2 == 0:
            self.before = merged
            return
        here = pl.ds(first // self.group, rows // self.group)
        heads = pl.ds((h - 1) * self.group, 2 * self.group)
        two = jnp.concatenate([self.before, merged], axis=1)
        self.out_ref[here, heads, :] = two.astype(jnp.bfloat16)
        if h + 1 == self.kv_dev:
            self.copies.append(
                pltpu.make_async_copy(
                    self.out_ref.at[here], self.out_hbm.at[here], self.sems.at[len(self.copies)]
                )
            )
            self.copies[-1].start()

    def wait(self):
        for copy in self.copies:
            copy.wait()


def row_chunk(blocks):
    return 512 if blocks % 2 else 256


def chunks_of(kv_dev, rows_all, chunk):
    return [(h, first) for first in range(0, rows_all, chunk) for h in range(kv_dev)]


def in_turns(stages, jobs):
    held = {}
    for turn in range(len(jobs) + len(stages) - 1):
        for n, stage in enumerate(stages):
            at = turn - n
            if 0 <= at < len(jobs):
                held[at] = stage(jobs[at], held.get(at))
        held.pop(turn - len(stages) + 1, None)


def scores_of(q, keys):
    return lax.dot_general(q, keys, (((1,), (1,)), ((), ())), preferred_element_type=jnp.float32)


def attend_kernel(lists_ref, q_ref, k_own_ref, v_own_ref, *refs, codes, code, last):
    parts = len(codes)
    k_parts, v_parts = refs[:parts], refs[parts : 2 * parts]
    out_hbm, *state, k_wide, v_wide, out_ref, sems = refs[2 * parts :]
    kv_dev, tokens, dim = k_own_ref.shape
    rows_all = q_ref.shape[1]
    group = rows_all // tokens
    block = tokens * kv_dev
    most = k_wide.shape[0] // block
    factor = dim ** (-0.5) * math.log2(math.e)

    bits = listed_bits(lists_ref, code)
    count = jnp.int32(0)
    for part_code, k_part, v_part in zip(codes, k_parts, v_parts):
        take = has(bits, part_code)

        @pl.when(take)
        def _take(k_part=k_part, v_part=v_part, count=count):
            rows = pl.ds(pl.multiple_of(count * block, block), block)
            k_wide[rows, :] = k_part[...].astype(jnp.float32)
            v_wide[rows, :] = v_part[...].astype(jnp.float32)

        count += take.astype(jnp.int32)

    def run(others, final):
        keys = (others + 1) * tokens
        chunk = row_chunk(others + 1 if final else 0)
        output = Output(out_ref, out_hbm, sems, kv_dev, group)

        def keys_of(h):
            if not others:
                return k_own_ref[h]
            return jnp.concatenate([k_own_ref[h], by_head(k_wide, h, kv_dev, keys - tokens)], axis=0)

        def values_of(h):
            if not others:
                return with_ones(v_own_ref[h])
            rest = by_head(v_wide, h, kv_dev, keys - tokens)
            return with_ones(jnp.concatenate([v_own_ref[h], rest], axis=0))

        k_ready, v_ready = Once(keys_of), Once(values_of)
        past = lax.broadcasted_iota(jnp.int32, (chunk, tokens), 0)
        past -= group * lax.broadcasted_iota(jnp.int32, (chunk, tokens), 1)

        def score(job, _):
            h, first = job
            return scores_of(q_ref[h, pl.ds(first, chunk), :], k_ready[h])

        def weigh(job, s):
            first = job[1]
            scores = [jnp.where(past >= -first, s[:, :tokens], NO_KEY)]
            scores += [s[:, (j + 1) * tokens : (j + 2) * tokens] for j in range(others)]
            top = jnp.max(functools.reduce(jnp.maximum, scores), axis=1, keepdims=True)
            probs = [jnp.exp2((part - top) * factor).astype(jnp.bfloat16) for part in scores]
            return jnp.concatenate(probs, axis=1), top

        def add_up(job, weighed):
            h, first = job
            probs, top = weighed
            both = jnp.dot(probs, v_ready[h], preferred_element_type=jnp.float32)
            if final:
                output.put(h, first, both)
            else:
                rows = pl.ds(first, chunk)
                state[0][h, rows, :] = jnp.broadcast_to(top, (chunk, dim))
                state[1][h, rows, :] = both

        in_turns([score, weigh, add_up], chunks_of(kv_dev, rows_all, chunk))
        output.wait()

    unfinished = False if last is None else has(bits, last)
    for others in range(most + 1):

        @pl.when(jnp.logical_and(count == others, jnp.logical_not(unfinished)))
        def _whole(others=others):
            run(others, True)

        if last is not None and others < most:

            @pl.when(jnp.logical_and(count == others, unfinished))
            def _part(others=others):
                run(others, False)


def attend(lists, queries, k_own, v_own, k_parts, v_parts, codes, code, last):
    kv_dev, rows, dim = queries.shape
    tokens = k_own.shape[1]
    rest = (lists.shape[0] - 1) * tokens * kv_dev
    out = jax.ShapeDtypeStruct((tokens, rows * kv_dev // tokens, dim), jnp.bfloat16)
    state = [] if last is None else [
        jax.ShapeDtypeStruct((kv_dev, rows, wide), jnp.float32) for wide in (dim, 2 * dim)
    ]
    hbm = pl.BlockSpec(memory_space=pltpu.HBM)
    return pl.pallas_call(
        functools.partial(attend_kernel, codes=codes, code=code, last=last),
        out_shape=(out, *state),
        in_specs=[vmem()] * (4 + 2 * len(k_parts)),
        out_specs=(hbm, *(vmem() for _ in state)),
        scratch_shapes=[
            pltpu.VMEM((rest, dim), jnp.float32),
            pltpu.VMEM((rest, dim), jnp.float32),
            pltpu.VMEM(out.shape, jnp.bfloat16),
            pltpu.SemaphoreType.DMA((rows // row_chunk(0),)),
        ],
        compiler_params=params(),
        name="attend",
    )(lists, queries, k_own, v_own, *k_parts, *v_parts)


def last_kernel(
    lists_ref, q_ref, top_ref, both_ref, k_ref, v_ref, _, out_hbm, k_wide, v_wide, out_ref, sems, *, code, last
):
    kv_dev, rows_all, dim = q_ref.shape
    tokens = k_ref.shape[0] // kv_dev
    group = rows_all // tokens
    factor = dim ** (-0.5) * math.log2(math.e)

    @pl.when(has(listed_bits(lists_ref, code), last))
    def _add():
        k_wide[...] = k_ref[...].astype(jnp.float32)
        v_wide[...] = v_ref[...].astype(jnp.float32)
        k_ready = Once(lambda h: by_head(k_wide, h, kv_dev, tokens))
        v_ready = Once(lambda h: with_ones(by_head(v_wide, h, kv_dev, tokens)))
        chunk = row_chunk(0)
        jobs = chunks_of(kv_dev, rows_all, chunk)
        output = Output(out_ref, out_hbm, sems, kv_dev, group)
        shifts = []

        def score(job, _):
            h, first = job
            return scores_of(q_ref[h, pl.ds(first, chunk), :], k_ready[h])

        def weigh(job, s):
            h, first = job
            shifted = (s - top_ref[h, pl.ds(first, chunk), :]) * factor
            shifts.append(jnp.max(shifted.reshape(chunk // 8, 8, tokens), axis=0))
            return jnp.exp2(shifted).astype(jnp.bfloat16)

        def add_up(job, probs):
            h, first = job
            both = jnp.dot(probs, v_ready[h], preferred_element_type=jnp.float32)
            output.put(h, first, both + both_ref[h, pl.ds(first, chunk), :])

        in_turns([score, weigh, add_up], jobs)
        output.wait()

        @pl.when(jnp.max(functools.reduce(jnp.maximum, shifts)) > LARGEST)
        def _rescale():
            again = Output(out_ref, out_hbm, sems, kv_dev, group)
            for h, first in jobs:
                rows = pl.ds(first, chunk)
                s = scores_of(q_ref[h, rows, :], k_ready[h])
                before = top_ref[h, rows, :]
                top = jnp.maximum(before, jnp.max(s, axis=1, keepdims=True))
                probs = jnp.exp2((s - top) * factor).astype(jnp.bfloat16)
                shrink = jnp.exp2((before - top) * factor)
                both = both_ref[h, rows, :] * jnp.concatenate([shrink, shrink], axis=1)
                both += jnp.dot(probs, v_ready[h], preferred_element_type=jnp.float32)
                again.put(h, first, both)
            again.wait()


def attend_last(lists, queries, state, k_last, v_last, out, code, last):
    top, both = state
    hbm = pl.BlockSpec(memory_space=pltpu.HBM)
    return pl.pallas_call(
        functools.partial(last_kernel, code=code, last=last),
        out_shape=jax.ShapeDtypeStruct(out.shape, out.dtype),
        in_specs=[vmem()] * 6 + [hbm],
        out_specs=hbm,
        input_output_aliases={6: 0},
        scratch_shapes=[
            pltpu.VMEM(k_last.shape, jnp.float32),
            pltpu.VMEM(k_last.shape, jnp.float32),
            pltpu.VMEM(out.shape, jnp.bfloat16),
            pltpu.SemaphoreType.DMA((queries.shape[1] // row_chunk(0),)),
        ],
        compiler_params=params(),
        name="attend_last",
    )(lists, queries, top, both, k_last, v_last, out)


def ring_place(block, members):
    return jnp.where((block & 1) == 0, block >> 1, members - 1 - (block >> 1))


def ring_code(members):
    def code(block, target):
        ahead = ring_place(block, members) - ring_place(target, members)
        return jnp.where(ahead < 0, ahead + members, ahead)

    return code


LAST_KEYS = {1: 2, 2: 3, 3: 4, 4: 5, 5: 1}, {}
LAST_VALUES = {1: 6, 2: 5, 3: 1, 4: 3, 5: 2, 6: 4}, {2: 0, 4: 4, 5: 1, 6: 3}


def round_the_ring(k_own, v_own, ready, members):
    ring = list(range(0, members, 2)) + list(range(members - 1, 0, -2))
    cores = lax.axis_size("head")
    here = ring_place(lax.axis_index("seq").astype(jnp.int32), members)

    def send(x, turn):
        return lax.ppermute(x, "seq", [(ring[p], ring[(p + turn) % members]) for p in range(members)])

    def send_last(parts, plan):
        steps, whats = plan
        x = parts[-1]
        for place, what in whats.items():
            x = jnp.where(here == place, parts[what], x)
        pairs = []
        for p in range(members):
            for core in range(cores):
                to = (steps[p], core) if p in steps else (p, (core + 1) % cores)
                pairs.append((ring[p] * cores + core, ring[to[0]] * cores + to[1]))
        return lax.ppermute(x, ("seq", "head"), pairs)

    half = members // 2
    k_two, v_two, k_all, v_all = [k_own, k_own], [v_own, v_own], [], []
    for distance in range(1, half):
        ahead = send(k_two[0], 1), send(v_two[1], -1)
        if distance == 1:
            k_two[1], v_two[0], ready = lax.optimization_barrier((k_two[1], v_two[0], ready))
        behind = send(v_two[0], 1), send(k_two[1], -1)
        ahead = lax.optimization_barrier(ahead)
        behind = lax.optimization_barrier(behind)
        k_two, v_two = [ahead[0], behind[1]], [behind[0], ahead[1]]
        k_all += k_two
        v_all += v_two
    k_last = send_last(k_all[:-1], LAST_KEYS)
    v_last = send_last(v_all[:-2] + v_all[-1:], LAST_VALUES)
    return k_all, v_all, k_last, v_last, ready


def others(row, target):
    slots = row.shape[-1]
    own_at = jnp.argmax(row == target[..., None], axis=-1)
    j = jnp.arange(slots - 1)
    return jnp.where(j >= own_at[..., None], row[..., 1:], row[..., :-1])


def relay(k_own, v_own, chosen, members):
    block, dim = k_own.shape
    stacked = jnp.stack([k_own, v_own]).reshape(2, members, block // members, dim)
    shares = lax.all_to_all(stacked, "seq", split_axis=1, concat_axis=1, tiled=True)
    wanted = others(chosen, jnp.arange(members, dtype=jnp.int32))
    picked = jnp.take(shares, jnp.maximum(wanted, 0), axis=1)
    arrived = lax.all_to_all(picked, "seq", split_axis=1, concat_axis=3, tiled=True)
    count = wanted.shape[1]
    k_parts, v_parts = ([arrived[n, 0, j].reshape(block, dim) for j in range(count)] for n in range(2))
    return k_parts, v_parts, jnp.where(wanted < 0, -1, jnp.arange(count, dtype=jnp.int32))


def per_device(queries, keys, values, chosen):
    members = lax.axis_size("seq")
    tokens, kv_dev, dim = keys.shape
    k_own = keys.reshape(tokens * kv_dev, dim)
    v_own = values.reshape(tokens * kv_dev, dim)
    if members in ROUND:
        ready = prepare(chosen.T, queries, k_own, v_own, kv_dev)
        k_parts, v_parts, k_last, v_last, ready = round_the_ring(k_own, v_own, ready, members)
        lists, q_ready, k_ready, v_ready = ready
        half, code = members // 2, ring_code(members)
        codes = [turn for far in range(1, half) for turn in (members - far, far)]
        out, *state = attend(
            lists, q_ready, k_ready, v_ready, k_parts, v_parts, codes, code, half
        )
        return attend_last(lists, q_ready, state, k_last, v_last, out, code, half)

    k_parts, v_parts, mine = relay(k_own, v_own, chosen, members)
    lists, *ready = prepare(mine.T, queries, k_own, v_own, kv_dev)
    lists = jnp.concatenate([lists, jnp.full_like(lists[:1], -1)])
    codes = list(range(len(k_parts)))
    return attend(lists, *ready, k_parts, v_parts, codes, lambda block, _: block, None)[0]


def solution(mesh):
    rows = P(("groups", "seq"), "head", None)
    return jax.shard_map(
        per_device,
        mesh=mesh,
        in_specs=(rows, rows, rows, P("groups", None)),
        out_specs=rows,
        check_vma=False,
    )
```

```python
import functools
import math

import jax
import jax.numpy as jnp
from jax import lax
from jax.experimental import pallas as pl
from jax.experimental.pallas import tpu as pltpu
from jax.sharding import PartitionSpec as P

NO_KEY = -1e30
LARGEST = 64.0
ROUND = (8,)


def params():
    return pltpu.CompilerParams(vmem_limit_bytes=16 * 2**20)


def vmem():
    return pl.BlockSpec(memory_space=pltpu.VMEM)


def prepare_kernel(
    lists_hbm, q_hbm, k_hbm, v_hbm, lists_out, q_out, k_out, v_out,
    q_ref, k_ref, v_ref, k_wide, v_wide, sems, *, kv_dev,
):
    whole = ((k_hbm, k_ref), (v_hbm, v_ref), (q_hbm, q_ref), (lists_hbm, lists_out))
    copies = [
        pltpu.make_async_copy(source, here, sems.at[n]) for n, (source, here) in enumerate(whole)
    ]
    for copy in copies:
        copy.start()
    tokens, heads, dim = q_ref.shape
    group = heads // kv_dev
    for copy, ref, wide, out in zip(copies, (k_ref, v_ref), (k_wide, v_wide), (k_out, v_out)):
        copy.wait()
        wide[...] = ref[...].astype(jnp.float32)
        for h in range(kv_dev):
            out[h] = wide[pl.ds(h, tokens, stride=kv_dev), :].astype(jnp.bfloat16)
    copies[2].wait()
    for h in range(kv_dev):
        q = q_ref[:, pl.ds(h * group, group), :].astype(jnp.float32)
        q_out[h] = q.reshape(tokens * group, dim).astype(jnp.bfloat16)
    copies[3].wait()


def prepare(lists, queries, k_own, v_own, kv_dev):
    tokens, heads, dim = queries.shape
    operands = [
        pltpu.with_memory_space_constraint(x, pltpu.HBM) for x in (lists, queries, k_own, v_own)
    ]
    by_head = jax.ShapeDtypeStruct((kv_dev, tokens, dim), jnp.bfloat16)
    return pl.pallas_call(
        functools.partial(prepare_kernel, kv_dev=kv_dev),
        out_shape=(
            jax.ShapeDtypeStruct(lists.shape, lists.dtype),
            jax.ShapeDtypeStruct((kv_dev, tokens * heads // kv_dev, dim), jnp.bfloat16),
            by_head,
            by_head,
        ),
        in_specs=[pl.BlockSpec(memory_space=pltpu.HBM)] * 4,
        out_specs=(vmem(), vmem(), vmem(), vmem()),
        scratch_shapes=[
            pltpu.VMEM(queries.shape, jnp.bfloat16),
            pltpu.VMEM(k_own.shape, jnp.bfloat16),
            pltpu.VMEM(k_own.shape, jnp.bfloat16),
            pltpu.VMEM(k_own.shape, jnp.float32),
            pltpu.VMEM(k_own.shape, jnp.float32),
            pltpu.SemaphoreType.DMA((4,)),
        ],
        compiler_params=params(),
        name="prepare",
    )(*operands)


def listed_bits(lists_ref, code):
    target = lax.axis_index("seq").astype(jnp.int32)
    entries = lists_ref[...]
    mine = lax.broadcasted_iota(jnp.int32, entries.shape, 1) == target
    bits = jnp.left_shift(1, code(jnp.maximum(entries, 0), target)).astype(jnp.float32)
    return jnp.sum(jnp.where(jnp.logical_and(mine, entries >= 0), bits, 0.0)).astype(jnp.int32)


def has(bits, code):
    return jnp.bitwise_and(lax.shift_right_logical(bits, jnp.int32(code)), 1) == 1


def by_head(wide, h, kv_dev, keys):
    return wide[pl.ds(h, keys, stride=kv_dev), :].astype(jnp.bfloat16)


def with_ones(values):
    return jnp.concatenate([values, jnp.ones_like(values)], axis=1)


class Once(dict):
    def __init__(self, make):
        super().__init__()
        self.make = make

    def __missing__(self, h):
        self[h] = self.make(h)
        return self[h]


class Output:
    def __init__(self, out_ref, out_hbm, sems, kv_dev, group):
        self.out_ref, self.out_hbm, self.sems = out_ref, out_hbm, sems
        self.kv_dev, self.group, self.copies, self.before = kv_dev, group, [], None

    def put(self, h, first, both):
        rows, dim = both.shape[0], both.shape[1] // 2
        merged = both[:, :dim] * pl.reciprocal(both[:, dim:])
        merged = merged.reshape(rows // self.group, self.group, dim)
        if h % 2 == 0:
            self.before = merged
            return
        here = pl.ds(first // self.group, rows // self.group)
        heads = pl.ds((h - 1) * self.group, 2 * self.group)
        two = jnp.concatenate([self.before, merged], axis=1)
        self.out_ref[here, heads, :] = two.astype(jnp.bfloat16)
        if h + 1 == self.kv_dev:
            self.copies.append(
                pltpu.make_async_copy(
                    self.out_ref.at[here], self.out_hbm.at[here], self.sems.at[len(self.copies)]
                )
            )
            self.copies[-1].start()

    def wait(self):
        for copy in self.copies:
            copy.wait()


def row_chunk(blocks):
    return 512 if blocks % 2 else 256


def chunks_of(kv_dev, rows_all, chunk):
    return [(h, first) for first in range(0, rows_all, chunk) for h in range(kv_dev)]


def in_turns(stages, jobs):
    held = {}
    for turn in range(len(jobs) + len(stages) - 1):
        for n, stage in enumerate(stages):
            at = turn - n
            if 0 <= at < len(jobs):
                held[at] = stage(jobs[at], held.get(at))
        held.pop(turn - len(stages) + 1, None)


def scores_of(q, keys):
    return lax.dot_general(q, keys, (((1,), (1,)), ((), ())), preferred_element_type=jnp.float32)


def attend_kernel(lists_ref, q_ref, k_own_ref, v_own_ref, *refs, codes, code, last):
    parts = len(codes)
    k_parts, v_parts = refs[:parts], refs[parts : 2 * parts]
    out_hbm, *state, k_wide, v_wide, out_ref, sems = refs[2 * parts :]
    kv_dev, tokens, dim = k_own_ref.shape
    rows_all = q_ref.shape[1]
    group = rows_all // tokens
    block = tokens * kv_dev
    most = k_wide.shape[0] // block
    factor = dim ** (-0.5) * math.log2(math.e)

    bits = listed_bits(lists_ref, code)
    count = jnp.int32(0)
    for part_code, k_part, v_part in zip(codes, k_parts, v_parts):
        take = has(bits, part_code)

        @pl.when(take)
        def _take(k_part=k_part, v_part=v_part, count=count):
            rows = pl.ds(pl.multiple_of(count * block, block), block)
            k_wide[rows, :] = k_part[...].astype(jnp.float32)
            v_wide[rows, :] = v_part[...].astype(jnp.float32)

        count += take.astype(jnp.int32)

    def run(others, final):
        keys = (others + 1) * tokens
        chunk = row_chunk(others + 1 if final else 0)
        output = Output(out_ref, out_hbm, sems, kv_dev, group)

        def keys_of(h):
            if not others:
                return k_own_ref[h]
            return jnp.concatenate([k_own_ref[h], by_head(k_wide, h, kv_dev, keys - tokens)], axis=0)

        def values_of(h):
            if not others:
                return with_ones(v_own_ref[h])
            rest = by_head(v_wide, h, kv_dev, keys - tokens)
            return with_ones(jnp.concatenate([v_own_ref[h], rest], axis=0))

        k_ready, v_ready = Once(keys_of), Once(values_of)
        past = lax.broadcasted_iota(jnp.int32, (chunk, tokens), 0)
        past -= group * lax.broadcasted_iota(jnp.int32, (chunk, tokens), 1)

        def score(job, _):
            h, first = job
            return scores_of(q_ref[h, pl.ds(first, chunk), :], k_ready[h])

        def weigh(job, s):
            first = job[1]
            scores = [jnp.where(past >= -first, s[:, :tokens], NO_KEY)]
            scores += [s[:, (j + 1) * tokens : (j + 2) * tokens] for j in range(others)]
            top = jnp.max(functools.reduce(jnp.maximum, scores), axis=1, keepdims=True)
            probs = [jnp.exp2((part - top) * factor).astype(jnp.bfloat16) for part in scores]
            return jnp.concatenate(probs, axis=1), top

        def add_up(job, weighed):
            h, first = job
            probs, top = weighed
            both = jnp.dot(probs, v_ready[h], preferred_element_type=jnp.float32)
            if final:
                output.put(h, first, both)
            else:
                rows = pl.ds(first, chunk)
                state[0][h, rows, :] = jnp.broadcast_to(top, (chunk, dim))
                state[1][h, rows, :] = both

        in_turns([score, weigh, add_up], chunks_of(kv_dev, rows_all, chunk))
        output.wait()

    unfinished = False if last is None else has(bits, last)
    for others in range(most + 1):

        @pl.when(jnp.logical_and(count == others, jnp.logical_not(unfinished)))
        def _whole(others=others):
            run(others, True)

        if last is not None and others < most:

            @pl.when(jnp.logical_and(count == others, unfinished))
            def _part(others=others):
                run(others, False)


def attend(lists, queries, k_own, v_own, k_parts, v_parts, codes, code, last):
    kv_dev, rows, dim = queries.shape
    tokens = k_own.shape[1]
    rest = (lists.shape[0] - 1) * tokens * kv_dev
    out = jax.ShapeDtypeStruct((tokens, rows * kv_dev // tokens, dim), jnp.bfloat16)
    state = [] if last is None else [
        jax.ShapeDtypeStruct((kv_dev, rows, wide), jnp.float32) for wide in (dim, 2 * dim)
    ]
    hbm = pl.BlockSpec(memory_space=pltpu.HBM)
    return pl.pallas_call(
        functools.partial(attend_kernel, codes=codes, code=code, last=last),
        out_shape=(out, *state),
        in_specs=[vmem()] * (4 + 2 * len(k_parts)),
        out_specs=(hbm, *(vmem() for _ in state)),
        scratch_shapes=[
            pltpu.VMEM((rest, dim), jnp.float32),
            pltpu.VMEM((rest, dim), jnp.float32),
            pltpu.VMEM(out.shape, jnp.bfloat16),
            pltpu.SemaphoreType.DMA((rows // row_chunk(0),)),
        ],
        compiler_params=params(),
        name="attend",
    )(lists, queries, k_own, v_own, *k_parts, *v_parts)


def last_kernel(
    lists_ref, q_ref, top_ref, both_ref, k_ref, v_ref, _, out_hbm, k_wide, v_wide, out_ref, sems, *, code, last
):
    kv_dev, rows_all, dim = q_ref.shape
    tokens = k_ref.shape[0] // kv_dev
    group = rows_all // tokens
    factor = dim ** (-0.5) * math.log2(math.e)

    @pl.when(has(listed_bits(lists_ref, code), last))
    def _add():
        k_wide[...] = k_ref[...].astype(jnp.float32)
        v_wide[...] = v_ref[...].astype(jnp.float32)
        k_ready = Once(lambda h: by_head(k_wide, h, kv_dev, tokens))
        v_ready = Once(lambda h: with_ones(by_head(v_wide, h, kv_dev, tokens)))
        chunk = row_chunk(0)
        jobs = chunks_of(kv_dev, rows_all, chunk)
        output = Output(out_ref, out_hbm, sems, kv_dev, group)
        shifts = []

        def score(job, _):
            h, first = job
            return scores_of(q_ref[h, pl.ds(first, chunk), :], k_ready[h])

        def weigh(job, s):
            h, first = job
            shifted = (s - top_ref[h, pl.ds(first, chunk), :]) * factor
            shifts.append(jnp.max(shifted.reshape(chunk // 8, 8, tokens), axis=0))
            return jnp.exp2(shifted).astype(jnp.bfloat16)

        def add_up(job, probs):
            h, first = job
            both = jnp.dot(probs, v_ready[h], preferred_element_type=jnp.float32)
            output.put(h, first, both + both_ref[h, pl.ds(first, chunk), :])

        in_turns([score, weigh, add_up], jobs)
        output.wait()

        @pl.when(jnp.max(functools.reduce(jnp.maximum, shifts)) > LARGEST)
        def _rescale():
            again = Output(out_ref, out_hbm, sems, kv_dev, group)
            for h, first in jobs:
                rows = pl.ds(first, chunk)
                s = scores_of(q_ref[h, rows, :], k_ready[h])
                before = top_ref[h, rows, :]
                top = jnp.maximum(before, jnp.max(s, axis=1, keepdims=True))
                probs = jnp.exp2((s - top) * factor).astype(jnp.bfloat16)
                shrink = jnp.exp2((before - top) * factor)
                both = both_ref[h, rows, :] * jnp.concatenate([shrink, shrink], axis=1)
                both += jnp.dot(probs, v_ready[h], preferred_element_type=jnp.float32)
                again.put(h, first, both)
            again.wait()


def attend_last(lists, queries, state, k_last, v_last, out, code, last):
    top, both = state
    hbm = pl.BlockSpec(memory_space=pltpu.HBM)
    return pl.pallas_call(
        functools.partial(last_kernel, code=code, last=last),
        out_shape=jax.ShapeDtypeStruct(out.shape, out.dtype),
        in_specs=[vmem()] * 6 + [hbm],
        out_specs=hbm,
        input_output_aliases={6: 0},
        scratch_shapes=[
            pltpu.VMEM(k_last.shape, jnp.float32),
            pltpu.VMEM(k_last.shape, jnp.float32),
            pltpu.VMEM(out.shape, jnp.bfloat16),
            pltpu.SemaphoreType.DMA((queries.shape[1] // row_chunk(0),)),
        ],
        compiler_params=params(),
        name="attend_last",
    )(lists, queries, top, both, k_last, v_last, out)


def ring_place(block, members):
    return jnp.where((block & 1) == 0, block >> 1, members - 1 - (block >> 1))


def ring_code(members):
    def code(block, target):
        ahead = ring_place(block, members) - ring_place(target, members)
        return jnp.where(ahead < 0, ahead + members, ahead)

    return code


LAST_KEYS = {1: 2, 2: 3, 3: 4, 4: 5, 5: 1}, {}
LAST_VALUES = {1: 6, 2: 5, 3: 1, 4: 3, 5: 2, 6: 4}, {2: 0, 4: 4, 5: 1, 6: 3}


def round_the_ring(k_own, v_own, ready, members):
    ring = list(range(0, members, 2)) + list(range(members - 1, 0, -2))
    cores = lax.axis_size("head")
    here = ring_place(lax.axis_index("seq").astype(jnp.int32), members)

    def send(x, turn):
        return lax.ppermute(x, "seq", [(ring[p], ring[(p + turn) % members]) for p in range(members)])

    def send_last(parts, plan):
        steps, whats = plan
        x = parts[-1]
        for place, what in whats.items():
            x = jnp.where(here == place, parts[what], x)
        pairs = []
        for p in range(members):
            for core in range(cores):
                to = (steps[p], core) if p in steps else (p, (core + 1) % cores)
                pairs.append((ring[p] * cores + core, ring[to[0]] * cores + to[1]))
        return lax.ppermute(x, ("seq", "head"), pairs)

    half = members // 2
    k_two, v_two, k_all, v_all = [k_own, k_own], [v_own, v_own], [], []
    for distance in range(1, half):
        ahead = send(k_two[0], 1), send(v_two[1], -1)
        if distance == 1:
            k_two[1], v_two[0], ready = lax.optimization_barrier((k_two[1], v_two[0], ready))
        behind = send(v_two[0], 1), send(k_two[1], -1)
        ahead = lax.optimization_barrier(ahead)
        if distance < half - 2:
            behind = lax.optimization_barrier(behind)
        k_two, v_two = [ahead[0], behind[1]], [behind[0], ahead[1]]
        k_all += k_two
        v_all += v_two
    k_last = send_last(k_all[:-1], LAST_KEYS)
    v_last = send_last(v_all[:-2] + v_all[-1:], LAST_VALUES)
    return k_all, v_all, k_last, v_last, ready


def others(row, target):
    slots = row.shape[-1]
    own_at = jnp.argmax(row == target[..., None], axis=-1)
    j = jnp.arange(slots - 1)
    return jnp.where(j >= own_at[..., None], row[..., 1:], row[..., :-1])


def relay(k_own, v_own, chosen, members):
    block, dim = k_own.shape
    stacked = jnp.stack([k_own, v_own]).reshape(2, members, block // members, dim)
    shares = lax.all_to_all(stacked, "seq", split_axis=1, concat_axis=1, tiled=True)
    wanted = others(chosen, jnp.arange(members, dtype=jnp.int32))
    picked = jnp.take(shares, jnp.maximum(wanted, 0), axis=1)
    arrived = lax.all_to_all(picked, "seq", split_axis=1, concat_axis=3, tiled=True)
    count = wanted.shape[1]
    k_parts, v_parts = ([arrived[n, 0, j].reshape(block, dim) for j in range(count)] for n in range(2))
    return k_parts, v_parts, jnp.where(wanted < 0, -1, jnp.arange(count, dtype=jnp.int32))


def per_device(queries, keys, values, chosen):
    members = lax.axis_size("seq")
    tokens, kv_dev, dim = keys.shape
    k_own = keys.reshape(tokens * kv_dev, dim)
    v_own = values.reshape(tokens * kv_dev, dim)
    if members in ROUND:
        ready = prepare(chosen.T, queries, k_own, v_own, kv_dev)
        k_parts, v_parts, k_last, v_last, ready = round_the_ring(k_own, v_own, ready, members)
        lists, q_ready, k_ready, v_ready = ready
        half, code = members // 2, ring_code(members)
        codes = [turn for far in range(1, half) for turn in (members - far, far)]
        out, *state = attend(
            lists, q_ready, k_ready, v_ready, k_parts, v_parts, codes, code, half
        )
        return attend_last(lists, q_ready, state, k_last, v_last, out, code, half)

    k_parts, v_parts, mine = relay(k_own, v_own, chosen, members)
    lists, *ready = prepare(mine.T, queries, k_own, v_own, kv_dev)
    lists = jnp.concatenate([lists, jnp.full_like(lists[:1], -1)])
    codes = list(range(len(k_parts)))
    return attend(lists, *ready, k_parts, v_parts, codes, lambda block, _: block, None)[0]


def solution(mesh):
    rows = P(("groups", "seq"), "head", None)
    return jax.shard_map(
        per_device,
        mesh=mesh,
        in_specs=(rows, rows, rows, P("groups", None)),
        out_specs=rows,
        check_vma=False,
    )
```
